32 devices in a mesh: gx: 4 (over z), gy: 4 (over y, core), gz: 2 (over x).
Axes of the slice: x: 2, y: 2, z: 4, core: 2. Of those that a mesh axis runs over, the one named last changes fastest.
Arguments:
- sol_pos: float32 [3, 4, 4, 2, 49152], P(None, 'gx', 'gy', 'gz'), as said below
- sol_vel: float32 [3, 4, 4, 2, 49152], P(None, 'gx', 'gy', 'gz'), may hold values from -6 to 6
- sol_rows: int32 [4, 4, 2], P('gx', 'gy', 'gz'), may hold values from 192 to 384, as said below
- mig_pos: float32 [3, 4, 4, 2, 6, 3072], P(None, 'gx', 'gy', 'gz'), as said below
- mig_vel: float32 [3, 4, 4, 2, 6, 3072], P(None, 'gx', 'gy', 'gz'), may hold values from -6 to 6
- mig_rows: int32 [4, 4, 2, 6], P('gx', 'gy', 'gz'), may hold values from 0 to 24, as said below
- bead_pos: float32 [3, 4, 4, 2, 256], P(None, 'gx', 'gy', 'gz'), as said below
- bead_vel: float32 [3, 4, 4, 2, 256], P(None, 'gx', 'gy', 'gz'), may hold values from -2.7 to 2.7
- bead_chains: int32 [4, 4, 2], P('gx', 'gy', 'gz'), may hold values from 5 to 32, as said below
- bond_list: int32 [2, 4, 4, 2, 224], P(None, 'gx', 'gy', 'gz'), may hold values from 0 to 255, as said below
- cell_axis: int32 [64, 64, 64], P('gx', 'gy', 'gz'), may hold values from 0 to 31
- shift: int32 [3], replicated, may hold values from 0 to 15
Outputs:
- sol_pos_out: float32 [3, 4, 4, 2, 67584], P(None, 'gx', 'gy', 'gz')
- sol_vel_out: float32 [3, 4, 4, 2, 67584], P(None, 'gx', 'gy', 'gz')
- bead_pos_out: float32 [3, 4, 4, 2, 256], P(None, 'gx', 'gy', 'gz')
- bead_vel_out: float32 [3, 4, 4, 2, 256], P(None, 'gx', 'gy', 'gz')
The draws below stay inside these ranges and needn't reach their ends.
Inputs may be any that keep to these rules, and one draw needn't show every extreme that they name: `sol_rows`: some device's resident slots are all live. `mig_rows`: some device receives full buffers across all six faces. `sol_pos`: every resident position lies in its device's region (cells i * 16 to (i + 1) * 16 - 1 along the first dimension, likewise for the others), and x * 16 is at least 0.1 from a whole number. `mig_pos`: buffer f holds positions in the region of the neighbour across face f, with the same margin. `bead_pos`: beads lie in their device's region with the same margin; bonded live beads are 0.88 to 1.13 apart and no two live beads are closer than 0.88. `bead_chains`: some device holds 32 chains. `bond_list`: a live bond joins two live slots of its device.
All inputs are finite; a program needn't handle non-finite values.
Results may differ from the reference program's by a relative error of at most 0.0003.
Values sent between devices are 32-bit elements; how exact they have to be, the bound alone decides.
No kernel may reach another device: no remote copies, remote signals or barrier semaphores. Data moves between devices by JAX's collectives and lax.ppermute only.
A program may use at most 128 MiB of HBM per device.

```python
import math
import jax
import jax.numpy as jnp
from jax import lax

CX = 16
CY = 16
CZ = 32
UNITS = 16
NAXES = 32
CHAIN = 8
CH_CAP = 32
M_ROWS = 24
NX = 64
NY = 64
NZ = 64
P_ROWS = 384
PCAP = 49152
MCAP = 3072
BEADS = 256
BONDS = 224
N_GX = 4
N_GY = 4
N_GZ = 2


def grid_counts():
    return (NX // CX, NY // CY, NZ // CZ)


def device_anchor(step_x, step_y, step_z):
    count_x, count_y, count_z = grid_counts()
    anchor_x = (jnp.arange(count_x) + step_x) % count_x * CX
    anchor_y = (jnp.arange(count_y) + step_y) % count_y * CY
    anchor_z = (jnp.arange(count_z) + step_z) % count_z * CZ
    return jnp.stack(jnp.broadcast_arrays(anchor_x[:, None, None], anchor_y[None, :, None], anchor_z[None, None, :])).astype(jnp.float32)


def fine_offset(key, extent_shape):
    return jax.random.uniform(key, extent_shape, jnp.float32, 0.1, 0.9)


def scatter_points(key, anchor, count):
    extent_shape = anchor.shape[1:] + (count,)
    streams = jax.random.split(key, 5)
    whole_cells = jnp.stack([jax.random.randint(streams[0], extent_shape, 0, CX), jax.random.randint(streams[1], extent_shape, 0, CY), jax.random.randint(streams[2], extent_shape, 0, CZ)])
    subcell = jax.random.randint(streams[3], (3,) + extent_shape, 0, UNITS)
    return anchor[..., None] + whole_cells.astype(jnp.float32) + (subcell.astype(jnp.float32) + fine_offset(streams[4], (3,) + extent_shape)) / UNITS


def draw_sol_pos(key, part):
    return scatter_points(jax.random.fold_in(key, 11), device_anchor(0, 0, 0), PCAP)


def draw_mig_pos(key, part):
    neighbours = [(-1, 0, 0), (1, 0, 0), (0, -1, 0), (0, 1, 0), (0, 0, -1), (0, 0, 1)]
    anchor = jnp.stack([device_anchor(offset_tuple[0], offset_tuple[1], offset_tuple[2]) for offset_tuple in neighbours], axis=-1)
    return scatter_points(jax.random.fold_in(key, 13), anchor, MCAP)


def draw_sol_rows(key, part):
    count_x, count_y, count_z = grid_counts()
    streams = jax.random.split(jax.random.fold_in(key, 17), 2)
    row_count = jax.random.randint(streams[0], (count_x * count_y * count_z,), P_ROWS // 2, P_ROWS + 1)
    chosen_dev = jax.random.randint(streams[1], (), 0, count_x * count_y * count_z)
    row_count = jnp.where(jnp.arange(count_x * count_y * count_z) == chosen_dev, P_ROWS, row_count)
    return row_count.reshape(count_x, count_y, count_z).astype(jnp.int32)


def draw_mig_rows(key, part):
    count_x, count_y, count_z = grid_counts()
    streams = jax.random.split(jax.random.fold_in(key, 19), 4)
    row_count = jax.random.randint(streams[0], (count_x, count_y, count_z, 6), 0, M_ROWS + 1)
    target_x = jax.random.randint(streams[1], (), 0, count_x)
    target_y = jax.random.randint(streams[2], (), 0, count_y)
    target_z = jax.random.randint(streams[3], (), 0, count_z)
    index_x = jnp.arange(count_x)[:, None, None, None]
    index_y = jnp.arange(count_y)[None, :, None, None]
    index_z = jnp.arange(count_z)[None, None, :, None]
    faces = jnp.arange(6)[None, None, None, :]
    face_dim = faces // 2
    face_sign = 2 * (faces % 2) - 1
    hit_x = (index_x + jnp.where(face_dim == 0, face_sign, 0)) % count_x == target_x
    hit_y = (index_y + jnp.where(face_dim == 1, face_sign, 0)) % count_y == target_y
    hit_z = (index_z + jnp.where(face_dim == 2, face_sign, 0)) % count_z == target_z
    full_face = hit_x & hit_y & hit_z
    return jnp.where(full_face, M_ROWS, row_count).astype(jnp.int32)


def fixed_segments():
    last_column = CX // CHAIN - 1
    plane = CY * CZ
    listed = [0, CZ - 1, (CY - 1) * CZ, last_column * plane + 4 * CZ + 4]
    if last_column > 0:
        listed.append(4 * CZ + 4)
    return listed


def bead_layout(key):
    count_x, count_y, count_z = grid_counts()
    devices = count_x * count_y * count_z
    streams = jax.random.split(jax.random.fold_in(key, 4242), 4)
    draw_level = jax.random.randint(streams[0], (devices,), 0, 16)
    chains = 5 + draw_level * draw_level * (CH_CAP - 5) // 225
    chosen_dev = jax.random.randint(streams[1], (), 0, devices)
    chains = jnp.where(jnp.arange(devices) == chosen_dev, CH_CAP, chains)
    segments = CX // CHAIN * CY * CZ
    fixed_rank = jnp.full((segments,), -1, jnp.int32)
    for rank_id, segment_id in enumerate(fixed_segments()):
        fixed_rank = fixed_rank.at[segment_id].set(rank_id)

    def pick_segments(sub_key):
        order = jax.random.permutation(sub_key, segments)
        place = jnp.argsort(order)
        score = jnp.where(fixed_rank >= 0, fixed_rank, 16 + place).astype(jnp.int32)
        return jnp.argsort(score)[:CH_CAP]
    chosen = jax.vmap(pick_segments)(jax.random.split(streams[2], devices))
    bead_ids = jnp.arange(BEADS)
    dead_flag = ((bead_ids // CHAIN)[None] >= chains[:, None]).astype(jnp.int32)
    scores = dead_flag * (4096 * BEADS) + jax.random.randint(streams[3], (devices, BEADS), 0, 4096) * BEADS + bead_ids[None]
    slot_bead = jnp.argsort(scores, axis=1)
    slot_of = jnp.argsort(slot_bead, axis=1)
    return (chains, chosen, slot_bead, slot_of)


def draw_bead_chains(key, part):
    count_x, count_y, count_z = grid_counts()
    chains, chosen, slot_bead, slot_of = bead_layout(key)
    return chains.reshape(count_x, count_y, count_z).astype(jnp.int32)


def draw_bond_list(key, part):
    count_x, count_y, count_z = grid_counts()
    chains, chosen, slot_bead, slot_of = bead_layout(key)
    bond_ids = jnp.arange(BONDS)
    head_bead = bond_ids // (CHAIN - 1) * CHAIN + bond_ids % (CHAIN - 1)
    first_end = slot_of[:, head_bead]
    second_end = slot_of[:, head_bead + 1]
    return jnp.stack([first_end, second_end]).reshape(2, count_x, count_y, count_z, BONDS).astype(jnp.int32)


def draw_bead_pos(key, part):
    count_x, count_y, count_z = grid_counts()
    devices = count_x * count_y * count_z
    chains, chosen, slot_bead, slot_of = bead_layout(key)
    chain_of = slot_bead // CHAIN
    place_in = slot_bead % CHAIN
    segment = jnp.take_along_axis(chosen, chain_of, axis=1)
    column = segment // (CY * CZ)
    remain = segment % (CY * CZ)
    lattice = jnp.stack([column * CHAIN + place_in, remain // CZ, remain % CZ]).astype(jnp.float32)
    anchor = device_anchor(0, 0, 0).reshape(3, devices, 1)
    streams = jax.random.split(jax.random.fold_in(key, 77), 2)
    subcell = jax.random.randint(streams[0], (3, devices, BEADS), 0, 2) + UNITS // 2 - 1
    placed = anchor + lattice + (subcell.astype(jnp.float32) + fine_offset(streams[1], (3, devices, BEADS))) / UNITS
    return placed.reshape(3, count_x, count_y, count_z, BEADS)


def plant(result, own_key, smallest, high):
    longest = result.shape.index(max(result.shape))
    spots = []
    for shift in (0, 1):
        where = [jax.random.randint(jax.random.fold_in(own_key, axis), (), 0, length) for axis, length in enumerate(result.shape)]
        where[longest] = (where[longest] + shift) % result.shape[longest]
        spots.append(tuple(where))
    return result.at[spots[0]].set(smallest).at[spots[1]].set(high)


def steps_of(rng, dims, cuts, least, high):
    def one(dim, blocks):
        heights = jax.random.uniform(jax.random.fold_in(jax.random.fold_in(rng, 6), dim), (blocks,), jnp.float32, least / len(cuts), high / len(cuts))
        return jnp.repeat(jnp.exp(heights), dims[dim] // blocks).reshape((-1,) + (1,) * (len(dims) - dim - 1))

    level = one(*cuts[0])
    for cut in cuts[1:]:
        level = level * one(*cut)
    return level


def normal_values(own_key, dims, width, bound, cuts=(), held_as=jnp.bfloat16):
    array = jax.random.normal(own_key, dims, jnp.float32) * width
    if len(cuts) > 0:
        array = steps_of(own_key, dims, cuts, -0.22, 0.18) * array
    return jnp.clip(array, min=-bound, max=bound).astype(held_as)


def setup_inputs(seed: int = 0) -> dict:
    streams_of = jax.random.split(jax.random.key(seed), 13)
    sol_pos = draw_sol_pos(jax.random.fold_in(streams_of[12], 71), 0)
    sol_vel = normal_values(streams_of[1], (3, N_GX, N_GY, N_GZ, PCAP), 1.0, 6.0, ((1, 4), (2, 4), (3, 2)), jnp.float32)
    sol_rows = draw_sol_rows(jax.random.fold_in(streams_of[12], 71), 0)
    mig_pos = draw_mig_pos(jax.random.fold_in(streams_of[12], 71), 0)
    mig_vel = normal_values(streams_of[4], (3, N_GX, N_GY, N_GZ, 6, MCAP), 1.0, 6.0, ((1, 4), (2, 4), (3, 2)), jnp.float32)
    mig_rows = draw_mig_rows(jax.random.fold_in(streams_of[12], 71), 0)
    bead_pos = draw_bead_pos(jax.random.fold_in(streams_of[12], 71), 0)
    bead_vel = normal_values(streams_of[7], (3, N_GX, N_GY, N_GZ, BEADS), 0.45, 2.7, ((1, 4), (2, 4), (3, 2)), jnp.float32)
    bead_chains = draw_bead_chains(jax.random.fold_in(streams_of[12], 71), 0)
    bond_list = draw_bond_list(jax.random.fold_in(streams_of[12], 71), 0)
    cell_axis = plant(jax.random.randint(streams_of[10], (NX, NY, NZ), 0, NAXES), jax.random.fold_in(streams_of[10], 1), 0, NAXES - 1).astype(jnp.int32)
    shift = jax.random.randint(streams_of[11], (3,), 0, UNITS).astype(jnp.int32)
    return dict(sol_pos=sol_pos, sol_vel=sol_vel, sol_rows=sol_rows, mig_pos=mig_pos, mig_vel=mig_vel, mig_rows=mig_rows, bead_pos=bead_pos, bead_vel=bead_vel, bead_chains=bead_chains, bond_list=bond_list, cell_axis=cell_axis, shift=shift)


bead_mass = 5.0
step_size = 0.02
spring = 30.0
reach_square = 2.25
far_point = -1000.0
cut_square = 2.0 ** (1.0 / 3.0)
turn_cosine = math.cos(130.0 * math.pi / 180.0)
turn_sine = math.sin(130.0 * math.pi / 180.0)
golden = math.pi * (3.0 - math.sqrt(5.0))

def axis_table():
    counter = jnp.arange(NAXES).astype(jnp.float32)
    height = 1.0 - (2.0 * counter + 1.0) / NAXES
    radius = jnp.sqrt(1.0 - height * height)
    return jnp.stack([radius * jnp.cos(golden * counter), radius * jnp.sin(golden * counter), height])

def rotate(relative, normal):
    along_axis = lax.optimization_barrier(jnp.sum(normal * relative, axis=0, keepdims=True))
    crossed = jnp.stack([normal[1] * relative[2] - normal[2] * relative[1], normal[2] * relative[0] - normal[0] * relative[2], normal[0] * relative[1] - normal[1] * relative[0]])
    return turn_cosine * relative + turn_sine * crossed + (1.0 - turn_cosine) * along_axis * normal

def pair_force(own_rows, ghost_rows):

    def add_block(running, ghost_block):
        differ = own_rows[:, :, None] - ghost_block[:, None, :]
        square = lax.optimization_barrier(jnp.sum(differ * differ, axis=0))
        inside = (square < cut_square) & (square > 0.25)
        inverse = 1.0 / jnp.where(inside, square, 1.0)
        sixth_power = inverse * inverse * inverse
        weight = jnp.where(inside, 24.0 * (2.0 * sixth_power * sixth_power - sixth_power) * inverse, 0.0)
        return (running + lax.optimization_barrier(jnp.sum(weight[None] * differ, axis=2)), None)
    running, unused = lax.scan(add_block, jnp.zeros_like(own_rows), ghost_rows)
    return running

def bond_force(own_rows, bond_pairs, bond_live):
    differ = own_rows[:, bond_pairs[0]] - own_rows[:, bond_pairs[1]]
    square = lax.optimization_barrier(jnp.sum(differ * differ, axis=0))
    weight = jnp.where(bond_live, -spring / (1.0 - square / reach_square), 0.0)
    pulling = weight[None] * differ
    slot_ids = jnp.arange(own_rows.shape[1], dtype=jnp.int32)
    first_hot = (bond_pairs[0][:, None] == slot_ids[None]).astype(own_rows.dtype)
    second_hot = (bond_pairs[1][:, None] == slot_ids[None]).astype(own_rows.dtype)
    return jnp.dot(pulling, first_hot, precision=lax.Precision.HIGHEST) - jnp.dot(pulling, second_hot, precision=lax.Precision.HIGHEST)

def ghost_blocks(position):
    count_x, count_y, count_z = position.shape[1:4]
    index_x = jnp.arange(count_x)[:, None, None]
    index_y = jnp.arange(count_y)[None, :, None]
    index_z = jnp.arange(count_z)[None, None, :]
    blocks = []
    for step_x in (-1, 0, 1):
        for step_y in (-1, 0, 1):
            for step_z in (-1, 0, 1):
                rolled = jnp.roll(position, (-step_x, -step_y, -step_z), axis=(1, 2, 3))
                image_shift = jnp.stack(jnp.broadcast_arrays(NX * ((index_x + step_x) // count_x), NY * ((index_y + step_y) // count_y), NZ * ((index_z + step_z) // count_z))).astype(position.dtype)
                blocks.append(rolled + image_shift[..., None])
    return jnp.stack(blocks, axis=4)

def all_forces(position, bond_pairs, bond_live):
    full_shape = position.shape
    devices = full_shape[1] * full_shape[2] * full_shape[3]
    ghosts = ghost_blocks(position).reshape(3, devices, 27, full_shape[4]).transpose(1, 2, 0, 3)
    own_all = position.reshape(3, devices, full_shape[4]).transpose(1, 0, 2)
    pair_all = bond_pairs.reshape(2, devices, -1).transpose(1, 0, 2)
    live_all = bond_live.reshape(devices, -1)

    def one_device(pieces):
        own_rows, ghost_rows, pair_rows, live_rows = pieces
        return pair_force(own_rows, ghost_rows) + bond_force(own_rows, pair_rows, live_rows)
    pushes = lax.map(one_device, (own_all, ghosts, pair_all, live_all))
    return pushes.transpose(1, 0, 2).reshape(full_shape)

def arrivals(buffers):
    pieces = []
    for face_id in range(6):
        along_axis = 1 + face_id // 2
        if face_id % 2 == 0:
            pieces.append(jnp.roll(buffers[:, :, :, :, face_id + 1], 1, axis=along_axis))
        else:
            pieces.append(jnp.roll(buffers[:, :, :, :, face_id - 1], -1, axis=along_axis))
    return jnp.concatenate(pieces, axis=-1)

def global_cell(position, shift):
    offset = shift.astype(position.dtype).reshape((3,) + (1,) * (position.ndim - 1))
    levels = jnp.floor(position * UNITS + offset).astype(jnp.int32) // UNITS
    return (levels[0] % NX * NY + levels[1] % NY) * NZ + levels[2] % NZ

def reference(sol_pos, sol_vel, sol_rows, mig_pos, mig_vel, mig_rows, bead_pos, bead_vel, bead_chains, bond_list, cell_axis, shift):
    resident_live = jnp.arange(PCAP, dtype=jnp.int32) < (128 * sol_rows)[..., None]
    arriving_rows = arrivals(mig_rows[None, ..., None])[0]
    arriving_live = jnp.arange(MCAP, dtype=jnp.int32) < (128 * arriving_rows)[..., None]
    arriving_live = arriving_live.reshape(arriving_live.shape[:3] + (6 * MCAP,))
    solvent_live = jnp.concatenate([resident_live, arriving_live], axis=-1)
    solvent_pos = jnp.concatenate([sol_pos, arrivals(mig_pos)], axis=-1)
    solvent_vel = jnp.concatenate([sol_vel, arrivals(mig_vel)], axis=-1)
    bead_live = jnp.arange(BEADS, dtype=jnp.int32) < (CHAIN * bead_chains)[..., None]
    bond_live = jnp.arange(BONDS, dtype=jnp.int32) < ((CHAIN - 1) * bead_chains)[..., None]
    solvent_count = solvent_live.size
    position = jnp.concatenate([solvent_pos.reshape(3, -1), bead_pos.reshape(3, -1)], axis=1)
    velocity = jnp.concatenate([solvent_vel.reshape(3, -1), bead_vel.reshape(3, -1)], axis=1)
    weight = jnp.concatenate([solvent_live.reshape(-1).astype(jnp.float32), bead_mass * bead_live.reshape(-1).astype(jnp.float32)])
    cell_id = global_cell(position, shift)
    moments = jnp.concatenate([weight[None], weight[None] * velocity], axis=0)
    moment_sums = jax.ops.segment_sum(moments.T, cell_id, num_segments=NX * NY * NZ)
    cell_mean = moment_sums[:, 1:] / jnp.maximum(moment_sums[:, :1], 1.0)
    normals = axis_table()[:, cell_axis.reshape(-1)]
    local_flow = cell_mean[cell_id].T
    collided = local_flow + rotate(velocity - local_flow, normals[:, cell_id])
    sol_new = collided[:, :solvent_count].reshape(solvent_vel.shape)
    bead_new = collided[:, solvent_count:].reshape(bead_vel.shape)
    sol_vel_out = jnp.where(solvent_live[None], sol_new, 0.0)
    cell_offset = solvent_pos - jnp.floor(solvent_pos) - 0.5
    sol_pos_out = jnp.where(solvent_live[None], cell_offset + 3.0 * step_size * sol_new, 0.0)
    half_kick = 0.5 * step_size / bead_mass

    def masked(bead_at):
        return jnp.where(bead_live[None], bead_at, far_point)
    moved = jnp.zeros_like(bead_pos)
    bead_speed = bead_new
    pushes = all_forces(masked(bead_pos + moved), bond_list, bond_live)
    for substep in range(3):
        bead_speed = bead_speed + half_kick * pushes
        moved = moved + step_size * bead_speed
        pushes = all_forces(masked(bead_pos + moved), bond_list, bond_live)
        bead_speed = bead_speed + half_kick * pushes
    return (sol_pos_out, sol_vel_out, jnp.where(bead_live[None], moved, 0.0), jnp.where(bead_live[None], bead_speed, 0.0))
```

```python
import functools
import math

import jax
import jax.numpy as jnp
from jax import lax
from jax.experimental import pallas as pl
from jax.experimental.pallas import tpu as pltpu
from jax.sharding import PartitionSpec as P

UNITS = 16
NAXES = 32
CHAIN = 8
LANES = 128
GROUP = 8

bead_mass = 5.0
step_size = 0.02
spring = 30.0
reach_square = 2.25
cut_square = 2.0 ** (1.0 / 3.0)
turn_cosine = math.cos(130.0 * math.pi / 180.0)
turn_sine = math.sin(130.0 * math.pi / 180.0)
golden = math.pi * (3.0 - math.sqrt(5.0))
half_kick = 0.5 * step_size / bead_mass
far_own = 3000.0
far_ghost = 9000.0
vmem_limit = 48 * 1024 * 1024
NT = (((1,), (1,)), ((), ()))
NN = (((1,), (0,)), ((), ()))
exact = lax.Precision.HIGHEST
f32 = jnp.float32
bf16 = jnp.bfloat16


def params():
    return pltpu.CompilerParams(vmem_limit_bytes=vmem_limit)


def vmem():
    return pl.BlockSpec(memory_space=pltpu.VMEM)


def smem():
    return pl.BlockSpec(memory_space=pltpu.SMEM)


def moved_along(value, axis, by):
    peers = lax.axis_size(axis)
    return lax.ppermute(value, axis, [(i, (i + by) % peers) for i in range(peers)])


class Cells:
    def __init__(self, size_x, size_y, size_z):
        self.nx, self.ny, self.nz = size_x + 1, size_y + 1, size_z
        self.planes = self.nx * self.ny
        self.rows = -(-self.planes // 16) * 16
        self.middle = self.rows // 2


def levels_of(position, meta):
    return [
        jnp.floor(jnp.floor(position[d] * UNITS + meta[d].astype(f32)) * (1.0 / UNITS))
        - meta[3 + d].astype(f32)
        for d in range(3)
    ]


def plane_of(levels, cells):
    return levels[0] * cells.ny + levels[1] - cells.middle


def wide(row):
    return jnp.broadcast_to(row, (16, LANES)).astype(bf16)


def plane_hot(plane, cells):
    ids = lax.broadcasted_iota(jnp.int32, (cells.rows, LANES), 0) - cells.middle
    ids = ids.astype(f32).astype(bf16).reshape(cells.rows // 16, 16, LANES)
    one, zero = jnp.ones((), bf16), jnp.zeros((), bf16)
    pieces = [
        jnp.where(ids == wide(plane[r : r + 1])[None], one, zero).reshape(cells.rows, LANES)
        for r in range(plane.shape[0])
    ]
    return jnp.concatenate(pieces, axis=1)


def split(value):
    high = value.astype(bf16).astype(f32)
    return high, value - high


def spread_moments(depth, weight, velocity, cells):
    nz = cells.nz
    ids = lax.broadcasted_iota(jnp.int32, (nz, LANES), 0).astype(f32).astype(bf16)
    ids = ids.reshape(nz // 16, 16, LANES)
    row_ids = lax.broadcasted_iota(jnp.int32, (16, LANES), 0).astype(f32).astype(bf16)
    zero = jnp.zeros((), bf16)
    parts = [split(weight * velocity[d]) for d in range(3)]
    channels = [weight] + [p[0] for p in parts] + [p[1] for p in parts]
    pieces = []
    for r in range(depth.shape[0]):
        at = wide(depth[r : r + 1])
        here = ids == at[None]
        values = [wide(c[r : r + 1]) for c in channels]
        tiles = [jnp.where(here, v[None], zero).reshape(nz, LANES) for v in values]
        top = jnp.zeros((16, LANES), bf16)
        for c, v in enumerate(values):
            top = jnp.where(row_ids == c, v, top)
        top = jnp.where(at == nz, top, zero)
        pieces.append(
            jnp.concatenate(
                tiles[:4] + [top, jnp.zeros((nz - 16, LANES), bf16)] + tiles[4:], axis=0
            )
        )
    return jnp.concatenate(pieces, axis=1)


def bin_group(total_ref, position, velocity, weight, meta, cells):
    levels = levels_of(position, meta)
    hot = plane_hot(plane_of(levels, cells), cells)
    spread = spread_moments(levels[2], weight, velocity, cells)
    total_ref[...] += lax.dot_general(hot, spread, NT, preferred_element_type=f32)


def row_iota():
    return lax.broadcasted_iota(jnp.int32, (GROUP, LANES), 0)


def bin_residents(cells, meta_ref, pos_ref, vel_ref, total_ref):
    meta = [meta_ref[k] for k in range(8)]
    total_ref[...] = jnp.zeros_like(total_ref)
    live_rows = meta[6]

    @pl.loop(0, (live_rows + GROUP - 1) // GROUP)
    def _(step):
        rows = pl.ds(pl.multiple_of(step * GROUP, GROUP), GROUP)
        position = [pos_ref[d, rows, :] for d in range(3)]
        velocity = [vel_ref[d, rows, :] for d in range(3)]
        weight = jnp.where(row_iota() + step * GROUP < live_rows, 1.0, 0.0)
        bin_group(total_ref, position, velocity, weight, meta, cells)


def arrival_group(ref, step, face_rows):
    offset = pl.multiple_of(step * GROUP, GROUP)
    comps = [ref[pl.ds(c * face_rows + offset, GROUP), :] for c in range(6)]
    live = (row_iota() + offset).astype(f32) < ref[pl.ds(6 * face_rows, GROUP), :]
    return comps[:3], comps[3:], live


def face_count(ref, face_rows):
    return jnp.max(ref[pl.ds(6 * face_rows, GROUP), :]).astype(jnp.int32)


def bead_mask(chains):
    slot = row_iota() * LANES + lax.broadcasted_iota(jnp.int32, (GROUP, LANES), 1)
    return slot < CHAIN * chains


def bin_arrivals(cells, face_rows, meta_ref, *refs):
    faces, (bead_pos_ref, bead_vel_ref, start_ref, total_ref, low_ref, high_ref, sums) = (
        refs[:6],
        refs[6:],
    )
    meta = [meta_ref[k] for k in range(8)]
    sums[...] = start_ref[...]
    weight = jnp.where(bead_mask(meta[7]), bead_mass, 0.0)
    bin_group(
        sums,
        [bead_pos_ref[d] for d in range(3)],
        [bead_vel_ref[d] for d in range(3)],
        weight,
        meta,
        cells,
    )
    for ref in faces:

        @pl.loop(0, (face_count(ref, face_rows) + GROUP - 1) // GROUP)
        def _(step):
            position, velocity, live = arrival_group(ref, step, face_rows)
            bin_group(sums, position, velocity, jnp.where(live, 1.0, 0.0), meta, cells)

    lane = lax.broadcasted_iota(jnp.int32, (cells.rows, LANES), 1)
    main, rest = sums[:, :LANES], sums[:, LANES:]
    main = main + jnp.where(lane < cells.nz, 0.0, rest)
    top = jnp.where(lane == 0, rest, rest + pltpu.roll(rest, LANES - 3, axis=1))
    top = jnp.where(lane < 4, top, 0.0)
    ny, edge = cells.ny, (cells.nx - 1) * cells.ny
    low_ref[...] = jnp.zeros_like(low_ref)
    high_ref[...] = jnp.zeros_like(high_ref)
    for half, value in enumerate([main, top]):
        total_ref[half] = value
        low_ref[half, :ny, :] = value[:ny]
        high_ref[half, :ny, :] = value[edge : edge + ny]


def add_faces_x(cells, total_ref, below_ref, above_ref, out_ref, low_ref, high_ref):
    nx, ny, edge = cells.nx, cells.ny, (cells.nx - 1) * cells.ny
    out_ref[...] = total_ref[...]
    low_ref[...] = jnp.zeros_like(low_ref)
    high_ref[...] = jnp.zeros_like(high_ref)
    for half in range(2):
        out_ref[half, :ny, :] += below_ref[half, :ny, :]
        out_ref[half, edge : edge + ny, :] += above_ref[half, :ny, :]
        low_ref[half, :nx, :] = out_ref[half, pl.ds(0, nx, stride=ny), :]
        high_ref[half, :nx, :] = out_ref[half, pl.ds(ny - 1, nx, stride=ny), :]


def add_faces_y(cells, total_ref, below_ref, above_ref, out_ref, face_ref, sums):
    nx, ny, nz = cells.nx, cells.ny, cells.nz
    sums[...] = total_ref[...]
    for half in range(2):
        sums[half, pl.ds(0, nx, stride=ny), :] += below_ref[half, :nx, :]
        sums[half, pl.ds(ny - 1, nx, stride=ny), :] += above_ref[half, :nx, :]
    main = sums[0].T
    top = sums[1].T[:GROUP]
    out_ref[:LANES, :] = main
    out_ref[LANES:, :] = top
    for c in range(4):
        face_ref[c : c + 1, :] = main[c * nz : c * nz + 1]
        face_ref[4 + c : 5 + c, :] = top[c : c + 1]


def cell_table(cells, total, faces_below, faces_above, axis_index):
    nz = cells.nz
    row_ids = lax.broadcasted_iota(jnp.int32, (nz, cells.rows), 0)
    sums = []
    tops = []
    for c in range(4):
        part = total[c * nz : (c + 1) * nz]
        sums.append(part + jnp.where(row_ids == 0, faces_below[4 + c : 5 + c], 0.0))
        tops.append(total[LANES + c : LANES + c + 1] + faces_above[c : c + 1])
    mass = jnp.maximum(sums[0], 1.0)
    top_mass = jnp.maximum(tops[0], 1.0)
    mean = [split(s / mass) for s in sums[1:]]
    top_mean = [split(t / top_mass) for t in tops[1:]]
    top_rows = (
        [axis_index[nz : nz + 1]] + [t[0] for t in top_mean] + [t[1] for t in top_mean]
    )
    top_tile = jnp.zeros((nz, cells.rows), f32)
    for c, value in enumerate(top_rows):
        top_tile = jnp.where(row_ids == c, value, top_tile)
    return jnp.concatenate(
        [axis_index[:nz]] + [m[0] for m in mean] + [top_tile] + [m[1] for m in mean], axis=0
    ).astype(bf16)


def direction_table():
    counter = jnp.arange(LANES).astype(f32)
    height = 1.0 - (2.0 * counter + 1.0) / NAXES
    radius = jnp.sqrt(jnp.maximum(1.0 - height * height, 0.0))
    rows = jnp.stack([radius * jnp.cos(golden * counter), radius * jnp.sin(golden * counter)])
    return jnp.broadcast_to(rows[:, None], (2, GROUP, LANES))


def collide(position, velocity, meta, table, dirs_ref, cells):
    nz = cells.nz
    levels = levels_of(position, meta)
    depth = levels[2]
    count = depth.shape[0]
    found = lax.dot_general(
        table, plane_hot(plane_of(levels, cells), cells), NN, preferred_element_type=f32
    )
    ids = lax.broadcasted_iota(jnp.int32, (nz, LANES), 0).astype(f32)
    rows = lax.broadcasted_iota(jnp.int32, (GROUP, LANES), 0)
    picked = [jnp.zeros((count, LANES), f32) for _ in range(4)]
    for r in range(count):
        block = found[:, r * LANES : (r + 1) * LANES]
        at = depth[r : r + 1]
        here = ids == at
        top = jnp.where(at == nz, block[4 * nz : 4 * nz + GROUP], 0.0)
        tops = top + pltpu.roll(top, GROUP - 3, axis=0)
        for c in range(4):
            value = block[c * nz : (c + 1) * nz]
            if c > 0:
                value = value + block[(4 + c) * nz : (5 + c) * nz]
            value = jnp.where(here, value, 0.0)
            value = jnp.sum(value.reshape(nz // GROUP, GROUP, LANES), axis=0)
            value = value + jnp.where(rows == c, tops if c > 0 else top, 0.0)
            value = jnp.sum(value, axis=0, keepdims=True)
            picked[c] = jnp.where(rows == r, value, picked[c])
    axis, flow = picked[0].astype(jnp.int32), picked[1:]
    normal = [
        jnp.take_along_axis(dirs_ref[0], axis, axis=1, mode="promise_in_bounds"),
        jnp.take_along_axis(dirs_ref[1], axis, axis=1, mode="promise_in_bounds"),
        1.0 - (2.0 * picked[0] + 1.0) * (1.0 / NAXES),
    ]
    rel = [velocity[d] - flow[d] for d in range(3)]
    along = (1.0 - turn_cosine) * (
        normal[0] * rel[0] + normal[1] * rel[1] + normal[2] * rel[2]
    )
    result = []
    for d in range(3):
        e, f = (d + 1) % 3, (d + 2) % 3
        crossed = normal[e] * rel[f] - normal[f] * rel[e]
        result.append(
            flow[d] + (turn_cosine * rel[d] + turn_sine * crossed + along * normal[d])
        )
    return result


def passed(position, speed):
    return position - jnp.floor(position) - 0.5 + 3.0 * step_size * speed


def copy_out(pairs, sems):
    copies = [pltpu.make_async_copy(a, b, sems.at[k]) for k, (a, b) in enumerate(pairs)]
    for copy in copies:
        copy.start()
    for copy in copies:
        copy.wait()


def collide_residents(
    cells, first, count, meta_ref, dirs_ref, table_ref, pos_ref, vel_ref, *refs
):
    out_pos, out_vel, held_pos, held_vel, sems = refs[-5:]
    meta = [meta_ref[k] for k in range(8)]
    table = table_ref[...]
    live_rows = meta[6] - first
    held_pos[...] = jnp.zeros_like(held_pos)
    held_vel[...] = jnp.zeros_like(held_vel)

    @pl.loop(0, jnp.clip((live_rows + GROUP - 1) // GROUP, 0, count // GROUP))
    def _(step):
        rows = pl.ds(pl.multiple_of(step * GROUP, GROUP), GROUP)
        position = [pos_ref[d, rows, :] for d in range(3)]
        velocity = [vel_ref[d, rows, :] for d in range(3)]
        live = row_iota() + step * GROUP < live_rows
        speed = collide(position, velocity, meta, table, dirs_ref, cells)
        for d in range(3):
            held_vel[d, rows, :] = jnp.where(live, speed[d], 0.0)
            held_pos[d, rows, :] = jnp.where(live, passed(position[d], speed[d]), 0.0)

    span = pl.ds(first, count)
    copy_out([(held_pos, out_pos.at[:, span, :]), (held_vel, out_vel.at[:, span, :])], sems)


def collide_arrivals(cells, first, face_rows, meta_ref, dirs_ref, table_ref, *refs):
    faces = refs[:6]
    out_pos, out_vel, held_pos, held_vel, sems = refs[-5:]
    meta = [meta_ref[k] for k in range(8)]
    table = table_ref[...]
    held_pos[...] = jnp.zeros_like(held_pos)
    held_vel[...] = jnp.zeros_like(held_vel)
    for face, ref in enumerate(faces):

        @pl.loop(0, (face_count(ref, face_rows) + GROUP - 1) // GROUP)
        def _(step):
            position, velocity, live = arrival_group(ref, step, face_rows)
            speed = collide(position, velocity, meta, table, dirs_ref, cells)
            rows = pl.ds(face * face_rows + pl.multiple_of(step * GROUP, GROUP), GROUP)
            for d in range(3):
                held_vel[d, rows, :] = jnp.where(live, speed[d], 0.0)
                held_pos[d, rows, :] = jnp.where(live, passed(position[d], speed[d]), 0.0)

    span = pl.ds(first, 6 * face_rows)
    copy_out([(held_pos, out_pos.at[:, span, :]), (held_vel, out_vel.at[:, span, :])], sems)


def pack_faces(face_rows, pos_ref, vel_ref, rows_ref, *out_refs):
    for face, out_ref in enumerate(out_refs):
        for c in range(6):
            source = pos_ref if c < 3 else vel_ref
            for k in range(face_rows):
                out_ref[c * face_rows + k : c * face_rows + k + 1, :] = source[
                    c % 3, face : face + 1, k * LANES : (k + 1) * LANES
                ]
        out_ref[6 * face_rows :, :] = jnp.full((GROUP, LANES), rows_ref[face], jnp.int32).astype(
            f32
        )


def bead_rows(parts):
    return jnp.concatenate(parts, axis=0)


def slot_live(slots, chains, rows):
    return lax.broadcasted_iota(jnp.int32, (rows, slots), 1) < CHAIN * chains


def payload(position, live):
    slots = position.shape[1]
    row_ids = lax.broadcasted_iota(jnp.int32, (GROUP, slots), 0)
    flag = jnp.where(live, 1.0, 0.0)
    return jnp.where(row_ids == 3, flag, jnp.where(row_ids < 3, position, 0.0))


def forces(own, chains, bonds_ref, blocks, centre, lengths):
    slots = own.shape[1]
    bond_slots = bonds_ref.shape[0]
    row_ids = lax.broadcasted_iota(jnp.int32, (GROUP, slots), 0)
    mid = jnp.zeros((GROUP, slots), f32)
    length = jnp.ones((GROUP, slots), f32)
    for d in range(3):
        mid = jnp.where(row_ids == d, centre[d], mid)
        length = jnp.where(row_ids == d, lengths[d], length)
    local = jnp.where(row_ids < 3, own - mid, 0.0)
    live = slot_live(slots, chains, GROUP)
    here = jnp.where(live, local, far_own)
    mine = [here[d : d + 1] for d in range(3)]
    total = [jnp.zeros((32, slots), f32) for _ in range(3)]
    for ref in blocks:
        for b in range(ref.shape[0] // GROUP):
            block = ref[b * GROUP : (b + 1) * GROUP, :]
            near = block - mid
            near = near - length * jnp.floor(near / length + 0.5)
            near = jnp.where(block[3:4] > 0.5, near, far_ghost)
            columns = near.T

            for k in range(slots // 32):
                differ = [mine[d] - columns[k * 32 : (k + 1) * 32, d : d + 1] for d in range(3)]
                square = (
                    differ[0] * differ[0] + differ[1] * differ[1] + differ[2] * differ[2]
                )
                inside = (square < cut_square) & (square > 0.25)
                inverse = 1.0 / jnp.where(inside, square, 1.0)
                sixth = inverse * inverse * inverse
                weight = jnp.where(
                    inside, 24.0 * (2.0 * sixth * sixth - sixth) * inverse, 0.0
                )
                total = [total[d] + weight * differ[d] for d in range(3)]
    pair = jnp.zeros((GROUP, slots), f32)
    for d in range(3):
        pair = jnp.where(row_ids == d, jnp.sum(total[d], axis=0, keepdims=True), pair)
    slot_ids = lax.broadcasted_iota(jnp.int32, (bond_slots, slots), 1)
    bond_ids = lax.broadcasted_iota(jnp.int32, (bond_slots, slots), 0)
    ends = bonds_ref[...]
    first = jnp.where(slot_ids == ends[:, 0:1], 1.0, 0.0)
    second = jnp.where(slot_ids == ends[:, 1:2], 1.0, 0.0)
    joins = jnp.where(bond_ids < (CHAIN - 1) * chains, first - second, 0.0)
    stretch = lax.dot_general(
        jnp.where(live, local, 0.0), joins, NT, precision=exact, preferred_element_type=f32
    )
    square = (
        stretch[0:1] * stretch[0:1] + stretch[1:2] * stretch[1:2] + stretch[2:3] * stretch[2:3]
    )
    bond_live = (
        lax.broadcasted_iota(jnp.int32, (1, bond_slots), 1) < (CHAIN - 1) * chains
    )
    pull = jnp.where(bond_live, -spring / (1.0 - square / reach_square), 0.0) * stretch
    return pair + lax.dot_general(pull, joins, NN, precision=exact, preferred_element_type=f32)


def centre_of(meta, sizes):
    return [meta[3 + d].astype(f32) + 0.5 * sizes[d] for d in range(3)]


def first_forces(sizes, lengths, meta_ref, start_ref, bonds_ref, a_ref, b_ref, c_ref, push_ref):
    meta = [meta_ref[k] for k in range(8)]
    push_ref[...] = forces(
        start_ref[...],
        meta[7],
        bonds_ref,
        [a_ref, b_ref, c_ref],
        centre_of(meta, sizes),
        lengths,
    )


def finish_cells(
    cells,
    meta_ref,
    dirs_ref,
    total_ref,
    below_ref,
    above_ref,
    axis_ref,
    bead_pos_ref,
    bead_vel_ref,
    start_ref,
    push_ref,
    table_ref,
    speed_ref,
    moved_ref,
    pay_ref,
):
    meta = [meta_ref[k] for k in range(8)]
    table_ref[...] = cell_table(
        cells, total_ref[...], below_ref[...], above_ref[...], axis_ref[...].astype(f32)
    )
    fresh = collide(
        [bead_pos_ref[d] for d in range(3)],
        [bead_vel_ref[d] for d in range(3)],
        meta,
        table_ref[...],
        dirs_ref,
        cells,
    )
    start = start_ref[...]
    slots = start.shape[1]
    row_ids = lax.broadcasted_iota(jnp.int32, (GROUP, slots), 0)
    speed = jnp.zeros((GROUP, slots), f32)
    for d in range(3):
        line = jnp.concatenate([fresh[d][k : k + 1] for k in range(slots // LANES)], axis=1)
        speed = jnp.where(row_ids == d, line, speed)
    speed = speed + half_kick * push_ref[...]
    moved = step_size * speed
    live = slot_live(slots, meta[7], GROUP)
    speed_ref[...] = speed
    moved_ref[...] = moved
    pay_ref[...] = payload(start + moved, live)


def substep(
    sizes,
    lengths,
    last,
    meta_ref,
    start_ref,
    bonds_ref,
    speed_ref,
    moved_ref,
    a_ref,
    b_ref,
    c_ref,
    speed_out,
    moved_out,
    *pay_refs,
):
    meta = [meta_ref[k] for k in range(8)]
    start = start_ref[...]
    moved = moved_ref[...]
    push = forces(
        start + moved, meta[7], bonds_ref, [a_ref, b_ref, c_ref], centre_of(meta, sizes), lengths
    )
    live = slot_live(start.shape[1], meta[7], GROUP)
    speed = speed_ref[...] + half_kick * push
    if last:
        speed_out[...] = jnp.where(live, speed, 0.0)
        moved_out[...] = jnp.where(live, moved, 0.0)
        return
    speed = speed + half_kick * push
    moved = moved + step_size * speed
    speed_out[...] = speed
    moved_out[...] = moved
    pay_refs[0][...] = payload(start + moved, live)


def neighbours(value, axis):
    peers = lax.axis_size(axis)
    if peers == 2:
        return [moved_along(value, axis, 1)]
    return [moved_along(value, axis, 1), moved_along(value, axis, -1)]


def halo(block):
    row = jnp.concatenate([block] + neighbours(block, "gz"), axis=0)
    plane = jnp.concatenate([row] + neighbours(row, "gy"), axis=0)
    sides = neighbours(plane, "gx")
    return [plane] + sides + sides[: 2 - len(sides)]


def like(*shape, dtype=f32):
    return jax.ShapeDtypeStruct(shape, dtype)


def with_upper(value, axis, dim):
    first = lax.slice_in_dim(value, 0, 1, axis=dim)
    return jnp.concatenate([value, moved_along(first, axis, -1)], axis=dim)


def shards(
    sol_pos,
    sol_vel,
    sol_rows,
    mig_pos,
    mig_vel,
    mig_rows,
    bead_pos,
    bead_vel,
    bead_chains,
    bond_list,
    cell_axis,
    shift,
):
    sizes = cell_axis.shape
    cells = Cells(*sizes)
    names = ("gx", "gy", "gz")
    lengths = tuple(float(sizes[d] * lax.axis_size(names[d])) for d in range(3))
    slots_here = sol_pos.shape[-1]
    buffer_slots = mig_pos.shape[-1]
    bead_slots = bead_pos.shape[-1]
    bond_slots = bond_list.shape[-1]
    rows_here = slots_here // LANES
    face_rows = buffer_slots // LANES
    rows_all = rows_here + 6 * face_rows
    anchor = jnp.stack([lax.axis_index(names[d]) * sizes[d] for d in range(3)])
    meta = jnp.concatenate(
        [shift, anchor.astype(jnp.int32), sol_rows.reshape(1), bead_chains.reshape(1)]
    )
    dirs = direction_table()
    position = sol_pos.reshape(3, rows_here, LANES)
    velocity = sol_vel.reshape(3, rows_here, LANES)

    packed = pl.pallas_call(
        functools.partial(pack_faces, face_rows),
        out_shape=[like(6 * face_rows + GROUP, LANES)] * 6,
        in_specs=[vmem(), vmem(), smem()],
        out_specs=[vmem()] * 6,
        compiler_params=params(),
        name="pack_faces",
    )(
        mig_pos.reshape(3, 6, buffer_slots),
        mig_vel.reshape(3, 6, buffer_slots),
        mig_rows.reshape(6),
    )
    arriving = [
        moved_along(packed[1], "gx", 1),
        moved_along(packed[0], "gx", -1),
        moved_along(packed[3], "gy", 1),
        moved_along(packed[2], "gy", -1),
        moved_along(packed[5], "gz", 1),
        moved_along(packed[4], "gz", -1),
    ]

    start = jnp.pad(bead_pos.reshape(3, bead_slots), ((0, GROUP - 3), (0, 0)))
    bead_rows_pos = jnp.pad(
        bead_pos.reshape(3, bead_slots // LANES, LANES),
        ((0, 0), (0, GROUP - bead_slots // LANES), (0, 0)),
    )
    bead_rows_vel = jnp.pad(
        bead_vel.reshape(3, bead_slots // LANES, LANES),
        ((0, 0), (0, GROUP - bead_slots // LANES), (0, 0)),
    )
    bonds = bond_list.reshape(2, bond_slots).T
    bead_live = jnp.arange(bead_slots, dtype=jnp.int32) < CHAIN * bead_chains.reshape(())
    first_pay = jnp.concatenate(
        [
            bead_pos.reshape(3, bead_slots),
            bead_live.astype(f32)[None],
            jnp.zeros((GROUP - 4, bead_slots), f32),
        ],
        axis=0,
    )
    ghosts = halo(first_pay)

    axis_index = with_upper(with_upper(with_upper(cell_axis, "gx", 0), "gy", 1), "gz", 2)
    axis_index = axis_index.transpose(2, 0, 1).reshape(cells.nz + 1, cells.planes)
    axis_index = jnp.pad(
        axis_index, ((0, GROUP - 1), (0, cells.rows - cells.planes))
    )

    totals = pl.pallas_call(
        functools.partial(bin_residents, cells),
        out_shape=like(cells.rows, 2 * LANES),
        in_specs=[smem(), vmem(), vmem()],
        out_specs=vmem(),
        compiler_params=params(),
        name="bin_residents",
    )(meta, position, velocity)

    push = pl.pallas_call(
        functools.partial(first_forces, sizes, lengths),
        out_shape=like(GROUP, bead_slots),
        in_specs=[smem()] + [vmem()] * 5,
        out_specs=vmem(),
        compiler_params=params(),
        name="first_forces",
    )(meta, start, bonds, *ghosts)

    face_x = like(2, -(-cells.ny // GROUP) * GROUP, LANES)
    face_y = like(2, -(-cells.nx // GROUP) * GROUP, LANES)
    totals, low, high = pl.pallas_call(
        functools.partial(bin_arrivals, cells, face_rows),
        out_shape=[like(2, cells.rows, LANES), face_x, face_x],
        in_specs=[smem()] + [vmem()] * 9,
        out_specs=[vmem()] * 3,
        scratch_shapes=[pltpu.VMEM((cells.rows, 2 * LANES), f32)],
        compiler_params=params(),
        name="bin_arrivals",
    )(meta, *arriving, bead_rows_pos, bead_rows_vel, totals)

    below, above = moved_along(high, "gx", 1), moved_along(low, "gx", -1)
    totals, low, high = pl.pallas_call(
        functools.partial(add_faces_x, cells),
        out_shape=[like(2, cells.rows, LANES), face_y, face_y],
        in_specs=[vmem()] * 3,
        out_specs=[vmem()] * 3,
        compiler_params=params(),
        name="add_faces_x",
    )(totals, below, above)
    below, above = moved_along(high, "gy", 1), moved_along(low, "gy", -1)
    totals, faces = pl.pallas_call(
        functools.partial(add_faces_y, cells),
        out_shape=[like(LANES + GROUP, cells.rows), like(GROUP, cells.rows)],
        in_specs=[vmem()] * 3,
        out_specs=[vmem()] * 2,
        scratch_shapes=[pltpu.VMEM((2, cells.rows, LANES), f32)],
        compiler_params=params(),
        name="add_faces_y",
    )(totals, below, above)
    sides = neighbours(faces, "gz")
    below, above = sides[0], sides[-1]

    bead_shape = like(GROUP, bead_slots)
    table, speed, moved, pay = pl.pallas_call(
        functools.partial(finish_cells, cells),
        out_shape=[like(2 * LANES, cells.rows, dtype=bf16), bead_shape, bead_shape, bead_shape],
        in_specs=[smem()] + [vmem()] * 9,
        out_specs=[vmem()] * 4,
        compiler_params=params(),
        name="finish_cells",
    )(
        meta,
        dirs,
        totals,
        below,
        above,
        axis_index,
        bead_rows_pos,
        bead_rows_vel,
        start,
        push,
    )

    any_spec = pl.BlockSpec(memory_space=pl.ANY)
    solvent_shape = like(3, rows_all, LANES)
    results = []
    cuts = 4
    count = rows_here // cuts
    for piece in range(cuts):
        earlier = results
        results = pl.pallas_call(
            functools.partial(collide_residents, cells, piece * count, count),
            out_shape=[solvent_shape] * 2,
            grid=(1,),
            in_specs=[smem(), vmem(), vmem()]
            + [pl.BlockSpec((3, count, LANES), lambda i, p=piece: (0, p, 0))] * 2
            + [any_spec] * len(earlier),
            out_specs=[any_spec] * 2,
            scratch_shapes=[pltpu.VMEM((3, count, LANES), f32)] * 2
            + [pltpu.SemaphoreType.DMA((2,))],
            input_output_aliases={5: 0, 6: 1} if earlier else {},
            compiler_params=params(),
            name=f"collide_residents_{piece}",
        )(meta, dirs, table, position, velocity, *earlier)
    results = pl.pallas_call(
        functools.partial(collide_arrivals, cells, rows_here, face_rows),
        out_shape=[solvent_shape] * 2,
        in_specs=[smem()] + [vmem()] * 8 + [any_spec] * 2,
        out_specs=[any_spec] * 2,
        scratch_shapes=[pltpu.VMEM((3, 6 * face_rows, LANES), f32)] * 2
        + [pltpu.SemaphoreType.DMA((2,))],
        input_output_aliases={9: 0, 10: 1},
        compiler_params=params(),
        name="collide_arrivals",
    )(meta, dirs, table, *arriving, *results)

    for step in range(3):
        last = step == 2
        outcome = pl.pallas_call(
            functools.partial(substep, sizes, lengths, last),
            out_shape=[bead_shape] * (2 if last else 3),
            in_specs=[smem()] + [vmem()] * 7,
            out_specs=[vmem()] * (2 if last else 3),
            compiler_params=params(),
            name=f"substep_{step}",
        )(meta, start, bonds, speed, moved, *halo(pay))
        speed, moved = outcome[:2]
        pay = outcome[-1]

    count_solvent = rows_all * LANES
    return (
        results[0].reshape(3, 1, 1, 1, count_solvent),
        results[1].reshape(3, 1, 1, 1, count_solvent),
        moved[:3].reshape(3, 1, 1, 1, bead_slots),
        speed[:3].reshape(3, 1, 1, 1, bead_slots),
    )


def solution(mesh):
    return jax.shard_map(
        shards,
        mesh=mesh,
        in_specs=(
            P(None, "gx", "gy", "gz", None),
            P(None, "gx", "gy", "gz", None),
            P("gx", "gy", "gz"),
            P(None, "gx", "gy", "gz", None, None),
            P(None, "gx", "gy", "gz", None, None),
            P("gx", "gy", "gz", None),
            P(None, "gx", "gy", "gz", None),
            P(None, "gx", "gy", "gz", None),
            P("gx", "gy", "gz"),
            P(None, "gx", "gy", "gz", None),
            P("gx", "gy", "gz"),
            P(),
        ),
        out_specs=(
            P(None, "gx", "gy", "gz", None),
            P(None, "gx", "gy", "gz", None),
            P(None, "gx", "gy", "gz", None),
            P(None, "gx", "gy", "gz", None),
        ),
        check_vma=False,
    )
```

```python
import functools
import math

import jax
import jax.numpy as jnp
from jax import lax
from jax.experimental import pallas as pl
from jax.experimental.pallas import tpu as pltpu
from jax.sharding import PartitionSpec as P

UNITS = 16
NAXES = 32
CHAIN = 8
LANES = 128
GROUP = 8
TWIN = 2

bead_mass = 5.0
step_size = 0.02
spring = 30.0
reach_square = 2.25
cut_square = 2.0 ** (1.0 / 3.0)
turn_cosine = math.cos(130.0 * math.pi / 180.0)
turn_sine = math.sin(130.0 * math.pi / 180.0)
golden = math.pi * (3.0 - math.sqrt(5.0))
half_kick = 0.5 * step_size / bead_mass
far_own = 3000.0
far_ghost = 9000.0
vmem_limit = 48 * 1024 * 1024
NT = (((1,), (1,)), ((), ()))
NN = (((1,), (0,)), ((), ()))
exact = lax.Precision.HIGHEST
f32 = jnp.float32
bf16 = jnp.bfloat16


def params():
    return pltpu.CompilerParams(vmem_limit_bytes=vmem_limit)


def vmem():
    return pl.BlockSpec(memory_space=pltpu.VMEM)


def smem():
    return pl.BlockSpec(memory_space=pltpu.SMEM)


def moved_along(value, axis, by):
    peers = lax.axis_size(axis)
    return lax.ppermute(value, axis, [(i, (i + by) % peers) for i in range(peers)])


class Cells:
    def __init__(self, size_x, size_y, size_z):
        self.sx, self.sy, self.nz = size_x, size_y, size_z
        self.inner = size_x * size_y
        self.edges = size_x + size_y + 1
        self.rows = -(-(self.inner + self.edges) // 16) * 16
        self.middle = self.rows // 2
        self.per = self.inner // self.edges
        self.depths = size_z + 1
        self.extra = -(-self.depths // self.per)
        self.height = -(-(self.depths + self.extra) // GROUP) * GROUP


def levels_of(position, meta):
    return [
        jnp.floor(jnp.floor(position[d] * UNITS + meta[d].astype(f32)) * (1.0 / UNITS))
        - meta[3 + d].astype(f32)
        for d in range(3)
    ]


def edge_of(levels, cells):
    outer = (levels[0] == cells.sx) | (levels[1] == cells.sy)
    return outer, jnp.where(levels[0] == cells.sx, levels[1], cells.sy + 1 + levels[0])


def plane_of(levels, cells):
    outer, edge = edge_of(levels, cells)
    return jnp.where(outer, cells.inner + edge, levels[0] * cells.sy + levels[1])


def place_of(levels, cells):
    outer, edge = edge_of(levels, cells)
    fold = jnp.floor((levels[2] + 0.5) * (1.0 / cells.per))
    row = jnp.where(outer, cells.depths + fold, levels[2])
    column = jnp.where(
        outer,
        (levels[2] - fold * cells.per) * cells.edges + edge,
        levels[0] * cells.sy + levels[1],
    )
    return row, column


def wide(row):
    return jnp.broadcast_to(row, (16, LANES)).astype(bf16)


def one_hot(column, height):
    middle = height // 2
    ids = lax.broadcasted_iota(jnp.int32, (height, LANES), 0) - middle
    ids = ids.astype(f32).astype(bf16).reshape(height // 16, 16, LANES)
    column = column - middle
    one, zero = jnp.ones((), bf16), jnp.zeros((), bf16)
    pieces = [
        jnp.where(ids == wide(column[r : r + 1])[None], one, zero).reshape(height, LANES)
        for r in range(column.shape[0])
    ]
    return jnp.concatenate(pieces, axis=1)


def split(value):
    high = value.astype(bf16).astype(f32)
    return high, value - high


def spread_moments(depth, weight, velocity, cells):
    nz = cells.nz
    ids = lax.broadcasted_iota(jnp.int32, (nz, LANES), 0).astype(f32).astype(bf16)
    ids = ids.reshape(nz // 16, 16, LANES)
    row_ids = lax.broadcasted_iota(jnp.int32, (16, LANES), 0).astype(f32).astype(bf16)
    zero = jnp.zeros((), bf16)
    parts = [split(weight * velocity[d]) for d in range(3)]
    channels = [weight] + [p[0] for p in parts] + [p[1] for p in parts]
    pieces = []
    for r in range(depth.shape[0]):
        at = wide(depth[r : r + 1])
        here = ids == at[None]
        values = [wide(c[r : r + 1]) for c in channels]
        tiles = [jnp.where(here, v[None], zero).reshape(nz, LANES) for v in values]
        top = jnp.zeros((16, LANES), bf16)
        for c, v in enumerate(values):
            top = jnp.where(row_ids == c, v, top)
        top = jnp.where(at == nz, top, zero)
        pieces.append(
            jnp.concatenate(
                tiles[:4] + [top, jnp.zeros((nz - 16, LANES), bf16)] + tiles[4:], axis=0
            )
        )
    return jnp.concatenate(pieces, axis=1)


def bin_group(total_ref, position, velocity, weight, meta, cells):
    levels = levels_of(position, meta)
    hot = one_hot(plane_of(levels, cells), cells.rows)
    spread = spread_moments(levels[2], weight, velocity, cells)
    total_ref[...] += lax.dot_general(hot, spread, NT, preferred_element_type=f32)


def row_iota():
    return lax.broadcasted_iota(jnp.int32, (GROUP, LANES), 0)


def bin_residents(cells, first, count, meta_ref, pos_ref, vel_ref, *refs):
    total_ref = refs[-1]
    meta = [meta_ref[k] for k in range(8)]
    if first == 0:
        total_ref[...] = jnp.zeros_like(total_ref)
    else:
        total_ref[...] = refs[0][...]
    live_rows = meta[6] - first
    stride = GROUP * TWIN

    @pl.loop(0, jnp.clip((live_rows + stride - 1) // stride, 0, count // stride))
    def _(step):
        for part in range(TWIN):
            offset = pl.multiple_of(step * stride + part * GROUP, GROUP)
            rows = pl.ds(offset, GROUP)
            position = [pos_ref[d, rows, :] for d in range(3)]
            velocity = [vel_ref[d, rows, :] for d in range(3)]
            weight = jnp.where(row_iota() + offset < live_rows, 1.0, 0.0)
            bin_group(total_ref, position, velocity, weight, meta, cells)


def arrival_group(ref, first, step, face_rows):
    offset = pl.multiple_of(step * GROUP, GROUP)
    comps = [ref[pl.ds(first + c * face_rows + offset, GROUP), :] for c in range(6)]
    live = (row_iota() + offset).astype(f32) < ref[pl.ds(first + 6 * face_rows, GROUP), :]
    return comps[:3], comps[3:], live


def face_count(ref, first, face_rows):
    return jnp.max(ref[pl.ds(first + 6 * face_rows, GROUP), :]).astype(jnp.int32)


def bead_mask(chains):
    slot = row_iota() * LANES + lax.broadcasted_iota(jnp.int32, (GROUP, LANES), 1)
    return slot < CHAIN * chains


def bin_arrivals(cells, face_rows, places, meta_ref, *refs):
    count = len(refs) - 8
    sources = refs[:count]
    bead_pos_ref, bead_vel_ref, axis_ref, start_ref, total_ref, low_ref, high_ref, sums = refs[
        count:
    ]
    meta = [meta_ref[k] for k in range(8)]
    sums[...] = start_ref[...]
    weight = jnp.where(bead_mask(meta[7]), bead_mass, 0.0)
    bin_group(
        sums,
        [bead_pos_ref[d] for d in range(3)],
        [bead_vel_ref[d] for d in range(3)],
        weight,
        meta,
        cells,
    )
    for which, first in places:
        ref = sources[which]

        @pl.loop(0, (face_count(ref, first, face_rows) + GROUP - 1) // GROUP)
        def _(step):
            position, velocity, live = arrival_group(ref, first, step, face_rows)
            bin_group(sums, position, velocity, jnp.where(live, 1.0, 0.0), meta, cells)

    nz, inner = cells.nz, cells.inner
    lane = lax.broadcasted_iota(jnp.int32, (cells.rows, LANES), 1)
    main, rest = sums[:, :LANES], sums[:, LANES:]
    main = main + jnp.where(lane < nz, 0.0, rest)
    top = jnp.where(lane == 0, rest, rest + pltpu.roll(rest, LANES - 3, axis=1))
    total_ref[0] = main
    total_ref[1] = jnp.where(lane < 4, top, 0.0)
    axis = axis_ref[...].astype(f32)
    total_ref[1, :inner, nz : 2 * nz] = axis
    sx, sy = cells.sx, cells.sy
    low_ref[...] = jnp.zeros_like(low_ref)
    high_ref[...] = jnp.zeros_like(high_ref)
    for half in range(2):
        corner = inner + sy + 1
        low_ref[half, :sy, :] = total_ref[half, :sy, :]
        low_ref[half, sy : sy + 1, :] = total_ref[half, corner : corner + 1, :]
        high_ref[half, : sy + 1, :] = total_ref[half, inner : inner + sy + 1, :]


def add_faces_x(cells, total_ref, below_ref, above_ref, out_ref, low_ref, high_ref):
    sx, sy, inner = cells.sx, cells.sy, cells.inner
    corner = inner + sy + 1
    out_ref[...] = total_ref[...]
    low_ref[...] = jnp.zeros_like(low_ref)
    high_ref[...] = jnp.zeros_like(high_ref)
    for half in range(2):
        out_ref[half, :sy, :] += below_ref[half, :sy, :]
        out_ref[half, corner : corner + 1, :] += below_ref[half, sy : sy + 1, :]
        out_ref[half, inner : inner + sy + 1, :] += above_ref[half, : sy + 1, :]
        low_ref[half, :sx, :] = out_ref[half, pl.ds(0, sx, stride=sy), :]
        low_ref[half, sx : sx + 1, :] = out_ref[half, inner : inner + 1, :]
        high_ref[half, :sx, :] = out_ref[half, corner : corner + sx, :]
        high_ref[half, sx : sx + 1, :] = out_ref[half, inner + sy : inner + sy + 1, :]


def add_faces_y(cells, total_ref, below_ref, above_ref, out_ref, face_ref, sums):
    sx, sy, nz, inner = cells.sx, cells.sy, cells.nz, cells.inner
    corner = inner + sy + 1
    sums[...] = total_ref[...]
    for half in range(2):
        sums[half, pl.ds(0, sx, stride=sy), :] += below_ref[half, :sx, :]
        sums[half, inner : inner + 1, :] += below_ref[half, sx : sx + 1, :]
        sums[half, corner : corner + sx, :] += above_ref[half, :sx, :]
        sums[half, inner + sy : inner + sy + 1, :] += above_ref[half, sx : sx + 1, :]
    main = sums[0].T
    rest = sums[1].T
    out_ref[:LANES, :] = main
    out_ref[LANES : LANES + nz, :] = rest[nz : 2 * nz]
    out_ref[LANES + nz :, :] = jnp.zeros((GROUP, cells.rows), f32)
    out_ref[LANES + nz : LANES + nz + 4, :] = rest[:4]
    face_ref[...] = jnp.zeros_like(face_ref)
    for c in range(5):
        face_ref[c : c + 1, :] = out_ref[c * nz : c * nz + 1, :]
        face_ref[GROUP + c : GROUP + c + 1, :] = out_ref[5 * nz + c : 5 * nz + c + 1, :]


def cell_table(cells, total_ref, below_ref, above_ref, table_ref, sheet, edge):
    nz, inner, height = cells.nz, cells.inner, cells.height
    row_ids = lax.broadcasted_iota(jnp.int32, (nz, cells.rows), 0)
    parts = []
    tops = []
    for c in range(5):
        face = jnp.where(row_ids == 0, below_ref[GROUP + c : GROUP + c + 1, :], 0.0)
        parts.append(total_ref[c * nz : (c + 1) * nz, :] + face)
        tops.append(
            total_ref[5 * nz + c : 5 * nz + c + 1, :] + above_ref[c : c + 1, :]
        )
    mass = jnp.maximum(parts[0], 1.0)
    top_mass = jnp.maximum(tops[0], 1.0)
    values = [parts[4]] + [p / mass for p in parts[1:4]]
    top_values = [tops[4]] + [t / top_mass for t in tops[1:4]]
    sheet[...] = jnp.zeros_like(sheet)
    edge[...] = jnp.zeros_like(edge)
    lane = lax.broadcasted_iota(jnp.int32, (cells.extra, LANES), 1)
    spare = LANES - (cells.rows - inner)
    for c in range(4):
        base = c * height
        sheet[base : base + nz, :] = values[c][:, :inner]
        sheet[base + nz : base + nz + 1, :] = top_values[c][:, :inner]
        edge[base : base + nz, :] = jnp.concatenate(
            [values[c][:, inner:], jnp.zeros((nz, spare), f32)], axis=1
        )
        edge[base + nz : base + nz + 1, :] = jnp.concatenate(
            [top_values[c][:, inner:], jnp.zeros((1, spare), f32)], axis=1
        )
        folded = [jnp.zeros((cells.extra, LANES), f32) for _ in range(inner // LANES)]
        for m in range(cells.per):
            begin = m * cells.edges
            piece = edge[pl.ds(base + m, cells.extra, stride=cells.per), :]
            piece = pltpu.roll(piece, begin % LANES, axis=1) if begin % LANES else piece
            for t in range(inner // LANES):
                low, high = begin - t * LANES, begin + cells.edges - t * LANES
                if high > 0 and low < LANES:
                    folded[t] = jnp.where((lane >= low) & (lane < high), piece, folded[t])
        sheet[base + nz + 1 : base + nz + 1 + cells.extra, :] = jnp.concatenate(folded, axis=1)
    whole = sheet[...]
    high = whole.astype(bf16).astype(f32)
    low = (whole - high)[height:]
    table_ref[...] = jnp.concatenate([high, low], axis=0).astype(bf16)


def direction_table():
    counter = jnp.arange(LANES).astype(f32)
    height = 1.0 - (2.0 * counter + 1.0) / NAXES
    radius = jnp.sqrt(jnp.maximum(1.0 - height * height, 0.0))
    rows = jnp.stack([radius * jnp.cos(golden * counter), radius * jnp.sin(golden * counter)])
    return jnp.broadcast_to(rows[:, None], (2, GROUP, LANES))


def fold_rows(values):
    sub = lax.broadcasted_iota(jnp.int32, (GROUP, LANES), 0)
    step = GROUP // 2
    while step:
        upper = (sub & step) == 0
        half = len(values) // 2
        joined = []
        for a, b in zip(values[:half], values[half:]):
            a = a + pltpu.roll(a, GROUP - step, axis=0)
            b = b + pltpu.roll(b, step, axis=0)
            joined.append(jnp.where(upper, a, b))
        values = joined
        step //= 2
    return values[0]


def collide(position, velocity, meta, table, dirs_ref, cells):
    height = cells.height
    row, column = place_of(levels_of(position, meta), cells)
    found = lax.dot_general(
        table, one_hot(column, cells.inner), NN, preferred_element_type=f32
    )
    ids = lax.broadcasted_iota(jnp.int32, (height, LANES), 0).astype(f32)
    picked = [[] for _ in range(4)]
    for r in range(GROUP):
        block = found[:, r * LANES : (r + 1) * LANES]
        here = ids == row[r : r + 1]
        for c in range(4):
            value = block[c * height : (c + 1) * height]
            if c > 0:
                value = value + block[(3 + c) * height : (4 + c) * height]
            value = jnp.where(here, value, 0.0)
            picked[c].append(
                jnp.sum(value.reshape(height // GROUP, GROUP, LANES), axis=0)
            )
    picked = [fold_rows(p) for p in picked]
    axis, flow = picked[0].astype(jnp.int32), picked[1:]
    normal = [
        jnp.take_along_axis(dirs_ref[0], axis, axis=1, mode="promise_in_bounds"),
        jnp.take_along_axis(dirs_ref[1], axis, axis=1, mode="promise_in_bounds"),
        1.0 - (2.0 * picked[0] + 1.0) * (1.0 / NAXES),
    ]
    rel = [velocity[d] - flow[d] for d in range(3)]
    along = (1.0 - turn_cosine) * (
        normal[0] * rel[0] + normal[1] * rel[1] + normal[2] * rel[2]
    )
    result = []
    for d in range(3):
        e, f = (d + 1) % 3, (d + 2) % 3
        crossed = normal[e] * rel[f] - normal[f] * rel[e]
        result.append(
            flow[d] + (turn_cosine * rel[d] + turn_sine * crossed + along * normal[d])
        )
    return result


def passed(position, speed):
    return position - jnp.floor(position) - 0.5 + 3.0 * step_size * speed


def copy_out(pairs, sems):
    copies = [pltpu.make_async_copy(a, b, sems.at[k]) for k, (a, b) in enumerate(pairs)]
    for copy in copies:
        copy.start()
    for copy in copies:
        copy.wait()


def collide_residents(
    cells, first, count, meta_ref, dirs_ref, table_ref, pos_ref, vel_ref, *refs
):
    out_pos, out_vel, held_pos, held_vel, sems = refs[-5:]
    meta = [meta_ref[k] for k in range(8)]
    table = table_ref[...]
    live_rows = meta[6] - first
    held_pos[...] = jnp.zeros_like(held_pos)
    held_vel[...] = jnp.zeros_like(held_vel)
    stride = GROUP * TWIN

    @pl.loop(0, jnp.clip((live_rows + stride - 1) // stride, 0, count // stride))
    def _(step):
        for part in range(TWIN):
            offset = pl.multiple_of(step * stride + part * GROUP, GROUP)
            rows = pl.ds(offset, GROUP)
            position = [pos_ref[d, rows, :] for d in range(3)]
            velocity = [vel_ref[d, rows, :] for d in range(3)]
            live = row_iota() + offset < live_rows
            speed = collide(position, velocity, meta, table, dirs_ref, cells)
            for d in range(3):
                held_vel[d, rows, :] = jnp.where(live, speed[d], 0.0)
                held_pos[d, rows, :] = jnp.where(live, passed(position[d], speed[d]), 0.0)

    span = pl.ds(first, count)
    copy_out([(held_pos, out_pos.at[:, span, :]), (held_vel, out_vel.at[:, span, :])], sems)


def collide_arrivals(cells, first, face_rows, places, meta_ref, dirs_ref, table_ref, *refs):
    out_pos, out_vel, held_pos, held_vel, sems = refs[-5:]
    meta = [meta_ref[k] for k in range(8)]
    table = table_ref[...]
    held_pos[...] = jnp.zeros_like(held_pos)
    held_vel[...] = jnp.zeros_like(held_vel)
    for k, (which, begin) in enumerate(places):
        ref = refs[which]

        @pl.loop(0, (face_count(ref, begin, face_rows) + GROUP - 1) // GROUP)
        def _(step):
            position, velocity, live = arrival_group(ref, begin, step, face_rows)
            speed = collide(position, velocity, meta, table, dirs_ref, cells)
            rows = pl.ds(k * face_rows + pl.multiple_of(step * GROUP, GROUP), GROUP)
            for d in range(3):
                held_vel[d, rows, :] = jnp.where(live, speed[d], 0.0)
                held_pos[d, rows, :] = jnp.where(live, passed(position[d], speed[d]), 0.0)

    span = pl.ds(first, len(places) * face_rows)
    copy_out([(held_pos, out_pos.at[:, span, :]), (held_vel, out_vel.at[:, span, :])], sems)


def pack_faces(face_rows, pos_ref, vel_ref, rows_ref, *out_refs):
    for face, out_ref in enumerate(out_refs):
        for c in range(6):
            source = pos_ref if c < 3 else vel_ref
            for k in range(face_rows):
                out_ref[c * face_rows + k : c * face_rows + k + 1, :] = source[
                    c % 3, face : face + 1, k * LANES : (k + 1) * LANES
                ]
        out_ref[6 * face_rows :, :] = jnp.full((GROUP, LANES), rows_ref[face], jnp.int32).astype(
            f32
        )


def stack_rows(parts, *refs):
    out_ref = refs[-1]
    at = 0
    for which, begin, count in parts:
        out_ref[at : at + count, :] = refs[which][begin : begin + count, :]
        at += count


def slot_live(slots, chains, rows):
    return lax.broadcasted_iota(jnp.int32, (rows, slots), 1) < CHAIN * chains


def payload(position, live):
    slots = position.shape[1]
    row_ids = lax.broadcasted_iota(jnp.int32, (GROUP, slots), 0)
    flag = jnp.where(live, 1.0, 0.0)
    return jnp.where(row_ids == 3, flag, jnp.where(row_ids < 3, position, 0.0))


def forces(own, chains, bonds_ref, blocks, centre, lengths):
    slots = own.shape[1]
    bond_slots = bonds_ref.shape[0]
    row_ids = lax.broadcasted_iota(jnp.int32, (GROUP, slots), 0)
    mid = jnp.zeros((GROUP, slots), f32)
    length = jnp.ones((GROUP, slots), f32)
    for d in range(3):
        mid = jnp.where(row_ids == d, centre[d], mid)
        length = jnp.where(row_ids == d, lengths[d], length)
    local = jnp.where(row_ids < 3, own - mid, 0.0)
    live = slot_live(slots, chains, GROUP)
    here = jnp.where(live, local, far_own)
    mine = [here[d : d + 1] for d in range(3)]
    total = [jnp.zeros((32, slots), f32) for _ in range(3)]
    for ref in blocks:
        for b in range(ref.shape[0] // GROUP):
            block = ref[b * GROUP : (b + 1) * GROUP, :]
            near = block - mid
            near = near - length * jnp.floor(near / length + 0.5)
            near = jnp.where(block[3:4] > 0.5, near, far_ghost)
            columns = near.T

            for k in range(slots // 32):
                differ = [mine[d] - columns[k * 32 : (k + 1) * 32, d : d + 1] for d in range(3)]
                square = (
                    differ[0] * differ[0] + differ[1] * differ[1] + differ[2] * differ[2]
                )
                inside = (square < cut_square) & (square > 0.25)
                inverse = 1.0 / jnp.where(inside, square, 1.0)
                sixth = inverse * inverse * inverse
                weight = jnp.where(
                    inside, 24.0 * (2.0 * sixth * sixth - sixth) * inverse, 0.0
                )
                total = [total[d] + weight * differ[d] for d in range(3)]
    pair = jnp.zeros((GROUP, slots), f32)
    for d in range(3):
        pair = jnp.where(row_ids == d, jnp.sum(total[d], axis=0, keepdims=True), pair)
    slot_ids = lax.broadcasted_iota(jnp.int32, (bond_slots, slots), 1)
    bond_ids = lax.broadcasted_iota(jnp.int32, (bond_slots, slots), 0)
    ends = bonds_ref[...]
    first = jnp.where(slot_ids == ends[:, 0:1], 1.0, 0.0)
    second = jnp.where(slot_ids == ends[:, 1:2], 1.0, 0.0)
    joins = jnp.where(bond_ids < (CHAIN - 1) * chains, first - second, 0.0)
    stretch = lax.dot_general(
        jnp.where(live, local, 0.0), joins, NT, precision=exact, preferred_element_type=f32
    )
    square = (
        stretch[0:1] * stretch[0:1] + stretch[1:2] * stretch[1:2] + stretch[2:3] * stretch[2:3]
    )
    bond_live = (
        lax.broadcasted_iota(jnp.int32, (1, bond_slots), 1) < (CHAIN - 1) * chains
    )
    pull = jnp.where(bond_live, -spring / (1.0 - square / reach_square), 0.0) * stretch
    return pair + lax.dot_general(pull, joins, NN, precision=exact, preferred_element_type=f32)


def centre_of(meta, sizes):
    return [meta[3 + d].astype(f32) + 0.5 * sizes[d] for d in range(3)]


def first_forces(sizes, lengths, meta_ref, start_ref, bonds_ref, a_ref, b_ref, c_ref, push_ref):
    meta = [meta_ref[k] for k in range(8)]
    push_ref[...] = forces(
        start_ref[...],
        meta[7],
        bonds_ref,
        [a_ref, b_ref, c_ref],
        centre_of(meta, sizes),
        lengths,
    )


def finish_cells(
    cells,
    meta_ref,
    dirs_ref,
    total_ref,
    below_ref,
    above_ref,
    bead_pos_ref,
    bead_vel_ref,
    start_ref,
    push_ref,
    table_ref,
    speed_ref,
    moved_ref,
    pay_ref,
    sheet,
    edge,
):
    meta = [meta_ref[k] for k in range(8)]
    cell_table(cells, total_ref, below_ref, above_ref, table_ref, sheet, edge)
    fresh = collide(
        [bead_pos_ref[d] for d in range(3)],
        [bead_vel_ref[d] for d in range(3)],
        meta,
        table_ref[...],
        dirs_ref,
        cells,
    )
    start = start_ref[...]
    slots = start.shape[1]
    row_ids = lax.broadcasted_iota(jnp.int32, (GROUP, slots), 0)
    speed = jnp.zeros((GROUP, slots), f32)
    for d in range(3):
        line = jnp.concatenate([fresh[d][k : k + 1] for k in range(slots // LANES)], axis=1)
        speed = jnp.where(row_ids == d, line, speed)
    speed = speed + half_kick * push_ref[...]
    moved = step_size * speed
    live = slot_live(slots, meta[7], GROUP)
    speed_ref[...] = speed
    moved_ref[...] = moved
    pay_ref[...] = payload(start + moved, live)


def substep(
    sizes,
    lengths,
    last,
    meta_ref,
    start_ref,
    bonds_ref,
    speed_ref,
    moved_ref,
    a_ref,
    b_ref,
    c_ref,
    order_ref,
    speed_out,
    moved_out,
    *pay_refs,
):
    meta = [meta_ref[k] for k in range(8)]
    start = start_ref[...]
    moved = moved_ref[...]
    push = forces(
        start + moved, meta[7], bonds_ref, [a_ref, b_ref, c_ref], centre_of(meta, sizes), lengths
    )
    live = slot_live(start.shape[1], meta[7], GROUP)
    speed = speed_ref[...] + half_kick * push
    if last:
        speed_out[...] = jnp.where(live, speed, 0.0)[:3]
        moved_out[...] = jnp.where(live, moved, 0.0)[:3]
        return
    speed = speed + half_kick * push
    moved = moved + step_size * speed
    speed_out[...] = speed
    moved_out[...] = moved
    pay_refs[0][...] = payload(start + moved, live)


def neighbours(value, axis):
    peers = lax.axis_size(axis)
    if peers == 2:
        return [moved_along(value, axis, 1)]
    return [moved_along(value, axis, 1), moved_along(value, axis, -1)]


def stacked(parts, operands, order=()):
    rows = sum(count for _, _, count in parts)
    width = operands[0].shape[1]
    return pl.pallas_call(
        functools.partial(stack_rows, tuple(parts)),
        out_shape=like(rows, width),
        in_specs=[vmem()] * len(operands) + [pl.BlockSpec(memory_space=pl.ANY)] * len(order),
        out_specs=vmem(),
        compiler_params=params(),
        name="stack_rows",
    )(*operands, *order)


def whole_rows(operands):
    return [(k, 0, value.shape[0]) for k, value in enumerate(operands)]


def halo(block, pieces):
    parts = [block] + neighbours(block, "gz")
    row = stacked(whole_rows(parts), parts, [pieces[0]()])
    parts = [row] + neighbours(row, "gy")
    plane = stacked(whole_rows(parts), parts, [pieces[1]()])
    sides = neighbours(plane, "gx")
    return [plane] + sides + sides[: 2 - len(sides)], pieces[2]()


def like(*shape, dtype=f32):
    return jax.ShapeDtypeStruct(shape, dtype)


def shards(
    sol_pos,
    sol_vel,
    sol_rows,
    mig_pos,
    mig_vel,
    mig_rows,
    bead_pos,
    bead_vel,
    bead_chains,
    bond_list,
    cell_axis,
    shift,
):
    sizes = cell_axis.shape
    cells = Cells(*sizes)
    names = ("gx", "gy", "gz")
    lengths = tuple(float(sizes[d] * lax.axis_size(names[d])) for d in range(3))
    slots_here = sol_pos.shape[-1]
    buffer_slots = mig_pos.shape[-1]
    bead_slots = bead_pos.shape[-1]
    bond_slots = bond_list.shape[-1]
    rows_here = slots_here // LANES
    face_rows = buffer_slots // LANES
    rows_all = rows_here + 6 * face_rows
    anchor = jnp.stack([lax.axis_index(names[d]) * sizes[d] for d in range(3)])
    meta = jnp.concatenate(
        [shift, anchor.astype(jnp.int32), sol_rows.reshape(1), bead_chains.reshape(1)]
    )
    dirs = direction_table()
    position = sol_pos.reshape(3, rows_here, LANES)
    velocity = sol_vel.reshape(3, rows_here, LANES)

    any_spec = pl.BlockSpec(memory_space=pl.ANY)
    face_height = 6 * face_rows + GROUP
    packed = pl.pallas_call(
        functools.partial(pack_faces, face_rows),
        out_shape=[like(face_height, LANES)] * 6,
        in_specs=[vmem(), vmem(), smem()],
        out_specs=[vmem()] * 6,
        compiler_params=params(),
        name="pack_faces",
    )(
        mig_pos.reshape(3, 6, buffer_slots),
        mig_vel.reshape(3, 6, buffer_slots),
        mig_rows.reshape(6),
    )

    bead_flat = bead_pos.reshape(3, bead_slots)
    start = jnp.pad(bead_flat, ((0, GROUP - 3), (0, 0)))
    tiles = bead_slots // LANES
    bead_pad = ((0, 0), (0, GROUP - tiles), (0, 0))
    bead_rows_pos = jnp.pad(bead_pos.reshape(3, tiles, LANES), bead_pad)
    bead_rows_vel = jnp.pad(bead_vel.reshape(3, tiles, LANES), bead_pad)
    bonds = bond_list.reshape(2, bond_slots).T
    bead_live = jnp.arange(bead_slots, dtype=jnp.int32) < CHAIN * bead_chains.reshape(())
    first_pay = jnp.concatenate(
        [bead_flat, bead_live.astype(f32)[None], jnp.zeros((GROUP - 4, bead_slots), f32)], axis=0
    )
    block = first_pay.reshape(GROUP, tiles, LANES).transpose(1, 0, 2).reshape(-1, LANES)

    thirds = 3
    count = rows_here // thirds
    axis_rows = cell_axis.reshape(cells.inner, sizes[2])

    def bin_piece(piece, earlier, order):
        return pl.pallas_call(
            functools.partial(bin_residents, cells, piece * count, count),
            out_shape=like(cells.rows, 2 * LANES),
            grid=(1,),
            in_specs=[smem()]
            + [pl.BlockSpec((3, count, LANES), lambda i, p=piece: (0, p, 0))] * 2
            + [vmem()] * len(earlier)
            + [any_spec] * len(order),
            out_specs=vmem(),
            compiler_params=params(),
            name=f"bin_residents_{piece}",
        )(meta, position, velocity, *earlier, *order)

    def swap(axis, low, high, body):
        if lax.axis_size(axis) == 2:
            both = [packed[low], packed[high], body]
            came = moved_along(stacked(whole_rows(both), both), axis, 1)
            return [came], [(0, face_height), (0, 0)], [(0, 2 * face_height)]
        up = stacked(whole_rows([packed[high], body]), [packed[high], body])
        down = stacked(whole_rows([packed[low], body]), [packed[low], body])
        came = [moved_along(up, axis, 1), moved_along(down, axis, -1)]
        return came, [(0, 0), (1, 0)], [(0, face_height), (1, face_height)]

    arrived, places, blocks = {}, {}, block
    totals = None
    for piece, (axis, low) in enumerate((("gz", 4), ("gy", 2), ("gx", 0))):
        came, spots, bodies = swap(axis, low, low + 1, blocks)
        totals = bin_piece(piece, [] if totals is None else [totals], [blocks])
        height = blocks.shape[0]
        arrived[axis], places[axis] = came, spots
        if axis != "gx":
            parts = [(0, 0, height)] + [(1 + w, at, height) for w, at in bodies]
            blocks = stacked(parts, [blocks] + came, [totals])
        else:
            around = [blocks] + [
                stacked([(0, at, height)], [came[w]]) for w, at in bodies
            ]
            around = around + around[1 : 1 + 3 - len(around)]

    def as_blocks(value):
        n = value.shape[0] // (GROUP * tiles)
        return (
            value.reshape(n, tiles, GROUP, LANES)
            .transpose(0, 2, 1, 3)
            .reshape(n * GROUP, bead_slots)
        )

    arriving, spots = [], []
    for axis in names:
        spots += [(len(arriving) + w, at) for w, at in places[axis]]
        arriving += arrived[axis]

    face_x = like(2, -(-(sizes[1] + 1) // GROUP) * GROUP, LANES)
    face_y = like(2, -(-(sizes[0] + 1) // GROUP) * GROUP, LANES)
    totals, low, high = pl.pallas_call(
        functools.partial(bin_arrivals, cells, face_rows, tuple(spots)),
        out_shape=[like(2, cells.rows, LANES), face_x, face_x],
        in_specs=[smem()] + [vmem()] * (len(arriving) + 4),
        out_specs=[vmem()] * 3,
        scratch_shapes=[pltpu.VMEM((cells.rows, 2 * LANES), f32)],
        compiler_params=params(),
        name="bin_arrivals",
    )(meta, *arriving, bead_rows_pos, bead_rows_vel, axis_rows, totals)

    push = pl.pallas_call(
        functools.partial(first_forces, sizes, lengths),
        out_shape=like(GROUP, bead_slots),
        in_specs=[smem()] + [vmem()] * 5,
        out_specs=vmem(),
        compiler_params=params(),
        name="first_forces",
    )(meta, start, bonds, *[as_blocks(value) for value in around])

    below, above = moved_along(high, "gx", 1), moved_along(low, "gx", -1)
    totals, low, high = pl.pallas_call(
        functools.partial(add_faces_x, cells),
        out_shape=[like(2, cells.rows, LANES), face_y, face_y],
        in_specs=[vmem()] * 3,
        out_specs=[vmem()] * 3,
        compiler_params=params(),
        name="add_faces_x",
    )(totals, below, above)
    below, above = moved_along(high, "gy", 1), moved_along(low, "gy", -1)
    totals, faces = pl.pallas_call(
        functools.partial(add_faces_y, cells),
        out_shape=[like(LANES + cells.nz + GROUP, cells.rows), like(2 * GROUP, cells.rows)],
        in_specs=[vmem()] * 3,
        out_specs=[vmem()] * 2,
        scratch_shapes=[pltpu.VMEM((2, cells.rows, LANES), f32)],
        compiler_params=params(),
        name="add_faces_y",
    )(totals, below, above)
    sides = neighbours(faces, "gz")
    below, above = sides[0], sides[-1]

    bead_shape = like(GROUP, bead_slots)
    table, speed, moved, pay = pl.pallas_call(
        functools.partial(finish_cells, cells),
        out_shape=[
            like(7 * cells.height, cells.inner, dtype=bf16),
            bead_shape,
            bead_shape,
            bead_shape,
        ],
        in_specs=[smem()] + [vmem()] * 8,
        out_specs=[vmem()] * 4,
        scratch_shapes=[
            pltpu.VMEM((4 * cells.height, cells.inner), f32),
            pltpu.VMEM((4 * cells.height, LANES), f32),
        ],
        compiler_params=params(),
        name="finish_cells",
    )(meta, dirs, totals, below, above, bead_rows_pos, bead_rows_vel, start, push)

    solvent_shape = like(3, rows_all, LANES)
    results = []
    cuts = 6
    span = rows_here // cuts

    def collide_piece(piece):
        earlier = list(results)
        if piece < cuts:
            body = functools.partial(collide_residents, cells, piece * span, span)
            rows = span
            sources = [position, velocity]
            specs = [pl.BlockSpec((3, span, LANES), lambda i: (0, piece, 0))] * 2
        else:
            begin = 2 * (piece - cuts)
            body = functools.partial(
                collide_arrivals,
                cells,
                rows_here + begin * face_rows,
                face_rows,
                tuple(spots[begin : begin + 2]),
            )
            rows = 2 * face_rows
            sources = arriving
            specs = [vmem()] * len(arriving)
        at = 3 + len(sources)
        results[:] = pl.pallas_call(
            body,
            out_shape=[solvent_shape] * 2,
            grid=(1,),
            in_specs=[smem(), vmem(), vmem()] + specs + [any_spec] * len(earlier),
            out_specs=[any_spec] * 2,
            scratch_shapes=[pltpu.VMEM((3, rows, LANES), f32)] * 2
            + [pltpu.SemaphoreType.DMA((2,))],
            input_output_aliases={at: 0, at + 1: 1} if earlier else {},
            compiler_params=params(),
            name=f"collide_{piece}",
        )(meta, dirs, table, *sources, *earlier)
        return results[1]

    for step in range(3):
        last = step == 2
        thunks = [functools.partial(collide_piece, 3 * step + k) for k in range(3)]
        ghosts, order = halo(pay, thunks)
        outcome = pl.pallas_call(
            functools.partial(substep, sizes, lengths, last),
            out_shape=[like(3, bead_slots)] * 2 if last else [bead_shape] * 3,
            in_specs=[smem()] + [vmem()] * 7 + [any_spec],
            out_specs=[vmem()] * (2 if last else 3),
            compiler_params=params(),
            name=f"substep_{step}",
        )(meta, start, bonds, speed, moved, *ghosts, order)
        speed, moved = outcome[:2]
        pay = outcome[-1]

    count_solvent = rows_all * LANES
    return (
        results[0].reshape(3, 1, 1, 1, count_solvent),
        results[1].reshape(3, 1, 1, 1, count_solvent),
        moved.reshape(3, 1, 1, 1, bead_slots),
        speed.reshape(3, 1, 1, 1, bead_slots),
    )


def solution(mesh):
    return jax.shard_map(
        shards,
        mesh=mesh,
        in_specs=(
            P(None, "gx", "gy", "gz", None),
            P(None, "gx", "gy", "gz", None),
            P("gx", "gy", "gz"),
            P(None, "gx", "gy", "gz", None, None),
            P(None, "gx", "gy", "gz", None, None),
            P("gx", "gy", "gz", None),
            P(None, "gx", "gy", "gz", None),
            P(None, "gx", "gy", "gz", None),
            P("gx", "gy", "gz"),
            P(None, "gx", "gy", "gz", None),
            P("gx", "gy", "gz"),
            P(),
        ),
        out_specs=(
            P(None, "gx", "gy", "gz", None),
            P(None, "gx", "gy", "gz", None),
            P(None, "gx", "gy", "gz", None),
            P(None, "gx", "gy", "gz", None),
        ),
        check_vma=False,
    )
```

```python
import functools
import math

import jax
import jax.numpy as jnp
from jax import lax
from jax.experimental import pallas as pl
from jax.experimental.pallas import tpu as pltpu
from jax.sharding import PartitionSpec as P

UNITS = 16
NAXES = 32
CHAIN = 8
LANES = 128
GROUP = 8
TWIN = 4

bead_mass = 5.0
step_size = 0.02
spring = 30.0
reach_square = 2.25
cut_square = 2.0 ** (1.0 / 3.0)
turn_cosine = math.cos(130.0 * math.pi / 180.0)
turn_sine = math.sin(130.0 * math.pi / 180.0)
golden = math.pi * (3.0 - math.sqrt(5.0))
half_kick = 0.5 * step_size / bead_mass
far_own = 3000.0
far_ghost = 9000.0
vmem_limit = 48 * 1024 * 1024
vmem_most = 48 * 1024 * 1024
NT = (((1,), (1,)), ((), ()))
NN = (((1,), (0,)), ((), ()))
exact = lax.Precision.HIGHEST
f32 = jnp.float32
bf16 = jnp.bfloat16


def params(limit=vmem_limit):
    return pltpu.CompilerParams(vmem_limit_bytes=limit)


def vmem():
    return pl.BlockSpec(memory_space=pltpu.VMEM)


def smem():
    return pl.BlockSpec(memory_space=pltpu.SMEM)


def moved_along(value, axis, by):
    peers = lax.axis_size(axis)
    return lax.ppermute(value, axis, [(i, (i + by) % peers) for i in range(peers)])


class Cells:
    def __init__(self, size_x, size_y, size_z):
        self.sx, self.sy, self.nz = size_x, size_y, size_z
        self.inner = size_x * size_y
        self.edges = size_x + size_y + 1
        self.rows = -(-(self.inner + self.edges) // 16) * 16
        self.middle = self.rows // 2
        self.per = self.inner // self.edges
        self.depths = size_z + 1
        self.extra = -(-self.depths // self.per)
        self.height = -(-(self.depths + self.extra) // GROUP) * GROUP


def levels_of(position, meta):
    return [
        jnp.floor(jnp.floor(position[d] * UNITS + meta[d].astype(f32)) * (1.0 / UNITS))
        - meta[3 + d].astype(f32)
        for d in range(3)
    ]


def edge_of(levels, cells):
    outer = (levels[0] == cells.sx) | (levels[1] == cells.sy)
    return outer, jnp.where(levels[0] == cells.sx, levels[1], cells.sy + 1 + levels[0])


def plane_of(levels, cells):
    outer, edge = edge_of(levels, cells)
    return jnp.where(outer, cells.inner + edge, levels[0] * cells.sy + levels[1])


def place_of(levels, cells):
    outer, edge = edge_of(levels, cells)
    fold = jnp.floor((levels[2] + 0.5) * (1.0 / cells.per))
    row = jnp.where(outer, cells.depths + fold, levels[2])
    column = jnp.where(
        outer,
        (levels[2] - fold * cells.per) * cells.edges + edge,
        levels[0] * cells.sy + levels[1],
    )
    return row, column


def wide(row):
    return jnp.broadcast_to(row, (16, LANES)).astype(bf16)


def one_hot(column, height):
    middle = height // 2
    ids = lax.broadcasted_iota(jnp.int32, (height, LANES), 0) - middle
    ids = ids.astype(f32).astype(bf16).reshape(height // 16, 16, LANES)
    column = column - middle
    one, zero = jnp.ones((), bf16), jnp.zeros((), bf16)
    pieces = [
        jnp.where(ids == wide(column[r : r + 1])[None], one, zero).reshape(height, LANES)
        for r in range(column.shape[0])
    ]
    return jnp.concatenate(pieces, axis=1)


def split(value):
    high = value.astype(bf16).astype(f32)
    return high, value - high


def spread_moments(depth, weight, velocity, cells):
    nz = cells.nz
    ids = lax.broadcasted_iota(jnp.int32, (nz, LANES), 0).astype(f32).astype(bf16)
    ids = ids.reshape(nz // 16, 16, LANES)
    row_ids = lax.broadcasted_iota(jnp.int32, (16, LANES), 0).astype(f32).astype(bf16)
    zero = jnp.zeros((), bf16)
    parts = [split(weight * velocity[d]) for d in range(3)]
    channels = [weight] + [p[0] for p in parts] + [p[1] for p in parts]
    pieces = []
    for r in range(depth.shape[0]):
        at = wide(depth[r : r + 1])
        here = ids == at[None]
        values = [wide(c[r : r + 1]) for c in channels]
        tiles = [jnp.where(here, v[None], zero).reshape(nz, LANES) for v in values]
        top = jnp.zeros((16, LANES), bf16)
        for c, v in enumerate(values):
            top = jnp.where(row_ids == c, v, top)
        top = jnp.where(at == nz, top, zero)
        pieces.append(
            jnp.concatenate(
                tiles[:4] + [top, jnp.zeros((nz - 16, LANES), bf16)] + tiles[4:], axis=0
            )
        )
    return jnp.concatenate(pieces, axis=1)


def bin_group(total_ref, position, velocity, weight, meta, cells):
    levels = levels_of(position, meta)
    hot = one_hot(plane_of(levels, cells), cells.rows)
    spread = spread_moments(levels[2], weight, velocity, cells)
    total_ref[...] += lax.dot_general(hot, spread, NT, preferred_element_type=f32)


def row_iota():
    return lax.broadcasted_iota(jnp.int32, (GROUP, LANES), 0)


def bin_residents(cells, first, count, meta_ref, pos_ref, vel_ref, *refs):
    total_ref = refs[-1]
    meta = [meta_ref[k] for k in range(8)]
    if first == 0:
        total_ref[...] = jnp.zeros_like(total_ref)
    else:
        total_ref[...] = refs[0][...]
    live_rows = meta[6] - first
    stride = GROUP * TWIN

    @pl.loop(0, jnp.clip((live_rows + stride - 1) // stride, 0, count // stride))
    def _(step):
        for part in range(TWIN):
            offset = pl.multiple_of(step * stride + part * GROUP, GROUP)
            rows = pl.ds(offset, GROUP)
            position = [pos_ref[d, rows, :] for d in range(3)]
            velocity = [vel_ref[d, rows, :] for d in range(3)]
            weight = jnp.where(row_iota() + offset < live_rows, 1.0, 0.0)
            bin_group(total_ref, position, velocity, weight, meta, cells)


def arrival_group(ref, first, step, face_rows):
    offset = pl.multiple_of(step * GROUP, GROUP)
    comps = [ref[pl.ds(first + c * face_rows + offset, GROUP), :] for c in range(6)]
    live = (row_iota() + offset).astype(f32) < ref[pl.ds(first + 6 * face_rows, GROUP), :]
    return comps[:3], comps[3:], live


def face_count(ref, first, face_rows):
    return jnp.max(ref[pl.ds(first + 6 * face_rows, GROUP), :]).astype(jnp.int32)


def bead_mask(chains):
    slot = row_iota() * LANES + lax.broadcasted_iota(jnp.int32, (GROUP, LANES), 1)
    return slot < CHAIN * chains


def bin_arrivals(cells, face_rows, places, meta_ref, *refs):
    count = len(refs) - 8
    sources = refs[:count]
    bead_pos_ref, bead_vel_ref, axis_ref, start_ref, total_ref, low_ref, high_ref, sums = refs[
        count:
    ]
    meta = [meta_ref[k] for k in range(8)]
    sums[...] = start_ref[...]
    weight = jnp.where(bead_mask(meta[7]), bead_mass, 0.0)
    bin_group(
        sums,
        [bead_pos_ref[d] for d in range(3)],
        [bead_vel_ref[d] for d in range(3)],
        weight,
        meta,
        cells,
    )
    for which, first in places:
        ref = sources[which]

        @pl.loop(0, (face_count(ref, first, face_rows) + GROUP - 1) // GROUP)
        def _(step):
            position, velocity, live = arrival_group(ref, first, step, face_rows)
            bin_group(sums, position, velocity, jnp.where(live, 1.0, 0.0), meta, cells)

    nz, inner = cells.nz, cells.inner
    lane = lax.broadcasted_iota(jnp.int32, (cells.rows, LANES), 1)
    main, rest = sums[:, :LANES], sums[:, LANES:]
    main = main + jnp.where(lane < nz, 0.0, rest)
    top = jnp.where(lane == 0, rest, rest + pltpu.roll(rest, LANES - 3, axis=1))
    total_ref[0] = main
    total_ref[1] = jnp.where(lane < 4, top, 0.0)
    axis = axis_ref[...].astype(f32)
    total_ref[1, :inner, nz : 2 * nz] = axis
    sx, sy = cells.sx, cells.sy
    low_ref[...] = jnp.zeros_like(low_ref)
    high_ref[...] = jnp.zeros_like(high_ref)
    for half in range(2):
        corner = inner + sy + 1
        low_ref[half, :sy, :] = total_ref[half, :sy, :]
        low_ref[half, sy : sy + 1, :] = total_ref[half, corner : corner + 1, :]
        high_ref[half, : sy + 1, :] = total_ref[half, inner : inner + sy + 1, :]


def add_faces_x(cells, total_ref, below_ref, above_ref, out_ref, low_ref, high_ref):
    sx, sy, inner = cells.sx, cells.sy, cells.inner
    corner = inner + sy + 1
    out_ref[...] = total_ref[...]
    low_ref[...] = jnp.zeros_like(low_ref)
    high_ref[...] = jnp.zeros_like(high_ref)
    for half in range(2):
        out_ref[half, :sy, :] += below_ref[half, :sy, :]
        out_ref[half, corner : corner + 1, :] += below_ref[half, sy : sy + 1, :]
        out_ref[half, inner : inner + sy + 1, :] += above_ref[half, : sy + 1, :]
        low_ref[half, :sx, :] = out_ref[half, pl.ds(0, sx, stride=sy), :]
        low_ref[half, sx : sx + 1, :] = out_ref[half, inner : inner + 1, :]
        high_ref[half, :sx, :] = out_ref[half, corner : corner + sx, :]
        high_ref[half, sx : sx + 1, :] = out_ref[half, inner + sy : inner + sy + 1, :]


def add_faces_y(cells, total_ref, below_ref, above_ref, out_ref, face_ref, sums):
    sx, sy, nz, inner = cells.sx, cells.sy, cells.nz, cells.inner
    corner = inner + sy + 1
    sums[...] = total_ref[...]
    for half in range(2):
        sums[half, pl.ds(0, sx, stride=sy), :] += below_ref[half, :sx, :]
        sums[half, inner : inner + 1, :] += below_ref[half, sx : sx + 1, :]
        sums[half, corner : corner + sx, :] += above_ref[half, :sx, :]
        sums[half, inner + sy : inner + sy + 1, :] += above_ref[half, sx : sx + 1, :]
    main = sums[0].T
    rest = sums[1].T
    out_ref[:LANES, :] = main
    out_ref[LANES : LANES + nz, :] = rest[nz : 2 * nz]
    out_ref[LANES + nz :, :] = jnp.zeros((GROUP, cells.rows), f32)
    out_ref[LANES + nz : LANES + nz + 4, :] = rest[:4]
    face_ref[...] = jnp.zeros_like(face_ref)
    for c in range(5):
        face_ref[c : c + 1, :] = out_ref[c * nz : c * nz + 1, :]
        face_ref[GROUP + c : GROUP + c + 1, :] = out_ref[5 * nz + c : 5 * nz + c + 1, :]


def cell_table(cells, total_ref, below_ref, above_ref, table_ref, sheet, edge):
    nz, inner, height = cells.nz, cells.inner, cells.height
    row_ids = lax.broadcasted_iota(jnp.int32, (nz, cells.rows), 0)
    parts = []
    tops = []
    for c in range(5):
        face = jnp.where(row_ids == 0, below_ref[GROUP + c : GROUP + c + 1, :], 0.0)
        parts.append(total_ref[c * nz : (c + 1) * nz, :] + face)
        tops.append(
            total_ref[5 * nz + c : 5 * nz + c + 1, :] + above_ref[c : c + 1, :]
        )
    mass = jnp.maximum(parts[0], 1.0)
    top_mass = jnp.maximum(tops[0], 1.0)
    values = [parts[4]] + [p / mass for p in parts[1:4]]
    top_values = [tops[4]] + [t / top_mass for t in tops[1:4]]
    sheet[...] = jnp.zeros_like(sheet)
    edge[...] = jnp.zeros_like(edge)
    lane = lax.broadcasted_iota(jnp.int32, (cells.extra, LANES), 1)
    spare = LANES - (cells.rows - inner)
    for c in range(4):
        base = c * height
        sheet[base : base + nz, :] = values[c][:, :inner]
        sheet[base + nz : base + nz + 1, :] = top_values[c][:, :inner]
        edge[base : base + nz, :] = jnp.concatenate(
            [values[c][:, inner:], jnp.zeros((nz, spare), f32)], axis=1
        )
        edge[base + nz : base + nz + 1, :] = jnp.concatenate(
            [top_values[c][:, inner:], jnp.zeros((1, spare), f32)], axis=1
        )
        folded = [jnp.zeros((cells.extra, LANES), f32) for _ in range(inner // LANES)]
        for m in range(cells.per):
            begin = m * cells.edges
            piece = edge[pl.ds(base + m, cells.extra, stride=cells.per), :]
            piece = pltpu.roll(piece, begin % LANES, axis=1) if begin % LANES else piece
            for t in range(inner // LANES):
                low, high = begin - t * LANES, begin + cells.edges - t * LANES
                if high > 0 and low < LANES:
                    folded[t] = jnp.where((lane >= low) & (lane < high), piece, folded[t])
        sheet[base + nz + 1 : base + nz + 1 + cells.extra, :] = jnp.concatenate(folded, axis=1)
    whole = sheet[...]
    high = whole.astype(bf16).astype(f32)
    low = (whole - high)[height:]
    table_ref[...] = jnp.concatenate([high, low], axis=0).astype(bf16)


def direction_table():
    counter = jnp.arange(LANES).astype(f32)
    height = 1.0 - (2.0 * counter + 1.0) / NAXES
    radius = jnp.sqrt(jnp.maximum(1.0 - height * height, 0.0))
    rows = jnp.stack([radius * jnp.cos(golden * counter), radius * jnp.sin(golden * counter)])
    return jnp.broadcast_to(rows[:, None], (2, GROUP, LANES))


def fold_rows(values):
    sub = lax.broadcasted_iota(jnp.int32, (GROUP, LANES), 0)
    step = GROUP // 2
    while step:
        upper = (sub & step) == 0
        half = len(values) // 2
        joined = []
        for a, b in zip(values[:half], values[half:]):
            a = a + pltpu.roll(a, GROUP - step, axis=0)
            b = b + pltpu.roll(b, step, axis=0)
            joined.append(jnp.where(upper, a, b))
        values = joined
        step //= 2
    return values[0]


def collide(position, velocity, meta, table, dirs_ref, cells):
    height = cells.height
    row, column = place_of(levels_of(position, meta), cells)
    found = lax.dot_general(
        table, one_hot(column, cells.inner), NN, preferred_element_type=f32
    )
    ids = lax.broadcasted_iota(jnp.int32, (height, LANES), 0).astype(f32)
    picked = [[] for _ in range(4)]
    for r in range(GROUP):
        block = found[:, r * LANES : (r + 1) * LANES]
        here = ids == row[r : r + 1]
        for c in range(4):
            value = block[c * height : (c + 1) * height]
            if c > 0:
                value = value + block[(3 + c) * height : (4 + c) * height]
            value = jnp.where(here, value, 0.0)
            picked[c].append(
                jnp.sum(value.reshape(height // GROUP, GROUP, LANES), axis=0)
            )
    picked = [fold_rows(p) for p in picked]
    axis, flow = picked[0].astype(jnp.int32), picked[1:]
    normal = [
        jnp.take_along_axis(dirs_ref[0], axis, axis=1, mode="promise_in_bounds"),
        jnp.take_along_axis(dirs_ref[1], axis, axis=1, mode="promise_in_bounds"),
        1.0 - (2.0 * picked[0] + 1.0) * (1.0 / NAXES),
    ]
    rel = [velocity[d] - flow[d] for d in range(3)]
    along = (1.0 - turn_cosine) * (
        normal[0] * rel[0] + normal[1] * rel[1] + normal[2] * rel[2]
    )
    result = []
    for d in range(3):
        e, f = (d + 1) % 3, (d + 2) % 3
        crossed = normal[e] * rel[f] - normal[f] * rel[e]
        result.append(
            flow[d] + (turn_cosine * rel[d] + turn_sine * crossed + along * normal[d])
        )
    return result


def passed(position, speed):
    return position - jnp.floor(position) - 0.5 + 3.0 * step_size * speed


def copy_out(pairs, sems):
    copies = [pltpu.make_async_copy(a, b, sems.at[k]) for k, (a, b) in enumerate(pairs)]
    for copy in copies:
        copy.start()
    for copy in copies:
        copy.wait()


def collide_residents(
    cells, first, count, meta_ref, dirs_ref, table_ref, pos_ref, vel_ref, *refs
):
    out_pos, out_vel, token, held_pos, held_vel, sems = refs[-6:]
    token[...] = jnp.zeros_like(token)
    meta = [meta_ref[k] for k in range(8)]
    table = table_ref[...]
    live_rows = meta[6] - first
    held_pos[...] = jnp.zeros_like(held_pos)
    held_vel[...] = jnp.zeros_like(held_vel)
    stride = GROUP * TWIN

    @pl.loop(0, jnp.clip((live_rows + stride - 1) // stride, 0, count // stride))
    def _(step):
        for part in range(TWIN):
            offset = pl.multiple_of(step * stride + part * GROUP, GROUP)
            rows = pl.ds(offset, GROUP)
            position = [pos_ref[d, rows, :] for d in range(3)]
            velocity = [vel_ref[d, rows, :] for d in range(3)]
            live = row_iota() + offset < live_rows
            speed = collide(position, velocity, meta, table, dirs_ref, cells)
            for d in range(3):
                held_vel[d, rows, :] = jnp.where(live, speed[d], 0.0)
                held_pos[d, rows, :] = jnp.where(live, passed(position[d], speed[d]), 0.0)

    span = pl.ds(first, count)
    copy_out([(held_pos, out_pos.at[:, span, :]), (held_vel, out_vel.at[:, span, :])], sems)


def collide_arrivals(cells, first, face_rows, places, meta_ref, dirs_ref, table_ref, *refs):
    out_pos, out_vel, token, held_pos, held_vel, sems = refs[-6:]
    token[...] = jnp.zeros_like(token)
    meta = [meta_ref[k] for k in range(8)]
    table = table_ref[...]
    held_pos[...] = jnp.zeros_like(held_pos)
    held_vel[...] = jnp.zeros_like(held_vel)
    for k, (which, begin) in enumerate(places):
        ref = refs[which]

        @pl.loop(0, (face_count(ref, begin, face_rows) + GROUP - 1) // GROUP)
        def _(step):
            position, velocity, live = arrival_group(ref, begin, step, face_rows)
            speed = collide(position, velocity, meta, table, dirs_ref, cells)
            rows = pl.ds(k * face_rows + pl.multiple_of(step * GROUP, GROUP), GROUP)
            for d in range(3):
                held_vel[d, rows, :] = jnp.where(live, speed[d], 0.0)
                held_pos[d, rows, :] = jnp.where(live, passed(position[d], speed[d]), 0.0)

    span = pl.ds(first, len(places) * face_rows)
    copy_out([(held_pos, out_pos.at[:, span, :]), (held_vel, out_vel.at[:, span, :])], sems)


def pack_inputs(
    meta_ref,
    pos_ref,
    vel_ref,
    bead_pos_ref,
    bead_vel_ref,
    start_ref,
    block_ref,
    rows_pos_ref,
    rows_vel_ref,
    *refs,
):
    out_refs, (held_pos, held_vel, sems) = refs[:6], refs[6:]
    copies = [(bead_pos_ref, held_pos), (bead_vel_ref, held_vel)]
    for face, out_ref in enumerate(out_refs):
        copies.append((pos_ref.at[:, face], out_ref.at[0:3]))
        copies.append((vel_ref.at[:, face], out_ref.at[3:6]))
    copies = [pltpu.make_async_copy(a, b, sems.at[k]) for k, (a, b) in enumerate(copies)]
    for copy in copies:
        copy.start()
    for face, out_ref in enumerate(out_refs):
        out_ref[6] = jnp.full(out_ref.shape[1:], meta_ref[8 + face], jnp.int32).astype(f32)
    slots = start_ref.shape[1]
    start_ref[...] = jnp.zeros_like(start_ref)
    rows_pos_ref[...] = jnp.zeros_like(rows_pos_ref)
    rows_vel_ref[...] = jnp.zeros_like(rows_vel_ref)
    for copy in copies:
        copy.wait()
    for d in range(3):
        for k in range(slots // LANES):
            lanes = slice(k * LANES, (k + 1) * LANES)
            start_ref[d : d + 1, lanes] = held_pos[d, k : k + 1, :]
            rows_pos_ref[d, k : k + 1, :] = held_pos[d, k : k + 1, :]
            rows_vel_ref[d, k : k + 1, :] = held_vel[d, k : k + 1, :]
    start = start_ref[...]
    whole = payload(start, slot_live(slots, meta_ref[7], GROUP))
    for k in range(slots // LANES):
        block_ref[k * GROUP : (k + 1) * GROUP, :] = whole[:, k * LANES : (k + 1) * LANES]


def stack_rows(parts, *refs):
    out_ref = refs[-1]
    at = 0
    for which, begin, count in parts:
        out_ref[at : at + count, :] = refs[which][begin : begin + count, :]
        at += count


def slot_live(slots, chains, rows):
    return lax.broadcasted_iota(jnp.int32, (rows, slots), 1) < CHAIN * chains


def payload(position, live):
    slots = position.shape[1]
    row_ids = lax.broadcasted_iota(jnp.int32, (GROUP, slots), 0)
    flag = jnp.where(live, 1.0, 0.0)
    return jnp.where(row_ids == 3, flag, jnp.where(row_ids < 3, position, 0.0))


def thirds_of(value):
    high = value.astype(bf16)
    rest = value - high.astype(f32)
    middle = rest.astype(bf16)
    low = (rest - middle.astype(f32)).astype(bf16)
    return jnp.concatenate([high.astype(f32), middle.astype(f32), low.astype(f32)], axis=0).astype(
        bf16
    )


def summed_thirds(value):
    return value[:GROUP] + (value[GROUP : 2 * GROUP] + value[2 * GROUP :])


def forces(own, chains, counts, bonds_ref, blocks, centre, lengths, mine_ref, packed, push):
    slots = own.shape[1]
    bond_slots = bonds_ref.shape[0]
    row_ids = lax.broadcasted_iota(jnp.int32, (GROUP, slots), 0)
    mid = jnp.zeros((GROUP, slots), f32)
    length = jnp.ones((GROUP, slots), f32)
    for d in range(3):
        mid = jnp.where(row_ids == d, centre[d], mid)
        length = jnp.where(row_ids == d, lengths[d], length)
    live = slot_live(slots, chains, GROUP)
    local = jnp.where(live & (row_ids < 3), own - mid, 0.0)
    columns = jnp.where(live, local, far_own).T
    for d in range(3):
        mine_ref[d] = jnp.broadcast_to(columns[:, d : d + 1], (slots, LANES))

    packed[...] = jnp.full(packed.shape, far_ghost, f32)
    lane = lax.broadcasted_iota(jnp.int32, (GROUP, LANES), 1)
    tiles = slots // LANES
    offset = jnp.int32(0)
    index = 0
    for ref in blocks:
        for b in range(ref.shape[0] // GROUP):
            near = ref[b * GROUP : (b + 1) * GROUP, :] - mid
            near = near - length * jnp.floor(near * (1.0 / length) + 0.5)
            tile, turn = offset // LANES, offset % LANES
            turned = [
                pltpu.roll(near[:, k * LANES : (k + 1) * LANES], turn, axis=1)
                for k in range(tiles)
            ]
            for k in range(tiles + 1):
                if k == 0:
                    value = turned[0]
                elif k == tiles:
                    value = turned[-1]
                else:
                    value = jnp.where(lane < turn, turned[k - 1], turned[k])
                place = (tile + k) * LANES + lane
                taken = (place >= offset) & (place < offset + counts[index])
                packed[tile + k] = jnp.where(taken, value, packed[tile + k])
            offset = offset + counts[index]
            index += 1

    push[...] = jnp.zeros_like(push)
    chunk = 64
    steps = (offset + 2 * LANES - 1) // (2 * LANES)

    @pl.loop(0, (CHAIN * chains + chunk - 1) // chunk)
    def _(part):
        rows = pl.ds(pl.multiple_of(part * chunk, chunk), chunk)
        mine = [mine_ref[d, rows, :] for d in range(3)]

        def add_tiles(step, total):
            for k in range(2):
                other = packed[2 * step + k]
                differ = [mine[d] - other[d : d + 1] for d in range(3)]
                square = (
                    differ[0] * differ[0] + differ[1] * differ[1] + differ[2] * differ[2]
                )
                inside = (square < cut_square) & (square > 0.25)
                inverse = 1.0 / jnp.where(inside, square, 1e30)
                sixth = inverse * inverse * inverse
                weight = (sixth * inverse) * (48.0 * sixth - 24.0)
                total = tuple(total[d] + weight * differ[d] for d in range(3))
            return total

        total = lax.fori_loop(
            0, steps, add_tiles, tuple(jnp.zeros((chunk, LANES), f32) for _ in range(3))
        )
        for d in range(3):
            push[d, rows, :] = total[d]

    pair = jnp.zeros((GROUP, slots), f32)
    for d in range(3):
        pair = jnp.where(row_ids == d, jnp.sum(push[d].T, axis=0, keepdims=True), pair)

    slot_ids = lax.broadcasted_iota(jnp.int32, (bond_slots, slots), 1)
    bond_ids = lax.broadcasted_iota(jnp.int32, (bond_slots, slots), 0)
    ends = bonds_ref[...]
    first = jnp.where(slot_ids == ends[:, 0:1], 1.0, 0.0)
    second = jnp.where(slot_ids == ends[:, 1:2], 1.0, 0.0)
    joins = jnp.where(bond_ids < (CHAIN - 1) * chains, first - second, 0.0).astype(bf16)
    stretch = summed_thirds(
        lax.dot_general(thirds_of(local), joins, NT, preferred_element_type=f32)
    )
    square = (
        stretch[0:1] * stretch[0:1] + stretch[1:2] * stretch[1:2] + stretch[2:3] * stretch[2:3]
    )
    bond_live = (
        lax.broadcasted_iota(jnp.int32, (1, bond_slots), 1) < (CHAIN - 1) * chains
    )
    pull = jnp.where(bond_live, -spring / (1.0 - square / reach_square), 0.0) * stretch
    return pair + summed_thirds(
        lax.dot_general(thirds_of(pull), joins, NN, preferred_element_type=f32)
    )


def force_scratch(slots, blocks):
    tiles = -(-(blocks * slots // LANES + 2) // 2) * 2
    return [
        pltpu.VMEM((3, slots, LANES), f32),
        pltpu.VMEM((tiles, GROUP, LANES), f32),
        pltpu.VMEM((3, slots, LANES), f32),
    ]


def centre_of(meta, sizes):
    return [meta[3 + d].astype(f32) + 0.5 * sizes[d] for d in range(3)]


def first_forces(sizes, lengths, sources, meta_ref, start_ref, bonds_ref, *refs):
    blocks, (push_ref, counts_ref), scratch = (
        refs[:sources],
        refs[sources : sources + 2],
        refs[sources + 2 :],
    )
    meta = [meta_ref[k] for k in range(8)]
    counts = []
    for ref in blocks:
        for b in range(ref.shape[0] // GROUP):
            live = ref[b * GROUP + 3 : b * GROUP + 4, :]
            counts.append(jnp.sum(live).astype(jnp.int32))
    for k, count in enumerate(counts):
        counts_ref[k] = count
    push_ref[...] = forces(
        start_ref[...],
        meta[7],
        counts,
        bonds_ref,
        blocks,
        centre_of(meta, sizes),
        lengths,
        *scratch,
    )


def finish_cells(
    cells,
    meta_ref,
    dirs_ref,
    total_ref,
    below_ref,
    above_ref,
    bead_pos_ref,
    bead_vel_ref,
    start_ref,
    push_ref,
    table_ref,
    speed_ref,
    moved_ref,
    pay_ref,
    sheet,
    edge,
):
    meta = [meta_ref[k] for k in range(8)]
    cell_table(cells, total_ref, below_ref, above_ref, table_ref, sheet, edge)
    fresh = collide(
        [bead_pos_ref[d] for d in range(3)],
        [bead_vel_ref[d] for d in range(3)],
        meta,
        table_ref[...],
        dirs_ref,
        cells,
    )
    start = start_ref[...]
    slots = start.shape[1]
    row_ids = lax.broadcasted_iota(jnp.int32, (GROUP, slots), 0)
    speed = jnp.zeros((GROUP, slots), f32)
    for d in range(3):
        line = jnp.concatenate([fresh[d][k : k + 1] for k in range(slots // LANES)], axis=1)
        speed = jnp.where(row_ids == d, line, speed)
    speed = speed + half_kick * push_ref[...]
    moved = step_size * speed
    live = slot_live(slots, meta[7], GROUP)
    speed_ref[...] = speed
    moved_ref[...] = moved
    pay_ref[...] = payload(start + moved, live)


def substep(
    sizes, lengths, last, sources, meta_ref, start_ref, bonds_ref, counts_ref, speed_ref, moved_ref, *refs
):
    blocks, outs, scratch = refs[:sources], refs[sources + 1 : -3], refs[-3:]
    meta = [meta_ref[k] for k in range(8)]
    counts = [
        counts_ref[k] for k in range(sum(ref.shape[0] // GROUP for ref in blocks))
    ]
    start = start_ref[...]
    moved = moved_ref[...]
    push = forces(
        start + moved,
        meta[7],
        counts,
        bonds_ref,
        blocks,
        centre_of(meta, sizes),
        lengths,
        *scratch,
    )
    live = slot_live(start.shape[1], meta[7], GROUP)
    speed = speed_ref[...] + half_kick * push
    if last:
        for d in range(3):
            outs[0][d, 0, 0, :, :] = jnp.where(live, speed, 0.0)[d : d + 1]
            outs[1][d, 0, 0, :, :] = jnp.where(live, moved, 0.0)[d : d + 1]
        return
    speed = speed + half_kick * push
    moved = moved + step_size * speed
    outs[0][...] = speed
    outs[1][...] = moved
    outs[2][...] = payload(start + moved, live)


def neighbours(value, axis):
    peers = lax.axis_size(axis)
    if peers == 2:
        return [moved_along(value, axis, 1)]
    return [moved_along(value, axis, 1), moved_along(value, axis, -1)]


def stacked(parts, operands, order=()):
    rows = sum(count for _, _, count in parts)
    width = operands[0].shape[1]
    return pl.pallas_call(
        functools.partial(stack_rows, tuple(parts)),
        out_shape=like(rows, width),
        in_specs=[vmem()] * len(operands) + [pl.BlockSpec(memory_space=pl.ANY)] * len(order),
        out_specs=vmem(),
        compiler_params=params(),
        name="stack_rows",
    )(*operands, *order)


def whole_rows(operands):
    return [(k, 0, value.shape[0]) for k, value in enumerate(operands)]


def halo(block, pieces):
    parts = [block] + neighbours(block, "gz")
    row = stacked(whole_rows(parts), parts, [pieces[0]()])
    parts = [row] + neighbours(row, "gy")
    plane = stacked(whole_rows(parts), parts, [pieces[1]()])
    sides = neighbours(plane, "gx")
    return [plane] + sides, pieces[2]()


def like(*shape, dtype=f32):
    return jax.ShapeDtypeStruct(shape, dtype)


def shards(
    sol_pos,
    sol_vel,
    sol_rows,
    mig_pos,
    mig_vel,
    mig_rows,
    bead_pos,
    bead_vel,
    bead_chains,
    bond_list,
    cell_axis,
    shift,
):
    sizes = cell_axis.shape
    cells = Cells(*sizes)
    names = ("gx", "gy", "gz")
    lengths = tuple(float(sizes[d] * lax.axis_size(names[d])) for d in range(3))
    slots_here = sol_pos.shape[-1]
    buffer_slots = mig_pos.shape[-1]
    bead_slots = bead_pos.shape[-1]
    bond_slots = bond_list.shape[-1]
    rows_here = slots_here // LANES
    face_rows = buffer_slots // LANES
    rows_all = rows_here + 6 * face_rows
    anchor = jnp.stack([lax.axis_index(names[d]) * sizes[d] for d in range(3)])
    meta = jnp.concatenate(
        [
            shift,
            anchor.astype(jnp.int32),
            sol_rows.reshape(1),
            bead_chains.reshape(1),
            mig_rows.reshape(6),
        ]
    )
    dirs = direction_table()
    position = sol_pos.reshape(3, rows_here, LANES)
    velocity = sol_vel.reshape(3, rows_here, LANES)

    any_spec = pl.BlockSpec(memory_space=pl.ANY)
    face_height = 7 * face_rows
    bead_shape = like(GROUP, bead_slots)
    tiles = bead_slots // LANES
    rows_shape = like(3, GROUP, LANES)
    start, block, bead_rows_pos, bead_rows_vel, *packed = pl.pallas_call(
        pack_inputs,
        out_shape=[bead_shape, like(tiles * GROUP, LANES), rows_shape, rows_shape]
        + [like(7, face_rows, LANES)] * 6,
        in_specs=[smem()] + [pl.BlockSpec(memory_space=pltpu.HBM)] * 4,
        out_specs=[vmem()] * 10,
        scratch_shapes=[pltpu.VMEM((3, tiles, LANES), f32)] * 2
        + [pltpu.SemaphoreType.DMA((14,))],
        compiler_params=params(vmem_most),
        name="pack_inputs",
    )(
        meta,
        mig_pos.reshape(3, 6, face_rows, LANES),
        mig_vel.reshape(3, 6, face_rows, LANES),
        bead_pos.reshape(3, tiles, LANES),
        bead_vel.reshape(3, tiles, LANES),
    )
    packed = [value.reshape(face_height, LANES) for value in packed]
    bonds = bond_list.reshape(2, bond_slots).T

    thirds = 3
    count = rows_here // thirds
    axis_rows = cell_axis.reshape(cells.inner, sizes[2])

    def bin_piece(piece, earlier, order):
        return pl.pallas_call(
            functools.partial(bin_residents, cells, piece * count, count),
            out_shape=like(cells.rows, 2 * LANES),
            grid=(1,),
            in_specs=[smem()]
            + [pl.BlockSpec((3, count, LANES), lambda i, p=piece: (0, p, 0))] * 2
            + [vmem()] * len(earlier)
            + [any_spec] * len(order),
            out_specs=vmem(),
            compiler_params=params(),
            name=f"bin_residents_{piece}",
        )(meta, position, velocity, *earlier, *order)

    def swap(axis, low, high, body):
        if lax.axis_size(axis) == 2:
            both = [packed[low], packed[high], body]
            came = moved_along(stacked(whole_rows(both), both), axis, 1)
            return [came], [(0, face_height), (0, 0)], [(0, 2 * face_height)]
        up = stacked(whole_rows([packed[high], body]), [packed[high], body])
        down = stacked(whole_rows([packed[low], body]), [packed[low], body])
        came = [moved_along(up, axis, 1), moved_along(down, axis, -1)]
        return came, [(0, 0), (1, 0)], [(0, face_height), (1, face_height)]

    arrived, places, blocks = {}, {}, block
    totals = None
    for piece, (axis, low) in enumerate((("gz", 4), ("gy", 2), ("gx", 0))):
        came, spots, bodies = swap(axis, low, low + 1, blocks)
        totals = bin_piece(piece, [] if totals is None else [totals], [blocks])
        height = blocks.shape[0]
        arrived[axis], places[axis] = came, spots
        if axis != "gx":
            parts = [(0, 0, height)] + [(1 + w, at, height) for w, at in bodies]
            blocks = stacked(parts, [blocks] + came, [totals])
        else:
            around = [blocks] + [
                stacked([(0, at, height)], [came[w]]) for w, at in bodies
            ]

    def as_blocks(value):
        n = value.shape[0] // (GROUP * tiles)
        return (
            value.reshape(n, tiles, GROUP, LANES)
            .transpose(0, 2, 1, 3)
            .reshape(n * GROUP, bead_slots)
        )

    arriving, spots = [], []
    for axis in names:
        spots += [(len(arriving) + w, at) for w, at in places[axis]]
        arriving += arrived[axis]

    face_x = like(2, -(-(sizes[1] + 1) // GROUP) * GROUP, LANES)
    face_y = like(2, -(-(sizes[0] + 1) // GROUP) * GROUP, LANES)
    totals, low, high = pl.pallas_call(
        functools.partial(bin_arrivals, cells, face_rows, tuple(spots)),
        out_shape=[like(2, cells.rows, LANES), face_x, face_x],
        in_specs=[smem()] + [vmem()] * (len(arriving) + 4),
        out_specs=[vmem()] * 3,
        scratch_shapes=[pltpu.VMEM((cells.rows, 2 * LANES), f32)],
        compiler_params=params(),
        name="bin_arrivals",
    )(meta, *arriving, bead_rows_pos, bead_rows_vel, axis_rows, totals)

    around = [as_blocks(value) for value in around]
    many = sum(value.shape[0] // GROUP for value in around)
    push, counts = pl.pallas_call(
        functools.partial(first_forces, sizes, lengths, len(around)),
        out_shape=[bead_shape, like(many, dtype=jnp.int32)],
        in_specs=[smem()] + [vmem()] * (2 + len(around)),
        out_specs=[vmem(), smem()],
        scratch_shapes=force_scratch(bead_slots, many),
        compiler_params=params(),
        name="first_forces",
    )(meta, start, bonds, *around)

    below, above = moved_along(high, "gx", 1), moved_along(low, "gx", -1)
    totals, low, high = pl.pallas_call(
        functools.partial(add_faces_x, cells),
        out_shape=[like(2, cells.rows, LANES), face_y, face_y],
        in_specs=[vmem()] * 3,
        out_specs=[vmem()] * 3,
        compiler_params=params(),
        name="add_faces_x",
    )(totals, below, above)
    below, above = moved_along(high, "gy", 1), moved_along(low, "gy", -1)
    totals, faces = pl.pallas_call(
        functools.partial(add_faces_y, cells),
        out_shape=[like(LANES + cells.nz + GROUP, cells.rows), like(2 * GROUP, cells.rows)],
        in_specs=[vmem()] * 3,
        out_specs=[vmem()] * 2,
        scratch_shapes=[pltpu.VMEM((2, cells.rows, LANES), f32)],
        compiler_params=params(),
        name="add_faces_y",
    )(totals, below, above)
    sides = neighbours(faces, "gz")
    below, above = sides[0], sides[-1]

    table, speed, moved, pay = pl.pallas_call(
        functools.partial(finish_cells, cells),
        out_shape=[
            like(7 * cells.height, cells.inner, dtype=bf16),
            bead_shape,
            bead_shape,
            bead_shape,
        ],
        in_specs=[smem()] + [vmem()] * 8,
        out_specs=[vmem()] * 4,
        scratch_shapes=[
            pltpu.VMEM((4 * cells.height, cells.inner), f32),
            pltpu.VMEM((4 * cells.height, LANES), f32),
        ],
        compiler_params=params(),
        name="finish_cells",
    )(meta, dirs, totals, below, above, bead_rows_pos, bead_rows_vel, start, push)

    solvent_shape = like(3, rows_all, LANES)
    results = []
    cuts = 6
    span = rows_here // cuts

    def collide_piece(piece):
        earlier = results[:2]
        if piece < cuts:
            body = functools.partial(collide_residents, cells, piece * span, span)
            rows = span
            sources = [position, velocity]
            specs = [pl.BlockSpec((3, span, LANES), lambda i: (0, piece, 0))] * 2
        else:
            begin = 2 * (piece - cuts)
            body = functools.partial(
                collide_arrivals,
                cells,
                rows_here + begin * face_rows,
                face_rows,
                tuple(spots[begin : begin + 2]),
            )
            rows = 2 * face_rows
            sources = arriving
            specs = [vmem()] * len(arriving)
        at = 3 + len(sources)
        results[:] = pl.pallas_call(
            body,
            out_shape=[solvent_shape, solvent_shape, like(GROUP, LANES)],
            grid=(1,),
            in_specs=[smem(), vmem(), vmem()] + specs + [any_spec] * len(earlier),
            out_specs=[any_spec, any_spec, vmem()],
            scratch_shapes=[pltpu.VMEM((3, rows, LANES), f32)] * 2
            + [pltpu.SemaphoreType.DMA((2,))],
            input_output_aliases={at: 0, at + 1: 1} if earlier else {},
            compiler_params=params(),
            name=f"collide_{piece}",
        )(meta, dirs, table, *sources, *earlier)
        return results[2]

    for step in range(3):
        last = step == 2
        thunks = [functools.partial(collide_piece, 3 * step + k) for k in range(3)]
        ghosts, order = halo(pay, thunks)
        final = like(3, 1, 1, 1, bead_slots)
        outcome = pl.pallas_call(
            functools.partial(substep, sizes, lengths, last, len(ghosts)),
            out_shape=[final] * 2 if last else [bead_shape] * 3,
            in_specs=[smem(), vmem(), vmem(), smem()]
            + [vmem()] * (2 + len(ghosts))
            + [any_spec],
            out_specs=[vmem()] * (2 if last else 3),
            scratch_shapes=force_scratch(bead_slots, many),
            compiler_params=params(),
            name=f"substep_{step}",
        )(meta, start, bonds, counts, speed, moved, *ghosts, order)
        speed, moved = outcome[:2]
        pay = outcome[-1]

    count_solvent = rows_all * LANES
    return (
        results[0].reshape(3, 1, 1, 1, count_solvent),
        results[1].reshape(3, 1, 1, 1, count_solvent),
        moved,
        speed,
    )


def solution(mesh):
    return jax.shard_map(
        shards,
        mesh=mesh,
        in_specs=(
            P(None, "gx", "gy", "gz", None),
            P(None, "gx", "gy", "gz", None),
            P("gx", "gy", "gz"),
            P(None, "gx", "gy", "gz", None, None),
            P(None, "gx", "gy", "gz", None, None),
            P("gx", "gy", "gz", None),
            P(None, "gx", "gy", "gz", None),
            P(None, "gx", "gy", "gz", None),
            P("gx", "gy", "gz"),
            P(None, "gx", "gy", "gz", None),
            P("gx", "gy", "gz"),
            P(),
        ),
        out_specs=(
            P(None, "gx", "gy", "gz", None),
            P(None, "gx", "gy", "gz", None),
            P(None, "gx", "gy", "gz", None),
            P(None, "gx", "gy", "gz", None),
        ),
        check_vma=False,
    )
```

```python
import functools
import math

import jax
import jax.numpy as jnp
from jax import lax
from jax.experimental import pallas as pl
from jax.experimental.pallas import tpu as pltpu
from jax.sharding import PartitionSpec as P

UNITS = 16
NAXES = 32
CHAIN = 8
LANES = 128
GROUP = 8
TWIN = 4
SENT = 4

bead_mass = 5.0
step_size = 0.02
spring = 30.0
reach_square = 2.25
cut_square = 2.0 ** (1.0 / 3.0)
turn_cosine = math.cos(130.0 * math.pi / 180.0)
turn_sine = math.sin(130.0 * math.pi / 180.0)
golden = math.pi * (3.0 - math.sqrt(5.0))
half_kick = 0.5 * step_size / bead_mass
far_own = 3000.0
far_ghost = 9000.0
vmem_limit = 48 * 1024 * 1024
vmem_most = 61 * 1024 * 1024
NT = (((1,), (1,)), ((), ()))
NN = (((1,), (0,)), ((), ()))
exact = lax.Precision.HIGHEST
f32 = jnp.float32
bf16 = jnp.bfloat16


def params(limit=vmem_limit):
    return pltpu.CompilerParams(vmem_limit_bytes=limit)


def vmem():
    return pl.BlockSpec(memory_space=pltpu.VMEM)


def smem():
    return pl.BlockSpec(memory_space=pltpu.SMEM)


def moved_along(value, axis, by):
    peers = lax.axis_size(axis)
    return lax.ppermute(value, axis, [(i, (i + by) % peers) for i in range(peers)])


class Cells:
    def __init__(self, size_x, size_y, size_z):
        self.sx, self.sy, self.nz = size_x, size_y, size_z
        self.inner = size_x * size_y
        self.edges = size_x + size_y + 1
        self.rows = -(-(self.inner + self.edges) // 16) * 16
        self.middle = self.rows // 2
        self.per = self.inner // self.edges
        self.depths = size_z + 1
        self.extra = -(-self.depths // self.per)
        self.height = -(-(self.depths + self.extra) // GROUP) * GROUP


def levels_of(position, meta):
    return [
        jnp.floor(jnp.floor(position[d] * UNITS + meta[d].astype(f32)) * (1.0 / UNITS))
        - meta[3 + d].astype(f32)
        for d in range(3)
    ]


def edge_of(levels, cells):
    outer = (levels[0] == cells.sx) | (levels[1] == cells.sy)
    return outer, jnp.where(levels[0] == cells.sx, levels[1], cells.sy + 1 + levels[0])


def plane_of(levels, cells):
    outer, edge = edge_of(levels, cells)
    return jnp.where(outer, cells.inner + edge, levels[0] * cells.sy + levels[1])


def place_of(levels, cells):
    outer, edge = edge_of(levels, cells)
    fold = jnp.floor((levels[2] + 0.5) * (1.0 / cells.per))
    row = jnp.where(outer, cells.depths + fold, levels[2])
    column = jnp.where(
        outer,
        (levels[2] - fold * cells.per) * cells.edges + edge,
        levels[0] * cells.sy + levels[1],
    )
    return row, column


def wide(row):
    return jnp.broadcast_to(row, (16, LANES)).astype(bf16)


def one_hot(column, height):
    middle = height // 2
    ids = lax.broadcasted_iota(jnp.int32, (height, LANES), 0) - middle
    ids = ids.astype(f32).astype(bf16).reshape(height // 16, 16, LANES)
    column = column - middle
    one, zero = jnp.ones((), bf16), jnp.zeros((), bf16)
    pieces = [
        jnp.where(ids == wide(column[r : r + 1])[None], one, zero).reshape(height, LANES)
        for r in range(column.shape[0])
    ]
    return jnp.concatenate(pieces, axis=1)


def split(value):
    high = value.astype(bf16).astype(f32)
    return high, value - high


def spread_moments(depth, weight, velocity, cells):
    nz = cells.nz
    ids = lax.broadcasted_iota(jnp.int32, (nz, LANES), 0).astype(f32).astype(bf16)
    ids = ids.reshape(nz // 16, 16, LANES)
    row_ids = lax.broadcasted_iota(jnp.int32, (16, LANES), 0).astype(f32).astype(bf16)
    zero = jnp.zeros((), bf16)
    parts = [split(weight * velocity[d]) for d in range(3)]
    channels = [weight] + [p[0] for p in parts] + [p[1] for p in parts]
    pieces = []
    for r in range(depth.shape[0]):
        at = wide(depth[r : r + 1])
        here = ids == at[None]
        values = [wide(c[r : r + 1]) for c in channels]
        tiles = [jnp.where(here, v[None], zero).reshape(nz, LANES) for v in values]
        top = jnp.zeros((16, LANES), bf16)
        for c, v in enumerate(values):
            top = jnp.where(row_ids == c, v, top)
        top = jnp.where(at == nz, top, zero)
        pieces.append(
            jnp.concatenate(
                tiles[:4] + [top, jnp.zeros((nz - 16, LANES), bf16)] + tiles[4:], axis=0
            )
        )
    return jnp.concatenate(pieces, axis=1)


def bin_group(total_ref, position, velocity, weight, meta, cells):
    levels = levels_of(position, meta)
    hot = one_hot(plane_of(levels, cells), cells.rows)
    spread = spread_moments(levels[2], weight, velocity, cells)
    total_ref[...] += lax.dot_general(hot, spread, NT, preferred_element_type=f32)


def row_iota():
    return lax.broadcasted_iota(jnp.int32, (GROUP, LANES), 0)


def bin_residents(cells, first, count, meta_ref, pos_ref, vel_ref, *refs):
    total_ref = refs[-1]
    meta = [meta_ref[k] for k in range(8)]
    if first == 0:
        total_ref[...] = jnp.zeros_like(total_ref)
    else:
        total_ref[...] = refs[0][...]
    live_rows = meta[6] - first
    stride = GROUP * TWIN

    @pl.loop(0, jnp.clip((live_rows + stride - 1) // stride, 0, count // stride))
    def _(step):
        for part in range(TWIN):
            offset = pl.multiple_of(step * stride + part * GROUP, GROUP)
            rows = pl.ds(offset, GROUP)
            position = [pos_ref[d, rows, :] for d in range(3)]
            velocity = [vel_ref[d, rows, :] for d in range(3)]
            weight = jnp.where(row_iota() + offset < live_rows, 1.0, 0.0)
            bin_group(total_ref, position, velocity, weight, meta, cells)


def arrival_group(ref, first, step, face_rows):
    offset = pl.multiple_of(step * GROUP, GROUP)
    comps = [ref[pl.ds(first + c * face_rows + offset, GROUP), :] for c in range(6)]
    live = (row_iota() + offset).astype(f32) < ref[pl.ds(first + 6 * face_rows, GROUP), :]
    return comps[:3], comps[3:], live


def face_count(ref, first, face_rows):
    return jnp.max(ref[pl.ds(first + 6 * face_rows, GROUP), :]).astype(jnp.int32)


def bead_mask(chains):
    slot = row_iota() * LANES + lax.broadcasted_iota(jnp.int32, (GROUP, LANES), 1)
    return slot < CHAIN * chains


def bin_arrivals(cells, face_rows, places, meta_ref, *refs):
    count = len(refs) - 8
    sources = refs[:count]
    bead_pos_ref, bead_vel_ref, axis_ref, start_ref, total_ref, low_ref, high_ref, sums = refs[
        count:
    ]
    meta = [meta_ref[k] for k in range(8)]
    sums[...] = start_ref[...]
    weight = jnp.where(bead_mask(meta[7]), bead_mass, 0.0)
    bin_group(
        sums,
        [bead_pos_ref[d] for d in range(3)],
        [bead_vel_ref[d] for d in range(3)],
        weight,
        meta,
        cells,
    )
    for which, first in places:
        ref = sources[which]

        @pl.loop(0, (face_count(ref, first, face_rows) + GROUP - 1) // GROUP)
        def _(step):
            position, velocity, live = arrival_group(ref, first, step, face_rows)
            bin_group(sums, position, velocity, jnp.where(live, 1.0, 0.0), meta, cells)

    nz, inner = cells.nz, cells.inner
    lane = lax.broadcasted_iota(jnp.int32, (cells.rows, LANES), 1)
    main, rest = sums[:, :LANES], sums[:, LANES:]
    main = main + jnp.where(lane < nz, 0.0, rest)
    top = jnp.where(lane == 0, rest, rest + pltpu.roll(rest, LANES - 3, axis=1))
    total_ref[0] = main
    total_ref[1] = jnp.where(lane < 4, top, 0.0)
    axis = axis_ref[...].astype(f32)
    total_ref[1, :inner, nz : 2 * nz] = axis
    sx, sy = cells.sx, cells.sy
    low_ref[...] = jnp.zeros_like(low_ref)
    high_ref[...] = jnp.zeros_like(high_ref)
    for half in range(2):
        corner = inner + sy + 1
        low_ref[half, :sy, :] = total_ref[half, :sy, :]
        low_ref[half, sy : sy + 1, :] = total_ref[half, corner : corner + 1, :]
        high_ref[half, : sy + 1, :] = total_ref[half, inner : inner + sy + 1, :]


def add_faces_x(cells, total_ref, below_ref, above_ref, out_ref, low_ref, high_ref):
    sx, sy, inner = cells.sx, cells.sy, cells.inner
    corner = inner + sy + 1
    out_ref[...] = total_ref[...]
    low_ref[...] = jnp.zeros_like(low_ref)
    high_ref[...] = jnp.zeros_like(high_ref)
    for half in range(2):
        out_ref[half, :sy, :] += below_ref[half, :sy, :]
        out_ref[half, corner : corner + 1, :] += below_ref[half, sy : sy + 1, :]
        out_ref[half, inner : inner + sy + 1, :] += above_ref[half, : sy + 1, :]
        low_ref[half, :sx, :] = out_ref[half, pl.ds(0, sx, stride=sy), :]
        low_ref[half, sx : sx + 1, :] = out_ref[half, inner : inner + 1, :]
        high_ref[half, :sx, :] = out_ref[half, corner : corner + sx, :]
        high_ref[half, sx : sx + 1, :] = out_ref[half, inner + sy : inner + sy + 1, :]


def add_faces_y(cells, total_ref, below_ref, above_ref, out_ref, face_ref, sums):
    sx, sy, nz, inner = cells.sx, cells.sy, cells.nz, cells.inner
    corner = inner + sy + 1
    sums[...] = total_ref[...]
    for half in range(2):
        sums[half, pl.ds(0, sx, stride=sy), :] += below_ref[half, :sx, :]
        sums[half, inner : inner + 1, :] += below_ref[half, sx : sx + 1, :]
        sums[half, corner : corner + sx, :] += above_ref[half, :sx, :]
        sums[half, inner + sy : inner + sy + 1, :] += above_ref[half, sx : sx + 1, :]
    main = sums[0].T
    rest = sums[1].T
    out_ref[:LANES, :] = main
    out_ref[LANES : LANES + nz, :] = rest[nz : 2 * nz]
    out_ref[LANES + nz :, :] = jnp.zeros((GROUP, cells.rows), f32)
    out_ref[LANES + nz : LANES + nz + 4, :] = rest[:4]
    face_ref[...] = jnp.zeros_like(face_ref)
    for c in range(5):
        face_ref[c : c + 1, :] = out_ref[c * nz : c * nz + 1, :]
        face_ref[GROUP + c : GROUP + c + 1, :] = out_ref[5 * nz + c : 5 * nz + c + 1, :]


def cell_table(cells, total_ref, below_ref, above_ref, table_ref, sheet, edge):
    nz, inner, height = cells.nz, cells.inner, cells.height
    row_ids = lax.broadcasted_iota(jnp.int32, (nz, cells.rows), 0)
    parts = []
    tops = []
    for c in range(5):
        face = jnp.where(row_ids == 0, below_ref[GROUP + c : GROUP + c + 1, :], 0.0)
        parts.append(total_ref[c * nz : (c + 1) * nz, :] + face)
        tops.append(
            total_ref[5 * nz + c : 5 * nz + c + 1, :] + above_ref[c : c + 1, :]
        )
    mass = jnp.maximum(parts[0], 1.0)
    top_mass = jnp.maximum(tops[0], 1.0)
    values = [parts[4]] + [p / mass for p in parts[1:4]]
    top_values = [tops[4]] + [t / top_mass for t in tops[1:4]]
    sheet[...] = jnp.zeros_like(sheet)
    edge[...] = jnp.zeros_like(edge)
    lane = lax.broadcasted_iota(jnp.int32, (cells.extra, LANES), 1)
    spare = LANES - (cells.rows - inner)
    for c in range(4):
        base = c * height
        sheet[base : base + nz, :] = values[c][:, :inner]
        sheet[base + nz : base + nz + 1, :] = top_values[c][:, :inner]
        edge[base : base + nz, :] = jnp.concatenate(
            [values[c][:, inner:], jnp.zeros((nz, spare), f32)], axis=1
        )
        edge[base + nz : base + nz + 1, :] = jnp.concatenate(
            [top_values[c][:, inner:], jnp.zeros((1, spare), f32)], axis=1
        )
        folded = [jnp.zeros((cells.extra, LANES), f32) for _ in range(inner // LANES)]
        for m in range(cells.per):
            begin = m * cells.edges
            piece = edge[pl.ds(base + m, cells.extra, stride=cells.per), :]
            piece = pltpu.roll(piece, begin % LANES, axis=1) if begin % LANES else piece
            for t in range(inner // LANES):
                low, high = begin - t * LANES, begin + cells.edges - t * LANES
                if high > 0 and low < LANES:
                    folded[t] = jnp.where((lane >= low) & (lane < high), piece, folded[t])
        sheet[base + nz + 1 : base + nz + 1 + cells.extra, :] = jnp.concatenate(folded, axis=1)
    whole = sheet[...]
    high = whole.astype(bf16).astype(f32)
    low = (whole - high)[height:]
    table_ref[...] = jnp.concatenate([high, low], axis=0).astype(bf16)


def direction_table():
    counter = jnp.arange(LANES).astype(f32)
    height = 1.0 - (2.0 * counter + 1.0) / NAXES
    radius = jnp.sqrt(jnp.maximum(1.0 - height * height, 0.0))
    rows = jnp.stack([radius * jnp.cos(golden * counter), radius * jnp.sin(golden * counter)])
    return jnp.broadcast_to(rows[:, None], (2, GROUP, LANES))


def fold_rows(values):
    sub = lax.broadcasted_iota(jnp.int32, (GROUP, LANES), 0)
    step = GROUP // 2
    while step:
        upper = (sub & step) == 0
        half = len(values) // 2
        joined = []
        for a, b in zip(values[:half], values[half:]):
            a = a + pltpu.roll(a, GROUP - step, axis=0)
            b = b + pltpu.roll(b, step, axis=0)
            joined.append(jnp.where(upper, a, b))
        values = joined
        step //= 2
    return values[0]


def collide(position, velocity, meta, table, dirs_ref, cells):
    height = cells.height
    row, column = place_of(levels_of(position, meta), cells)
    found = lax.dot_general(
        table, one_hot(column, cells.inner), NN, preferred_element_type=f32
    )
    ids = lax.broadcasted_iota(jnp.int32, (height, LANES), 0).astype(f32)
    picked = [[] for _ in range(4)]
    for r in range(GROUP):
        block = found[:, r * LANES : (r + 1) * LANES]
        here = ids == row[r : r + 1]
        for c in range(4):
            value = block[c * height : (c + 1) * height]
            if c > 0:
                value = value + block[(3 + c) * height : (4 + c) * height]
            value = jnp.where(here, value, 0.0)
            picked[c].append(
                jnp.sum(value.reshape(height // GROUP, GROUP, LANES), axis=0)
            )
    picked = [fold_rows(p) for p in picked]
    axis, flow = picked[0].astype(jnp.int32), picked[1:]
    normal = [
        jnp.take_along_axis(dirs_ref[0], axis, axis=1, mode="promise_in_bounds"),
        jnp.take_along_axis(dirs_ref[1], axis, axis=1, mode="promise_in_bounds"),
        1.0 - (2.0 * picked[0] + 1.0) * (1.0 / NAXES),
    ]
    rel = [velocity[d] - flow[d] for d in range(3)]
    along = (1.0 - turn_cosine) * (
        normal[0] * rel[0] + normal[1] * rel[1] + normal[2] * rel[2]
    )
    result = []
    for d in range(3):
        e, f = (d + 1) % 3, (d + 2) % 3
        crossed = normal[e] * rel[f] - normal[f] * rel[e]
        result.append(
            flow[d] + (turn_cosine * rel[d] + turn_sine * crossed + along * normal[d])
        )
    return result


def passed(position, speed):
    return position - jnp.floor(position) - 0.5 + 3.0 * step_size * speed


def copy_out(pairs, sems):
    copies = [pltpu.make_async_copy(a, b, sems.at[k]) for k, (a, b) in enumerate(pairs)]
    for copy in copies:
        copy.start()
    for copy in copies:
        copy.wait()


def collide_residents(
    cells, first, count, meta_ref, dirs_ref, table_ref, pos_ref, vel_ref, *refs
):
    out_pos, out_vel, token, held_pos, held_vel, sems = refs[-6:]
    token[...] = jnp.zeros_like(token)
    meta = [meta_ref[k] for k in range(8)]
    table = table_ref[...]
    live_rows = meta[6] - first
    held_pos[...] = jnp.zeros_like(held_pos)
    held_vel[...] = jnp.zeros_like(held_vel)
    stride = GROUP * TWIN

    @pl.loop(0, jnp.clip((live_rows + stride - 1) // stride, 0, count // stride))
    def _(step):
        for part in range(TWIN):
            offset = pl.multiple_of(step * stride + part * GROUP, GROUP)
            rows = pl.ds(offset, GROUP)
            position = [pos_ref[d, rows, :] for d in range(3)]
            velocity = [vel_ref[d, rows, :] for d in range(3)]
            live = row_iota() + offset < live_rows
            speed = collide(position, velocity, meta, table, dirs_ref, cells)
            for d in range(3):
                held_vel[d, rows, :] = jnp.where(live, speed[d], 0.0)
                held_pos[d, rows, :] = jnp.where(live, passed(position[d], speed[d]), 0.0)

    span = pl.ds(first, count)
    copy_out([(held_pos, out_pos.at[:, span, :]), (held_vel, out_vel.at[:, span, :])], sems)


def collide_arrivals(cells, first, face_rows, places, meta_ref, dirs_ref, table_ref, *refs):
    out_pos, out_vel, token, held_pos, held_vel, sems = refs[-6:]
    token[...] = jnp.zeros_like(token)
    meta = [meta_ref[k] for k in range(8)]
    table = table_ref[...]
    held_pos[...] = jnp.zeros_like(held_pos)
    held_vel[...] = jnp.zeros_like(held_vel)
    for k, (which, begin) in enumerate(places):
        ref = refs[which]

        @pl.loop(0, (face_count(ref, begin, face_rows) + GROUP - 1) // GROUP)
        def _(step):
            position, velocity, live = arrival_group(ref, begin, step, face_rows)
            speed = collide(position, velocity, meta, table, dirs_ref, cells)
            rows = pl.ds(k * face_rows + pl.multiple_of(step * GROUP, GROUP), GROUP)
            for d in range(3):
                held_vel[d, rows, :] = jnp.where(live, speed[d], 0.0)
                held_pos[d, rows, :] = jnp.where(live, passed(position[d], speed[d]), 0.0)

    span = pl.ds(first, len(places) * face_rows)
    copy_out([(held_pos, out_pos.at[:, span, :]), (held_vel, out_vel.at[:, span, :])], sems)


def pack_inputs(
    sheets,
    face_rows,
    meta_ref,
    pos_ref,
    vel_ref,
    bead_pos_ref,
    bead_vel_ref,
    start_ref,
    block_ref,
    rows_pos_ref,
    rows_vel_ref,
    *refs,
):
    out_refs, (held_pos, held_vel, sems) = refs[: len(sheets)], refs[len(sheets) :]
    copies = [(bead_pos_ref, held_pos), (bead_vel_ref, held_vel)]
    for faces, out_ref in zip(sheets, out_refs):
        for k, face in enumerate(faces):
            first = k * (6 * face_rows + GROUP)
            for c in range(6):
                source = pos_ref if c < 3 else vel_ref
                rows = pl.ds(first + c * face_rows, face_rows)
                copies.append((source.at[c % 3, face], out_ref.at[rows]))
    copies = [pltpu.make_async_copy(a, b, sems.at[k]) for k, (a, b) in enumerate(copies)]
    for copy in copies:
        copy.start()
    for faces, out_ref in zip(sheets, out_refs):
        for k, face in enumerate(faces):
            first = k * (6 * face_rows + GROUP) + 6 * face_rows
            out_ref[first : first + GROUP, :] = jnp.full(
                (GROUP, LANES), meta_ref[8 + face], jnp.int32
            ).astype(f32)
    slots = start_ref.shape[1]
    start_ref[...] = jnp.zeros_like(start_ref)
    rows_pos_ref[...] = jnp.zeros_like(rows_pos_ref)
    rows_vel_ref[...] = jnp.zeros_like(rows_vel_ref)
    for copy in copies:
        copy.wait()
    for d in range(3):
        for k in range(slots // LANES):
            lanes = slice(k * LANES, (k + 1) * LANES)
            start_ref[d : d + 1, lanes] = held_pos[d, k : k + 1, :]
            rows_pos_ref[d, k : k + 1, :] = held_pos[d, k : k + 1, :]
            rows_vel_ref[d, k : k + 1, :] = held_vel[d, k : k + 1, :]
    start = start_ref[...]
    block_ref[...] = payload(start, slot_live(slots, meta_ref[7], GROUP))


def stack_rows(parts, *refs):
    out_ref = refs[-1]
    at = 0
    for which, begin, count in parts:
        out_ref[at : at + count, :] = refs[which][begin : begin + count, :]
        at += count


def slot_live(slots, chains, rows):
    return lax.broadcasted_iota(jnp.int32, (rows, slots), 1) < CHAIN * chains


def payload(position, live):
    slots = position.shape[1]
    row_ids = lax.broadcasted_iota(jnp.int32, (SENT, slots), 0)
    flag = jnp.where(live[:SENT], 1.0, 0.0)
    return jnp.where(row_ids == 3, flag, position[:SENT])


def thirds_of(value):
    high = value.astype(bf16)
    rest = value - high.astype(f32)
    middle = rest.astype(bf16)
    low = (rest - middle.astype(f32)).astype(bf16)
    return jnp.concatenate([high.astype(f32), middle.astype(f32), low.astype(f32)], axis=0).astype(
        bf16
    )


def summed_thirds(value):
    return value[:GROUP] + (value[GROUP : 2 * GROUP] + value[2 * GROUP :])


def forces(own, chains, counts, bonds_ref, fetch, centre, lengths, mine_ref, packed, push):
    slots = own.shape[1]
    bond_slots = bonds_ref.shape[0]
    row_ids = lax.broadcasted_iota(jnp.int32, (GROUP, slots), 0)
    mid = jnp.zeros((GROUP, slots), f32)
    length = jnp.ones((GROUP, slots), f32)
    for d in range(3):
        mid = jnp.where(row_ids == d, centre[d], mid)
        length = jnp.where(row_ids == d, lengths[d], length)
    live = slot_live(slots, chains, GROUP)
    local = jnp.where(live & (row_ids < 3), own - mid, 0.0)
    columns = jnp.where(live, local, far_own).T
    for d in range(3):
        mine_ref[d] = jnp.broadcast_to(columns[:, d : d + 1], (slots, LANES))

    packed[...] = jnp.full(packed.shape, far_ghost, f32)
    lane = lax.broadcasted_iota(jnp.int32, (SENT, LANES), 1)
    tiles = slots // LANES
    offset = jnp.int32(0)
    for block, count in zip(fetch(), counts):
        near = block - mid[:SENT]
        near = near - length[:SENT] * jnp.floor(near * (1.0 / length[:SENT]) + 0.5)
        tile, turn = offset // LANES, offset % LANES
        turned = [
            pltpu.roll(near[:, k * LANES : (k + 1) * LANES], turn, axis=1) for k in range(tiles)
        ]
        for k in range(tiles + 1):
            if k == 0:
                value = turned[0]
            elif k == tiles:
                value = turned[-1]
            else:
                value = jnp.where(lane < turn, turned[k - 1], turned[k])
            place = (tile + k) * LANES + lane
            taken = (place >= offset) & (place < offset + count)
            packed[tile + k, :SENT, :] = jnp.where(taken, value, packed[tile + k, :SENT, :])
        offset = offset + count

    push[...] = jnp.zeros_like(push)
    chunk = 64
    steps = (offset + 2 * LANES - 1) // (2 * LANES)

    @pl.loop(0, (CHAIN * chains + chunk - 1) // chunk)
    def _(part):
        rows = pl.ds(pl.multiple_of(part * chunk, chunk), chunk)
        mine = [mine_ref[d, rows, :] for d in range(3)]

        def add_tiles(step, total):
            for k in range(2):
                other = packed[2 * step + k]
                differ = [mine[d] - other[d : d + 1] for d in range(3)]
                square = (
                    differ[0] * differ[0] + differ[1] * differ[1] + differ[2] * differ[2]
                )
                inside = (square < cut_square) & (square > 0.25)
                inverse = 1.0 / jnp.where(inside, square, 1e30)
                sixth = inverse * inverse * inverse
                weight = (sixth * inverse) * (48.0 * sixth - 24.0)
                total = tuple(total[d] + weight * differ[d] for d in range(3))
            return total

        total = lax.fori_loop(
            0, steps, add_tiles, tuple(jnp.zeros((chunk, LANES), f32) for _ in range(3))
        )
        for d in range(3):
            push[d, rows, :] = total[d]

    pair = jnp.zeros((GROUP, slots), f32)
    for d in range(3):
        pair = jnp.where(row_ids == d, jnp.sum(push[d].T, axis=0, keepdims=True), pair)

    slot_ids = lax.broadcasted_iota(jnp.int32, (bond_slots, slots), 1)
    bond_ids = lax.broadcasted_iota(jnp.int32, (bond_slots, slots), 0)
    ends = bonds_ref[...]
    first = jnp.where(slot_ids == ends[:, 0:1], 1.0, 0.0)
    second = jnp.where(slot_ids == ends[:, 1:2], 1.0, 0.0)
    joins = jnp.where(bond_ids < (CHAIN - 1) * chains, first - second, 0.0).astype(bf16)
    stretch = summed_thirds(
        lax.dot_general(thirds_of(local), joins, NT, preferred_element_type=f32)
    )
    square = (
        stretch[0:1] * stretch[0:1] + stretch[1:2] * stretch[1:2] + stretch[2:3] * stretch[2:3]
    )
    bond_live = (
        lax.broadcasted_iota(jnp.int32, (1, bond_slots), 1) < (CHAIN - 1) * chains
    )
    pull = jnp.where(bond_live, -spring / (1.0 - square / reach_square), 0.0) * stretch
    return pair + summed_thirds(
        lax.dot_general(thirds_of(pull), joins, NN, preferred_element_type=f32)
    )


def force_scratch(slots, blocks):
    tiles = -(-(blocks * slots // LANES + 2) // 2) * 2
    return [
        pltpu.VMEM((blocks, SENT, slots), f32),
        pltpu.SemaphoreType.DMA((blocks,)),
        pltpu.VMEM((3, slots, LANES), f32),
        pltpu.VMEM((tiles, GROUP, LANES), f32),
        pltpu.VMEM((3, slots, LANES), f32),
    ]


def centre_of(meta, sizes):
    return [meta[3 + d].astype(f32) + 0.5 * sizes[d] for d in range(3)]


def fetching(meta, sizes, peers, blocks_ref, held, sems):
    copies = [
        pltpu.make_async_copy(blocks_ref.at[which], held.at[k], sems.at[k])
        for k, which in enumerate(surrounding(meta, sizes, peers))
    ]
    for copy in copies:
        copy.start()

    def fetch():
        for copy in copies:
            copy.wait()
        return [held[k] for k in range(len(copies))]

    return fetch


def first_forces(
    sizes,
    peers,
    meta_ref,
    start_ref,
    bonds_ref,
    blocks_ref,
    push_ref,
    counts_ref,
    held,
    sems,
    *scratch,
):
    meta = [meta_ref[k] for k in range(8)]
    blocks = fetching(meta, sizes, peers, blocks_ref, held, sems)()
    counts = [jnp.sum(block[3:4]).astype(jnp.int32) for block in blocks]
    for k, count in enumerate(counts):
        counts_ref[k] = count
    push_ref[...] = forces(
        start_ref[...],
        meta[7],
        counts,
        bonds_ref,
        lambda: blocks,
        centre_of(meta, sizes),
        lengths_of(sizes, peers),
        *scratch,
    )


def lengths_of(sizes, peers):
    return [float(size * count) for size, count in zip(sizes, peers)]


def finish_cells(
    cells,
    meta_ref,
    dirs_ref,
    total_ref,
    below_ref,
    above_ref,
    bead_pos_ref,
    bead_vel_ref,
    start_ref,
    push_ref,
    table_ref,
    speed_ref,
    moved_ref,
    pay_ref,
    sheet,
    edge,
):
    meta = [meta_ref[k] for k in range(8)]
    cell_table(cells, total_ref, below_ref, above_ref, table_ref, sheet, edge)
    fresh = collide(
        [bead_pos_ref[d] for d in range(3)],
        [bead_vel_ref[d] for d in range(3)],
        meta,
        table_ref[...],
        dirs_ref,
        cells,
    )
    start = start_ref[...]
    slots = start.shape[1]
    row_ids = lax.broadcasted_iota(jnp.int32, (GROUP, slots), 0)
    speed = jnp.zeros((GROUP, slots), f32)
    for d in range(3):
        line = jnp.concatenate([fresh[d][k : k + 1] for k in range(slots // LANES)], axis=1)
        speed = jnp.where(row_ids == d, line, speed)
    speed = speed + half_kick * push_ref[...]
    moved = step_size * speed
    live = slot_live(slots, meta[7], GROUP)
    speed_ref[...] = speed
    moved_ref[...] = moved
    pay_ref[...] = payload(start + moved, live)


def substep(
    sizes,
    peers,
    last,
    meta_ref,
    start_ref,
    bonds_ref,
    counts_ref,
    speed_ref,
    moved_ref,
    blocks_ref,
    order_ref,
    *refs,
):
    outs, (held, sems, *scratch) = refs[:-5], refs[-5:]
    meta = [meta_ref[k] for k in range(8)]
    fetch = fetching(meta, sizes, peers, blocks_ref, held, sems)
    counts = [counts_ref[k] for k in range(held.shape[0])]
    start = start_ref[...]
    moved = moved_ref[...]
    push = forces(
        start + moved,
        meta[7],
        counts,
        bonds_ref,
        fetch,
        centre_of(meta, sizes),
        lengths_of(sizes, peers),
        *scratch,
    )
    live = slot_live(start.shape[1], meta[7], GROUP)
    speed = speed_ref[...] + half_kick * push
    if last:
        for d in range(3):
            outs[0][d, 0, 0, :, :] = jnp.where(live, speed, 0.0)[d : d + 1]
            outs[1][d, 0, 0, :, :] = jnp.where(live, moved, 0.0)[d : d + 1]
        return
    speed = speed + half_kick * push
    moved = moved + step_size * speed
    outs[0][...] = speed
    outs[1][...] = moved
    outs[2][...] = payload(start + moved, live)


def neighbours(value, axis):
    peers = lax.axis_size(axis)
    if peers == 2:
        return [moved_along(value, axis, 1)]
    return [moved_along(value, axis, 1), moved_along(value, axis, -1)]


def stacked(parts, operands, order=()):
    rows = sum(count for _, _, count in parts)
    width = operands[0].shape[1]
    return pl.pallas_call(
        functools.partial(stack_rows, tuple(parts)),
        out_shape=like(rows, width),
        in_specs=[vmem()] * len(operands) + [pl.BlockSpec(memory_space=pl.ANY)] * len(order),
        out_specs=vmem(),
        compiler_params=params(),
        name="stack_rows",
    )(*operands, *order)


def whole_rows(operands):
    return [(k, 0, value.shape[0]) for k, value in enumerate(operands)]


def surrounding(meta, sizes, peers):
    found = [jnp.int32(0)]
    for d in range(3):
        here = meta[3 + d] // sizes[d]
        steps = range(peers[d]) if peers[d] < 3 else (-1, 0, 1)
        spots = [lax.rem(here + (step + peers[d]), peers[d]) for step in steps]
        found = [f * peers[d] + spot for f in found for spot in spots]
    return found


def like(*shape, dtype=f32):
    return jax.ShapeDtypeStruct(shape, dtype)


def shards(
    sol_pos,
    sol_vel,
    sol_rows,
    mig_pos,
    mig_vel,
    mig_rows,
    bead_pos,
    bead_vel,
    bead_chains,
    bond_list,
    cell_axis,
    shift,
):
    sizes = cell_axis.shape
    cells = Cells(*sizes)
    names = ("gx", "gy", "gz")
    peers = tuple(lax.axis_size(name) for name in names)
    slots_here = sol_pos.shape[-1]
    buffer_slots = mig_pos.shape[-1]
    bead_slots = bead_pos.shape[-1]
    bond_slots = bond_list.shape[-1]
    rows_here = slots_here // LANES
    face_rows = buffer_slots // LANES
    rows_all = rows_here + 6 * face_rows
    anchor = jnp.stack([lax.axis_index(names[d]) * sizes[d] for d in range(3)])
    meta = jnp.concatenate(
        [
            shift,
            anchor.astype(jnp.int32),
            sol_rows.reshape(1),
            bead_chains.reshape(1),
            mig_rows.reshape(6),
        ]
    )
    dirs = direction_table()
    position = sol_pos.reshape(3, rows_here, LANES)
    velocity = sol_vel.reshape(3, rows_here, LANES)

    any_spec = pl.BlockSpec(memory_space=pl.ANY)
    face_height = 6 * face_rows + GROUP
    bead_shape = like(GROUP, bead_slots)
    tiles = bead_slots // LANES
    rows_shape = like(3, GROUP, LANES)
    routes = []
    for d, axis in enumerate(names):
        if lax.axis_size(axis) == 2:
            routes.append((axis, 1, (2 * d, 2 * d + 1)))
        else:
            routes += [(axis, 1, (2 * d + 1,)), (axis, -1, (2 * d,))]
    start, block, bead_rows_pos, bead_rows_vel, *packed = pl.pallas_call(
        functools.partial(pack_inputs, [faces for _, _, faces in routes], face_rows),
        out_shape=[bead_shape, like(SENT, bead_slots), rows_shape, rows_shape]
        + [like(len(faces) * face_height, LANES) for _, _, faces in routes],
        in_specs=[smem()] + [pl.BlockSpec(memory_space=pltpu.HBM)] * 4,
        out_specs=[vmem()] * (4 + len(routes)),
        scratch_shapes=[pltpu.VMEM((3, tiles, LANES), f32)] * 2
        + [pltpu.SemaphoreType.DMA((38,))],
        compiler_params=params(vmem_most),
        name="pack_inputs",
    )(
        meta,
        mig_pos.reshape(3, 6, face_rows, LANES),
        mig_vel.reshape(3, 6, face_rows, LANES),
        bead_pos.reshape(3, tiles, LANES),
        bead_vel.reshape(3, tiles, LANES),
    )
    arriving, spots = [], [None] * 6
    for (axis, step, faces), value in zip(routes, packed):
        for k, face in enumerate(faces):
            spots[face ^ 1] = (len(arriving), k * face_height)
        arriving.append(moved_along(value, axis, step))
    around = lax.all_gather(block, names)
    bonds = bond_list.reshape(2, bond_slots).T

    thirds = 3
    count = rows_here // thirds
    axis_rows = cell_axis.reshape(cells.inner, sizes[2])

    def bin_piece(piece, earlier, order):
        return pl.pallas_call(
            functools.partial(bin_residents, cells, piece * count, count),
            out_shape=like(cells.rows, 2 * LANES),
            grid=(1,),
            in_specs=[smem()]
            + [pl.BlockSpec((3, count, LANES), lambda i, p=piece: (0, p, 0))] * 2
            + [vmem()] * len(earlier)
            + [any_spec] * len(order),
            out_specs=vmem(),
            compiler_params=params(),
            name=f"bin_residents_{piece}",
        )(meta, position, velocity, *earlier, *order)

    totals = []
    for piece in range(thirds):
        totals = [bin_piece(piece, totals, [])]
    totals = totals[0]

    face_x = like(2, -(-(sizes[1] + 1) // GROUP) * GROUP, LANES)
    face_y = like(2, -(-(sizes[0] + 1) // GROUP) * GROUP, LANES)
    totals, low, high = pl.pallas_call(
        functools.partial(bin_arrivals, cells, face_rows, tuple(spots)),
        out_shape=[like(2, cells.rows, LANES), face_x, face_x],
        in_specs=[smem()] + [vmem()] * (len(arriving) + 4),
        out_specs=[vmem()] * 3,
        scratch_shapes=[pltpu.VMEM((cells.rows, 2 * LANES), f32)],
        compiler_params=params(),
        name="bin_arrivals",
    )(meta, *arriving, bead_rows_pos, bead_rows_vel, axis_rows, totals)

    many = math.prod(min(count, 3) for count in peers)
    hbm_spec = pl.BlockSpec(memory_space=pltpu.HBM)
    push, counts = pl.pallas_call(
        functools.partial(first_forces, sizes, peers),
        out_shape=[bead_shape, like(many, dtype=jnp.int32)],
        in_specs=[smem(), vmem(), vmem(), hbm_spec],
        out_specs=[vmem(), smem()],
        scratch_shapes=force_scratch(bead_slots, many),
        compiler_params=params(),
        name="first_forces",
    )(meta, start, bonds, around)

    below, above = moved_along(high, "gx", 1), moved_along(low, "gx", -1)
    totals, low, high = pl.pallas_call(
        functools.partial(add_faces_x, cells),
        out_shape=[like(2, cells.rows, LANES), face_y, face_y],
        in_specs=[vmem()] * 3,
        out_specs=[vmem()] * 3,
        compiler_params=params(),
        name="add_faces_x",
    )(totals, below, above)
    below, above = moved_along(high, "gy", 1), moved_along(low, "gy", -1)
    totals, faces = pl.pallas_call(
        functools.partial(add_faces_y, cells),
        out_shape=[like(LANES + cells.nz + GROUP, cells.rows), like(2 * GROUP, cells.rows)],
        in_specs=[vmem()] * 3,
        out_specs=[vmem()] * 2,
        scratch_shapes=[pltpu.VMEM((2, cells.rows, LANES), f32)],
        compiler_params=params(),
        name="add_faces_y",
    )(totals, below, above)
    sides = neighbours(faces, "gz")
    below, above = sides[0], sides[-1]

    table, speed, moved, pay = pl.pallas_call(
        functools.partial(finish_cells, cells),
        out_shape=[
            like(7 * cells.height, cells.inner, dtype=bf16),
            bead_shape,
            bead_shape,
            like(SENT, bead_slots),
        ],
        in_specs=[smem()] + [vmem()] * 8,
        out_specs=[vmem()] * 4,
        scratch_shapes=[
            pltpu.VMEM((4 * cells.height, cells.inner), f32),
            pltpu.VMEM((4 * cells.height, LANES), f32),
        ],
        compiler_params=params(),
        name="finish_cells",
    )(meta, dirs, totals, below, above, bead_rows_pos, bead_rows_vel, start, push)

    solvent_shape = like(3, rows_all, LANES)
    results = []
    cuts = 6
    span = rows_here // cuts

    def collide_piece(piece):
        earlier = results[:2]
        if piece < cuts:
            body = functools.partial(collide_residents, cells, piece * span, span)
            rows = span
            sources = [position, velocity]
            specs = [pl.BlockSpec((3, span, LANES), lambda i: (0, piece, 0))] * 2
        else:
            begin = 2 * (piece - cuts)
            body = functools.partial(
                collide_arrivals,
                cells,
                rows_here + begin * face_rows,
                face_rows,
                tuple(spots[begin : begin + 2]),
            )
            rows = 2 * face_rows
            sources = arriving
            specs = [vmem()] * len(arriving)
        at = 3 + len(sources)
        results[:] = pl.pallas_call(
            body,
            out_shape=[solvent_shape, solvent_shape, like(GROUP, LANES)],
            grid=(1,),
            in_specs=[smem(), vmem(), vmem()] + specs + [any_spec] * len(earlier),
            out_specs=[any_spec, any_spec, vmem()],
            scratch_shapes=[pltpu.VMEM((3, rows, LANES), f32)] * 2
            + [pltpu.SemaphoreType.DMA((2,))],
            input_output_aliases={at: 0, at + 1: 1} if earlier else {},
            compiler_params=params(),
            name=f"collide_{piece}",
        )(meta, dirs, table, *sources, *earlier)
        return results[2]

    for step in range(3):
        last = step == 2
        ghosts = lax.all_gather(pay, names)
        for piece in range(3 * step, 3 * step + 3):
            order = collide_piece(piece)
        final = like(3, 1, 1, 1, bead_slots)
        outcome = pl.pallas_call(
            functools.partial(substep, sizes, peers, last),
            out_shape=[final] * 2 if last else [bead_shape] * 2 + [like(SENT, bead_slots)],
            in_specs=[smem(), vmem(), vmem(), smem(), vmem(), vmem(), hbm_spec, any_spec],
            out_specs=[vmem()] * (2 if last else 3),
            scratch_shapes=force_scratch(bead_slots, many),
            compiler_params=params(),
            name=f"substep_{step}",
        )(meta, start, bonds, counts, speed, moved, ghosts, order)
        speed, moved = outcome[:2]
        pay = outcome[-1]

    count_solvent = rows_all * LANES
    return (
        results[0].reshape(3, 1, 1, 1, count_solvent),
        results[1].reshape(3, 1, 1, 1, count_solvent),
        moved,
        speed,
    )


def solution(mesh):
    return jax.shard_map(
        shards,
        mesh=mesh,
        in_specs=(
            P(None, "gx", "gy", "gz", None),
            P(None, "gx", "gy", "gz", None),
            P("gx", "gy", "gz"),
            P(None, "gx", "gy", "gz", None, None),
            P(None, "gx", "gy", "gz", None, None),
            P("gx", "gy", "gz", None),
            P(None, "gx", "gy", "gz", None),
            P(None, "gx", "gy", "gz", None),
            P("gx", "gy", "gz"),
            P(None, "gx", "gy", "gz", None),
            P("gx", "gy", "gz"),
            P(),
        ),
        out_specs=(
            P(None, "gx", "gy", "gz", None),
            P(None, "gx", "gy", "gz", None),
            P(None, "gx", "gy", "gz", None),
            P(None, "gx", "gy", "gz", None),
        ),
        check_vma=False,
    )
```

```python
import functools
import math

import jax
import jax.numpy as jnp
from jax import lax
from jax.experimental import pallas as pl
from jax.experimental.pallas import tpu as pltpu
from jax.sharding import PartitionSpec as P

UNITS = 16
NAXES = 32
CHAIN = 8
LANES = 128
GROUP = 8
TWIN = 4
PAIR = 2
TRIO = 3

bead_mass = 5.0
step_size = 0.02
spring = 30.0
reach_square = 2.25
cut_square = 2.0 ** (1.0 / 3.0)
turn_cosine = math.cos(130.0 * math.pi / 180.0)
turn_sine = math.sin(130.0 * math.pi / 180.0)
golden = math.pi * (3.0 - math.sqrt(5.0))
half_kick = 0.5 * step_size / bead_mass
far_own = 3000.0
far_ghost = 9000.0
vmem_limit = 48 * 1024 * 1024
vmem_most = 48 * 1024 * 1024
NT = (((1,), (1,)), ((), ()))
NN = (((1,), (0,)), ((), ()))
exact = lax.Precision.HIGHEST
f32 = jnp.float32
bf16 = jnp.bfloat16


def params(limit=vmem_limit):
    return pltpu.CompilerParams(vmem_limit_bytes=limit)


def vmem():
    return pl.BlockSpec(memory_space=pltpu.VMEM)


def smem():
    return pl.BlockSpec(memory_space=pltpu.SMEM)


def moved_along(value, axis, by):
    peers = lax.axis_size(axis)
    return lax.ppermute(value, axis, [(i, (i + by) % peers) for i in range(peers)])


class Cells:
    def __init__(self, size_x, size_y, size_z):
        self.sx, self.sy, self.nz = size_x, size_y, size_z
        self.inner = size_x * size_y
        self.edges = size_x + size_y + 1
        self.rows = -(-(self.inner + self.edges) // 16) * 16
        self.middle = self.rows // 2
        self.per = self.inner // self.edges
        self.depths = size_z + 1
        self.extra = -(-self.depths // self.per)
        self.height = -(-(self.depths + self.extra) // GROUP) * GROUP


def levels_of(position, meta):
    return [
        jnp.floor(jnp.floor(position[d] * UNITS + meta[d].astype(f32)) * (1.0 / UNITS))
        - meta[3 + d].astype(f32)
        for d in range(3)
    ]


def edge_of(levels, cells):
    outer = (levels[0] == cells.sx) | (levels[1] == cells.sy)
    return outer, jnp.where(levels[0] == cells.sx, levels[1], cells.sy + 1 + levels[0])


def plane_of(levels, cells):
    outer, edge = edge_of(levels, cells)
    return jnp.where(outer, cells.inner + edge, levels[0] * cells.sy + levels[1])


def place_of(levels, cells):
    outer, edge = edge_of(levels, cells)
    fold = jnp.floor((levels[2] + 0.5) * (1.0 / cells.per))
    row = jnp.where(outer, cells.depths + fold, levels[2])
    column = jnp.where(
        outer,
        (levels[2] - fold * cells.per) * cells.edges + edge,
        levels[0] * cells.sy + levels[1],
    )
    return row, column


def wide(row):
    return jnp.broadcast_to(row, (16, LANES)).astype(bf16)


def one_hot(column, height):
    middle = height // 2
    ids = lax.broadcasted_iota(jnp.int32, (height, LANES), 0) - middle
    ids = ids.astype(f32).astype(bf16).reshape(height // 16, 16, LANES)
    column = column - middle
    one, zero = jnp.ones((), bf16), jnp.zeros((), bf16)
    pieces = [
        jnp.where(ids == wide(column[r : r + 1])[None], one, zero).reshape(height, LANES)
        for r in range(column.shape[0])
    ]
    return jnp.concatenate(pieces, axis=1)


def split(value):
    high = value.astype(bf16).astype(f32)
    return high, value - high


def spread_moments(depth, weight, velocity, cells):
    nz = cells.nz
    ids = lax.broadcasted_iota(jnp.int32, (nz, LANES), 0).astype(f32).astype(bf16)
    ids = ids.reshape(nz // 16, 16, LANES)
    row_ids = lax.broadcasted_iota(jnp.int32, (16, LANES), 0).astype(f32).astype(bf16)
    zero = jnp.zeros((), bf16)
    parts = [split(weight * velocity[d]) for d in range(3)]
    channels = [weight] + [p[0] for p in parts] + [p[1] for p in parts]
    pieces = []
    for r in range(depth.shape[0]):
        at = wide(depth[r : r + 1])
        here = ids == at[None]
        values = [wide(c[r : r + 1]) for c in channels]
        tiles = [jnp.where(here, v[None], zero).reshape(nz, LANES) for v in values]
        top = jnp.zeros((16, LANES), bf16)
        for c, v in enumerate(values):
            top = jnp.where(row_ids == c, v, top)
        top = jnp.where(at == nz, top, zero)
        pieces.append(
            jnp.concatenate(
                tiles[:4] + [top, jnp.zeros((nz - 16, LANES), bf16)] + tiles[4:], axis=0
            )
        )
    return jnp.concatenate(pieces, axis=1)


def bin_group(total_ref, position, velocity, weight, meta, cells):
    levels = levels_of(position, meta)
    hot = one_hot(plane_of(levels, cells), cells.rows)
    spread = spread_moments(levels[2], weight, velocity, cells)
    total_ref[...] += lax.dot_general(hot, spread, NT, preferred_element_type=f32)


def row_iota():
    return lax.broadcasted_iota(jnp.int32, (GROUP, LANES), 0)


def bin_residents(cells, first, count, meta_ref, pos_ref, vel_ref, *refs):
    total_ref = refs[-1]
    meta = [meta_ref[k] for k in range(8)]
    if first == 0:
        total_ref[...] = jnp.zeros_like(total_ref)
    else:
        total_ref[...] = refs[0][...]
    live_rows = meta[6] - first
    stride = GROUP * TWIN

    @pl.loop(0, jnp.clip((live_rows + stride - 1) // stride, 0, count // stride))
    def _(step):
        for part in range(TWIN):
            offset = pl.multiple_of(step * stride + part * GROUP, GROUP)
            rows = pl.ds(offset, GROUP)
            position = [pos_ref[d, rows, :] for d in range(3)]
            velocity = [vel_ref[d, rows, :] for d in range(3)]
            weight = jnp.where(row_iota() + offset < live_rows, 1.0, 0.0)
            bin_group(total_ref, position, velocity, weight, meta, cells)


def face_count(ref, first, face_rows):
    return jnp.max(ref[pl.ds(first + 6 * face_rows, GROUP), :]).astype(jnp.int32)


def take_faces(faces, face_rows, held, counts_ref, index, offset):
    for k, (ref, first) in enumerate(faces):
        count = face_count(ref, first, face_rows)
        counts_ref[index + k] = count
        for c in range(6):
            begin = first + c * face_rows
            held[c, pl.ds(offset, face_rows), :] = ref[begin : begin + face_rows, :]
        offset = offset + count
    return offset


def bin_held(held, begin, end, sums, meta, cells):
    stride = GROUP * PAIR

    @pl.loop(0, (end - begin + stride - 1) // stride)
    def _(step):
        for part in range(PAIR):
            offset = begin + step * stride + part * GROUP
            rows = pl.ds(offset, GROUP)
            comps = [held[c, rows, :] for c in range(6)]
            weight = jnp.where(row_iota() + offset < end, 1.0, 0.0)
            bin_group(sums, comps[:3], comps[3:], weight, meta, cells)


def bead_mask(chains):
    slot = row_iota() * LANES + lax.broadcasted_iota(jnp.int32, (GROUP, LANES), 1)
    return slot < CHAIN * chains


def bin_first_arrivals(cells, face_rows, places, meta_ref, *refs):
    count = len(refs) - 7
    sources = refs[:count]
    bead_pos_ref, bead_vel_ref, start_ref, order_ref, total_ref, held, counts_ref = refs[count:]
    meta = [meta_ref[k] for k in range(8)]
    total_ref[...] = start_ref[...]
    held[...] = jnp.zeros_like(held)
    faces = [(sources[which], first) for which, first in places]
    end = take_faces(faces, face_rows, held, counts_ref, 0, 0)
    weight = jnp.where(bead_mask(meta[7]), bead_mass, 0.0)
    bin_group(
        total_ref,
        [bead_pos_ref[d] for d in range(3)],
        [bead_vel_ref[d] for d in range(3)],
        weight,
        meta,
        cells,
    )
    bin_held(held, 0, end, total_ref, meta, cells)


def bin_arrivals(cells, face_rows, places, known, meta_ref, *refs):
    count = len(refs) - 10
    sources = refs[:count]
    (
        axis_ref,
        held_ref,
        known_ref,
        start_ref,
        total_ref,
        low_ref,
        high_ref,
        held,
        counts_ref,
        sums,
    ) = refs[count:]
    meta = [meta_ref[k] for k in range(8)]
    sums[...] = start_ref[...]
    held[...] = held_ref[...]
    begin = 0
    for k in range(known):
        counts_ref[k] = known_ref[k]
        begin = begin + known_ref[k]
    faces = [(sources[which], first) for which, first in places]
    end = take_faces(faces, face_rows, held, counts_ref, known, begin)
    bin_held(held, begin, end, sums, meta, cells)
    nz, inner = cells.nz, cells.inner
    lane = lax.broadcasted_iota(jnp.int32, (cells.rows, LANES), 1)
    main, rest = sums[:, :LANES], sums[:, LANES:]
    main = main + jnp.where(lane < nz, 0.0, rest)
    top = jnp.where(lane == 0, rest, rest + pltpu.roll(rest, LANES - 3, axis=1))
    total_ref[0] = main
    total_ref[1] = jnp.where(lane < 4, top, 0.0)
    axis = axis_ref[...].astype(f32)
    total_ref[1, :inner, nz : 2 * nz] = axis
    sx, sy = cells.sx, cells.sy
    low_ref[...] = jnp.zeros_like(low_ref)
    high_ref[...] = jnp.zeros_like(high_ref)
    for half in range(2):
        corner = inner + sy + 1
        low_ref[half, :sy, :] = total_ref[half, :sy, :]
        low_ref[half, sy : sy + 1, :] = total_ref[half, corner : corner + 1, :]
        high_ref[half, : sy + 1, :] = total_ref[half, inner : inner + sy + 1, :]


def add_faces_x(cells, total_ref, below_ref, above_ref, out_ref, low_ref, high_ref):
    sx, sy, inner = cells.sx, cells.sy, cells.inner
    corner = inner + sy + 1
    out_ref[...] = total_ref[...]
    low_ref[...] = jnp.zeros_like(low_ref)
    high_ref[...] = jnp.zeros_like(high_ref)
    for half in range(2):
        out_ref[half, :sy, :] += below_ref[half, :sy, :]
        out_ref[half, corner : corner + 1, :] += below_ref[half, sy : sy + 1, :]
        out_ref[half, inner : inner + sy + 1, :] += above_ref[half, : sy + 1, :]
        low_ref[half, :sx, :] = out_ref[half, pl.ds(0, sx, stride=sy), :]
        low_ref[half, sx : sx + 1, :] = out_ref[half, inner : inner + 1, :]
        high_ref[half, :sx, :] = out_ref[half, corner : corner + sx, :]
        high_ref[half, sx : sx + 1, :] = out_ref[half, inner + sy : inner + sy + 1, :]


def add_faces_y(cells, total_ref, below_ref, above_ref, out_ref, face_ref, sums):
    sx, sy, nz, inner = cells.sx, cells.sy, cells.nz, cells.inner
    corner = inner + sy + 1
    sums[...] = total_ref[...]
    for half in range(2):
        sums[half, pl.ds(0, sx, stride=sy), :] += below_ref[half, :sx, :]
        sums[half, inner : inner + 1, :] += below_ref[half, sx : sx + 1, :]
        sums[half, corner : corner + sx, :] += above_ref[half, :sx, :]
        sums[half, inner + sy : inner + sy + 1, :] += above_ref[half, sx : sx + 1, :]
    main = sums[0].T
    rest = sums[1].T
    out_ref[:LANES, :] = main
    out_ref[LANES : LANES + nz, :] = rest[nz : 2 * nz]
    out_ref[LANES + nz :, :] = jnp.zeros((GROUP, cells.rows), f32)
    out_ref[LANES + nz : LANES + nz + 4, :] = rest[:4]
    face_ref[...] = jnp.zeros_like(face_ref)
    for c in range(5):
        face_ref[c : c + 1, :] = out_ref[c * nz : c * nz + 1, :]
        face_ref[GROUP + c : GROUP + c + 1, :] = out_ref[5 * nz + c : 5 * nz + c + 1, :]


def cell_table(cells, total_ref, below_ref, above_ref, table_ref, sheet, edge):
    nz, inner, height = cells.nz, cells.inner, cells.height
    row_ids = lax.broadcasted_iota(jnp.int32, (nz, cells.rows), 0)
    parts = []
    tops = []
    for c in range(5):
        face = jnp.where(row_ids == 0, below_ref[GROUP + c : GROUP + c + 1, :], 0.0)
        parts.append(total_ref[c * nz : (c + 1) * nz, :] + face)
        tops.append(
            total_ref[5 * nz + c : 5 * nz + c + 1, :] + above_ref[c : c + 1, :]
        )
    mass = jnp.maximum(parts[0], 1.0)
    top_mass = jnp.maximum(tops[0], 1.0)
    values = [parts[4]] + [p / mass for p in parts[1:4]]
    top_values = [tops[4]] + [t / top_mass for t in tops[1:4]]
    sheet[...] = jnp.zeros_like(sheet)
    edge[...] = jnp.zeros_like(edge)
    lane = lax.broadcasted_iota(jnp.int32, (cells.extra, LANES), 1)
    spare = LANES - (cells.rows - inner)
    for c in range(4):
        base = c * height
        sheet[base : base + nz, :] = values[c][:, :inner]
        sheet[base + nz : base + nz + 1, :] = top_values[c][:, :inner]
        edge[base : base + nz, :] = jnp.concatenate(
            [values[c][:, inner:], jnp.zeros((nz, spare), f32)], axis=1
        )
        edge[base + nz : base + nz + 1, :] = jnp.concatenate(
            [top_values[c][:, inner:], jnp.zeros((1, spare), f32)], axis=1
        )
        folded = [jnp.zeros((cells.extra, LANES), f32) for _ in range(inner // LANES)]
        for m in range(cells.per):
            begin = m * cells.edges
            piece = edge[pl.ds(base + m, cells.extra, stride=cells.per), :]
            piece = pltpu.roll(piece, begin % LANES, axis=1) if begin % LANES else piece
            for t in range(inner // LANES):
                low, high = begin - t * LANES, begin + cells.edges - t * LANES
                if high > 0 and low < LANES:
                    folded[t] = jnp.where((lane >= low) & (lane < high), piece, folded[t])
        sheet[base + nz + 1 : base + nz + 1 + cells.extra, :] = jnp.concatenate(folded, axis=1)
    whole = sheet[...]
    high = whole.astype(bf16).astype(f32)
    low = (whole - high)[height:]
    table_ref[...] = jnp.concatenate([high, low], axis=0).astype(bf16)


def direction_table():
    counter = jnp.arange(LANES).astype(f32)
    height = 1.0 - (2.0 * counter + 1.0) / NAXES
    radius = jnp.sqrt(jnp.maximum(1.0 - height * height, 0.0))
    rows = jnp.stack([radius * jnp.cos(golden * counter), radius * jnp.sin(golden * counter)])
    return jnp.broadcast_to(rows[:, None], (2, GROUP, LANES))


def fold_rows(values):
    sub = lax.broadcasted_iota(jnp.int32, (GROUP, LANES), 0)
    step = GROUP // 2
    while step:
        upper = (sub & step) == 0
        half = len(values) // 2
        joined = []
        for a, b in zip(values[:half], values[half:]):
            a = a + pltpu.roll(a, GROUP - step, axis=0)
            b = b + pltpu.roll(b, step, axis=0)
            joined.append(jnp.where(upper, a, b))
        values = joined
        step //= 2
    return values[0]


def collide(position, velocity, meta, table, dirs_ref, cells):
    height = cells.height
    row, column = place_of(levels_of(position, meta), cells)
    found = lax.dot_general(
        table, one_hot(column, cells.inner), NN, preferred_element_type=f32
    )
    ids = lax.broadcasted_iota(jnp.int32, (height, LANES), 0).astype(f32)
    picked = [[] for _ in range(4)]
    for r in range(GROUP):
        block = found[:, r * LANES : (r + 1) * LANES]
        here = ids == row[r : r + 1]
        for c in range(4):
            value = block[c * height : (c + 1) * height]
            if c > 0:
                value = value + block[(3 + c) * height : (4 + c) * height]
            value = jnp.where(here, value, 0.0)
            picked[c].append(
                jnp.sum(value.reshape(height // GROUP, GROUP, LANES), axis=0)
            )
    picked = [fold_rows(p) for p in picked]
    axis, flow = picked[0].astype(jnp.int32), picked[1:]
    normal = [
        jnp.take_along_axis(dirs_ref[0], axis, axis=1, mode="promise_in_bounds"),
        jnp.take_along_axis(dirs_ref[1], axis, axis=1, mode="promise_in_bounds"),
        1.0 - (2.0 * picked[0] + 1.0) * (1.0 / NAXES),
    ]
    rel = [velocity[d] - flow[d] for d in range(3)]
    along = (1.0 - turn_cosine) * (
        normal[0] * rel[0] + normal[1] * rel[1] + normal[2] * rel[2]
    )
    result = []
    for d in range(3):
        e, f = (d + 1) % 3, (d + 2) % 3
        crossed = normal[e] * rel[f] - normal[f] * rel[e]
        result.append(
            flow[d] + (turn_cosine * rel[d] + turn_sine * crossed + along * normal[d])
        )
    return result


def passed(position, speed):
    return position - jnp.floor(position) - 0.5 + 3.0 * step_size * speed


def copy_out(pairs, sems):
    copies = [pltpu.make_async_copy(a, b, sems.at[k]) for k, (a, b) in enumerate(pairs)]
    for copy in copies:
        copy.start()
    for copy in copies:
        copy.wait()


def collide_residents(
    cells, first, count, meta_ref, dirs_ref, table_ref, pos_ref, vel_ref, *refs
):
    out_pos, out_vel, token, held_pos, held_vel, sems = refs[-6:]
    token[...] = jnp.zeros_like(token)
    meta = [meta_ref[k] for k in range(8)]
    table = table_ref[...]
    live_rows = meta[6] - first
    held_pos[...] = jnp.zeros_like(held_pos)
    held_vel[...] = jnp.zeros_like(held_vel)
    stride = GROUP * TWIN

    @pl.loop(0, jnp.clip((live_rows + stride - 1) // stride, 0, count // stride))
    def _(step):
        for part in range(TWIN):
            offset = pl.multiple_of(step * stride + part * GROUP, GROUP)
            rows = pl.ds(offset, GROUP)
            position = [pos_ref[d, rows, :] for d in range(3)]
            velocity = [vel_ref[d, rows, :] for d in range(3)]
            live = row_iota() + offset < live_rows
            speed = collide(position, velocity, meta, table, dirs_ref, cells)
            for d in range(3):
                held_vel[d, rows, :] = jnp.where(live, speed[d], 0.0)
                held_pos[d, rows, :] = jnp.where(live, passed(position[d], speed[d]), 0.0)

    span = pl.ds(first, count)
    copy_out([(held_pos, out_pos.at[:, span, :]), (held_vel, out_vel.at[:, span, :])], sems)


def collide_held(cells, first, count, many, meta_ref, dirs_ref, table_ref, held, counts_ref, *refs):
    out_ref, token = refs[-2:]
    token[...] = jnp.zeros_like(token)
    meta = [meta_ref[k] for k in range(8)]
    table = table_ref[...]
    out_ref[...] = jnp.zeros_like(out_ref)
    end = sum([counts_ref[k] for k in range(many)], jnp.int32(0)) - first
    stride = GROUP * TRIO

    @pl.loop(0, jnp.clip((end + stride - 1) // stride, 0, count // stride))
    def _(step):
        for part in range(TRIO):
            offset = pl.multiple_of(step * stride + part * GROUP, GROUP)
            comps = [held[c, pl.ds(first + offset, GROUP), :] for c in range(6)]
            speed = collide(comps[:3], comps[3:], meta, table, dirs_ref, cells)
            for d in range(3):
                out_ref[d, pl.ds(offset, GROUP), :] = speed[d]
                out_ref[3 + d, pl.ds(offset, GROUP), :] = passed(comps[d], speed[d])


def place_arrivals(first, face_rows, sequence, counts_ref, *refs):
    pieces = refs[: len(refs) - 9]
    out_pos, out_vel, token, held_pos, held_vel, sems, packed = refs[-7:]
    token[...] = jnp.zeros_like(token)
    packed[...] = jnp.zeros_like(packed)
    at = 0
    for piece in pieces:
        packed[:, at : at + piece.shape[1], :] = piece[...]
        at += piece.shape[1]
    rows = lax.broadcasted_iota(jnp.int32, (face_rows, LANES), 0)
    offset = 0
    for k, face in enumerate(sequence):
        count = counts_ref[k]
        place = slice(face * face_rows, (face + 1) * face_rows)
        for d in range(3):
            speed = packed[d, pl.ds(offset, face_rows), :]
            moved = packed[3 + d, pl.ds(offset, face_rows), :]
            held_vel[d, place, :] = jnp.where(rows < count, speed, 0.0)
            held_pos[d, place, :] = jnp.where(rows < count, moved, 0.0)
        offset = offset + count
    span = pl.ds(first, len(sequence) * face_rows)
    copy_out([(held_pos, out_pos.at[:, span, :]), (held_vel, out_vel.at[:, span, :])], sems)


def pack_inputs(
    meta_ref,
    pos_ref,
    vel_ref,
    bead_pos_ref,
    bead_vel_ref,
    order_ref,
    start_ref,
    block_ref,
    rows_pos_ref,
    rows_vel_ref,
    *refs,
):
    out_refs, (held_pos, held_vel, sems) = refs[:6], refs[6:]
    copies = [(bead_pos_ref, held_pos), (bead_vel_ref, held_vel)]
    for face, out_ref in enumerate(out_refs):
        copies.append((pos_ref.at[:, face], out_ref.at[0:3]))
        copies.append((vel_ref.at[:, face], out_ref.at[3:6]))
    copies = [pltpu.make_async_copy(a, b, sems.at[k]) for k, (a, b) in enumerate(copies)]
    for copy in copies:
        copy.start()
    for face, out_ref in enumerate(out_refs):
        out_ref[6] = jnp.full(out_ref.shape[1:], meta_ref[8 + face], jnp.int32).astype(f32)
    slots = start_ref.shape[1]
    start_ref[...] = jnp.zeros_like(start_ref)
    rows_pos_ref[...] = jnp.zeros_like(rows_pos_ref)
    rows_vel_ref[...] = jnp.zeros_like(rows_vel_ref)
    for copy in copies:
        copy.wait()
    for d in range(3):
        for k in range(slots // LANES):
            lanes = slice(k * LANES, (k + 1) * LANES)
            start_ref[d : d + 1, lanes] = held_pos[d, k : k + 1, :]
            rows_pos_ref[d, k : k + 1, :] = held_pos[d, k : k + 1, :]
            rows_vel_ref[d, k : k + 1, :] = held_vel[d, k : k + 1, :]
    start = start_ref[...]
    whole = payload(start, slot_live(slots, meta_ref[7], GROUP))
    for k in range(slots // LANES):
        block_ref[k * GROUP : (k + 1) * GROUP, :] = whole[:, k * LANES : (k + 1) * LANES]


def stack_rows(parts, *refs):
    out_ref = refs[-1]
    at = 0
    for which, begin, count in parts:
        out_ref[at : at + count, :] = refs[which][begin : begin + count, :]
        at += count


def slot_live(slots, chains, rows):
    return lax.broadcasted_iota(jnp.int32, (rows, slots), 1) < CHAIN * chains


def payload(position, live):
    slots = position.shape[1]
    row_ids = lax.broadcasted_iota(jnp.int32, (GROUP, slots), 0)
    flag = jnp.where(live, 1.0, 0.0)
    return jnp.where(row_ids == 3, flag, jnp.where(row_ids < 3, position, 0.0))


def thirds_of(value):
    high = value.astype(bf16)
    rest = value - high.astype(f32)
    middle = rest.astype(bf16)
    low = (rest - middle.astype(f32)).astype(bf16)
    return jnp.concatenate([high.astype(f32), middle.astype(f32), low.astype(f32)], axis=0).astype(
        bf16
    )


def summed_thirds(value):
    return value[:GROUP] + (value[GROUP : 2 * GROUP] + value[2 * GROUP :])


def forces(own, chains, counts, bonds_ref, blocks, centre, lengths, mine_ref, packed, push):
    slots = own.shape[1]
    bond_slots = bonds_ref.shape[0]
    row_ids = lax.broadcasted_iota(jnp.int32, (GROUP, slots), 0)
    mid = jnp.zeros((GROUP, slots), f32)
    length = jnp.ones((GROUP, slots), f32)
    for d in range(3):
        mid = jnp.where(row_ids == d, centre[d], mid)
        length = jnp.where(row_ids == d, lengths[d], length)
    live = slot_live(slots, chains, GROUP)
    local = jnp.where(live & (row_ids < 3), own - mid, 0.0)
    columns = jnp.where(live, local, far_own).T
    for d in range(3):
        mine_ref[d] = jnp.broadcast_to(columns[:, d : d + 1], (slots, LANES))

    packed[...] = jnp.full(packed.shape, far_ghost, f32)
    lane = lax.broadcasted_iota(jnp.int32, (GROUP, LANES), 1)
    tiles = slots // LANES
    offset = jnp.int32(0)
    index = 0
    for ref in blocks:
        for b in range(ref.shape[0] // GROUP):
            near = ref[b * GROUP : (b + 1) * GROUP, :] - mid
            near = near - length * jnp.floor(near * (1.0 / length) + 0.5)
            tile, turn = offset // LANES, offset % LANES
            turned = [
                pltpu.roll(near[:, k * LANES : (k + 1) * LANES], turn, axis=1)
                for k in range(tiles)
            ]
            for k in range(tiles + 1):
                if k == 0:
                    value = turned[0]
                elif k == tiles:
                    value = turned[-1]
                else:
                    value = jnp.where(lane < turn, turned[k - 1], turned[k])
                place = (tile + k) * LANES + lane
                taken = (place >= offset) & (place < offset + counts[index])
                packed[tile + k] = jnp.where(taken, value, packed[tile + k])
            offset = offset + counts[index]
            index += 1

    push[...] = jnp.zeros_like(push)
    chunk = 64
    steps = (offset + 2 * LANES - 1) // (2 * LANES)

    @pl.loop(0, (CHAIN * chains + chunk - 1) // chunk)
    def _(part):
        rows = pl.ds(pl.multiple_of(part * chunk, chunk), chunk)
        mine = [mine_ref[d, rows, :] for d in range(3)]

        def add_tiles(step, total):
            for k in range(2):
                other = packed[2 * step + k]
                differ = [mine[d] - other[d : d + 1] for d in range(3)]
                square = (
                    differ[0] * differ[0] + differ[1] * differ[1] + differ[2] * differ[2]
                )
                inside = (square < cut_square) & (square > 0.25)
                inverse = 1.0 / jnp.where(inside, square, 1e30)
                sixth = inverse * inverse * inverse
                weight = (sixth * inverse) * (48.0 * sixth - 24.0)
                total = tuple(total[d] + weight * differ[d] for d in range(3))
            return total

        total = lax.fori_loop(
            0, steps, add_tiles, tuple(jnp.zeros((chunk, LANES), f32) for _ in range(3))
        )
        for d in range(3):
            push[d, rows, :] = total[d]

    pair = jnp.zeros((GROUP, slots), f32)
    for d in range(3):
        pair = jnp.where(row_ids == d, jnp.sum(push[d].T, axis=0, keepdims=True), pair)

    slot_ids = lax.broadcasted_iota(jnp.int32, (bond_slots, slots), 1)
    bond_ids = lax.broadcasted_iota(jnp.int32, (bond_slots, slots), 0)
    ends = bonds_ref[...]
    first = jnp.where(slot_ids == ends[:, 0:1], 1.0, 0.0)
    second = jnp.where(slot_ids == ends[:, 1:2], 1.0, 0.0)
    joins = jnp.where(bond_ids < (CHAIN - 1) * chains, first - second, 0.0).astype(bf16)
    stretch = summed_thirds(
        lax.dot_general(thirds_of(local), joins, NT, preferred_element_type=f32)
    )
    square = (
        stretch[0:1] * stretch[0:1] + stretch[1:2] * stretch[1:2] + stretch[2:3] * stretch[2:3]
    )
    bond_live = (
        lax.broadcasted_iota(jnp.int32, (1, bond_slots), 1) < (CHAIN - 1) * chains
    )
    pull = jnp.where(bond_live, -spring / (1.0 - square / reach_square), 0.0) * stretch
    return pair + summed_thirds(
        lax.dot_general(thirds_of(pull), joins, NN, preferred_element_type=f32)
    )


def force_scratch(slots, blocks):
    tiles = -(-(blocks * slots // LANES + 2) // 2) * 2
    return [
        pltpu.VMEM((3, slots, LANES), f32),
        pltpu.VMEM((tiles, GROUP, LANES), f32),
        pltpu.VMEM((3, slots, LANES), f32),
    ]


def centre_of(meta, sizes):
    return [meta[3 + d].astype(f32) + 0.5 * sizes[d] for d in range(3)]


def first_forces(sizes, lengths, sources, meta_ref, start_ref, bonds_ref, *refs):
    blocks, (push_ref, counts_ref), scratch = (
        refs[:sources],
        refs[sources : sources + 2],
        refs[sources + 2 :],
    )
    meta = [meta_ref[k] for k in range(8)]
    counts = []
    for ref in blocks:
        for b in range(ref.shape[0] // GROUP):
            live = ref[b * GROUP + 3 : b * GROUP + 4, :]
            counts.append(jnp.sum(live).astype(jnp.int32))
    for k, count in enumerate(counts):
        counts_ref[k] = count
    push_ref[...] = forces(
        start_ref[...],
        meta[7],
        counts,
        bonds_ref,
        blocks,
        centre_of(meta, sizes),
        lengths,
        *scratch,
    )


def finish_cells(
    cells,
    meta_ref,
    dirs_ref,
    total_ref,
    below_ref,
    above_ref,
    bead_pos_ref,
    bead_vel_ref,
    start_ref,
    push_ref,
    table_ref,
    speed_ref,
    moved_ref,
    pay_ref,
    sheet,
    edge,
):
    meta = [meta_ref[k] for k in range(8)]
    cell_table(cells, total_ref, below_ref, above_ref, table_ref, sheet, edge)
    fresh = collide(
        [bead_pos_ref[d] for d in range(3)],
        [bead_vel_ref[d] for d in range(3)],
        meta,
        table_ref[...],
        dirs_ref,
        cells,
    )
    start = start_ref[...]
    slots = start.shape[1]
    row_ids = lax.broadcasted_iota(jnp.int32, (GROUP, slots), 0)
    speed = jnp.zeros((GROUP, slots), f32)
    for d in range(3):
        line = jnp.concatenate([fresh[d][k : k + 1] for k in range(slots // LANES)], axis=1)
        speed = jnp.where(row_ids == d, line, speed)
    speed = speed + half_kick * push_ref[...]
    moved = step_size * speed
    live = slot_live(slots, meta[7], GROUP)
    speed_ref[...] = speed
    moved_ref[...] = moved
    pay_ref[...] = payload(start + moved, live)


def substep(
    sizes, lengths, last, sources, meta_ref, start_ref, bonds_ref, counts_ref, speed_ref, moved_ref, *refs
):
    blocks, outs, scratch = refs[:sources], refs[sources + 1 : -3], refs[-3:]
    meta = [meta_ref[k] for k in range(8)]
    counts = [
        counts_ref[k] for k in range(sum(ref.shape[0] // GROUP for ref in blocks))
    ]
    start = start_ref[...]
    moved = moved_ref[...]
    push = forces(
        start + moved,
        meta[7],
        counts,
        bonds_ref,
        blocks,
        centre_of(meta, sizes),
        lengths,
        *scratch,
    )
    live = slot_live(start.shape[1], meta[7], GROUP)
    speed = speed_ref[...] + half_kick * push
    if last:
        for d in range(3):
            outs[0][d, 0, 0, :, :] = jnp.where(live, speed, 0.0)[d : d + 1]
            outs[1][d, 0, 0, :, :] = jnp.where(live, moved, 0.0)[d : d + 1]
        return
    speed = speed + half_kick * push
    moved = moved + step_size * speed
    outs[0][...] = speed
    outs[1][...] = moved
    outs[2][...] = payload(start + moved, live)


def neighbours(value, axis):
    peers = lax.axis_size(axis)
    if peers == 2:
        return [moved_along(value, axis, 1)]
    return [moved_along(value, axis, 1), moved_along(value, axis, -1)]


def stacked(parts, operands, order=()):
    rows = sum(count for _, _, count in parts)
    width = operands[0].shape[1]
    return pl.pallas_call(
        functools.partial(stack_rows, tuple(parts)),
        out_shape=like(rows, width),
        in_specs=[vmem()] * len(operands) + [pl.BlockSpec(memory_space=pl.ANY)] * len(order),
        out_specs=vmem(),
        compiler_params=params(),
        name="stack_rows",
    )(*operands, *order)


def whole_rows(operands):
    return [(k, 0, value.shape[0]) for k, value in enumerate(operands)]


def halo(block, pieces):
    parts = [block] + neighbours(block, "gz")
    row = stacked(whole_rows(parts), parts, [pieces[0]()])
    parts = [row] + neighbours(row, "gy")
    plane = stacked(whole_rows(parts), parts, [pieces[1]()])
    sides = neighbours(plane, "gx")
    return [plane] + sides, pieces[2]()


def like(*shape, dtype=f32):
    return jax.ShapeDtypeStruct(shape, dtype)


def shards(
    sol_pos,
    sol_vel,
    sol_rows,
    mig_pos,
    mig_vel,
    mig_rows,
    bead_pos,
    bead_vel,
    bead_chains,
    bond_list,
    cell_axis,
    shift,
):
    sizes = cell_axis.shape
    cells = Cells(*sizes)
    names = ("gx", "gy", "gz")
    lengths = tuple(float(sizes[d] * lax.axis_size(names[d])) for d in range(3))
    slots_here = sol_pos.shape[-1]
    buffer_slots = mig_pos.shape[-1]
    bead_slots = bead_pos.shape[-1]
    bond_slots = bond_list.shape[-1]
    rows_here = slots_here // LANES
    face_rows = buffer_slots // LANES
    rows_all = rows_here + 6 * face_rows
    anchor = jnp.stack([lax.axis_index(names[d]) * sizes[d] for d in range(3)])
    meta = jnp.concatenate(
        [
            shift,
            anchor.astype(jnp.int32),
            sol_rows.reshape(1),
            bead_chains.reshape(1),
            mig_rows.reshape(6),
        ]
    )
    dirs = direction_table()
    position = sol_pos.reshape(3, rows_here, LANES)
    velocity = sol_vel.reshape(3, rows_here, LANES)

    any_spec = pl.BlockSpec(memory_space=pl.ANY)
    thirds = 3
    count = rows_here // thirds
    axis_rows = cell_axis.reshape(cells.inner, sizes[2])

    def bin_piece(piece, earlier, order):
        return pl.pallas_call(
            functools.partial(bin_residents, cells, piece * count, count),
            out_shape=like(cells.rows, 2 * LANES),
            grid=(1,),
            in_specs=[smem()]
            + [pl.BlockSpec((3, count, LANES), lambda i, p=piece: (0, p, 0))] * 2
            + [vmem()] * len(earlier)
            + [any_spec] * len(order),
            out_specs=vmem(),
            compiler_params=params(),
            name=f"bin_residents_{piece}",
        )(meta, position, velocity, *earlier, *order)

    totals = bin_piece(0, [], [])
    face_height = 7 * face_rows
    bead_shape = like(GROUP, bead_slots)
    tiles = bead_slots // LANES
    rows_shape = like(3, GROUP, LANES)
    start, block, bead_rows_pos, bead_rows_vel, *packed = pl.pallas_call(
        pack_inputs,
        out_shape=[bead_shape, like(tiles * GROUP, LANES), rows_shape, rows_shape]
        + [like(7, face_rows, LANES)] * 6,
        in_specs=[smem()] + [pl.BlockSpec(memory_space=pltpu.HBM)] * 4 + [any_spec],
        out_specs=[vmem()] * 10,
        scratch_shapes=[pltpu.VMEM((3, tiles, LANES), f32)] * 2
        + [pltpu.SemaphoreType.DMA((14,))],
        compiler_params=params(vmem_most),
        name="pack_inputs",
    )(
        meta,
        mig_pos.reshape(3, 6, face_rows, LANES),
        mig_vel.reshape(3, 6, face_rows, LANES),
        bead_pos.reshape(3, tiles, LANES),
        bead_vel.reshape(3, tiles, LANES),
        totals,
    )
    packed = [value.reshape(face_height, LANES) for value in packed]
    bonds = bond_list.reshape(2, bond_slots).T

    def swap(axis, low, high, body):
        if lax.axis_size(axis) == 2:
            both = [packed[low], packed[high], body]
            came = moved_along(stacked(whole_rows(both), both), axis, 1)
            return [came], [(0, face_height), (0, 0)], [(0, 2 * face_height)]
        up = stacked(whole_rows([packed[high], body]), [packed[high], body])
        down = stacked(whole_rows([packed[low], body]), [packed[low], body])
        came = [moved_along(up, axis, 1), moved_along(down, axis, -1)]
        return came, [(0, 0), (1, 0)], [(0, face_height), (1, face_height)]

    arriving, spots, blocks = [], [None] * 6, block
    for piece, (axis, low) in enumerate((("gz", 4), ("gy", 2), ("gx", 0))):
        came, places, bodies = swap(axis, low, low + 1, blocks)
        for k, (which, at) in enumerate(places):
            spots[low + k] = (len(arriving) + which, at)
        arriving += came
        height = blocks.shape[0]
        if axis != "gx":
            totals = bin_piece(piece + 1, [totals], [blocks])
            parts = [(0, 0, height)] + [(1 + w, at, height) for w, at in bodies]
            blocks = stacked(parts, [blocks] + came, [totals])
        else:
            around = [blocks] + [
                stacked([(0, at, height)], [came[w]]) for w, at in bodies
            ]

    def as_blocks(value):
        n = value.shape[0] // (GROUP * tiles)
        return (
            value.reshape(n, tiles, GROUP, LANES)
            .transpose(0, 2, 1, 3)
            .reshape(n * GROUP, bead_slots)
        )

    sequence = (4, 5, 2, 3, 0, 1)
    early, late = sequence[:4], sequence[4:]
    sooner = max(spots[face][0] for face in early) + 1
    held_rows = -(-6 * face_rows // 32) * 32
    held_shape = like(6, held_rows, LANES)
    totals, held, counted = pl.pallas_call(
        functools.partial(
            bin_first_arrivals, cells, face_rows, [spots[face] for face in early]
        ),
        out_shape=[like(cells.rows, 2 * LANES), held_shape, like(4, dtype=jnp.int32)],
        in_specs=[smem()] + [vmem()] * (sooner + 3) + [any_spec],
        out_specs=[vmem(), vmem(), smem()],
        compiler_params=params(),
        name="bin_first_arrivals",
    )(meta, *arriving[:sooner], bead_rows_pos, bead_rows_vel, totals, blocks)

    face_x = like(2, -(-(sizes[1] + 1) // GROUP) * GROUP, LANES)
    face_y = like(2, -(-(sizes[0] + 1) // GROUP) * GROUP, LANES)
    later = arriving[sooner:]
    totals, low, high, held, counted = pl.pallas_call(
        functools.partial(
            bin_arrivals,
            cells,
            face_rows,
            [(spots[face][0] - sooner, spots[face][1]) for face in late],
            len(early),
        ),
        out_shape=[
            like(2, cells.rows, LANES),
            face_x,
            face_x,
            held_shape,
            like(6, dtype=jnp.int32),
        ],
        in_specs=[smem()] + [vmem()] * (len(later) + 2) + [smem(), vmem()],
        out_specs=[vmem()] * 4 + [smem()],
        scratch_shapes=[pltpu.VMEM((cells.rows, 2 * LANES), f32)],
        compiler_params=params(),
        name="bin_arrivals",
    )(meta, *later, axis_rows, held, counted, totals)

    around = [as_blocks(value) for value in around]
    many = sum(value.shape[0] // GROUP for value in around)
    push, counts = pl.pallas_call(
        functools.partial(first_forces, sizes, lengths, len(around)),
        out_shape=[bead_shape, like(many, dtype=jnp.int32)],
        in_specs=[smem()] + [vmem()] * (2 + len(around)),
        out_specs=[vmem(), smem()],
        scratch_shapes=force_scratch(bead_slots, many),
        compiler_params=params(),
        name="first_forces",
    )(meta, start, bonds, *around)

    below, above = moved_along(high, "gx", 1), moved_along(low, "gx", -1)
    totals, low, high = pl.pallas_call(
        functools.partial(add_faces_x, cells),
        out_shape=[like(2, cells.rows, LANES), face_y, face_y],
        in_specs=[vmem()] * 3,
        out_specs=[vmem()] * 3,
        compiler_params=params(),
        name="add_faces_x",
    )(totals, below, above)
    below, above = moved_along(high, "gy", 1), moved_along(low, "gy", -1)
    totals, faces = pl.pallas_call(
        functools.partial(add_faces_y, cells),
        out_shape=[like(LANES + cells.nz + GROUP, cells.rows), like(2 * GROUP, cells.rows)],
        in_specs=[vmem()] * 3,
        out_specs=[vmem()] * 2,
        scratch_shapes=[pltpu.VMEM((2, cells.rows, LANES), f32)],
        compiler_params=params(),
        name="add_faces_y",
    )(totals, below, above)
    sides = neighbours(faces, "gz")
    below, above = sides[0], sides[-1]

    table, speed, moved, pay = pl.pallas_call(
        functools.partial(finish_cells, cells),
        out_shape=[
            like(7 * cells.height, cells.inner, dtype=bf16),
            bead_shape,
            bead_shape,
            bead_shape,
        ],
        in_specs=[smem()] + [vmem()] * 8,
        out_specs=[vmem()] * 4,
        scratch_shapes=[
            pltpu.VMEM((4 * cells.height, cells.inner), f32),
            pltpu.VMEM((4 * cells.height, LANES), f32),
        ],
        compiler_params=params(),
        name="finish_cells",
    )(meta, dirs, totals, below, above, bead_rows_pos, bead_rows_vel, start, push)

    solvent_shape = like(3, rows_all, LANES)
    results = []
    cuts = 6
    span = rows_here // cuts

    held_span = 2 * face_rows
    packed_results = []

    def collide_piece(piece):
        if piece < cuts:
            earlier = results[:2]
            results[:] = pl.pallas_call(
                functools.partial(collide_residents, cells, piece * span, span),
                out_shape=[solvent_shape, solvent_shape, like(GROUP, LANES)],
                grid=(1,),
                in_specs=[smem(), vmem(), vmem()]
                + [pl.BlockSpec((3, span, LANES), lambda i: (0, piece, 0))] * 2
                + [any_spec] * len(earlier),
                out_specs=[any_spec, any_spec, vmem()],
                scratch_shapes=[pltpu.VMEM((3, span, LANES), f32)] * 2
                + [pltpu.SemaphoreType.DMA((2,))],
                input_output_aliases={5: 0, 6: 1} if earlier else {},
                compiler_params=params(),
                name=f"collide_{piece}",
            )(meta, dirs, table, position, velocity, *earlier)
            return results[2]
        value, token = pl.pallas_call(
            functools.partial(collide_held, cells, (piece - cuts) * held_span, held_span, 6),
            out_shape=[like(6, held_span, LANES), like(GROUP, LANES)],
            in_specs=[smem()] + [vmem()] * 3 + [smem(), any_spec],
            out_specs=[vmem()] * 2,
            compiler_params=params(),
            name=f"collide_{piece}",
        )(meta, dirs, table, held, counted, results[2])
        packed_results.append(value)
        if piece < cuts + 2:
            return token
        results[:] = pl.pallas_call(
            functools.partial(place_arrivals, rows_here, face_rows, sequence),
            out_shape=[solvent_shape, solvent_shape, like(GROUP, LANES)],
            in_specs=[smem()] + [vmem()] * 3 + [any_spec] * 2,
            out_specs=[any_spec, any_spec, vmem()],
            scratch_shapes=[pltpu.VMEM((3, 6 * face_rows, LANES), f32)] * 2
            + [
                pltpu.SemaphoreType.DMA((2,)),
                pltpu.VMEM((6, 7 * face_rows, LANES), f32),
            ],
            input_output_aliases={4: 0, 5: 1},
            compiler_params=params(),
            name="place_arrivals",
        )(counted, *packed_results, *results[:2])
        return results[2]

    for step in range(3):
        last = step == 2
        thunks = [functools.partial(collide_piece, 3 * step + k) for k in range(3)]
        ghosts, order = halo(pay, thunks)
        final = like(3, 1, 1, 1, bead_slots)
        outcome = pl.pallas_call(
            functools.partial(substep, sizes, lengths, last, len(ghosts)),
            out_shape=[final] * 2 if last else [bead_shape] * 3,
            in_specs=[smem(), vmem(), vmem(), smem()]
            + [vmem()] * (2 + len(ghosts))
            + [any_spec],
            out_specs=[vmem()] * (2 if last else 3),
            scratch_shapes=force_scratch(bead_slots, many),
            compiler_params=params(),
            name=f"substep_{step}",
        )(meta, start, bonds, counts, speed, moved, *ghosts, order)
        speed, moved = outcome[:2]
        pay = outcome[-1]

    count_solvent = rows_all * LANES
    return (
        results[0].reshape(3, 1, 1, 1, count_solvent),
        results[1].reshape(3, 1, 1, 1, count_solvent),
        moved,
        speed,
    )


def solution(mesh):
    return jax.shard_map(
        shards,
        mesh=mesh,
        in_specs=(
            P(None, "gx", "gy", "gz", None),
            P(None, "gx", "gy", "gz", None),
            P("gx", "gy", "gz"),
            P(None, "gx", "gy", "gz", None, None),
            P(None, "gx", "gy", "gz", None, None),
            P("gx", "gy", "gz", None),
            P(None, "gx", "gy", "gz", None),
            P(None, "gx", "gy", "gz", None),
            P("gx", "gy", "gz"),
            P(None, "gx", "gy", "gz", None),
            P("gx", "gy", "gz"),
            P(),
        ),
        out_specs=(
            P(None, "gx", "gy", "gz", None),
            P(None, "gx", "gy", "gz", None),
            P(None, "gx", "gy", "gz", None),
            P(None, "gx", "gy", "gz", None),
        ),
        check_vma=False,
    )
```

```python
import functools
import math

import jax
import jax.numpy as jnp
from jax import lax
from jax.experimental import pallas as pl
from jax.experimental.pallas import tpu as pltpu
from jax.sharding import PartitionSpec as P

UNITS = 16
NAXES = 32
CHAIN = 8
LANES = 128
GROUP = 8
TWIN = 4
PAIR = 2
TRIO = 3

bead_mass = 5.0
step_size = 0.02
spring = 30.0
reach_square = 2.25
cut_square = 2.0 ** (1.0 / 3.0)
turn_cosine = math.cos(130.0 * math.pi / 180.0)
turn_sine = math.sin(130.0 * math.pi / 180.0)
golden = math.pi * (3.0 - math.sqrt(5.0))
half_kick = 0.5 * step_size / bead_mass
far_own = 3000.0
far_ghost = 9000.0
vmem_limit = 48 * 1024 * 1024
vmem_most = 48 * 1024 * 1024
NT = (((1,), (1,)), ((), ()))
NN = (((1,), (0,)), ((), ()))
exact = lax.Precision.HIGHEST
f32 = jnp.float32
bf16 = jnp.bfloat16


def params(limit=vmem_limit):
    return pltpu.CompilerParams(vmem_limit_bytes=limit)


def vmem():
    return pl.BlockSpec(memory_space=pltpu.VMEM)


def smem():
    return pl.BlockSpec(memory_space=pltpu.SMEM)


def moved_along(value, axis, by):
    peers = lax.axis_size(axis)
    return lax.ppermute(value, axis, [(i, (i + by) % peers) for i in range(peers)])


class Cells:
    def __init__(self, size_x, size_y, size_z):
        self.sx, self.sy, self.nz = size_x, size_y, size_z
        self.inner = size_x * size_y
        self.edges = size_x + size_y + 1
        self.rows = -(-(self.inner + self.edges) // 16) * 16
        self.middle = self.rows // 2
        self.per = self.inner // self.edges
        self.depths = size_z + 1
        self.extra = -(-self.depths // self.per)
        self.height = -(-(self.depths + self.extra) // GROUP) * GROUP


def levels_of(position, meta):
    return [
        jnp.floor(jnp.floor(position[d] * UNITS + meta[d].astype(f32)) * (1.0 / UNITS))
        - meta[3 + d].astype(f32)
        for d in range(3)
    ]


def edge_of(levels, cells):
    outer = (levels[0] == cells.sx) | (levels[1] == cells.sy)
    return outer, jnp.where(levels[0] == cells.sx, levels[1], cells.sy + 1 + levels[0])


def plane_of(levels, cells):
    outer, edge = edge_of(levels, cells)
    return jnp.where(outer, cells.inner + edge, levels[0] * cells.sy + levels[1])


def place_of(levels, cells):
    outer, edge = edge_of(levels, cells)
    fold = jnp.floor((levels[2] + 0.5) * (1.0 / cells.per))
    row = jnp.where(outer, cells.depths + fold, levels[2])
    column = jnp.where(
        outer,
        (levels[2] - fold * cells.per) * cells.edges + edge,
        levels[0] * cells.sy + levels[1],
    )
    return row, column


def wide(row):
    return jnp.broadcast_to(row, (16, LANES)).astype(bf16)


def one_hot(column, height):
    middle = height // 2
    ids = lax.broadcasted_iota(jnp.int32, (height, LANES), 0) - middle
    ids = ids.astype(f32).astype(bf16).reshape(height // 16, 16, LANES)
    column = column - middle
    one, zero = jnp.ones((), bf16), jnp.zeros((), bf16)
    pieces = [
        jnp.where(ids == wide(column[r : r + 1])[None], one, zero).reshape(height, LANES)
        for r in range(column.shape[0])
    ]
    return jnp.concatenate(pieces, axis=1)


def split(value):
    high = value.astype(bf16).astype(f32)
    return high, value - high


def spread_moments(depth, weight, velocity, cells):
    nz = cells.nz
    ids = lax.broadcasted_iota(jnp.int32, (nz, LANES), 0).astype(f32).astype(bf16)
    ids = ids.reshape(nz // 16, 16, LANES)
    row_ids = lax.broadcasted_iota(jnp.int32, (16, LANES), 0).astype(f32).astype(bf16)
    zero = jnp.zeros((), bf16)
    parts = [split(weight * velocity[d]) for d in range(3)]
    channels = [weight] + [p[0] for p in parts] + [p[1] for p in parts]
    pieces = []
    for r in range(depth.shape[0]):
        at = wide(depth[r : r + 1])
        here = ids == at[None]
        values = [wide(c[r : r + 1]) for c in channels]
        tiles = [jnp.where(here, v[None], zero).reshape(nz, LANES) for v in values]
        top = jnp.zeros((16, LANES), bf16)
        for c, v in enumerate(values):
            top = jnp.where(row_ids == c, v, top)
        top = jnp.where(at == nz, top, zero)
        pieces.append(
            jnp.concatenate(
                tiles[:4] + [top, jnp.zeros((nz - 16, LANES), bf16)] + tiles[4:], axis=0
            )
        )
    return jnp.concatenate(pieces, axis=1)


def bin_group(total_ref, position, velocity, weight, meta, cells):
    levels = levels_of(position, meta)
    hot = one_hot(plane_of(levels, cells), cells.rows)
    spread = spread_moments(levels[2], weight, velocity, cells)
    total_ref[...] += lax.dot_general(hot, spread, NT, preferred_element_type=f32)


def row_iota():
    return lax.broadcasted_iota(jnp.int32, (GROUP, LANES), 0)


def bin_residents(cells, first, count, meta_ref, pos_ref, vel_ref, *refs):
    total_ref = refs[-1]
    meta = [meta_ref[k] for k in range(8)]
    if first == 0:
        total_ref[...] = jnp.zeros_like(total_ref)
    else:
        total_ref[...] = refs[0][...]
    live_rows = meta[6] - first
    stride = GROUP * TWIN

    @pl.loop(0, jnp.clip((live_rows + stride - 1) // stride, 0, count // stride))
    def _(step):
        for part in range(TWIN):
            offset = pl.multiple_of(step * stride + part * GROUP, GROUP)
            rows = pl.ds(first + offset, GROUP)
            position = [pos_ref[d, rows, :] for d in range(3)]
            velocity = [vel_ref[d, rows, :] for d in range(3)]
            weight = jnp.where(row_iota() + offset < live_rows, 1.0, 0.0)
            bin_group(total_ref, position, velocity, weight, meta, cells)


def face_count(ref, first, face_rows):
    return jnp.max(ref[pl.ds(first + 6 * face_rows, GROUP), :]).astype(jnp.int32)


def take_faces(faces, face_rows, held, counts_ref, index, offset):
    for k, (ref, first) in enumerate(faces):
        count = face_count(ref, first, face_rows)
        counts_ref[index + k] = count
        for c in range(6):
            begin = first + c * face_rows
            held[c, pl.ds(offset, face_rows), :] = ref[begin : begin + face_rows, :]
        offset = offset + count
    return offset


def bin_held(held, begin, end, sums, meta, cells):
    stride = GROUP * PAIR

    @pl.loop(0, (end - begin + stride - 1) // stride)
    def _(step):
        for part in range(PAIR):
            offset = begin + step * stride + part * GROUP
            rows = pl.ds(offset, GROUP)
            comps = [held[c, rows, :] for c in range(6)]
            weight = jnp.where(row_iota() + offset < end, 1.0, 0.0)
            bin_group(sums, comps[:3], comps[3:], weight, meta, cells)


def bead_mask(chains):
    slot = row_iota() * LANES + lax.broadcasted_iota(jnp.int32, (GROUP, LANES), 1)
    return slot < CHAIN * chains


def bin_first_arrivals(cells, face_rows, places, meta_ref, *refs):
    count = len(refs) - 7
    sources = refs[:count]
    bead_pos_ref, bead_vel_ref, start_ref, order_ref, total_ref, held, counts_ref = refs[count:]
    meta = [meta_ref[k] for k in range(8)]
    total_ref[...] = start_ref[...]
    held[...] = jnp.zeros_like(held)
    faces = [(sources[which], first) for which, first in places]
    end = take_faces(faces, face_rows, held, counts_ref, 0, 0)
    weight = jnp.where(bead_mask(meta[7]), bead_mass, 0.0)
    bin_group(
        total_ref,
        [bead_pos_ref[d] for d in range(3)],
        [bead_vel_ref[d] for d in range(3)],
        weight,
        meta,
        cells,
    )
    bin_held(held, 0, end, total_ref, meta, cells)


def bin_arrivals(cells, face_rows, places, known, meta_ref, *refs):
    count = len(refs) - 10
    sources = refs[:count]
    (
        axis_ref,
        held_ref,
        known_ref,
        start_ref,
        total_ref,
        low_ref,
        high_ref,
        held,
        counts_ref,
        sums,
    ) = refs[count:]
    meta = [meta_ref[k] for k in range(8)]
    sums[...] = start_ref[...]
    held[...] = held_ref[...]
    begin = 0
    for k in range(known):
        counts_ref[k] = known_ref[k]
        begin = begin + known_ref[k]
    faces = [(sources[which], first) for which, first in places]
    end = take_faces(faces, face_rows, held, counts_ref, known, begin)
    bin_held(held, begin, end, sums, meta, cells)
    nz, inner = cells.nz, cells.inner
    lane = lax.broadcasted_iota(jnp.int32, (cells.rows, LANES), 1)
    main, rest = sums[:, :LANES], sums[:, LANES:]
    main = main + jnp.where(lane < nz, 0.0, rest)
    top = jnp.where(lane == 0, rest, rest + pltpu.roll(rest, LANES - 3, axis=1))
    total_ref[0] = main
    total_ref[1] = jnp.where(lane < 4, top, 0.0)
    axis = axis_ref[...].astype(f32)
    total_ref[1, :inner, nz : 2 * nz] = axis
    sx, sy = cells.sx, cells.sy
    low_ref[...] = jnp.zeros_like(low_ref)
    high_ref[...] = jnp.zeros_like(high_ref)
    for half in range(2):
        corner = inner + sy + 1
        low_ref[half, :sy, :] = total_ref[half, :sy, :]
        low_ref[half, sy : sy + 1, :] = total_ref[half, corner : corner + 1, :]
        high_ref[half, : sy + 1, :] = total_ref[half, inner : inner + sy + 1, :]


def add_faces_x(cells, total_ref, below_ref, above_ref, out_ref, low_ref, high_ref):
    sx, sy, inner = cells.sx, cells.sy, cells.inner
    corner = inner + sy + 1
    out_ref[...] = total_ref[...]
    low_ref[...] = jnp.zeros_like(low_ref)
    high_ref[...] = jnp.zeros_like(high_ref)
    for half in range(2):
        out_ref[half, :sy, :] += below_ref[half, :sy, :]
        out_ref[half, corner : corner + 1, :] += below_ref[half, sy : sy + 1, :]
        out_ref[half, inner : inner + sy + 1, :] += above_ref[half, : sy + 1, :]
        low_ref[half, :sx, :] = out_ref[half, pl.ds(0, sx, stride=sy), :]
        low_ref[half, sx : sx + 1, :] = out_ref[half, inner : inner + 1, :]
        high_ref[half, :sx, :] = out_ref[half, corner : corner + sx, :]
        high_ref[half, sx : sx + 1, :] = out_ref[half, inner + sy : inner + sy + 1, :]


def add_faces_y(cells, total_ref, below_ref, above_ref, out_ref, face_ref, sums):
    sx, sy, nz, inner = cells.sx, cells.sy, cells.nz, cells.inner
    corner = inner + sy + 1
    sums[...] = total_ref[...]
    for half in range(2):
        sums[half, pl.ds(0, sx, stride=sy), :] += below_ref[half, :sx, :]
        sums[half, inner : inner + 1, :] += below_ref[half, sx : sx + 1, :]
        sums[half, corner : corner + sx, :] += above_ref[half, :sx, :]
        sums[half, inner + sy : inner + sy + 1, :] += above_ref[half, sx : sx + 1, :]
    main = sums[0].T
    rest = sums[1].T
    out_ref[:LANES, :] = main
    out_ref[LANES : LANES + nz, :] = rest[nz : 2 * nz]
    out_ref[LANES + nz :, :] = jnp.zeros((GROUP, cells.rows), f32)
    out_ref[LANES + nz : LANES + nz + 4, :] = rest[:4]
    face_ref[...] = jnp.zeros_like(face_ref)
    for c in range(5):
        face_ref[c : c + 1, :] = out_ref[c * nz : c * nz + 1, :]
        face_ref[GROUP + c : GROUP + c + 1, :] = out_ref[5 * nz + c : 5 * nz + c + 1, :]


def cell_table(cells, total_ref, below_ref, above_ref, table_ref, sheet, edge):
    nz, inner, height = cells.nz, cells.inner, cells.height
    row_ids = lax.broadcasted_iota(jnp.int32, (nz, cells.rows), 0)
    parts = []
    tops = []
    for c in range(5):
        face = jnp.where(row_ids == 0, below_ref[GROUP + c : GROUP + c + 1, :], 0.0)
        parts.append(total_ref[c * nz : (c + 1) * nz, :] + face)
        tops.append(
            total_ref[5 * nz + c : 5 * nz + c + 1, :] + above_ref[c : c + 1, :]
        )
    mass = jnp.maximum(parts[0], 1.0)
    top_mass = jnp.maximum(tops[0], 1.0)
    values = [parts[4]] + [p / mass for p in parts[1:4]]
    top_values = [tops[4]] + [t / top_mass for t in tops[1:4]]
    sheet[...] = jnp.zeros_like(sheet)
    edge[...] = jnp.zeros_like(edge)
    lane = lax.broadcasted_iota(jnp.int32, (cells.extra, LANES), 1)
    spare = LANES - (cells.rows - inner)
    for c in range(4):
        base = c * height
        sheet[base : base + nz, :] = values[c][:, :inner]
        sheet[base + nz : base + nz + 1, :] = top_values[c][:, :inner]
        edge[base : base + nz, :] = jnp.concatenate(
            [values[c][:, inner:], jnp.zeros((nz, spare), f32)], axis=1
        )
        edge[base + nz : base + nz + 1, :] = jnp.concatenate(
            [top_values[c][:, inner:], jnp.zeros((1, spare), f32)], axis=1
        )
        folded = [jnp.zeros((cells.extra, LANES), f32) for _ in range(inner // LANES)]
        for m in range(cells.per):
            begin = m * cells.edges
            piece = edge[pl.ds(base + m, cells.extra, stride=cells.per), :]
            piece = pltpu.roll(piece, begin % LANES, axis=1) if begin % LANES else piece
            for t in range(inner // LANES):
                low, high = begin - t * LANES, begin + cells.edges - t * LANES
                if high > 0 and low < LANES:
                    folded[t] = jnp.where((lane >= low) & (lane < high), piece, folded[t])
        sheet[base + nz + 1 : base + nz + 1 + cells.extra, :] = jnp.concatenate(folded, axis=1)
    whole = sheet[...]
    high = whole.astype(bf16).astype(f32)
    low = (whole - high)[height:]
    table_ref[...] = jnp.concatenate([high, low], axis=0).astype(bf16)


def direction_table():
    counter = jnp.arange(LANES).astype(f32)
    height = 1.0 - (2.0 * counter + 1.0) / NAXES
    radius = jnp.sqrt(jnp.maximum(1.0 - height * height, 0.0))
    rows = jnp.stack([radius * jnp.cos(golden * counter), radius * jnp.sin(golden * counter)])
    return jnp.broadcast_to(rows[:, None], (2, GROUP, LANES))


def fold_rows(values):
    sub = lax.broadcasted_iota(jnp.int32, (GROUP, LANES), 0)
    step = GROUP // 2
    while step:
        upper = (sub & step) == 0
        half = len(values) // 2
        joined = []
        for a, b in zip(values[:half], values[half:]):
            a = a + pltpu.roll(a, GROUP - step, axis=0)
            b = b + pltpu.roll(b, step, axis=0)
            joined.append(jnp.where(upper, a, b))
        values = joined
        step //= 2
    return values[0]


def collide(position, velocity, meta, table, dirs_ref, cells):
    height = cells.height
    row, column = place_of(levels_of(position, meta), cells)
    found = lax.dot_general(
        table, one_hot(column, cells.inner), NN, preferred_element_type=f32
    )
    ids = lax.broadcasted_iota(jnp.int32, (height, LANES), 0).astype(f32)
    picked = [[] for _ in range(4)]
    for r in range(GROUP):
        block = found[:, r * LANES : (r + 1) * LANES]
        here = ids == row[r : r + 1]
        for c in range(4):
            value = block[c * height : (c + 1) * height]
            if c > 0:
                value = value + block[(3 + c) * height : (4 + c) * height]
            value = jnp.where(here, value, 0.0)
            picked[c].append(
                jnp.sum(value.reshape(height // GROUP, GROUP, LANES), axis=0)
            )
    picked = [fold_rows(p) for p in picked]
    axis, flow = picked[0].astype(jnp.int32), picked[1:]
    normal = [
        jnp.take_along_axis(dirs_ref[0], axis, axis=1, mode="promise_in_bounds"),
        jnp.take_along_axis(dirs_ref[1], axis, axis=1, mode="promise_in_bounds"),
        1.0 - (2.0 * picked[0] + 1.0) * (1.0 / NAXES),
    ]
    rel = [velocity[d] - flow[d] for d in range(3)]
    along = (1.0 - turn_cosine) * (
        normal[0] * rel[0] + normal[1] * rel[1] + normal[2] * rel[2]
    )
    result = []
    for d in range(3):
        e, f = (d + 1) % 3, (d + 2) % 3
        crossed = normal[e] * rel[f] - normal[f] * rel[e]
        result.append(
            flow[d] + (turn_cosine * rel[d] + turn_sine * crossed + along * normal[d])
        )
    return result


def passed(position, speed):
    return position - jnp.floor(position) - 0.5 + 3.0 * step_size * speed


def writing(spans, refs, sems):
    copies = []
    for k, ((first, count), (value, out)) in enumerate(zip(spans, refs)):
        copies.append(
            pltpu.make_async_copy(value, out.at[:, pl.ds(first, count), :], sems.at[k])
        )
    for copy in copies:
        copy.start()

    def finish():
        for copy in copies:
            copy.wait()

    return finish


def collide_residents(
    cells, first, count, before, meta_ref, dirs_ref, table_ref, pos_ref, vel_ref, *refs
):
    out_pos, out_vel, new_pos, new_vel, token, sems = refs[-6:]
    finish = writing([before] * 2, [(refs[0], out_pos), (refs[1], out_vel)], sems) if before else None
    token[...] = jnp.zeros_like(token)
    meta = [meta_ref[k] for k in range(8)]
    table = table_ref[...]
    live_rows = meta[6] - first
    new_pos[...] = jnp.zeros_like(new_pos)
    new_vel[...] = jnp.zeros_like(new_vel)
    stride = GROUP * TWIN

    @pl.loop(0, jnp.clip((live_rows + stride - 1) // stride, 0, count // stride))
    def _(step):
        for part in range(TWIN):
            offset = pl.multiple_of(step * stride + part * GROUP, GROUP)
            rows = pl.ds(first + offset, GROUP)
            position = [pos_ref[d, rows, :] for d in range(3)]
            velocity = [vel_ref[d, rows, :] for d in range(3)]
            live = row_iota() + offset < live_rows
            speed = collide(position, velocity, meta, table, dirs_ref, cells)
            rows = pl.ds(offset, GROUP)
            for d in range(3):
                new_vel[d, rows, :] = jnp.where(live, speed[d], 0.0)
                new_pos[d, rows, :] = jnp.where(live, passed(position[d], speed[d]), 0.0)

    if finish:
        finish()


def collide_held(
    cells, first, count, many, before, meta_ref, dirs_ref, table_ref, held, counts_ref, *refs
):
    if before:
        out_pos, out_vel, out_ref, token, sems = refs[-5:]
        finish = writing([before] * 2, [(refs[0], out_pos), (refs[1], out_vel)], sems)
    else:
        out_ref, token = refs[-2:]
        finish = None
    token[...] = jnp.zeros_like(token)
    meta = [meta_ref[k] for k in range(8)]
    table = table_ref[...]
    out_ref[...] = jnp.zeros_like(out_ref)
    end = sum([counts_ref[k] for k in range(many)], jnp.int32(0)) - first
    stride = GROUP * TRIO

    @pl.loop(0, jnp.clip((end + stride - 1) // stride, 0, count // stride))
    def _(step):
        for part in range(TRIO):
            offset = pl.multiple_of(step * stride + part * GROUP, GROUP)
            comps = [held[c, pl.ds(first + offset, GROUP), :] for c in range(6)]
            speed = collide(comps[:3], comps[3:], meta, table, dirs_ref, cells)
            for d in range(3):
                out_ref[d, pl.ds(offset, GROUP), :] = speed[d]
                out_ref[3 + d, pl.ds(offset, GROUP), :] = passed(comps[d], speed[d])

    if finish:
        finish()


def place_arrivals(face_rows, sequence, counts_ref, *refs):
    pieces = refs[:-4]
    new_pos, new_vel, token, packed = refs[-4:]
    token[...] = jnp.zeros_like(token)
    packed[...] = jnp.zeros_like(packed)
    at = 0
    for piece in pieces:
        packed[:, at : at + piece.shape[1], :] = piece[...]
        at += piece.shape[1]
    rows = lax.broadcasted_iota(jnp.int32, (face_rows, LANES), 0)
    offset = 0
    for k, face in enumerate(sequence):
        count = counts_ref[k]
        place = slice(face * face_rows, (face + 1) * face_rows)
        for d in range(3):
            speed = packed[d, pl.ds(offset, face_rows), :]
            moved = packed[3 + d, pl.ds(offset, face_rows), :]
            new_vel[d, place, :] = jnp.where(rows < count, speed, 0.0)
            new_pos[d, place, :] = jnp.where(rows < count, moved, 0.0)
        offset = offset + count


def pack_inputs(
    meta_ref,
    pos_ref,
    vel_ref,
    bead_pos_ref,
    bead_vel_ref,
    bond_ref,
    order_ref,
    start_ref,
    joins_ref,
    block_ref,
    rows_pos_ref,
    rows_vel_ref,
    *refs,
):
    out_refs, (held_pos, held_vel, sems) = refs[:6], refs[6:]
    copies = [(bead_pos_ref, held_pos), (bead_vel_ref, held_vel)]
    for face, out_ref in enumerate(out_refs):
        copies.append((pos_ref.at[:, face], out_ref.at[0:3]))
        copies.append((vel_ref.at[:, face], out_ref.at[3:6]))
    copies = [pltpu.make_async_copy(a, b, sems.at[k]) for k, (a, b) in enumerate(copies)]
    for copy in copies:
        copy.start()
    for face, out_ref in enumerate(out_refs):
        out_ref[6] = jnp.full(out_ref.shape[1:], meta_ref[8 + face], jnp.int32).astype(f32)
    slots = start_ref.shape[1]
    start_ref[...] = jnp.zeros_like(start_ref)
    rows_pos_ref[...] = jnp.zeros_like(rows_pos_ref)
    rows_vel_ref[...] = jnp.zeros_like(rows_vel_ref)
    for copy in copies:
        copy.wait()
    for d in range(3):
        for k in range(slots // LANES):
            lanes = slice(k * LANES, (k + 1) * LANES)
            start_ref[d : d + 1, lanes] = held_pos[d, k : k + 1, :]
            rows_pos_ref[d, k : k + 1, :] = held_pos[d, k : k + 1, :]
            rows_vel_ref[d, k : k + 1, :] = held_vel[d, k : k + 1, :]
    bond_slots = bond_ref.shape[-1]
    bonds = [bond_ref[k, 0, 0, :, :].astype(f32) for k in range(2)]
    ends = jnp.concatenate(bonds + [jnp.zeros((GROUP - 2, bond_slots), f32)], axis=0)
    room = joins_ref.shape[0] - bond_slots
    ends = jnp.concatenate([ends, jnp.zeros((GROUP, room), f32)], axis=1).T if room else ends.T
    slot_ids = lax.broadcasted_iota(jnp.int32, joins_ref.shape, 1).astype(f32)
    bond_ids = lax.broadcasted_iota(jnp.int32, joins_ref.shape, 0)
    joins = jnp.where(slot_ids == ends[:, 0:1], 1.0, 0.0)
    joins = joins - jnp.where(slot_ids == ends[:, 1:2], 1.0, 0.0)
    live_bonds = jnp.minimum((CHAIN - 1) * meta_ref[7], bond_slots)
    joins_ref[...] = jnp.where(bond_ids < live_bonds, joins, 0.0).astype(bf16)
    start = start_ref[...]
    whole = payload(start, slot_live(slots, meta_ref[7], GROUP))
    for k in range(slots // LANES):
        block_ref[k * GROUP : (k + 1) * GROUP, :] = whole[:, k * LANES : (k + 1) * LANES]


def stack_rows(parts, *refs):
    out_ref = refs[-1]
    at = 0
    for which, begin, count in parts:
        out_ref[at : at + count, :] = refs[which][begin : begin + count, :]
        at += count


def slot_live(slots, chains, rows):
    return lax.broadcasted_iota(jnp.int32, (rows, slots), 1) < CHAIN * chains


def payload(position, live):
    slots = position.shape[1]
    row_ids = lax.broadcasted_iota(jnp.int32, (GROUP, slots), 0)
    flag = jnp.where(live, 1.0, 0.0)
    return jnp.where(row_ids == 3, flag, jnp.where(row_ids < 3, position, 0.0))


def thirds_of(value):
    high = value.astype(bf16)
    rest = value - high.astype(f32)
    middle = rest.astype(bf16)
    low = (rest - middle.astype(f32)).astype(bf16)
    return jnp.concatenate([high.astype(f32), middle.astype(f32), low.astype(f32)], axis=0).astype(
        bf16
    )


def summed_thirds(value):
    return value[:GROUP] + (value[GROUP : 2 * GROUP] + value[2 * GROUP :])


def forces(own, chains, counts, joins_ref, blocks, centre, lengths, mine_ref, packed, push):
    slots = own.shape[1]
    row_ids = lax.broadcasted_iota(jnp.int32, (GROUP, slots), 0)
    mid = jnp.zeros((GROUP, slots), f32)
    length = jnp.ones((GROUP, slots), f32)
    for d in range(3):
        mid = jnp.where(row_ids == d, centre[d], mid)
        length = jnp.where(row_ids == d, lengths[d], length)
    live = slot_live(slots, chains, GROUP)
    local = jnp.where(live & (row_ids < 3), own - mid, 0.0)
    columns = jnp.where(live, local, far_own).T
    for d in range(3):
        mine_ref[d] = jnp.broadcast_to(columns[:, d : d + 1], (slots, LANES))

    joins = joins_ref[...]
    stretch = summed_thirds(
        lax.dot_general(thirds_of(local), joins, NT, preferred_element_type=f32)
    )
    square = (
        stretch[0:1] * stretch[0:1] + stretch[1:2] * stretch[1:2] + stretch[2:3] * stretch[2:3]
    )
    bond_live = (
        lax.broadcasted_iota(jnp.int32, (1, joins.shape[0]), 1) < (CHAIN - 1) * chains
    )
    pull = jnp.where(bond_live, -spring / (1.0 - square / reach_square), 0.0) * stretch
    bond = summed_thirds(
        lax.dot_general(thirds_of(pull), joins, NN, preferred_element_type=f32)
    )

    packed[...] = jnp.full(packed.shape, far_ghost, f32)
    lane = lax.broadcasted_iota(jnp.int32, (GROUP, LANES), 1)
    tiles = slots // LANES
    offset = jnp.int32(0)
    index = 0
    for ref in blocks:
        for b in range(ref.shape[0] // GROUP):
            near = ref[b * GROUP : (b + 1) * GROUP, :] - mid
            near = near - length * jnp.floor(near * (1.0 / length) + 0.5)
            tile, turn = offset // LANES, offset % LANES
            turned = [
                pltpu.roll(near[:, k * LANES : (k + 1) * LANES], turn, axis=1)
                for k in range(tiles)
            ]
            for k in range(tiles + 1):
                if k == 0:
                    value = turned[0]
                elif k == tiles:
                    value = turned[-1]
                else:
                    value = jnp.where(lane < turn, turned[k - 1], turned[k])
                place = (tile + k) * LANES + lane
                taken = (place >= offset) & (place < offset + counts[index])
                packed[tile + k] = jnp.where(taken, value, packed[tile + k])
            offset = offset + counts[index]
            index += 1

    push[...] = jnp.zeros_like(push)
    chunk = 64
    steps = (offset + 2 * LANES - 1) // (2 * LANES)

    @pl.loop(0, (CHAIN * chains + chunk - 1) // chunk)
    def _(part):
        rows = pl.ds(pl.multiple_of(part * chunk, chunk), chunk)
        mine = [mine_ref[d, rows, :] for d in range(3)]

        def add_tiles(step, total):
            for k in range(2):
                other = packed[2 * step + k]
                differ = [mine[d] - other[d : d + 1] for d in range(3)]
                square = (
                    differ[0] * differ[0] + differ[1] * differ[1] + differ[2] * differ[2]
                )
                inside = (square < cut_square) & (square > 0.25)
                inverse = 1.0 / jnp.where(inside, square, 1e30)
                sixth = inverse * inverse * inverse
                weight = (sixth * inverse) * (48.0 * sixth - 24.0)
                total = tuple(total[d] + weight * differ[d] for d in range(3))
            return total

        total = lax.fori_loop(
            0, steps, add_tiles, tuple(jnp.zeros((chunk, LANES), f32) for _ in range(3))
        )
        for d in range(3):
            push[d, rows, :] = total[d]

    pair = jnp.zeros((GROUP, slots), f32)
    for d in range(3):
        pair = jnp.where(row_ids == d, jnp.sum(push[d].T, axis=0, keepdims=True), pair)
    return pair + bond


def force_scratch(slots, blocks):
    tiles = -(-(blocks * slots // LANES + 2) // 2) * 2
    return [
        pltpu.VMEM((3, slots, LANES), f32),
        pltpu.VMEM((tiles, GROUP, LANES), f32),
        pltpu.VMEM((3, slots, LANES), f32),
    ]


def centre_of(meta, sizes):
    return [meta[3 + d].astype(f32) + 0.5 * sizes[d] for d in range(3)]


def first_forces(sizes, lengths, sources, meta_ref, start_ref, joins_ref, *refs):
    blocks, (push_ref, counts_ref), scratch = (
        refs[:sources],
        refs[sources : sources + 2],
        refs[sources + 2 :],
    )
    meta = [meta_ref[k] for k in range(8)]
    counts = []
    for ref in blocks:
        for b in range(ref.shape[0] // GROUP):
            live = ref[b * GROUP + 3 : b * GROUP + 4, :]
            counts.append(jnp.sum(live).astype(jnp.int32))
    for k, count in enumerate(counts):
        counts_ref[k] = count
    push_ref[...] = forces(
        start_ref[...],
        meta[7],
        counts,
        joins_ref,
        blocks,
        centre_of(meta, sizes),
        lengths,
        *scratch,
    )


def finish_cells(
    cells,
    meta_ref,
    dirs_ref,
    total_ref,
    below_ref,
    above_ref,
    bead_pos_ref,
    bead_vel_ref,
    start_ref,
    push_ref,
    table_ref,
    speed_ref,
    moved_ref,
    pay_ref,
    sheet,
    edge,
):
    meta = [meta_ref[k] for k in range(8)]
    cell_table(cells, total_ref, below_ref, above_ref, table_ref, sheet, edge)
    fresh = collide(
        [bead_pos_ref[d] for d in range(3)],
        [bead_vel_ref[d] for d in range(3)],
        meta,
        table_ref[...],
        dirs_ref,
        cells,
    )
    start = start_ref[...]
    slots = start.shape[1]
    row_ids = lax.broadcasted_iota(jnp.int32, (GROUP, slots), 0)
    speed = jnp.zeros((GROUP, slots), f32)
    for d in range(3):
        line = jnp.concatenate([fresh[d][k : k + 1] for k in range(slots // LANES)], axis=1)
        speed = jnp.where(row_ids == d, line, speed)
    speed = speed + half_kick * push_ref[...]
    moved = step_size * speed
    live = slot_live(slots, meta[7], GROUP)
    speed_ref[...] = speed
    moved_ref[...] = moved
    pay_ref[...] = payload(start + moved, live)


def substep(
    sizes, lengths, sources, last, meta_ref, start_ref, joins_ref, counts_ref, speed_ref, moved_ref, *refs
):
    blocks, rest = refs[:sources], refs[sources:]
    if last:
        new_pos, new_vel, _, _, *outs, sems, a, b, c = rest
        finish = writing([last] * 2, [(new_pos, outs[2]), (new_vel, outs[3])], sems)
        scratch = (a, b, c)
    else:
        _, *outs, a, b, c = rest
        scratch = (a, b, c)
    meta = [meta_ref[k] for k in range(8)]
    counts = [
        counts_ref[k] for k in range(sum(ref.shape[0] // GROUP for ref in blocks))
    ]
    start = start_ref[...]
    moved = moved_ref[...]
    push = forces(
        start + moved,
        meta[7],
        counts,
        joins_ref,
        blocks,
        centre_of(meta, sizes),
        lengths,
        *scratch,
    )
    live = slot_live(start.shape[1], meta[7], GROUP)
    speed = speed_ref[...] + half_kick * push
    if last:
        for d in range(3):
            outs[0][d, 0, 0, :, :] = jnp.where(live, speed, 0.0)[d : d + 1]
            outs[1][d, 0, 0, :, :] = jnp.where(live, moved, 0.0)[d : d + 1]
        finish()
        return
    speed = speed + half_kick * push
    moved = moved + step_size * speed
    outs[0][...] = speed
    outs[1][...] = moved
    outs[2][...] = payload(start + moved, live)


def neighbours(value, axis):
    peers = lax.axis_size(axis)
    if peers == 2:
        return [moved_along(value, axis, 1)]
    return [moved_along(value, axis, 1), moved_along(value, axis, -1)]


def stacked(parts, operands, order=()):
    rows = sum(count for _, _, count in parts)
    width = operands[0].shape[1]
    return pl.pallas_call(
        functools.partial(stack_rows, tuple(parts)),
        out_shape=like(rows, width),
        in_specs=[vmem()] * len(operands) + [pl.BlockSpec(memory_space=pl.ANY)] * len(order),
        out_specs=vmem(),
        compiler_params=params(),
        name="stack_rows",
    )(*operands, *order)


def whole_rows(operands):
    return [(k, 0, value.shape[0]) for k, value in enumerate(operands)]


def halo(block, pieces):
    parts = [block] + neighbours(block, "gz")
    row = stacked(whole_rows(parts), parts, [pieces[0]()])
    parts = [row] + neighbours(row, "gy")
    plane = stacked(whole_rows(parts), parts, [pieces[1]()])
    sides = neighbours(plane, "gx")
    return [plane] + sides, pieces[2]()


def like(*shape, dtype=f32):
    return jax.ShapeDtypeStruct(shape, dtype)


def shards(
    sol_pos,
    sol_vel,
    sol_rows,
    mig_pos,
    mig_vel,
    mig_rows,
    bead_pos,
    bead_vel,
    bead_chains,
    bond_list,
    cell_axis,
    shift,
):
    sizes = cell_axis.shape
    cells = Cells(*sizes)
    names = ("gx", "gy", "gz")
    lengths = tuple(float(sizes[d] * lax.axis_size(names[d])) for d in range(3))
    slots_here = sol_pos.shape[-1]
    buffer_slots = mig_pos.shape[-1]
    bead_slots = bead_pos.shape[-1]
    bond_slots = bond_list.shape[-1]
    rows_here = slots_here // LANES
    face_rows = buffer_slots // LANES
    rows_all = rows_here + 6 * face_rows
    anchor = jnp.stack([lax.axis_index(names[d]) * sizes[d] for d in range(3)])
    meta = jnp.concatenate(
        [
            shift,
            anchor.astype(jnp.int32),
            sol_rows.reshape(1),
            bead_chains.reshape(1),
            mig_rows.reshape(6),
        ]
    )
    dirs = direction_table()
    position = sol_pos.reshape(3, rows_here, LANES)
    velocity = sol_vel.reshape(3, rows_here, LANES)

    any_spec = pl.BlockSpec(memory_space=pl.ANY)
    thirds = 3
    count = rows_here // thirds
    axis_rows = cell_axis.reshape(cells.inner, sizes[2])

    def bin_piece(piece, earlier, order):
        return pl.pallas_call(
            functools.partial(bin_residents, cells, piece * count, count),
            out_shape=like(cells.rows, 2 * LANES),
            in_specs=[smem()]
            + [vmem()] * (2 + len(earlier))
            + [any_spec] * len(order),
            out_specs=vmem(),
            compiler_params=params(),
            name=f"bin_residents_{piece}",
        )(meta, position, velocity, *earlier, *order)

    totals = bin_piece(0, [], [])
    face_height = 7 * face_rows
    bead_shape = like(GROUP, bead_slots)
    tiles = bead_slots // LANES
    rows_shape = like(3, GROUP, LANES)
    bond_rows = -(-bond_slots // LANES) * LANES
    start, joins, block, bead_rows_pos, bead_rows_vel, *packed = pl.pallas_call(
        pack_inputs,
        out_shape=[
            bead_shape,
            like(bond_rows, bead_slots, dtype=bf16),
            like(tiles * GROUP, LANES),
            rows_shape,
            rows_shape,
        ]
        + [like(7, face_rows, LANES)] * 6,
        in_specs=[smem()]
        + [pl.BlockSpec(memory_space=pltpu.HBM)] * 4
        + [vmem(), any_spec],
        out_specs=[vmem()] * 11,
        scratch_shapes=[pltpu.VMEM((3, tiles, LANES), f32)] * 2
        + [pltpu.SemaphoreType.DMA((14,))],
        compiler_params=params(vmem_most),
        name="pack_inputs",
    )(
        meta,
        mig_pos.reshape(3, 6, face_rows, LANES),
        mig_vel.reshape(3, 6, face_rows, LANES),
        bead_pos.reshape(3, tiles, LANES),
        bead_vel.reshape(3, tiles, LANES),
        bond_list,
        totals,
    )
    packed = [value.reshape(face_height, LANES) for value in packed]

    def swap(axis, low, high, body):
        if lax.axis_size(axis) == 2:
            both = [packed[low], packed[high], body]
            came = moved_along(stacked(whole_rows(both), both), axis, 1)
            return [came], [(0, face_height), (0, 0)], [(0, 2 * face_height)]
        up = stacked(whole_rows([packed[high], body]), [packed[high], body])
        down = stacked(whole_rows([packed[low], body]), [packed[low], body])
        came = [moved_along(up, axis, 1), moved_along(down, axis, -1)]
        return came, [(0, 0), (1, 0)], [(0, face_height), (1, face_height)]

    arriving, spots, blocks = [], [None] * 6, block
    for piece, (axis, low) in enumerate((("gz", 4), ("gy", 2), ("gx", 0))):
        came, places, bodies = swap(axis, low, low + 1, blocks)
        for k, (which, at) in enumerate(places):
            spots[low + k] = (len(arriving) + which, at)
        arriving += came
        height = blocks.shape[0]
        if axis != "gx":
            totals = bin_piece(piece + 1, [totals], [blocks])
            parts = [(0, 0, height)] + [(1 + w, at, height) for w, at in bodies]
            blocks = stacked(parts, [blocks] + came, [totals])
        else:
            around = [blocks] + [
                stacked([(0, at, height)], [came[w]]) for w, at in bodies
            ]

    def as_blocks(value):
        n = value.shape[0] // (GROUP * tiles)
        return (
            value.reshape(n, tiles, GROUP, LANES)
            .transpose(0, 2, 1, 3)
            .reshape(n * GROUP, bead_slots)
        )

    sequence = (4, 5, 2, 3, 0, 1)
    early, late = sequence[:4], sequence[4:]
    sooner = max(spots[face][0] for face in early) + 1
    held_rows = -(-6 * face_rows // 32) * 32
    held_shape = like(6, held_rows, LANES)
    totals, held, counted = pl.pallas_call(
        functools.partial(
            bin_first_arrivals, cells, face_rows, [spots[face] for face in early]
        ),
        out_shape=[like(cells.rows, 2 * LANES), held_shape, like(4, dtype=jnp.int32)],
        in_specs=[smem()] + [vmem()] * (sooner + 3) + [any_spec],
        out_specs=[vmem(), vmem(), smem()],
        compiler_params=params(),
        name="bin_first_arrivals",
    )(meta, *arriving[:sooner], bead_rows_pos, bead_rows_vel, totals, blocks)

    face_x = like(2, -(-(sizes[1] + 1) // GROUP) * GROUP, LANES)
    face_y = like(2, -(-(sizes[0] + 1) // GROUP) * GROUP, LANES)
    later = arriving[sooner:]
    totals, low, high, held, counted = pl.pallas_call(
        functools.partial(
            bin_arrivals,
            cells,
            face_rows,
            [(spots[face][0] - sooner, spots[face][1]) for face in late],
            len(early),
        ),
        out_shape=[
            like(2, cells.rows, LANES),
            face_x,
            face_x,
            held_shape,
            like(6, dtype=jnp.int32),
        ],
        in_specs=[smem()] + [vmem()] * (len(later) + 2) + [smem(), vmem()],
        out_specs=[vmem()] * 4 + [smem()],
        scratch_shapes=[pltpu.VMEM((cells.rows, 2 * LANES), f32)],
        compiler_params=params(),
        name="bin_arrivals",
    )(meta, *later, axis_rows, held, counted, totals)

    around = [as_blocks(value) for value in around]
    many = sum(value.shape[0] // GROUP for value in around)
    push, counts = pl.pallas_call(
        functools.partial(first_forces, sizes, lengths, len(around)),
        out_shape=[bead_shape, like(many, dtype=jnp.int32)],
        in_specs=[smem()] + [vmem()] * (2 + len(around)),
        out_specs=[vmem(), smem()],
        scratch_shapes=force_scratch(bead_slots, many),
        compiler_params=params(),
        name="first_forces",
    )(meta, start, joins, *around)

    below, above = moved_along(high, "gx", 1), moved_along(low, "gx", -1)
    totals, low, high = pl.pallas_call(
        functools.partial(add_faces_x, cells),
        out_shape=[like(2, cells.rows, LANES), face_y, face_y],
        in_specs=[vmem()] * 3,
        out_specs=[vmem()] * 3,
        compiler_params=params(),
        name="add_faces_x",
    )(totals, below, above)
    below, above = moved_along(high, "gy", 1), moved_along(low, "gy", -1)
    totals, faces = pl.pallas_call(
        functools.partial(add_faces_y, cells),
        out_shape=[like(LANES + cells.nz + GROUP, cells.rows), like(2 * GROUP, cells.rows)],
        in_specs=[vmem()] * 3,
        out_specs=[vmem()] * 2,
        scratch_shapes=[pltpu.VMEM((2, cells.rows, LANES), f32)],
        compiler_params=params(),
        name="add_faces_y",
    )(totals, below, above)
    sides = neighbours(faces, "gz")
    below, above = sides[0], sides[-1]

    table, speed, moved, pay = pl.pallas_call(
        functools.partial(finish_cells, cells),
        out_shape=[
            like(7 * cells.height, cells.inner, dtype=bf16),
            bead_shape,
            bead_shape,
            bead_shape,
        ],
        in_specs=[smem()] + [vmem()] * 8,
        out_specs=[vmem()] * 4,
        scratch_shapes=[
            pltpu.VMEM((4 * cells.height, cells.inner), f32),
            pltpu.VMEM((4 * cells.height, LANES), f32),
        ],
        compiler_params=params(),
        name="finish_cells",
    )(meta, dirs, totals, below, above, bead_rows_pos, bead_rows_vel, start, push)

    solvent_shape = like(3, rows_all, LANES)
    cuts = 6
    span = rows_here // cuts

    held_span = 2 * face_rows
    written, pending, packed_results, tokens = [], [], [], []

    def collide_piece(piece):
        token = like(GROUP, LANES)
        whole = [solvent_shape] * 2
        write_sems = [pltpu.SemaphoreType.DMA((2,))]
        if piece < cuts:
            before = ((piece - 1) * span, span) if piece else None
            extra = pending + written
            at = 5 + len(pending)
            *outs, order = pl.pallas_call(
                functools.partial(collide_residents, cells, piece * span, span, before),
                out_shape=whole + [like(3, span, LANES)] * 2 + [token],
                in_specs=[smem()] + [vmem()] * (4 + len(pending)) + [any_spec] * len(written),
                out_specs=[any_spec] * 2 + [vmem()] * 3,
                scratch_shapes=write_sems,
                input_output_aliases={at: 0, at + 1: 1} if written else {},
                compiler_params=params(),
                name=f"collide_{piece}",
            )(meta, dirs, table, position, velocity, *extra)
            written[:], pending[:] = outs[:2], outs[2:]
            tokens.append(order)
            return order
        before = ((cuts - 1) * span, span) if piece == cuts else None
        extra = pending + written if before else [tokens[-1]]
        outs = pl.pallas_call(
            functools.partial(
                collide_held, cells, (piece - cuts) * held_span, held_span, 6, before
            ),
            out_shape=(whole if before else []) + [like(6, held_span, LANES), token],
            in_specs=[smem()]
            + [vmem()] * 3
            + [smem()]
            + ([vmem()] * 2 + [any_spec] * 2 if before else [any_spec]),
            out_specs=([any_spec] * 2 if before else []) + [vmem()] * 2,
            scratch_shapes=write_sems if before else [],
            input_output_aliases={7: 0, 8: 1} if before else {},
            compiler_params=params(),
            name=f"collide_{piece}",
        )(meta, dirs, table, held, counted, *extra)
        if before:
            written[:] = outs[:2]
        packed_results.append(outs[-2])
        tokens.append(outs[-1])
        if piece < cuts + 2:
            return outs[-1]
        *pending[:], order = pl.pallas_call(
            functools.partial(place_arrivals, face_rows, sequence),
            out_shape=[like(3, 6 * face_rows, LANES)] * 2 + [token],
            in_specs=[smem()] + [vmem()] * 3,
            out_specs=[vmem()] * 3,
            scratch_shapes=[pltpu.VMEM((6, 7 * face_rows, LANES), f32)],
            compiler_params=params(),
            name="place_arrivals",
        )(counted, *packed_results)
        return order

    for step in range(3):
        last = step == 2
        thunks = [functools.partial(collide_piece, 3 * step + k) for k in range(3)]
        ghosts, order = halo(pay, thunks)
        final = like(3, 1, 1, 1, bead_slots)
        tail = pending + written if last else [order]
        at = 6 + len(ghosts) + 2
        outcome = pl.pallas_call(
            functools.partial(
                substep,
                sizes,
                lengths,
                len(ghosts),
                (rows_here, 6 * face_rows) if last else None,
            ),
            out_shape=[final] * 2 + [solvent_shape] * 2 if last else [bead_shape] * 3,
            in_specs=[smem(), vmem(), vmem(), smem()]
            + [vmem()] * (2 + len(ghosts))
            + ([vmem()] * 2 + [any_spec] * 2 if last else [any_spec]),
            out_specs=[vmem()] * 2 + [any_spec] * 2 if last else [vmem()] * 3,
            scratch_shapes=([pltpu.SemaphoreType.DMA((2,))] if last else [])
            + force_scratch(bead_slots, many),
            input_output_aliases={at: 2, at + 1: 3} if last else {},
            compiler_params=params(),
            name=f"substep_{step}",
        )(meta, start, joins, counts, speed, moved, *ghosts, *tail)
        if last:
            written[:] = outcome[2:]
        speed, moved = outcome[:2]
        pay = outcome[-1]

    count_solvent = rows_all * LANES
    return (
        written[0].reshape(3, 1, 1, 1, count_solvent),
        written[1].reshape(3, 1, 1, 1, count_solvent),
        moved,
        speed,
    )


def solution(mesh):
    return jax.shard_map(
        shards,
        mesh=mesh,
        in_specs=(
            P(None, "gx", "gy", "gz", None),
            P(None, "gx", "gy", "gz", None),
            P("gx", "gy", "gz"),
            P(None, "gx", "gy", "gz", None, None),
            P(None, "gx", "gy", "gz", None, None),
            P("gx", "gy", "gz", None),
            P(None, "gx", "gy", "gz", None),
            P(None, "gx", "gy", "gz", None),
            P("gx", "gy", "gz"),
            P(None, "gx", "gy", "gz", None),
            P("gx", "gy", "gz"),
            P(),
        ),
        out_specs=(
            P(None, "gx", "gy", "gz", None),
            P(None, "gx", "gy", "gz", None),
            P(None, "gx", "gy", "gz", None),
            P(None, "gx", "gy", "gz", None),
        ),
        check_vma=False,
    )
```

```python
import functools
import math

import jax
import jax.numpy as jnp
from jax import lax
from jax.experimental import pallas as pl
from jax.experimental.pallas import tpu as pltpu
from jax.sharding import PartitionSpec as P

UNITS = 16
NAXES = 32
CHAIN = 8
LANES = 128
GROUP = 8
TWIN = 4
PAIR = 2
TRIO = 3

bead_mass = 5.0
step_size = 0.02
spring = 30.0
reach_square = 2.25
cut_square = 2.0 ** (1.0 / 3.0)
turn_cosine = math.cos(130.0 * math.pi / 180.0)
turn_sine = math.sin(130.0 * math.pi / 180.0)
golden = math.pi * (3.0 - math.sqrt(5.0))
half_kick = 0.5 * step_size / bead_mass
far_own = 3000.0
far_ghost = 9000.0
vmem_limit = 48 * 1024 * 1024
vmem_most = 48 * 1024 * 1024
NT = (((1,), (1,)), ((), ()))
NN = (((1,), (0,)), ((), ()))
exact = lax.Precision.HIGHEST
f32 = jnp.float32
bf16 = jnp.bfloat16


def params(limit=vmem_limit):
    return pltpu.CompilerParams(vmem_limit_bytes=limit)


def vmem():
    return pl.BlockSpec(memory_space=pltpu.VMEM)


def smem():
    return pl.BlockSpec(memory_space=pltpu.SMEM)


def moved_along(value, axis, by):
    peers = lax.axis_size(axis)
    return lax.ppermute(value, axis, [(i, (i + by) % peers) for i in range(peers)])


class Cells:
    def __init__(self, size_x, size_y, size_z):
        self.sx, self.sy, self.nz = size_x, size_y, size_z
        self.inner = size_x * size_y
        self.edges = size_x + size_y + 1
        self.rows = -(-(self.inner + self.edges) // 16) * 16
        self.middle = self.rows // 2
        self.per = self.inner // self.edges
        self.depths = size_z + 1
        self.extra = -(-self.depths // self.per)
        self.height = -(-(self.depths + self.extra) // GROUP) * GROUP


def levels_of(position, meta):
    return [
        jnp.floor(jnp.floor(position[d] * UNITS + meta[d].astype(f32)) * (1.0 / UNITS))
        - meta[3 + d].astype(f32)
        for d in range(3)
    ]


def edge_of(levels, cells):
    outer = (levels[0] == cells.sx) | (levels[1] == cells.sy)
    return outer, jnp.where(levels[0] == cells.sx, levels[1], cells.sy + 1 + levels[0])


def plane_of(levels, cells):
    outer, edge = edge_of(levels, cells)
    return jnp.where(outer, cells.inner + edge, levels[0] * cells.sy + levels[1])


def place_of(levels, cells):
    outer, edge = edge_of(levels, cells)
    fold = jnp.floor((levels[2] + 0.5) * (1.0 / cells.per))
    row = jnp.where(outer, cells.depths + fold, levels[2])
    column = jnp.where(
        outer,
        (levels[2] - fold * cells.per) * cells.edges + edge,
        levels[0] * cells.sy + levels[1],
    )
    return row, column


def wide(row):
    return jnp.broadcast_to(row, (16, LANES)).astype(bf16)


def one_hot_rows(rows, height):
    middle = height // 2
    ids = lax.broadcasted_iota(jnp.int32, (height, LANES), 0) - middle
    ids = ids.astype(f32).astype(bf16).reshape(height // 16, 16, LANES)
    one, zero = jnp.ones((), bf16), jnp.zeros((), bf16)
    pieces = [
        jnp.where(ids == wide(row - middle)[None], one, zero).reshape(height, LANES)
        for row in rows
    ]
    return jnp.concatenate(pieces, axis=1)


def one_hot(column, height):
    return one_hot_rows([column[r : r + 1] for r in range(column.shape[0])], height)


def split(value):
    high = value.astype(bf16).astype(f32)
    return high, value - high


def spread_moments(depth, weight, velocity, cells):
    nz = cells.nz
    ids = lax.broadcasted_iota(jnp.int32, (nz, LANES), 0).astype(f32).astype(bf16)
    ids = ids.reshape(nz // 16, 16, LANES)
    row_ids = lax.broadcasted_iota(jnp.int32, (16, LANES), 0).astype(f32).astype(bf16)
    zero = jnp.zeros((), bf16)
    parts = [split(weight * velocity[d]) for d in range(3)]
    channels = [weight] + [p[0] for p in parts] + [p[1] for p in parts]
    pieces = []
    for r in range(depth.shape[0]):
        at = wide(depth[r : r + 1])
        here = ids == at[None]
        values = [wide(c[r : r + 1]) for c in channels]
        tiles = [jnp.where(here, v[None], zero).reshape(nz, LANES) for v in values]
        top = jnp.zeros((16, LANES), bf16)
        for c, v in enumerate(values):
            top = jnp.where(row_ids == c, v, top)
        top = jnp.where(at == nz, top, zero)
        pieces.append(
            jnp.concatenate(
                tiles[:4] + [top, jnp.zeros((nz - 16, LANES), bf16)] + tiles[4:], axis=0
            )
        )
    return jnp.concatenate(pieces, axis=1)


def bin_group(total_ref, position, velocity, weight, meta, cells):
    levels = levels_of(position, meta)
    hot = one_hot(plane_of(levels, cells), cells.rows)
    spread = spread_moments(levels[2], weight, velocity, cells)
    total_ref[...] += lax.dot_general(hot, spread, NT, preferred_element_type=f32)


def row_iota():
    return lax.broadcasted_iota(jnp.int32, (GROUP, LANES), 0)


def bin_residents(cells, first, count, meta_ref, pos_ref, vel_ref, *refs):
    total_ref = refs[-1]
    meta = [meta_ref[k] for k in range(8)]
    if first == 0:
        total_ref[...] = jnp.zeros_like(total_ref)
    else:
        total_ref[...] = refs[0][...]
    live_rows = meta[6] - first
    stride = GROUP * TWIN

    @pl.loop(0, jnp.clip((live_rows + stride - 1) // stride, 0, count // stride))
    def _(step):
        for part in range(TWIN):
            offset = pl.multiple_of(step * stride + part * GROUP, GROUP)
            rows = pl.ds(first + offset, GROUP)
            position = [pos_ref[d, rows, :] for d in range(3)]
            velocity = [vel_ref[d, rows, :] for d in range(3)]
            weight = jnp.where(row_iota() + offset < live_rows, 1.0, 0.0)
            bin_group(total_ref, position, velocity, weight, meta, cells)


def face_count(ref, first, face_rows):
    return jnp.max(ref[pl.ds(first + 6 * face_rows, GROUP), :]).astype(jnp.int32)


def take_faces(faces, face_rows, held, counts_ref, index, offset):
    for k, (ref, first) in enumerate(faces):
        count = face_count(ref, first, face_rows)
        counts_ref[index + k] = count
        for c in range(6):
            begin = first + c * face_rows
            held[c, pl.ds(offset, face_rows), :] = ref[begin : begin + face_rows, :]
        offset = offset + count
    return offset


def bin_held(held, begin, end, sums, meta, cells):
    stride = GROUP * PAIR

    @pl.loop(0, (end - begin + stride - 1) // stride)
    def _(step):
        for part in range(PAIR):
            offset = begin + step * stride + part * GROUP
            rows = pl.ds(offset, GROUP)
            comps = [held[c, rows, :] for c in range(6)]
            weight = jnp.where(row_iota() + offset < end, 1.0, 0.0)
            bin_group(sums, comps[:3], comps[3:], weight, meta, cells)


def bead_mask(chains):
    slot = row_iota() * LANES + lax.broadcasted_iota(jnp.int32, (GROUP, LANES), 1)
    return slot < CHAIN * chains


def bin_first_arrivals(cells, face_rows, places, meta_ref, *refs):
    count = len(refs) - 7
    sources = refs[:count]
    bead_pos_ref, bead_vel_ref, start_ref, order_ref, total_ref, held, counts_ref = refs[count:]
    meta = [meta_ref[k] for k in range(8)]
    total_ref[...] = start_ref[...]
    held[...] = jnp.zeros_like(held)
    faces = [(sources[which], first) for which, first in places]
    end = take_faces(faces, face_rows, held, counts_ref, 0, 0)
    weight = jnp.where(bead_mask(meta[7]), bead_mass, 0.0)
    bin_group(
        total_ref,
        [bead_pos_ref[d] for d in range(3)],
        [bead_vel_ref[d] for d in range(3)],
        weight,
        meta,
        cells,
    )
    bin_held(held, 0, end, total_ref, meta, cells)


def bin_arrivals(cells, face_rows, places, known, meta_ref, *refs):
    count = len(refs) - 10
    sources = refs[:count]
    (
        axis_ref,
        held_ref,
        known_ref,
        start_ref,
        total_ref,
        low_ref,
        high_ref,
        held,
        counts_ref,
        sums,
    ) = refs[count:]
    meta = [meta_ref[k] for k in range(8)]
    sums[...] = start_ref[...]
    held[...] = held_ref[...]
    begin = 0
    for k in range(known):
        counts_ref[k] = known_ref[k]
        begin = begin + known_ref[k]
    faces = [(sources[which], first) for which, first in places]
    end = take_faces(faces, face_rows, held, counts_ref, known, begin)
    bin_held(held, begin, end, sums, meta, cells)
    nz, inner = cells.nz, cells.inner
    lane = lax.broadcasted_iota(jnp.int32, (cells.rows, LANES), 1)
    main, rest = sums[:, :LANES], sums[:, LANES:]
    main = main + jnp.where(lane < nz, 0.0, rest)
    top = jnp.where(lane == 0, rest, rest + pltpu.roll(rest, LANES - 3, axis=1))
    total_ref[0] = main
    total_ref[1] = jnp.where(lane < 4, top, 0.0)
    axis = axis_ref[...].astype(f32)
    total_ref[1, :inner, nz : 2 * nz] = axis
    sx, sy = cells.sx, cells.sy
    low_ref[...] = jnp.zeros_like(low_ref)
    high_ref[...] = jnp.zeros_like(high_ref)
    for half in range(2):
        corner = inner + sy + 1
        low_ref[half, :sy, :] = total_ref[half, :sy, :]
        low_ref[half, sy : sy + 1, :] = total_ref[half, corner : corner + 1, :]
        high_ref[half, : sy + 1, :] = total_ref[half, inner : inner + sy + 1, :]


def add_faces_x(cells, total_ref, below_ref, above_ref, out_ref, low_ref, high_ref):
    sx, sy, inner = cells.sx, cells.sy, cells.inner
    corner = inner + sy + 1
    out_ref[...] = total_ref[...]
    low_ref[...] = jnp.zeros_like(low_ref)
    high_ref[...] = jnp.zeros_like(high_ref)
    for half in range(2):
        out_ref[half, :sy, :] += below_ref[half, :sy, :]
        out_ref[half, corner : corner + 1, :] += below_ref[half, sy : sy + 1, :]
        out_ref[half, inner : inner + sy + 1, :] += above_ref[half, : sy + 1, :]
        low_ref[half, :sx, :] = out_ref[half, pl.ds(0, sx, stride=sy), :]
        low_ref[half, sx : sx + 1, :] = out_ref[half, inner : inner + 1, :]
        high_ref[half, :sx, :] = out_ref[half, corner : corner + sx, :]
        high_ref[half, sx : sx + 1, :] = out_ref[half, inner + sy : inner + sy + 1, :]


def add_faces_y(cells, total_ref, below_ref, above_ref, out_ref, face_ref, sums):
    sx, sy, nz, inner = cells.sx, cells.sy, cells.nz, cells.inner
    corner = inner + sy + 1
    sums[...] = total_ref[...]
    for half in range(2):
        sums[half, pl.ds(0, sx, stride=sy), :] += below_ref[half, :sx, :]
        sums[half, inner : inner + 1, :] += below_ref[half, sx : sx + 1, :]
        sums[half, corner : corner + sx, :] += above_ref[half, :sx, :]
        sums[half, inner + sy : inner + sy + 1, :] += above_ref[half, sx : sx + 1, :]
    main = sums[0].T
    rest = sums[1].T
    out_ref[:LANES, :] = main
    out_ref[LANES : LANES + nz, :] = rest[nz : 2 * nz]
    out_ref[LANES + nz :, :] = jnp.zeros((GROUP, cells.rows), f32)
    out_ref[LANES + nz : LANES + nz + 4, :] = rest[:4]
    face_ref[...] = jnp.zeros_like(face_ref)
    for c in range(5):
        face_ref[c : c + 1, :] = out_ref[c * nz : c * nz + 1, :]
        face_ref[GROUP + c : GROUP + c + 1, :] = out_ref[5 * nz + c : 5 * nz + c + 1, :]


def cell_table(cells, total_ref, below_ref, above_ref, table_ref, sheet, edge):
    nz, inner, height = cells.nz, cells.inner, cells.height
    row_ids = lax.broadcasted_iota(jnp.int32, (nz, cells.rows), 0)
    parts = []
    tops = []
    for c in range(5):
        face = jnp.where(row_ids == 0, below_ref[GROUP + c : GROUP + c + 1, :], 0.0)
        parts.append(total_ref[c * nz : (c + 1) * nz, :] + face)
        tops.append(
            total_ref[5 * nz + c : 5 * nz + c + 1, :] + above_ref[c : c + 1, :]
        )
    mass = jnp.maximum(parts[0], 1.0)
    top_mass = jnp.maximum(tops[0], 1.0)
    values = [parts[4]] + [p / mass for p in parts[1:4]]
    top_values = [tops[4]] + [t / top_mass for t in tops[1:4]]
    sheet[...] = jnp.zeros_like(sheet)
    edge[...] = jnp.zeros_like(edge)
    lane = lax.broadcasted_iota(jnp.int32, (cells.extra, LANES), 1)
    spare = LANES - (cells.rows - inner)
    for c in range(4):
        base = c * height
        sheet[base : base + nz, :] = values[c][:, :inner]
        sheet[base + nz : base + nz + 1, :] = top_values[c][:, :inner]
        edge[base : base + nz, :] = jnp.concatenate(
            [values[c][:, inner:], jnp.zeros((nz, spare), f32)], axis=1
        )
        edge[base + nz : base + nz + 1, :] = jnp.concatenate(
            [top_values[c][:, inner:], jnp.zeros((1, spare), f32)], axis=1
        )
        folded = [jnp.zeros((cells.extra, LANES), f32) for _ in range(inner // LANES)]
        for m in range(cells.per):
            begin = m * cells.edges
            piece = edge[pl.ds(base + m, cells.extra, stride=cells.per), :]
            piece = pltpu.roll(piece, begin % LANES, axis=1) if begin % LANES else piece
            for t in range(inner // LANES):
                low, high = begin - t * LANES, begin + cells.edges - t * LANES
                if high > 0 and low < LANES:
                    folded[t] = jnp.where((lane >= low) & (lane < high), piece, folded[t])
        sheet[base + nz + 1 : base + nz + 1 + cells.extra, :] = jnp.concatenate(folded, axis=1)
    whole = sheet[...]
    high = whole.astype(bf16).astype(f32)
    low = (whole - high)[height:]
    table_ref[...] = jnp.concatenate([high, low], axis=0).astype(bf16)


def direction_table():
    counter = jnp.arange(LANES).astype(f32)
    height = 1.0 - (2.0 * counter + 1.0) / NAXES
    radius = jnp.sqrt(jnp.maximum(1.0 - height * height, 0.0))
    rows = jnp.stack([radius * jnp.cos(golden * counter), radius * jnp.sin(golden * counter)])
    return jnp.broadcast_to(rows[:, None], (2, GROUP, LANES))


def fold_rows(values):
    sub = lax.broadcasted_iota(jnp.int32, (GROUP, LANES), 0)
    step = GROUP // 2
    while step:
        upper = (sub & step) == 0
        half = len(values) // 2
        joined = []
        for a, b in zip(values[:half], values[half:]):
            a = a + pltpu.roll(a, GROUP - step, axis=0)
            b = b + pltpu.roll(b, step, axis=0)
            joined.append(jnp.where(upper, a, b))
        values = joined
        step //= 2
    return values[0]


def collide(position, velocity, meta, table, dirs_ref, cells):
    height = cells.height
    row, column = place_of(levels_of(position, meta), cells)
    found = lax.dot_general(
        table, one_hot(column, cells.inner), NN, preferred_element_type=f32
    )
    ids = lax.broadcasted_iota(jnp.int32, (height, LANES), 0).astype(f32)
    picked = [[] for _ in range(4)]
    for r in range(GROUP):
        block = found[:, r * LANES : (r + 1) * LANES]
        here = ids == row[r : r + 1]
        for c in range(4):
            value = block[c * height : (c + 1) * height]
            if c > 0:
                value = value + block[(3 + c) * height : (4 + c) * height]
            value = jnp.where(here, value, 0.0)
            picked[c].append(
                jnp.sum(value.reshape(height // GROUP, GROUP, LANES), axis=0)
            )
    picked = [fold_rows(p) for p in picked]
    axis, flow = picked[0].astype(jnp.int32), picked[1:]
    normal = [
        jnp.take_along_axis(dirs_ref[0], axis, axis=1, mode="promise_in_bounds"),
        jnp.take_along_axis(dirs_ref[1], axis, axis=1, mode="promise_in_bounds"),
        1.0 - (2.0 * picked[0] + 1.0) * (1.0 / NAXES),
    ]
    rel = [velocity[d] - flow[d] for d in range(3)]
    along = (1.0 - turn_cosine) * (
        normal[0] * rel[0] + normal[1] * rel[1] + normal[2] * rel[2]
    )
    result = []
    for d in range(3):
        e, f = (d + 1) % 3, (d + 2) % 3
        crossed = normal[e] * rel[f] - normal[f] * rel[e]
        result.append(
            flow[d] + (turn_cosine * rel[d] + turn_sine * crossed + along * normal[d])
        )
    return result


def passed(position, speed):
    return position - jnp.floor(position) - 0.5 + 3.0 * step_size * speed


def writing(spans, refs, sems):
    copies = []
    for k, ((first, count), (value, out)) in enumerate(zip(spans, refs)):
        copies.append(
            pltpu.make_async_copy(value, out.at[:, pl.ds(first, count), :], sems.at[k])
        )
    for copy in copies:
        copy.start()

    def finish():
        for copy in copies:
            copy.wait()

    return finish


def collide_residents(
    cells, first, count, before, meta_ref, dirs_ref, table_ref, pos_ref, vel_ref, *refs
):
    out_pos, out_vel, new_pos, new_vel, token, sems = refs[-6:]
    finish = writing([before] * 2, [(refs[0], out_pos), (refs[1], out_vel)], sems) if before else None
    token[...] = jnp.zeros_like(token)
    meta = [meta_ref[k] for k in range(8)]
    table = table_ref[...]
    live_rows = meta[6] - first
    new_pos[...] = jnp.zeros_like(new_pos)
    new_vel[...] = jnp.zeros_like(new_vel)
    stride = GROUP * TWIN

    @pl.loop(0, jnp.clip((live_rows + stride - 1) // stride, 0, count // stride))
    def _(step):
        for part in range(TWIN):
            offset = pl.multiple_of(step * stride + part * GROUP, GROUP)
            rows = pl.ds(first + offset, GROUP)
            position = [pos_ref[d, rows, :] for d in range(3)]
            velocity = [vel_ref[d, rows, :] for d in range(3)]
            live = row_iota() + offset < live_rows
            speed = collide(position, velocity, meta, table, dirs_ref, cells)
            rows = pl.ds(offset, GROUP)
            for d in range(3):
                new_vel[d, rows, :] = jnp.where(live, speed[d], 0.0)
                new_pos[d, rows, :] = jnp.where(live, passed(position[d], speed[d]), 0.0)

    if finish:
        finish()


def collide_held(
    cells, first, count, many, before, meta_ref, dirs_ref, table_ref, held, counts_ref, *refs
):
    if before:
        out_pos, out_vel, out_ref, token, sems = refs[-5:]
        finish = writing([before] * 2, [(refs[0], out_pos), (refs[1], out_vel)], sems)
    else:
        out_ref, token = refs[-2:]
        finish = None
    token[...] = jnp.zeros_like(token)
    meta = [meta_ref[k] for k in range(8)]
    table = table_ref[...]
    out_ref[...] = jnp.zeros_like(out_ref)
    end = sum([counts_ref[k] for k in range(many)], jnp.int32(0)) - first
    stride = GROUP * TRIO

    @pl.loop(0, jnp.clip((end + stride - 1) // stride, 0, count // stride))
    def _(step):
        for part in range(TRIO):
            offset = pl.multiple_of(step * stride + part * GROUP, GROUP)
            comps = [held[c, pl.ds(first + offset, GROUP), :] for c in range(6)]
            speed = collide(comps[:3], comps[3:], meta, table, dirs_ref, cells)
            for d in range(3):
                out_ref[d, pl.ds(offset, GROUP), :] = speed[d]
                out_ref[3 + d, pl.ds(offset, GROUP), :] = passed(comps[d], speed[d])

    if finish:
        finish()


def place_arrivals(face_rows, sequence, counts_ref, *refs):
    pieces = refs[:-4]
    new_pos, new_vel, token, packed = refs[-4:]
    token[...] = jnp.zeros_like(token)
    packed[...] = jnp.zeros_like(packed)
    at = 0
    for piece in pieces:
        packed[:, at : at + piece.shape[1], :] = piece[...]
        at += piece.shape[1]
    rows = lax.broadcasted_iota(jnp.int32, (face_rows, LANES), 0)
    offset = 0
    for k, face in enumerate(sequence):
        count = counts_ref[k]
        place = slice(face * face_rows, (face + 1) * face_rows)
        for d in range(3):
            speed = packed[d, pl.ds(offset, face_rows), :]
            moved = packed[3 + d, pl.ds(offset, face_rows), :]
            new_vel[d, place, :] = jnp.where(rows < count, speed, 0.0)
            new_pos[d, place, :] = jnp.where(rows < count, moved, 0.0)
        offset = offset + count


def pack_inputs(
    meta_ref,
    pos_ref,
    vel_ref,
    bead_pos_ref,
    bead_vel_ref,
    bond_ref,
    order_ref,
    start_ref,
    block_ref,
    rows_pos_ref,
    rows_vel_ref,
    *refs,
):
    out_refs, (held_pos, held_vel, sems) = refs[:6], refs[6:]
    copies = [(bead_pos_ref, held_pos), (bead_vel_ref, held_vel)]
    for face, out_ref in enumerate(out_refs):
        copies.append((pos_ref.at[:, face], out_ref.at[0:3]))
        copies.append((vel_ref.at[:, face], out_ref.at[3:6]))
    copies = [pltpu.make_async_copy(a, b, sems.at[k]) for k, (a, b) in enumerate(copies)]
    for copy in copies:
        copy.start()
    for face, out_ref in enumerate(out_refs):
        out_ref[6] = jnp.full(out_ref.shape[1:], meta_ref[8 + face], jnp.int32).astype(f32)
    slots = start_ref.shape[1]
    start_ref[...] = jnp.zeros_like(start_ref)
    rows_pos_ref[...] = jnp.zeros_like(rows_pos_ref)
    rows_vel_ref[...] = jnp.zeros_like(rows_vel_ref)
    for copy in copies:
        copy.wait()
    for d in range(3):
        for k in range(slots // LANES):
            lanes = slice(k * LANES, (k + 1) * LANES)
            start_ref[d : d + 1, lanes] = held_pos[d, k : k + 1, :]
            rows_pos_ref[d, k : k + 1, :] = held_pos[d, k : k + 1, :]
            rows_vel_ref[d, k : k + 1, :] = held_vel[d, k : k + 1, :]
    bond_slots = bond_ref.shape[-1]
    ends = jnp.concatenate(
        [bond_ref[k, 0, 0, :, :].astype(f32) for k in range(2)]
        + [jnp.zeros((GROUP - 2, bond_slots), f32)],
        axis=0,
    )
    if bond_slots < slots:
        ends = jnp.concatenate([ends, jnp.zeros((GROUP, slots - bond_slots), f32)], axis=1)
    start = start_ref[...]
    whole = payload(start, slot_live(slots, meta_ref[7], GROUP), ends)
    for k in range(slots // LANES):
        block_ref[k * GROUP : (k + 1) * GROUP, :] = whole[:, k * LANES : (k + 1) * LANES]


def stack_rows(parts, *refs):
    out_ref = refs[-1]
    at = 0
    for which, begin, count in parts:
        out_ref[at : at + count, :] = refs[which][begin : begin + count, :]
        at += count


def slot_live(slots, chains, rows):
    return lax.broadcasted_iota(jnp.int32, (rows, slots), 1) < CHAIN * chains


def payload(position, live, more):
    row_ids = lax.broadcasted_iota(jnp.int32, position.shape, 0)
    flag = jnp.where(live, 1.0, 0.0)
    rest = pltpu.roll(more, 4, axis=0)
    return jnp.where(row_ids == 3, flag, jnp.where(row_ids < 3, position, rest))


def thirds_of(value):
    high = value.astype(bf16).astype(f32)
    middle = (value - high).astype(bf16).astype(f32)
    low = value - high - middle
    return jnp.concatenate([high, middle, low, jnp.zeros_like(value)], axis=0).astype(bf16)


def summed_thirds(value):
    return value[:GROUP] + (value[GROUP : 2 * GROUP] + value[2 * GROUP : 3 * GROUP])


def joins_of(block, chains, bond_slots):
    ends = block.T
    slots = block.shape[1]
    slot_ids = lax.broadcasted_iota(jnp.int32, (slots, slots), 1).astype(f32)
    bond_ids = lax.broadcasted_iota(jnp.int32, (slots, slots), 0)
    joins = jnp.where(slot_ids == ends[:, 4:5], 1.0, 0.0)
    joins = joins - jnp.where(slot_ids == ends[:, 5:6], 1.0, 0.0)
    live = jnp.minimum((CHAIN - 1) * chains, bond_slots)
    return jnp.where(bond_ids < live, joins, 0.0).astype(bf16)


def bond_forces(local, joins, chains):
    stretch = summed_thirds(
        lax.dot_general(thirds_of(local), joins, NT, preferred_element_type=f32)
    )
    square = (
        stretch[0:1] * stretch[0:1] + stretch[1:2] * stretch[1:2] + stretch[2:3] * stretch[2:3]
    )
    live = lax.broadcasted_iota(jnp.int32, (1, joins.shape[0]), 1) < (CHAIN - 1) * chains
    pull = jnp.where(live, -spring / (1.0 - square / reach_square), 0.0) * stretch
    return summed_thirds(lax.dot_general(thirds_of(pull), joins, NN, preferred_element_type=f32))


def forces(blocks, counts, joins, mains, home, centre, lengths, mine_ref, packed, push, near_mask):
    slots = blocks[0].shape[1]
    tiles = slots // LANES
    row_ids = lax.broadcasted_iota(jnp.int32, (GROUP, slots), 0)
    lane_ids = lax.broadcasted_iota(jnp.int32, (GROUP, slots), 1)
    mid = jnp.zeros((GROUP, slots), f32)
    length = jnp.full((GROUP, slots), 1e9, f32)
    for d in range(3):
        mid = jnp.where(row_ids == d, centre[d], mid)
        if d < 2:
            length = jnp.where(row_ids == d, lengths[d], length)
    inverse_length = 1.0 / length
    shifted = [block - mid for block in blocks]
    near = shifted[:home] + [
        value - length * jnp.floor(value * inverse_length + 0.5) for value in shifted[home:]
    ]

    low = jnp.full((GROUP, slots), far_ghost, f32)
    high = jnp.full((GROUP, slots), -far_ghost, f32)
    bonds = []
    for b in range(mains):
        live = lane_ids < counts[b]
        columns = jnp.where(live, near[b], far_own).T
        for d in range(3):
            mine_ref[d, b * slots : (b + 1) * slots, :] = jnp.broadcast_to(
                columns[:, d : d + 1], (slots, LANES)
            )
        low = jnp.minimum(low, jnp.where(live, near[b], far_ghost))
        high = jnp.maximum(high, jnp.where(live, near[b], -far_ghost))
        local = jnp.where(live & (row_ids < 3), near[b], 0.0)
        bonds.append(bond_forces(local, joins[b], counts[b] // CHAIN))

    packed[...] = jnp.full(packed.shape, far_ghost, f32)
    lane = lax.broadcasted_iota(jnp.int32, (GROUP, LANES), 1)
    offset = jnp.int32(0)
    for value, count in zip(near[:home], counts[:home]):
        tile, turn = offset // LANES, offset % LANES
        turned = [
            pltpu.roll(value[:, k * LANES : (k + 1) * LANES], turn, axis=1)
            for k in range(tiles)
        ]
        for k in range(tiles + 1):
            if k == 0:
                piece = turned[0]
            elif k == tiles:
                piece = turned[-1]
            else:
                piece = jnp.where(lane < turn, turned[k - 1], turned[k])
            place = (tile + k) * LANES + lane
            taken = (place >= offset) & (place < offset + count)
            packed[tile + k] = jnp.where(taken, piece, packed[tile + k])
        offset = offset + count
    first_tile = (offset + LANES - 1) // LANES

    reach = 1.001 * math.sqrt(cut_square)
    low = jnp.min(low, axis=1, keepdims=True) - reach
    high = jnp.max(high, axis=1, keepdims=True) + reach
    others = near[home:]
    near_mask[...] = jnp.zeros_like(near_mask)
    for k, value in enumerate(others):
        inside = jnp.where((value >= low) & (value <= high), 1.0, 0.0)
        inside = inside[0:1] * inside[1:2]
        live = lane_ids[0:1] < counts[home + k]
        near_mask[k : k + 1, :] = jnp.where(live, inside, 0.0)
    mask = near_mask[...]
    height = mask.shape[0]
    mask_bf16 = mask.astype(bf16)
    upto = jnp.where(
        lax.broadcasted_iota(jnp.int32, (slots, slots), 0)
        <= lax.broadcasted_iota(jnp.int32, (slots, slots), 1),
        1.0,
        0.0,
    ).astype(bf16)
    above = jnp.where(
        lax.broadcasted_iota(jnp.int32, (height, height), 1)
        < lax.broadcasted_iota(jnp.int32, (height, height), 0),
        1.0,
        0.0,
    ).astype(bf16)
    within = lax.dot_general(mask_bf16, upto, NN, preferred_element_type=f32)
    before = lax.dot_general(above, mask_bf16, NN, preferred_element_type=f32)
    before = jnp.sum(before, axis=1, keepdims=True)
    place = jnp.where(mask > 0.5, within + before - 1.0, -1.0)
    found = jnp.sum(mask).astype(jnp.int32)
    parts = jnp.concatenate([thirds_of(value) for value in others], axis=1)
    found_tiles = (found + LANES - 1) // LANES

    @pl.loop(0, found_tiles)
    def _(tile):
        goal = place - (tile * LANES).astype(f32)
        rows = [
            goal[k : k + 1, t * LANES : (t + 1) * LANES]
            for k in range(len(others))
            for t in range(tiles)
        ]
        chosen = one_hot_rows(rows, LANES)
        value = summed_thirds(
            lax.dot_general(parts, chosen, NT, preferred_element_type=f32)
        )
        packed[first_tile + tile] = jnp.where(tile * LANES + lane < found, value, far_ghost)

    push[...] = jnp.zeros_like(push)
    chunk = 64
    steps = (first_tile + found_tiles + 1) // 2
    period = lengths[2]

    for b in range(mains):

        @pl.loop(0, (counts[b] + chunk - 1) // chunk)
        def _(part):
            rows = pl.ds(pl.multiple_of(b * slots + part * chunk, chunk), chunk)
            mine = [mine_ref[d, rows, :] for d in range(3)]

            def add_tiles(step, total):
                for k in range(2):
                    other = packed[2 * step + k]
                    differ = [mine[d] - other[d : d + 1] for d in range(3)]
                    differ[2] = differ[2] - period * jnp.floor(
                        differ[2] * (1.0 / period) + 0.5
                    )
                    square = (
                        differ[0] * differ[0] + differ[1] * differ[1] + differ[2] * differ[2]
                    )
                    inside = (square < cut_square) & (square > 0.25)
                    inverse = 1.0 / jnp.where(inside, square, 1e30)
                    sixth = inverse * inverse * inverse
                    weight = (sixth * inverse) * (48.0 * sixth - 24.0)
                    total = tuple(total[d] + weight * differ[d] for d in range(3))
                return total

            total = lax.fori_loop(
                0, steps, add_tiles, tuple(jnp.zeros((chunk, LANES), f32) for _ in range(3))
            )
            for d in range(3):
                push[d, rows, :] = total[d]

    result = []
    for b in range(mains):
        pair = jnp.zeros((GROUP, slots), f32)
        for d in range(3):
            line = jnp.sum(push[d, b * slots : (b + 1) * slots, :].T, axis=0, keepdims=True)
            pair = jnp.where(row_ids == d, line, pair)
        result.append(pair + bonds[b])
    return result


def force_scratch(slots, blocks, home, mains):
    tiles = home * slots // LANES + 2 + (blocks - home) * slots // LANES
    return [
        pltpu.VMEM((3, mains * slots, LANES), f32),
        pltpu.VMEM((-(-tiles // 2) * 2, GROUP, LANES), f32),
        pltpu.VMEM((3, mains * slots, LANES), f32),
        pltpu.VMEM((-(-(blocks - home) // 16) * 16, slots), f32),
    ]


def blocks_of(refs):
    return [
        ref[b * GROUP : (b + 1) * GROUP, :]
        for ref in refs
        for b in range(ref.shape[0] // GROUP)
    ]


def centre_of(meta, sizes):
    return [meta[3 + d].astype(f32) + 0.5 * sizes[d] for d in range(3)]


def first_forces(sizes, lengths, sources, home, bond_slots, meta_ref, *refs):
    sources_refs, (push_ref, counts_ref, joins_ref), scratch = (
        refs[:sources],
        refs[sources : sources + 3],
        refs[sources + 3 :],
    )
    meta = [meta_ref[k] for k in range(8)]
    blocks = blocks_of(sources_refs)
    counts = [jnp.sum(block[3:4]).astype(jnp.int32) for block in blocks]
    for k, count in enumerate(counts):
        counts_ref[k] = count
    joins = []
    for b in range(home):
        joins.append(joins_of(blocks[b], counts[b] // CHAIN, bond_slots))
        joins_ref[b] = joins[b]
    push_ref[...] = forces(
        blocks, counts, joins, 1, home, centre_of(meta, sizes), lengths, *scratch
    )[0]


def finish_cells(
    cells,
    meta_ref,
    dirs_ref,
    total_ref,
    below_ref,
    above_ref,
    bead_pos_ref,
    bead_vel_ref,
    start_ref,
    push_ref,
    table_ref,
    speed_ref,
    moved_ref,
    pay_ref,
    sheet,
    edge,
):
    meta = [meta_ref[k] for k in range(8)]
    cell_table(cells, total_ref, below_ref, above_ref, table_ref, sheet, edge)
    fresh = collide(
        [bead_pos_ref[d] for d in range(3)],
        [bead_vel_ref[d] for d in range(3)],
        meta,
        table_ref[...],
        dirs_ref,
        cells,
    )
    start = start_ref[...]
    slots = start.shape[1]
    row_ids = lax.broadcasted_iota(jnp.int32, (GROUP, slots), 0)
    speed = jnp.zeros((GROUP, slots), f32)
    for d in range(3):
        line = jnp.concatenate([fresh[d][k : k + 1] for k in range(slots // LANES)], axis=1)
        speed = jnp.where(row_ids == d, line, speed)
    speed = speed + half_kick * push_ref[...]
    moved = step_size * speed
    live = slot_live(slots, meta[7], GROUP)
    speed_ref[...] = speed
    moved_ref[...] = moved
    pay_ref[...] = payload(start + moved, live, speed)


def substep(
    sizes, lengths, sources, home, step, last, meta_ref, start_ref, joins_ref, counts_ref, speed_ref, moved_ref, *refs
):
    came, rest = refs[:sources], refs[sources:]
    if last:
        new_pos, new_vel, _, _, *outs, sems, a, b, c, e = rest
        finish = writing([last] * 2, [(new_pos, outs[2]), (new_vel, outs[3])], sems)
    else:
        _, *outs, a, b, c, e = rest
    meta = [meta_ref[k] for k in range(8)]
    blocks = blocks_of(came)
    counts = [counts_ref[k] for k in range(len(blocks))]
    mains = 1 if last else home
    joins = [joins_ref[b] for b in range(mains)]
    pushes = forces(
        blocks, counts, joins, mains, home, centre_of(meta, sizes), lengths, a, b, c, e
    )
    slots = start_ref.shape[1]
    row_ids = lax.broadcasted_iota(jnp.int32, (GROUP, slots), 0)
    for b in range(mains):
        rows = slice(b * GROUP, (b + 1) * GROUP)
        live = lax.broadcasted_iota(jnp.int32, (GROUP, slots), 1) < counts[b]
        start = start_ref[rows, :]
        if step == 0 and b > 0:
            speed = jnp.where(row_ids < 3, pltpu.roll(blocks[b], 4, axis=0), 0.0)
            moved = step_size * speed
        else:
            speed, moved = speed_ref[rows, :], moved_ref[rows, :]
        speed = speed + half_kick * pushes[b]
        if last:
            for d in range(3):
                outs[0][d, 0, 0, :, :] = jnp.where(live, speed, 0.0)[d : d + 1]
                outs[1][d, 0, 0, :, :] = jnp.where(live, moved, 0.0)[d : d + 1]
            finish()
            return
        speed = speed + half_kick * pushes[b]
        moved = moved + step_size * speed
        outs[0][rows, :] = speed
        outs[1][rows, :] = moved
        outs[2][rows, :] = payload(start + moved, live, speed)


def neighbours(value, axis):
    peers = lax.axis_size(axis)
    if peers == 2:
        return [moved_along(value, axis, 1)]
    return [moved_along(value, axis, 1), moved_along(value, axis, -1)]


def stacked(parts, operands, order=()):
    rows = sum(count for _, _, count in parts)
    width = operands[0].shape[1]
    return pl.pallas_call(
        functools.partial(stack_rows, tuple(parts)),
        out_shape=like(rows, width),
        in_specs=[vmem()] * len(operands) + [pl.BlockSpec(memory_space=pl.ANY)] * len(order),
        out_specs=vmem(),
        compiler_params=params(),
        name="stack_rows",
    )(*operands, *order)


def whole_rows(operands):
    return [(k, 0, value.shape[0]) for k, value in enumerate(operands)]


def halo(rows, axes, pieces):
    for axis, piece in zip(axes[:-1], pieces):
        parts = [rows] + neighbours(rows, axis)
        rows = stacked(whole_rows(parts), parts, [piece()])
    sides = neighbours(rows, axes[-1])
    return [rows] + sides, pieces[-1]()


def like(*shape, dtype=f32):
    return jax.ShapeDtypeStruct(shape, dtype)


def shards(
    sol_pos,
    sol_vel,
    sol_rows,
    mig_pos,
    mig_vel,
    mig_rows,
    bead_pos,
    bead_vel,
    bead_chains,
    bond_list,
    cell_axis,
    shift,
):
    sizes = cell_axis.shape
    cells = Cells(*sizes)
    names = ("gx", "gy", "gz")
    lengths = tuple(float(sizes[d] * lax.axis_size(names[d])) for d in range(3))
    slots_here = sol_pos.shape[-1]
    buffer_slots = mig_pos.shape[-1]
    bead_slots = bead_pos.shape[-1]
    bond_slots = bond_list.shape[-1]
    rows_here = slots_here // LANES
    face_rows = buffer_slots // LANES
    rows_all = rows_here + 6 * face_rows
    anchor = jnp.stack([lax.axis_index(names[d]) * sizes[d] for d in range(3)])
    meta = jnp.concatenate(
        [
            shift,
            anchor.astype(jnp.int32),
            sol_rows.reshape(1),
            bead_chains.reshape(1),
            mig_rows.reshape(6),
        ]
    )
    dirs = direction_table()
    position = sol_pos.reshape(3, rows_here, LANES)
    velocity = sol_vel.reshape(3, rows_here, LANES)

    any_spec = pl.BlockSpec(memory_space=pl.ANY)
    thirds = 3
    count = rows_here // thirds
    axis_rows = cell_axis.reshape(cells.inner, sizes[2])

    def bin_piece(piece, earlier, order):
        sources = [position, velocity] if piece else [position[:, :count], velocity[:, :count]]
        return pl.pallas_call(
            functools.partial(bin_residents, cells, piece * count, count),
            out_shape=like(cells.rows, 2 * LANES),
            in_specs=[smem()]
            + [vmem()] * (2 + len(earlier))
            + [any_spec] * len(order),
            out_specs=vmem(),
            compiler_params=params(),
            name=f"bin_residents_{piece}",
        )(meta, *sources, *earlier, *order)

    totals = bin_piece(0, [], [])
    face_height = 7 * face_rows
    bead_shape = like(GROUP, bead_slots)
    tiles = bead_slots // LANES
    rows_shape = like(3, GROUP, LANES)
    start, block, bead_rows_pos, bead_rows_vel, *packed = pl.pallas_call(
        pack_inputs,
        out_shape=[
            bead_shape,
            like(tiles * GROUP, LANES),
            rows_shape,
            rows_shape,
        ]
        + [like(7, face_rows, LANES)] * 6,
        in_specs=[smem()]
        + [pl.BlockSpec(memory_space=pltpu.HBM)] * 4
        + [vmem(), any_spec],
        out_specs=[vmem()] * 10,
        scratch_shapes=[pltpu.VMEM((3, tiles, LANES), f32)] * 2
        + [pltpu.SemaphoreType.DMA((14,))],
        compiler_params=params(vmem_most),
        name="pack_inputs",
    )(
        meta,
        mig_pos.reshape(3, 6, face_rows, LANES),
        mig_vel.reshape(3, 6, face_rows, LANES),
        bead_pos.reshape(3, tiles, LANES),
        bead_vel.reshape(3, tiles, LANES),
        bond_list,
        totals,
    )
    packed = [value.reshape(face_height, LANES) for value in packed]

    def swap(axis, low, high, body):
        if lax.axis_size(axis) == 2:
            both = [packed[low], packed[high], body]
            came = moved_along(stacked(whole_rows(both), both), axis, 1)
            return [came], [(0, face_height), (0, 0)], [(0, 2 * face_height)]
        up = stacked(whole_rows([packed[high], body]), [packed[high], body])
        down = stacked(whole_rows([packed[low], body]), [packed[low], body])
        came = [moved_along(up, axis, 1), moved_along(down, axis, -1)]
        return came, [(0, 0), (1, 0)], [(0, face_height), (1, face_height)]

    arriving, spots, blocks = [], [None] * 6, block
    for piece, (axis, low) in enumerate((("gz", 4), ("gy", 2), ("gx", 0))):
        came, places, bodies = swap(axis, low, low + 1, blocks)
        for k, (which, at) in enumerate(places):
            spots[low + k] = (len(arriving) + which, at)
        arriving += came
        height = blocks.shape[0]
        if axis != "gx":
            totals = bin_piece(piece + 1, [totals], [blocks])
            parts = [(0, 0, height)] + [(1 + w, at, height) for w, at in bodies]
            blocks = stacked(parts, [blocks] + came, [totals])
        else:
            around = [blocks] + [
                stacked([(0, at, height)], [came[w]]) for w, at in bodies
            ]

    def as_blocks(value):
        n = value.shape[0] // (GROUP * tiles)
        return (
            value.reshape(n, tiles, GROUP, LANES)
            .transpose(0, 2, 1, 3)
            .reshape(n * GROUP, bead_slots)
        )

    sequence = (4, 5, 2, 3, 0, 1)
    early, late = sequence[:4], sequence[4:]
    sooner = max(spots[face][0] for face in early) + 1
    held_rows = -(-6 * face_rows // 32) * 32
    held_shape = like(6, held_rows, LANES)
    totals, held, counted = pl.pallas_call(
        functools.partial(
            bin_first_arrivals, cells, face_rows, [spots[face] for face in early]
        ),
        out_shape=[like(cells.rows, 2 * LANES), held_shape, like(4, dtype=jnp.int32)],
        in_specs=[smem()] + [vmem()] * (sooner + 3) + [any_spec],
        out_specs=[vmem(), vmem(), smem()],
        compiler_params=params(),
        name="bin_first_arrivals",
    )(meta, *arriving[:sooner], bead_rows_pos, bead_rows_vel, totals, blocks)

    face_x = like(2, -(-(sizes[1] + 1) // GROUP) * GROUP, LANES)
    face_y = like(2, -(-(sizes[0] + 1) // GROUP) * GROUP, LANES)
    later = arriving[sooner:]
    totals, low, high, held, counted = pl.pallas_call(
        functools.partial(
            bin_arrivals,
            cells,
            face_rows,
            [(spots[face][0] - sooner, spots[face][1]) for face in late],
            len(early),
        ),
        out_shape=[
            like(2, cells.rows, LANES),
            face_x,
            face_x,
            held_shape,
            like(6, dtype=jnp.int32),
        ],
        in_specs=[smem()] + [vmem()] * (len(later) + 2) + [smem(), vmem()],
        out_specs=[vmem()] * 4 + [smem()],
        scratch_shapes=[pltpu.VMEM((cells.rows, 2 * LANES), f32)],
        compiler_params=params(),
        name="bin_arrivals",
    )(meta, *later, axis_rows, held, counted, totals)

    around = [as_blocks(value) for value in around]
    many = sum(value.shape[0] // GROUP for value in around)
    home = 2 if lax.axis_size("gz") == 2 else 1
    push, counts, joins = pl.pallas_call(
        functools.partial(first_forces, sizes, lengths, len(around), home, bond_slots),
        out_shape=[
            bead_shape,
            like(many, dtype=jnp.int32),
            like(home, bead_slots, bead_slots, dtype=bf16),
        ],
        in_specs=[smem()] + [vmem()] * len(around),
        out_specs=[vmem(), smem(), vmem()],
        scratch_shapes=force_scratch(bead_slots, many, home, 1),
        compiler_params=params(),
        name="first_forces",
    )(meta, *around)
    starts = around[0]

    below, above = moved_along(high, "gx", 1), moved_along(low, "gx", -1)
    totals, low, high = pl.pallas_call(
        functools.partial(add_faces_x, cells),
        out_shape=[like(2, cells.rows, LANES), face_y, face_y],
        in_specs=[vmem()] * 3,
        out_specs=[vmem()] * 3,
        compiler_params=params(),
        name="add_faces_x",
    )(totals, below, above)
    below, above = moved_along(high, "gy", 1), moved_along(low, "gy", -1)
    totals, faces = pl.pallas_call(
        functools.partial(add_faces_y, cells),
        out_shape=[like(LANES + cells.nz + GROUP, cells.rows), like(2 * GROUP, cells.rows)],
        in_specs=[vmem()] * 3,
        out_specs=[vmem()] * 2,
        scratch_shapes=[pltpu.VMEM((2, cells.rows, LANES), f32)],
        compiler_params=params(),
        name="add_faces_y",
    )(totals, below, above)
    sides = neighbours(faces, "gz")
    below, above = sides[0], sides[-1]

    table, speed, moved, pay = pl.pallas_call(
        functools.partial(finish_cells, cells),
        out_shape=[
            like(7 * cells.height, cells.inner, dtype=bf16),
            bead_shape,
            bead_shape,
            bead_shape,
        ],
        in_specs=[smem()] + [vmem()] * 8,
        out_specs=[vmem()] * 4,
        scratch_shapes=[
            pltpu.VMEM((4 * cells.height, cells.inner), f32),
            pltpu.VMEM((4 * cells.height, LANES), f32),
        ],
        compiler_params=params(),
        name="finish_cells",
    )(meta, dirs, totals, below, above, bead_rows_pos, bead_rows_vel, start, push)

    solvent_shape = like(3, rows_all, LANES)
    windows = [("gz", "gy", "gx")] + [("gy", "gx") if home == 2 else ("gz", "gy", "gx")] * 2
    cuts = sum(len(axes) for axes in windows) - 3
    span = rows_here // cuts

    held_span = 2 * face_rows
    written, pending, packed_results, tokens = [], [], [], []

    def collide_piece(piece):
        token = like(GROUP, LANES)
        whole = [solvent_shape] * 2
        write_sems = [pltpu.SemaphoreType.DMA((2,))]
        if piece < cuts:
            before = ((piece - 1) * span, span) if piece else None
            extra = pending + written
            at = 5 + len(pending)
            *outs, order = pl.pallas_call(
                functools.partial(collide_residents, cells, piece * span, span, before),
                out_shape=whole + [like(3, span, LANES)] * 2 + [token],
                in_specs=[smem()] + [vmem()] * (4 + len(pending)) + [any_spec] * len(written),
                out_specs=[any_spec] * 2 + [vmem()] * 3,
                scratch_shapes=write_sems,
                input_output_aliases={at: 0, at + 1: 1} if written else {},
                compiler_params=params(),
                name=f"collide_{piece}",
            )(meta, dirs, table, position, velocity, *extra)
            written[:], pending[:] = outs[:2], outs[2:]
            tokens.append(order)
            return order
        before = ((cuts - 1) * span, span) if piece == cuts else None
        extra = pending + written if before else [tokens[-1]]
        outs = pl.pallas_call(
            functools.partial(
                collide_held, cells, (piece - cuts) * held_span, held_span, 6, before
            ),
            out_shape=(whole if before else []) + [like(6, held_span, LANES), token],
            in_specs=[smem()]
            + [vmem()] * 3
            + [smem()]
            + ([vmem()] * 2 + [any_spec] * 2 if before else [any_spec]),
            out_specs=([any_spec] * 2 if before else []) + [vmem()] * 2,
            scratch_shapes=write_sems if before else [],
            input_output_aliases={7: 0, 8: 1} if before else {},
            compiler_params=params(),
            name=f"collide_{piece}",
        )(meta, dirs, table, held, counted, *extra)
        if before:
            written[:] = outs[:2]
        packed_results.append(outs[-2])
        tokens.append(outs[-1])
        if piece < cuts + 2:
            return outs[-1]
        *pending[:], order = pl.pallas_call(
            functools.partial(place_arrivals, face_rows, sequence),
            out_shape=[like(3, 6 * face_rows, LANES)] * 2 + [token],
            in_specs=[smem()] + [vmem()] * 3,
            out_specs=[vmem()] * 3,
            scratch_shapes=[pltpu.VMEM((6, 7 * face_rows, LANES), f32)],
            compiler_params=params(),
            name="place_arrivals",
        )(counted, *packed_results)
        return order

    piece = 0
    for step, axes in enumerate(windows):
        last = step == 2
        thunks = [functools.partial(collide_piece, piece + k) for k in range(len(axes))]
        piece += len(axes)
        ghosts, order = halo(pay, axes, thunks)
        final = like(3, 1, 1, 1, bead_slots)
        state = like(home * GROUP, bead_slots)
        tail = pending + written if last else [order]
        at = 6 + len(ghosts) + 2
        outcome = pl.pallas_call(
            functools.partial(
                substep,
                sizes,
                lengths,
                len(ghosts),
                home,
                step,
                (rows_here, 6 * face_rows) if last else None,
            ),
            out_shape=[final] * 2 + [solvent_shape] * 2 if last else [state] * 3,
            in_specs=[smem(), vmem(), vmem(), smem()]
            + [vmem()] * (2 + len(ghosts))
            + ([vmem()] * 2 + [any_spec] * 2 if last else [any_spec]),
            out_specs=[vmem()] * 2 + [any_spec] * 2 if last else [vmem()] * 3,
            scratch_shapes=([pltpu.SemaphoreType.DMA((2,))] if last else [])
            + force_scratch(bead_slots, many, home, 1 if last else home),
            input_output_aliases={at: 2, at + 1: 3} if last else {},
            compiler_params=params(),
            name=f"substep_{step}",
        )(meta, starts, joins, counts, speed, moved, *ghosts, *tail)
        if last:
            written[:] = outcome[2:]
        speed, moved = outcome[:2]
        pay = outcome[-1]

    count_solvent = rows_all * LANES
    return (
        written[0].reshape(3, 1, 1, 1, count_solvent),
        written[1].reshape(3, 1, 1, 1, count_solvent),
        moved,
        speed,
    )


def solution(mesh):
    return jax.shard_map(
        shards,
        mesh=mesh,
        in_specs=(
            P(None, "gx", "gy", "gz", None),
            P(None, "gx", "gy", "gz", None),
            P("gx", "gy", "gz"),
            P(None, "gx", "gy", "gz", None, None),
            P(None, "gx", "gy", "gz", None, None),
            P("gx", "gy", "gz", None),
            P(None, "gx", "gy", "gz", None),
            P(None, "gx", "gy", "gz", None),
            P("gx", "gy", "gz"),
            P(None, "gx", "gy", "gz", None),
            P("gx", "gy", "gz"),
            P(),
        ),
        out_specs=(
            P(None, "gx", "gy", "gz", None),
            P(None, "gx", "gy", "gz", None),
            P(None, "gx", "gy", "gz", None),
            P(None, "gx", "gy", "gz", None),
        ),
        check_vma=False,
    )
```

```python
import functools
import math

import jax
import jax.numpy as jnp
from jax import lax
from jax.experimental import pallas as pl
from jax.experimental.pallas import tpu as pltpu
from jax.sharding import PartitionSpec as P

UNITS = 16
NAXES = 32
CHAIN = 8
LANES = 128
GROUP = 8
TWIN = 4
SENT = 4
PAIR = 2
TRIO = 3

bead_mass = 5.0
step_size = 0.02
spring = 30.0
reach_square = 2.25
cut_square = 2.0 ** (1.0 / 3.0)
turn_cosine = math.cos(130.0 * math.pi / 180.0)
turn_sine = math.sin(130.0 * math.pi / 180.0)
golden = math.pi * (3.0 - math.sqrt(5.0))
half_kick = 0.5 * step_size / bead_mass
far_own = 3000.0
far_ghost = 9000.0
vmem_limit = 48 * 1024 * 1024
vmem_most = 48 * 1024 * 1024
NT = (((1,), (1,)), ((), ()))
NN = (((1,), (0,)), ((), ()))
exact = lax.Precision.HIGHEST
f32 = jnp.float32
bf16 = jnp.bfloat16


def params(limit=vmem_limit):
    return pltpu.CompilerParams(vmem_limit_bytes=limit)


def vmem():
    return pl.BlockSpec(memory_space=pltpu.VMEM)


def smem():
    return pl.BlockSpec(memory_space=pltpu.SMEM)


def moved_along(value, axis, by):
    peers = lax.axis_size(axis)
    return lax.ppermute(value, axis, [(i, (i + by) % peers) for i in range(peers)])


class Cells:
    def __init__(self, size_x, size_y, size_z):
        self.sx, self.sy, self.nz = size_x, size_y, size_z
        self.inner = size_x * size_y
        self.edges = size_x + size_y + 1
        self.rows = -(-(self.inner + self.edges) // 16) * 16
        self.middle = self.rows // 2
        self.per = self.inner // self.edges
        self.depths = size_z + 1
        self.extra = -(-self.depths // self.per)
        self.height = -(-(self.depths + self.extra) // GROUP) * GROUP


def levels_of(position, meta):
    return [
        jnp.floor(jnp.floor(position[d] * UNITS + meta[d].astype(f32)) * (1.0 / UNITS))
        - meta[3 + d].astype(f32)
        for d in range(3)
    ]


def edge_of(levels, cells):
    outer = (levels[0] == cells.sx) | (levels[1] == cells.sy)
    return outer, jnp.where(levels[0] == cells.sx, levels[1], cells.sy + 1 + levels[0])


def plane_of(levels, cells):
    outer, edge = edge_of(levels, cells)
    return jnp.where(outer, cells.inner + edge, levels[0] * cells.sy + levels[1])


def place_of(levels, cells):
    outer, edge = edge_of(levels, cells)
    fold = jnp.floor((levels[2] + 0.5) * (1.0 / cells.per))
    row = jnp.where(outer, cells.depths + fold, levels[2])
    column = jnp.where(
        outer,
        (levels[2] - fold * cells.per) * cells.edges + edge,
        levels[0] * cells.sy + levels[1],
    )
    return row, column


def wide(row):
    return jnp.broadcast_to(row, (16, LANES)).astype(bf16)


def one_hot_rows(rows, height):
    middle = height // 2
    ids = lax.broadcasted_iota(jnp.int32, (height, LANES), 0) - middle
    ids = ids.astype(f32).astype(bf16).reshape(height // 16, 16, LANES)
    one, zero = jnp.ones((), bf16), jnp.zeros((), bf16)
    pieces = [
        jnp.where(ids == wide(row - middle)[None], one, zero).reshape(height, LANES)
        for row in rows
    ]
    return jnp.concatenate(pieces, axis=1)


def one_hot(column, height):
    return one_hot_rows([column[r : r + 1] for r in range(column.shape[0])], height)


def split(value):
    high = value.astype(bf16).astype(f32)
    return high, value - high


def spread_moments(depth, weight, velocity, cells):
    nz = cells.nz
    ids = lax.broadcasted_iota(jnp.int32, (nz, LANES), 0).astype(f32).astype(bf16)
    ids = ids.reshape(nz // 16, 16, LANES)
    row_ids = lax.broadcasted_iota(jnp.int32, (16, LANES), 0).astype(f32).astype(bf16)
    zero = jnp.zeros((), bf16)
    parts = [split(weight * velocity[d]) for d in range(3)]
    channels = [weight] + [p[0] for p in parts] + [p[1] for p in parts]
    pieces = []
    for r in range(depth.shape[0]):
        at = wide(depth[r : r + 1])
        here = ids == at[None]
        values = [wide(c[r : r + 1]) for c in channels]
        tiles = [jnp.where(here, v[None], zero).reshape(nz, LANES) for v in values]
        top = jnp.zeros((16, LANES), bf16)
        for c, v in enumerate(values):
            top = jnp.where(row_ids == c, v, top)
        top = jnp.where(at == nz, top, zero)
        pieces.append(
            jnp.concatenate(
                tiles[:4] + [top, jnp.zeros((nz - 16, LANES), bf16)] + tiles[4:], axis=0
            )
        )
    return jnp.concatenate(pieces, axis=1)


def bin_group(total_ref, position, velocity, weight, meta, cells):
    levels = levels_of(position, meta)
    hot = one_hot(plane_of(levels, cells), cells.rows)
    spread = spread_moments(levels[2], weight, velocity, cells)
    total_ref[...] += lax.dot_general(hot, spread, NT, preferred_element_type=f32)


def row_iota():
    return lax.broadcasted_iota(jnp.int32, (GROUP, LANES), 0)


def bin_residents(cells, first, count, meta_ref, pos_ref, vel_ref, *refs):
    total_ref = refs[-1]
    meta = [meta_ref[k] for k in range(8)]
    if first == 0:
        total_ref[...] = jnp.zeros_like(total_ref)
    else:
        total_ref[...] = refs[0][...]
    live_rows = meta[6] - first
    stride = GROUP * TWIN

    @pl.loop(0, jnp.clip((live_rows + stride - 1) // stride, 0, count // stride))
    def _(step):
        for part in range(TWIN):
            offset = pl.multiple_of(step * stride + part * GROUP, GROUP)
            rows = pl.ds(first + offset, GROUP)
            position = [pos_ref[d, rows, :] for d in range(3)]
            velocity = [vel_ref[d, rows, :] for d in range(3)]
            weight = jnp.where(row_iota() + offset < live_rows, 1.0, 0.0)
            bin_group(total_ref, position, velocity, weight, meta, cells)


def face_count(ref, first, face_rows):
    return jnp.max(ref[pl.ds(first + 6 * face_rows, GROUP), :]).astype(jnp.int32)


def take_faces(faces, face_rows, held, counts_ref, index, offset):
    for k, (ref, first) in enumerate(faces):
        count = face_count(ref, first, face_rows)
        counts_ref[index + k] = count
        for c in range(6):
            begin = first + c * face_rows
            held[c, pl.ds(offset, face_rows), :] = ref[begin : begin + face_rows, :]
        offset = offset + count
    return offset


def bin_held(held, begin, end, sums, meta, cells):
    stride = GROUP * PAIR

    @pl.loop(0, (end - begin + stride - 1) // stride)
    def _(step):
        for part in range(PAIR):
            offset = begin + step * stride + part * GROUP
            rows = pl.ds(offset, GROUP)
            comps = [held[c, rows, :] for c in range(6)]
            weight = jnp.where(row_iota() + offset < end, 1.0, 0.0)
            bin_group(sums, comps[:3], comps[3:], weight, meta, cells)


def bead_mask(chains):
    slot = row_iota() * LANES + lax.broadcasted_iota(jnp.int32, (GROUP, LANES), 1)
    return slot < CHAIN * chains


def bin_first_arrivals(cells, face_rows, places, meta_ref, *refs):
    count = len(refs) - 7
    sources = refs[:count]
    bead_pos_ref, bead_vel_ref, start_ref, order_ref, total_ref, held, counts_ref = refs[count:]
    meta = [meta_ref[k] for k in range(8)]
    total_ref[...] = start_ref[...]
    held[...] = jnp.zeros_like(held)
    faces = [(sources[which], first) for which, first in places]
    end = take_faces(faces, face_rows, held, counts_ref, 0, 0)
    weight = jnp.where(bead_mask(meta[7]), bead_mass, 0.0)
    bin_group(
        total_ref,
        [bead_pos_ref[d] for d in range(3)],
        [bead_vel_ref[d] for d in range(3)],
        weight,
        meta,
        cells,
    )
    bin_held(held, 0, end, total_ref, meta, cells)


def bin_arrivals(cells, face_rows, places, known, meta_ref, *refs):
    count = len(refs) - 10
    sources = refs[:count]
    (
        axis_ref,
        held_ref,
        known_ref,
        start_ref,
        total_ref,
        low_ref,
        high_ref,
        held,
        counts_ref,
        sums,
    ) = refs[count:]
    meta = [meta_ref[k] for k in range(8)]
    sums[...] = start_ref[...]
    held[...] = held_ref[...]
    begin = 0
    for k in range(known):
        counts_ref[k] = known_ref[k]
        begin = begin + known_ref[k]
    faces = [(sources[which], first) for which, first in places]
    end = take_faces(faces, face_rows, held, counts_ref, known, begin)
    bin_held(held, begin, end, sums, meta, cells)
    nz, inner = cells.nz, cells.inner
    lane = lax.broadcasted_iota(jnp.int32, (cells.rows, LANES), 1)
    main, rest = sums[:, :LANES], sums[:, LANES:]
    main = main + jnp.where(lane < nz, 0.0, rest)
    top = jnp.where(lane == 0, rest, rest + pltpu.roll(rest, LANES - 3, axis=1))
    total_ref[0] = main
    total_ref[1] = jnp.where(lane < 4, top, 0.0)
    axis = axis_ref[...].astype(f32)
    total_ref[1, :inner, nz : 2 * nz] = axis
    sx, sy = cells.sx, cells.sy
    low_ref[...] = jnp.zeros_like(low_ref)
    high_ref[...] = jnp.zeros_like(high_ref)
    for half in range(2):
        corner = inner + sy + 1
        low_ref[half, :sy, :] = total_ref[half, :sy, :]
        low_ref[half, sy : sy + 1, :] = total_ref[half, corner : corner + 1, :]
        high_ref[half, : sy + 1, :] = total_ref[half, inner : inner + sy + 1, :]


def add_faces_x(cells, total_ref, below_ref, above_ref, order_ref, out_ref, low_ref, high_ref):
    sx, sy, inner = cells.sx, cells.sy, cells.inner
    corner = inner + sy + 1
    out_ref[...] = total_ref[...]
    low_ref[...] = jnp.zeros_like(low_ref)
    high_ref[...] = jnp.zeros_like(high_ref)
    for half in range(2):
        out_ref[half, :sy, :] += below_ref[half, :sy, :]
        out_ref[half, corner : corner + 1, :] += below_ref[half, sy : sy + 1, :]
        out_ref[half, inner : inner + sy + 1, :] += above_ref[half, : sy + 1, :]
        low_ref[half, :sx, :] = out_ref[half, pl.ds(0, sx, stride=sy), :]
        low_ref[half, sx : sx + 1, :] = out_ref[half, inner : inner + 1, :]
        high_ref[half, :sx, :] = out_ref[half, corner : corner + sx, :]
        high_ref[half, sx : sx + 1, :] = out_ref[half, inner + sy : inner + sy + 1, :]


def add_faces_y(cells, total_ref, below_ref, above_ref, out_ref, face_ref, sums):
    sx, sy, nz, inner = cells.sx, cells.sy, cells.nz, cells.inner
    corner = inner + sy + 1
    sums[...] = total_ref[...]
    for half in range(2):
        sums[half, pl.ds(0, sx, stride=sy), :] += below_ref[half, :sx, :]
        sums[half, inner : inner + 1, :] += below_ref[half, sx : sx + 1, :]
        sums[half, corner : corner + sx, :] += above_ref[half, :sx, :]
        sums[half, inner + sy : inner + sy + 1, :] += above_ref[half, sx : sx + 1, :]
    main = sums[0].T
    rest = sums[1].T
    out_ref[:LANES, :] = main
    out_ref[LANES : LANES + nz, :] = rest[nz : 2 * nz]
    out_ref[LANES + nz :, :] = jnp.zeros((GROUP, cells.rows), f32)
    out_ref[LANES + nz : LANES + nz + 4, :] = rest[:4]
    face_ref[...] = jnp.zeros_like(face_ref)
    for c in range(5):
        face_ref[c : c + 1, :] = out_ref[c * nz : c * nz + 1, :]
        face_ref[GROUP + c : GROUP + c + 1, :] = out_ref[5 * nz + c : 5 * nz + c + 1, :]


def cell_table(cells, total_ref, below_ref, above_ref, table_ref, sheet, edge):
    nz, inner, height = cells.nz, cells.inner, cells.height
    row_ids = lax.broadcasted_iota(jnp.int32, (nz, cells.rows), 0)
    parts = []
    tops = []
    for c in range(5):
        face = jnp.where(row_ids == 0, below_ref[GROUP + c : GROUP + c + 1, :], 0.0)
        parts.append(total_ref[c * nz : (c + 1) * nz, :] + face)
        tops.append(
            total_ref[5 * nz + c : 5 * nz + c + 1, :] + above_ref[c : c + 1, :]
        )
    mass = jnp.maximum(parts[0], 1.0)
    top_mass = jnp.maximum(tops[0], 1.0)
    values = [parts[4]] + [p / mass for p in parts[1:4]]
    top_values = [tops[4]] + [t / top_mass for t in tops[1:4]]
    sheet[...] = jnp.zeros_like(sheet)
    edge[...] = jnp.zeros_like(edge)
    lane = lax.broadcasted_iota(jnp.int32, (cells.extra, LANES), 1)
    spare = LANES - (cells.rows - inner)
    for c in range(4):
        base = c * height
        sheet[base : base + nz, :] = values[c][:, :inner]
        sheet[base + nz : base + nz + 1, :] = top_values[c][:, :inner]
        edge[base : base + nz, :] = jnp.concatenate(
            [values[c][:, inner:], jnp.zeros((nz, spare), f32)], axis=1
        )
        edge[base + nz : base + nz + 1, :] = jnp.concatenate(
            [top_values[c][:, inner:], jnp.zeros((1, spare), f32)], axis=1
        )
        folded = [jnp.zeros((cells.extra, LANES), f32) for _ in range(inner // LANES)]
        for m in range(cells.per):
            begin = m * cells.edges
            piece = edge[pl.ds(base + m, cells.extra, stride=cells.per), :]
            piece = pltpu.roll(piece, begin % LANES, axis=1) if begin % LANES else piece
            for t in range(inner // LANES):
                low, high = begin - t * LANES, begin + cells.edges - t * LANES
                if high > 0 and low < LANES:
                    folded[t] = jnp.where((lane >= low) & (lane < high), piece, folded[t])
        sheet[base + nz + 1 : base + nz + 1 + cells.extra, :] = jnp.concatenate(folded, axis=1)
    whole = sheet[...]
    high = whole.astype(bf16).astype(f32)
    low = (whole - high)[height:]
    table_ref[...] = jnp.concatenate([high, low], axis=0).astype(bf16)


def direction_table():
    counter = jnp.arange(LANES).astype(f32)
    height = 1.0 - (2.0 * counter + 1.0) / NAXES
    radius = jnp.sqrt(jnp.maximum(1.0 - height * height, 0.0))
    rows = jnp.stack([radius * jnp.cos(golden * counter), radius * jnp.sin(golden * counter)])
    return jnp.broadcast_to(rows[:, None], (2, GROUP, LANES))


def fold_rows(values):
    sub = lax.broadcasted_iota(jnp.int32, (GROUP, LANES), 0)
    step = GROUP // 2
    while step:
        upper = (sub & step) == 0
        half = len(values) // 2
        joined = []
        for a, b in zip(values[:half], values[half:]):
            a = a + pltpu.roll(a, GROUP - step, axis=0)
            b = b + pltpu.roll(b, step, axis=0)
            joined.append(jnp.where(upper, a, b))
        values = joined
        step //= 2
    return values[0]


def collide(position, velocity, meta, table, dirs_ref, cells):
    height = cells.height
    row, column = place_of(levels_of(position, meta), cells)
    found = lax.dot_general(
        table, one_hot(column, cells.inner), NN, preferred_element_type=f32
    )
    ids = lax.broadcasted_iota(jnp.int32, (height, LANES), 0).astype(f32)
    picked = [[] for _ in range(4)]
    for r in range(GROUP):
        block = found[:, r * LANES : (r + 1) * LANES]
        here = ids == row[r : r + 1]
        for c in range(4):
            value = block[c * height : (c + 1) * height]
            if c > 0:
                value = value + block[(3 + c) * height : (4 + c) * height]
            value = jnp.where(here, value, 0.0)
            picked[c].append(
                jnp.sum(value.reshape(height // GROUP, GROUP, LANES), axis=0)
            )
    picked = [fold_rows(p) for p in picked]
    axis, flow = picked[0].astype(jnp.int32), picked[1:]
    normal = [
        jnp.take_along_axis(dirs_ref[0], axis, axis=1, mode="promise_in_bounds"),
        jnp.take_along_axis(dirs_ref[1], axis, axis=1, mode="promise_in_bounds"),
        1.0 - (2.0 * picked[0] + 1.0) * (1.0 / NAXES),
    ]
    rel = [velocity[d] - flow[d] for d in range(3)]
    along = (1.0 - turn_cosine) * (
        normal[0] * rel[0] + normal[1] * rel[1] + normal[2] * rel[2]
    )
    result = []
    for d in range(3):
        e, f = (d + 1) % 3, (d + 2) % 3
        crossed = normal[e] * rel[f] - normal[f] * rel[e]
        result.append(
            flow[d] + (turn_cosine * rel[d] + turn_sine * crossed + along * normal[d])
        )
    return result


def passed(position, speed):
    return position - jnp.floor(position) - 0.5 + 3.0 * step_size * speed


def writing(spans, refs, sems):
    copies = []
    for k, ((first, count), (value, out)) in enumerate(zip(spans, refs)):
        copies.append(
            pltpu.make_async_copy(value, out.at[:, pl.ds(first, count), :], sems.at[k])
        )
    for copy in copies:
        copy.start()

    def finish():
        for copy in copies:
            copy.wait()

    return finish


def collide_residents(
    cells, first, count, before, meta_ref, dirs_ref, table_ref, pos_ref, vel_ref, *refs
):
    out_pos, out_vel, new_pos, new_vel, token, sems = refs[-6:]
    finish = writing([before] * 2, [(refs[0], out_pos), (refs[1], out_vel)], sems) if before else None
    token[...] = jnp.zeros_like(token)
    meta = [meta_ref[k] for k in range(8)]
    table = table_ref[...]
    live_rows = meta[6] - first
    new_pos[...] = jnp.zeros_like(new_pos)
    new_vel[...] = jnp.zeros_like(new_vel)
    stride = GROUP * TWIN

    @pl.loop(0, jnp.clip((live_rows + stride - 1) // stride, 0, count // stride))
    def _(step):
        for part in range(TWIN):
            offset = pl.multiple_of(step * stride + part * GROUP, GROUP)
            rows = pl.ds(first + offset, GROUP)
            position = [pos_ref[d, rows, :] for d in range(3)]
            velocity = [vel_ref[d, rows, :] for d in range(3)]
            live = row_iota() + offset < live_rows
            speed = collide(position, velocity, meta, table, dirs_ref, cells)
            rows = pl.ds(offset, GROUP)
            for d in range(3):
                new_vel[d, rows, :] = jnp.where(live, speed[d], 0.0)
                new_pos[d, rows, :] = jnp.where(live, passed(position[d], speed[d]), 0.0)

    if finish:
        finish()


def collide_held(
    cells, first, count, many, before, meta_ref, dirs_ref, table_ref, held, counts_ref, *refs
):
    if before:
        out_pos, out_vel, out_ref, token, sems = refs[-5:]
        finish = writing([before] * 2, [(refs[0], out_pos), (refs[1], out_vel)], sems)
    else:
        out_ref, token = refs[-2:]
        finish = None
    token[...] = jnp.zeros_like(token)
    meta = [meta_ref[k] for k in range(8)]
    table = table_ref[...]
    out_ref[...] = jnp.zeros_like(out_ref)
    end = sum([counts_ref[k] for k in range(many)], jnp.int32(0)) - first
    stride = GROUP * TRIO

    @pl.loop(0, jnp.clip((end + stride - 1) // stride, 0, count // stride))
    def _(step):
        for part in range(TRIO):
            offset = pl.multiple_of(step * stride + part * GROUP, GROUP)
            comps = [held[c, pl.ds(first + offset, GROUP), :] for c in range(6)]
            speed = collide(comps[:3], comps[3:], meta, table, dirs_ref, cells)
            for d in range(3):
                out_ref[d, pl.ds(offset, GROUP), :] = speed[d]
                out_ref[3 + d, pl.ds(offset, GROUP), :] = passed(comps[d], speed[d])

    if finish:
        finish()


def place_arrivals(face_rows, sequence, counts_ref, *refs):
    pieces = refs[:-4]
    new_pos, new_vel, token, packed = refs[-4:]
    token[...] = jnp.zeros_like(token)
    packed[...] = jnp.zeros_like(packed)
    at = 0
    for piece in pieces:
        packed[:, at : at + piece.shape[1], :] = piece[...]
        at += piece.shape[1]
    rows = lax.broadcasted_iota(jnp.int32, (face_rows, LANES), 0)
    offset = 0
    for k, face in enumerate(sequence):
        count = counts_ref[k]
        place = slice(face * face_rows, (face + 1) * face_rows)
        for d in range(3):
            speed = packed[d, pl.ds(offset, face_rows), :]
            moved = packed[3 + d, pl.ds(offset, face_rows), :]
            new_vel[d, place, :] = jnp.where(rows < count, speed, 0.0)
            new_pos[d, place, :] = jnp.where(rows < count, moved, 0.0)
        offset = offset + count


def pack_inputs(
    meta_ref,
    pos_ref,
    vel_ref,
    bead_pos_ref,
    bead_vel_ref,
    bond_ref,
    order_ref,
    start_ref,
    block_ref,
    rows_pos_ref,
    rows_vel_ref,
    *refs,
):
    out_refs, (held_pos, held_vel, sems) = refs[:6], refs[6:]
    copies = [(bead_pos_ref, held_pos), (bead_vel_ref, held_vel)]
    for face, out_ref in enumerate(out_refs):
        copies.append((pos_ref.at[:, face], out_ref.at[0:3]))
        copies.append((vel_ref.at[:, face], out_ref.at[3:6]))
    copies = [pltpu.make_async_copy(a, b, sems.at[k]) for k, (a, b) in enumerate(copies)]
    for copy in copies:
        copy.start()
    for face, out_ref in enumerate(out_refs):
        out_ref[6] = jnp.full(out_ref.shape[1:], meta_ref[8 + face], jnp.int32).astype(f32)
    slots = start_ref.shape[1]
    start_ref[...] = jnp.zeros_like(start_ref)
    rows_pos_ref[...] = jnp.zeros_like(rows_pos_ref)
    rows_vel_ref[...] = jnp.zeros_like(rows_vel_ref)
    for copy in copies:
        copy.wait()
    for d in range(3):
        for k in range(slots // LANES):
            lanes = slice(k * LANES, (k + 1) * LANES)
            start_ref[d : d + 1, lanes] = held_pos[d, k : k + 1, :]
            rows_pos_ref[d, k : k + 1, :] = held_pos[d, k : k + 1, :]
            rows_vel_ref[d, k : k + 1, :] = held_vel[d, k : k + 1, :]
    bond_slots = bond_ref.shape[-1]
    ends = jnp.concatenate(
        [bond_ref[k, 0, 0, :, :].astype(f32) for k in range(2)]
        + [jnp.zeros((GROUP - 2, bond_slots), f32)],
        axis=0,
    )
    if bond_slots < slots:
        ends = jnp.concatenate([ends, jnp.zeros((GROUP, slots - bond_slots), f32)], axis=1)
    start = start_ref[...]
    whole = payload(start, slot_live(slots, meta_ref[7], GROUP), ends)
    for k in range(slots // LANES):
        block_ref[k * GROUP : (k + 1) * GROUP, :] = whole[:, k * LANES : (k + 1) * LANES]


def stack_rows(parts, *refs):
    out_ref = refs[-1]
    at = 0
    for which, begin, count in parts:
        out_ref[at : at + count, :] = refs[which][begin : begin + count, :]
        at += count


def slot_live(slots, chains, rows):
    return lax.broadcasted_iota(jnp.int32, (rows, slots), 1) < CHAIN * chains


def payload(position, live, more):
    row_ids = lax.broadcasted_iota(jnp.int32, position.shape, 0)
    flag = jnp.where(live, 1.0, 0.0)
    rest = pltpu.roll(more, 4, axis=0)
    return jnp.where(row_ids == 3, flag, jnp.where(row_ids < 3, position, rest))


def thirds_of(value):
    high = value.astype(bf16).astype(f32)
    middle = (value - high).astype(bf16).astype(f32)
    low = value - high - middle
    return jnp.concatenate([high, middle, low, jnp.zeros_like(value)], axis=0).astype(bf16)


def summed_thirds(value):
    rows = value.shape[0] // 4
    return value[:rows] + (value[rows : 2 * rows] + value[2 * rows : 3 * rows])


def joins_of(block, chains, bond_slots):
    ends = block.T
    slots = block.shape[1]
    slot_ids = lax.broadcasted_iota(jnp.int32, (slots, slots), 1).astype(f32)
    bond_ids = lax.broadcasted_iota(jnp.int32, (slots, slots), 0)
    joins = jnp.where(slot_ids == ends[:, 4:5], 1.0, 0.0)
    joins = joins - jnp.where(slot_ids == ends[:, 5:6], 1.0, 0.0)
    live = jnp.minimum((CHAIN - 1) * chains, bond_slots)
    return jnp.where(bond_ids < live, joins, 0.0).astype(bf16)


def bond_forces(local, joins, chains):
    stretch = summed_thirds(
        lax.dot_general(thirds_of(local), joins, NT, preferred_element_type=f32)
    )
    square = (
        stretch[0:1] * stretch[0:1] + stretch[1:2] * stretch[1:2] + stretch[2:3] * stretch[2:3]
    )
    live = lax.broadcasted_iota(jnp.int32, (1, joins.shape[0]), 1) < (CHAIN - 1) * chains
    pull = jnp.where(live, -spring / (1.0 - square / reach_square), 0.0) * stretch
    return summed_thirds(lax.dot_general(thirds_of(pull), joins, NN, preferred_element_type=f32))


def forces(blocks, counts, joins, mains, home, centre, lengths, mine_ref, packed, push, near_mask):
    slots = blocks[0].shape[1]
    tiles = slots // LANES
    row_ids = lax.broadcasted_iota(jnp.int32, (GROUP, slots), 0)
    lane_ids = lax.broadcasted_iota(jnp.int32, (GROUP, slots), 1)
    mid = jnp.zeros((GROUP, slots), f32)
    length = jnp.full((GROUP, slots), 1e9, f32)
    for d in range(3):
        mid = jnp.where(row_ids == d, centre[d], mid)
        if d < 2:
            length = jnp.where(row_ids == d, lengths[d], length)
    inverse_length = 1.0 / length
    near = [block - mid for block in blocks[:home]]
    for block in blocks[home:]:
        rows = block.shape[0]
        value = block - mid[:rows]
        near.append(value - length[:rows] * jnp.floor(value * inverse_length[:rows] + 0.5))

    low = jnp.full((GROUP, slots), far_ghost, f32)
    high = jnp.full((GROUP, slots), -far_ghost, f32)
    bonds = []
    for b in range(mains):
        live = lane_ids < counts[b]
        columns = jnp.where(live, near[b], far_own).T
        for d in range(3):
            mine_ref[d, b * slots : (b + 1) * slots, :] = jnp.broadcast_to(
                columns[:, d : d + 1], (slots, LANES)
            )
        low = jnp.minimum(low, jnp.where(live, near[b], far_ghost))
        high = jnp.maximum(high, jnp.where(live, near[b], -far_ghost))
        local = jnp.where(live & (row_ids < 3), near[b], 0.0)
        bonds.append(bond_forces(local, joins[b], counts[b] // CHAIN))

    packed[...] = jnp.full(packed.shape, far_ghost, f32)
    lane = lax.broadcasted_iota(jnp.int32, (GROUP, LANES), 1)
    offset = jnp.int32(0)
    for value, count in zip(near[:home], counts[:home]):
        tile, turn = offset // LANES, offset % LANES
        turned = [
            pltpu.roll(value[:, k * LANES : (k + 1) * LANES], turn, axis=1)
            for k in range(tiles)
        ]
        for k in range(tiles + 1):
            if k == 0:
                piece = turned[0]
            elif k == tiles:
                piece = turned[-1]
            else:
                piece = jnp.where(lane < turn, turned[k - 1], turned[k])
            place = (tile + k) * LANES + lane
            taken = (place >= offset) & (place < offset + count)
            packed[tile + k] = jnp.where(taken, piece, packed[tile + k])
        offset = offset + count
    first_tile = (offset + LANES - 1) // LANES

    reach = 1.001 * math.sqrt(cut_square)
    low = jnp.min(low, axis=1, keepdims=True) - reach
    high = jnp.max(high, axis=1, keepdims=True) + reach
    others = near[home:]
    near_mask[...] = jnp.zeros_like(near_mask)
    for k, value in enumerate(others):
        inside = jnp.where((value >= low[:SENT]) & (value <= high[:SENT]), 1.0, 0.0)
        inside = inside[0:1] * inside[1:2]
        live = lane_ids[0:1] < counts[home + k]
        near_mask[k : k + 1, :] = jnp.where(live, inside, 0.0)
    mask = near_mask[...]
    height = mask.shape[0]
    mask_bf16 = mask.astype(bf16)
    upto = jnp.where(
        lax.broadcasted_iota(jnp.int32, (slots, slots), 0)
        <= lax.broadcasted_iota(jnp.int32, (slots, slots), 1),
        1.0,
        0.0,
    ).astype(bf16)
    above = jnp.where(
        lax.broadcasted_iota(jnp.int32, (height, height), 1)
        < lax.broadcasted_iota(jnp.int32, (height, height), 0),
        1.0,
        0.0,
    ).astype(bf16)
    within = lax.dot_general(mask_bf16, upto, NN, preferred_element_type=f32)
    before = lax.dot_general(above, mask_bf16, NN, preferred_element_type=f32)
    before = jnp.sum(before, axis=1, keepdims=True)
    place = jnp.where(mask > 0.5, within + before - 1.0, -1.0)
    found = jnp.sum(mask).astype(jnp.int32)
    parts = jnp.concatenate([thirds_of(value) for value in others], axis=1)
    found_tiles = (found + LANES - 1) // LANES

    @pl.loop(0, found_tiles)
    def _(tile):
        goal = place - (tile * LANES).astype(f32)
        rows = [
            goal[k : k + 1, t * LANES : (t + 1) * LANES]
            for k in range(len(others))
            for t in range(tiles)
        ]
        chosen = one_hot_rows(rows, LANES)
        value = summed_thirds(
            lax.dot_general(parts, chosen, NT, preferred_element_type=f32)
        )
        there = tile * LANES + lane[:SENT] < found
        packed[first_tile + tile, :SENT, :] = jnp.where(there, value, far_ghost)

    push[...] = jnp.zeros_like(push)
    chunk = 64
    steps = (first_tile + found_tiles + 1) // 2
    period = lengths[2]

    for b in range(mains):

        @pl.loop(0, (counts[b] + chunk - 1) // chunk)
        def _(part):
            rows = pl.ds(pl.multiple_of(b * slots + part * chunk, chunk), chunk)
            mine = [mine_ref[d, rows, :] for d in range(3)]

            def add_tiles(step, total):
                for k in range(2):
                    other = packed[2 * step + k]
                    differ = [mine[d] - other[d : d + 1] for d in range(3)]
                    differ[2] = differ[2] - period * jnp.floor(
                        differ[2] * (1.0 / period) + 0.5
                    )
                    square = (
                        differ[0] * differ[0] + differ[1] * differ[1] + differ[2] * differ[2]
                    )
                    inside = (square < cut_square) & (square > 0.25)
                    inverse = 1.0 / jnp.where(inside, square, 1e30)
                    sixth = inverse * inverse * inverse
                    weight = (sixth * inverse) * (48.0 * sixth - 24.0)
                    total = tuple(total[d] + weight * differ[d] for d in range(3))
                return total

            total = lax.fori_loop(
                0, steps, add_tiles, tuple(jnp.zeros((chunk, LANES), f32) for _ in range(3))
            )
            for d in range(3):
                push[d, rows, :] = total[d]

    result = []
    for b in range(mains):
        pair = jnp.zeros((GROUP, slots), f32)
        for d in range(3):
            line = jnp.sum(push[d, b * slots : (b + 1) * slots, :].T, axis=0, keepdims=True)
            pair = jnp.where(row_ids == d, line, pair)
        result.append(pair + bonds[b])
    return result


def force_scratch(slots, blocks, home, mains):
    tiles = home * slots // LANES + 2 + (blocks - home) * slots // LANES
    return [
        pltpu.VMEM((3, mains * slots, LANES), f32),
        pltpu.VMEM((-(-tiles // 2) * 2, GROUP, LANES), f32),
        pltpu.VMEM((3, mains * slots, LANES), f32),
        pltpu.VMEM((-(-(blocks - home) // 16) * 16, slots), f32),
    ]


def blocks_of(home, home_ref, refs):
    others = [
        ref[b * SENT : (b + 1) * SENT, :]
        for ref in refs
        for b in range(ref.shape[0] // SENT)
    ]
    return [home_ref[b * GROUP : (b + 1) * GROUP, :] for b in range(home)] + others[home:]


def centre_of(meta, sizes):
    return [meta[3 + d].astype(f32) + 0.5 * sizes[d] for d in range(3)]


def joined_blocks(ref, rows, tiles):
    return [
        jnp.concatenate(
            [ref[(b * tiles + k) * rows : (b * tiles + k + 1) * rows, :] for k in range(tiles)],
            axis=1,
        )
        for b in range(ref.shape[0] // (rows * tiles))
    ]


def first_forces(sizes, lengths, sources, home, bond_slots, meta_ref, home_ref, *refs):
    sources_refs, (push_ref, counts_ref, joins_ref, starts_ref), scratch = (
        refs[:sources],
        refs[sources : sources + 4],
        refs[sources + 4 :],
    )
    meta = [meta_ref[k] for k in range(8)]
    tiles = push_ref.shape[1] // LANES
    blocks = [block for ref in sources_refs for block in joined_blocks(ref, SENT, tiles)]
    blocks = joined_blocks(home_ref, GROUP, tiles) + blocks[home:]
    counts = [jnp.sum(block[3:4]).astype(jnp.int32) for block in blocks]
    for k, count in enumerate(counts):
        counts_ref[k] = count
    joins = []
    for b in range(home):
        starts_ref[b * GROUP : (b + 1) * GROUP, :] = blocks[b]
        joins.append(joins_of(blocks[b], counts[b] // CHAIN, bond_slots))
        joins_ref[b] = joins[b]
    push_ref[...] = forces(
        blocks, counts, joins, 1, home, centre_of(meta, sizes), lengths, *scratch
    )[0]


def finish_cells(
    cells,
    meta_ref,
    dirs_ref,
    total_ref,
    below_ref,
    above_ref,
    bead_pos_ref,
    bead_vel_ref,
    start_ref,
    push_ref,
    table_ref,
    speed_ref,
    moved_ref,
    pay_ref,
    sheet,
    edge,
):
    meta = [meta_ref[k] for k in range(8)]
    cell_table(cells, total_ref, below_ref, above_ref, table_ref, sheet, edge)
    fresh = collide(
        [bead_pos_ref[d] for d in range(3)],
        [bead_vel_ref[d] for d in range(3)],
        meta,
        table_ref[...],
        dirs_ref,
        cells,
    )
    start = start_ref[...]
    slots = start.shape[1]
    row_ids = lax.broadcasted_iota(jnp.int32, (GROUP, slots), 0)
    speed = jnp.zeros((GROUP, slots), f32)
    for d in range(3):
        line = jnp.concatenate([fresh[d][k : k + 1] for k in range(slots // LANES)], axis=1)
        speed = jnp.where(row_ids == d, line, speed)
    speed = speed + half_kick * push_ref[...]
    moved = step_size * speed
    live = slot_live(slots, meta[7], GROUP)
    speed_ref[...] = speed
    moved_ref[...] = moved
    pay_ref[...] = payload(start + moved, live, speed)


def substep(
    sizes, lengths, sources, home, step, last, meta_ref, start_ref, joins_ref, counts_ref, speed_ref, moved_ref, *refs
):
    came, rest = refs[:sources], refs[sources:]
    if last:
        new_pos, new_vel, _, _, *outs, sems, a, b, c, e = rest
        finish = writing([last] * 2, [(new_pos, outs[2]), (new_vel, outs[3])], sems)
    else:
        _, *outs, a, b, c, e = rest
    meta = [meta_ref[k] for k in range(8)]
    blocks = blocks_of(home, came[0], came[1:])
    counts = [counts_ref[k] for k in range(len(blocks))]
    mains = 1 if last else home
    joins = [joins_ref[b] for b in range(mains)]
    pushes = forces(
        blocks, counts, joins, mains, home, centre_of(meta, sizes), lengths, a, b, c, e
    )
    slots = start_ref.shape[1]
    row_ids = lax.broadcasted_iota(jnp.int32, (GROUP, slots), 0)
    for b in range(mains):
        rows = slice(b * GROUP, (b + 1) * GROUP)
        live = lax.broadcasted_iota(jnp.int32, (GROUP, slots), 1) < counts[b]
        start = start_ref[rows, :]
        if step == 0 and b > 0:
            speed = jnp.where(row_ids < 3, pltpu.roll(blocks[b], 4, axis=0), 0.0)
            moved = step_size * speed
        else:
            speed, moved = speed_ref[rows, :], moved_ref[rows, :]
        speed = speed + half_kick * pushes[b]
        if last:
            for d in range(3):
                outs[0][d, 0, 0, :, :] = jnp.where(live, speed, 0.0)[d : d + 1]
                outs[1][d, 0, 0, :, :] = jnp.where(live, moved, 0.0)[d : d + 1]
            finish()
            return
        speed = speed + half_kick * pushes[b]
        moved = moved + step_size * speed
        outs[0][rows, :] = speed
        outs[1][rows, :] = moved
        outs[2][rows, :] = payload(start + moved, live, speed)


def neighbours(value, axis):
    peers = lax.axis_size(axis)
    if peers == 2:
        return [moved_along(value, axis, 1)]
    return [moved_along(value, axis, 1), moved_along(value, axis, -1)]


def stacked(parts, operands, order=()):
    rows = sum(count for _, _, count in parts)
    width = operands[0].shape[1]
    return pl.pallas_call(
        functools.partial(stack_rows, tuple(parts)),
        out_shape=like(rows, width),
        in_specs=[vmem()] * len(operands) + [pl.BlockSpec(memory_space=pl.ANY)] * len(order),
        out_specs=vmem(),
        compiler_params=params(),
        name="stack_rows",
    )(*operands, *order)


def whole_rows(operands):
    return [(k, 0, value.shape[0]) for k, value in enumerate(operands)]


def halo(pay, axes, home, pieces):
    rows = pay
    axes, pieces = list(axes), list(pieces)
    if axes[0] == "gz":
        parts = [pay] + neighbours(pay, "gz")
        rows = stacked(whole_rows(parts), parts, [pieces.pop(0)()])
        axes.pop(0)
    count = rows.shape[0] // GROUP
    sent = stacked([(0, b * GROUP, SENT) for b in range(count)], [rows])
    for axis, piece in zip(axes[:-1], pieces):
        parts = [sent] + neighbours(sent, axis)
        sent = stacked(whole_rows(parts), parts, [piece()])
    sides = neighbours(sent, axes[-1])
    own = rows if count == home else pay
    return [own, sent] + sides, pieces[-1]()


def like(*shape, dtype=f32):
    return jax.ShapeDtypeStruct(shape, dtype)


def shards(
    sol_pos,
    sol_vel,
    sol_rows,
    mig_pos,
    mig_vel,
    mig_rows,
    bead_pos,
    bead_vel,
    bead_chains,
    bond_list,
    cell_axis,
    shift,
):
    sizes = cell_axis.shape
    cells = Cells(*sizes)
    names = ("gx", "gy", "gz")
    lengths = tuple(float(sizes[d] * lax.axis_size(names[d])) for d in range(3))
    slots_here = sol_pos.shape[-1]
    buffer_slots = mig_pos.shape[-1]
    bead_slots = bead_pos.shape[-1]
    bond_slots = bond_list.shape[-1]
    rows_here = slots_here // LANES
    face_rows = buffer_slots // LANES
    rows_all = rows_here + 6 * face_rows
    anchor = jnp.stack([lax.axis_index(names[d]) * sizes[d] for d in range(3)])
    meta = jnp.concatenate(
        [
            shift,
            anchor.astype(jnp.int32),
            sol_rows.reshape(1),
            bead_chains.reshape(1),
            mig_rows.reshape(6),
        ]
    )
    dirs = direction_table()
    position = sol_pos.reshape(3, rows_here, LANES)
    velocity = sol_vel.reshape(3, rows_here, LANES)

    any_spec = pl.BlockSpec(memory_space=pl.ANY)
    thirds = 3
    count = rows_here // thirds
    axis_rows = cell_axis.reshape(cells.inner, sizes[2])

    def bin_piece(piece, earlier, order):
        sources = [position, velocity] if piece else [position[:, :count], velocity[:, :count]]
        return pl.pallas_call(
            functools.partial(bin_residents, cells, piece * count, count),
            out_shape=like(cells.rows, 2 * LANES),
            in_specs=[smem()]
            + [vmem()] * (2 + len(earlier))
            + [any_spec] * len(order),
            out_specs=vmem(),
            compiler_params=params(),
            name=f"bin_residents_{piece}",
        )(meta, *sources, *earlier, *order)

    totals = bin_piece(0, [], [])
    face_height = 7 * face_rows
    bead_shape = like(GROUP, bead_slots)
    tiles = bead_slots // LANES
    rows_shape = like(3, GROUP, LANES)
    start, block, bead_rows_pos, bead_rows_vel, *packed = pl.pallas_call(
        pack_inputs,
        out_shape=[
            bead_shape,
            like(tiles * GROUP, LANES),
            rows_shape,
            rows_shape,
        ]
        + [like(7, face_rows, LANES)] * 6,
        in_specs=[smem()]
        + [pl.BlockSpec(memory_space=pltpu.HBM)] * 4
        + [vmem(), any_spec],
        out_specs=[vmem()] * 10,
        scratch_shapes=[pltpu.VMEM((3, tiles, LANES), f32)] * 2
        + [pltpu.SemaphoreType.DMA((14,))],
        compiler_params=params(vmem_most),
        name="pack_inputs",
    )(
        meta,
        mig_pos.reshape(3, 6, face_rows, LANES),
        mig_vel.reshape(3, 6, face_rows, LANES),
        bead_pos.reshape(3, tiles, LANES),
        bead_vel.reshape(3, tiles, LANES),
        bond_list,
        totals,
    )
    packed = [value.reshape(face_height, LANES) for value in packed]

    def swap(axis, low, high, body):
        if lax.axis_size(axis) == 2:
            both = [packed[low], packed[high], body]
            came = moved_along(stacked(whole_rows(both), both), axis, 1)
            return [came], [(0, face_height), (0, 0)], [(0, 2 * face_height)]
        up = stacked(whole_rows([packed[high], body]), [packed[high], body])
        down = stacked(whole_rows([packed[low], body]), [packed[low], body])
        came = [moved_along(up, axis, 1), moved_along(down, axis, -1)]
        return came, [(0, 0), (1, 0)], [(0, face_height), (1, face_height)]

    def short(operand, first):
        return [(operand, first + k * GROUP, SENT) for k in range(tiles)]

    home = 2 if lax.axis_size("gz") == 2 else 1
    arriving, spots, blocks = [], [None] * 6, block
    for piece, (axis, low) in enumerate((("gz", 4), ("gx", 0), ("gy", 2))):
        came, places, bodies = swap(axis, low, low + 1, blocks)
        for k, (which, at) in enumerate(places):
            spots[low + k] = (len(arriving) + which, at)
        arriving += came
        height = blocks.shape[0]
        if axis == "gy":
            around = [blocks] + [stacked([(0, at, height)], [came[w]]) for w, at in bodies]
            break
        totals = bin_piece(piece + 1, [totals], [blocks])
        if axis == "gz":
            own = [(0, 0, height)] + [(1 + w, at, height) for w, at in bodies][: home - 1]
            starts = stacked(own, [blocks] + came)
            parts = short(0, 0) + [p for w, at in bodies for p in short(1 + w, at)]
        else:
            parts = [(0, 0, height)] + [(1 + w, at, height) for w, at in bodies]
        blocks = stacked(parts, [blocks] + came, [totals])

    sequence = (4, 5, 0, 1, 2, 3)
    early, late = sequence[:4], sequence[4:]
    sooner = max(spots[face][0] for face in early) + 1
    held_rows = -(-6 * face_rows // 32) * 32
    held_shape = like(6, held_rows, LANES)
    totals, held, counted = pl.pallas_call(
        functools.partial(
            bin_first_arrivals, cells, face_rows, [spots[face] for face in early]
        ),
        out_shape=[like(cells.rows, 2 * LANES), held_shape, like(4, dtype=jnp.int32)],
        in_specs=[smem()] + [vmem()] * (sooner + 3) + [any_spec],
        out_specs=[vmem(), vmem(), smem()],
        compiler_params=params(),
        name="bin_first_arrivals",
    )(meta, *arriving[:sooner], bead_rows_pos, bead_rows_vel, totals, blocks)

    face_x = like(2, -(-(sizes[1] + 1) // GROUP) * GROUP, LANES)
    face_y = like(2, -(-(sizes[0] + 1) // GROUP) * GROUP, LANES)
    later = arriving[sooner:]
    totals, low, high, held, counted = pl.pallas_call(
        functools.partial(
            bin_arrivals,
            cells,
            face_rows,
            [(spots[face][0] - sooner, spots[face][1]) for face in late],
            len(early),
        ),
        out_shape=[
            like(2, cells.rows, LANES),
            face_x,
            face_x,
            held_shape,
            like(6, dtype=jnp.int32),
        ],
        in_specs=[smem()] + [vmem()] * (len(later) + 2) + [smem(), vmem()],
        out_specs=[vmem()] * 4 + [smem()],
        scratch_shapes=[pltpu.VMEM((cells.rows, 2 * LANES), f32)],
        compiler_params=params(),
        name="bin_arrivals",
    )(meta, *later, axis_rows, held, counted, totals)

    many = sum(value.shape[0] // (SENT * tiles) for value in around)
    push, counts, joins, starts = pl.pallas_call(
        functools.partial(first_forces, sizes, lengths, len(around), home, bond_slots),
        out_shape=[
            bead_shape,
            like(many, dtype=jnp.int32),
            like(home, bead_slots, bead_slots, dtype=bf16),
            like(home * GROUP, bead_slots),
        ],
        in_specs=[smem()] + [vmem()] * (1 + len(around)),
        out_specs=[vmem(), smem(), vmem(), vmem()],
        scratch_shapes=force_scratch(bead_slots, many, home, 1),
        compiler_params=params(),
        name="first_forces",
    )(meta, starts, *around)

    below, above = moved_along(high, "gx", 1), moved_along(low, "gx", -1)
    totals, low, high = pl.pallas_call(
        functools.partial(add_faces_x, cells),
        out_shape=[like(2, cells.rows, LANES), face_y, face_y],
        in_specs=[vmem()] * 3 + [any_spec],
        out_specs=[vmem()] * 3,
        compiler_params=params(),
        name="add_faces_x",
    )(totals, below, above, push)
    below, above = moved_along(high, "gy", 1), moved_along(low, "gy", -1)
    totals, faces = pl.pallas_call(
        functools.partial(add_faces_y, cells),
        out_shape=[like(LANES + cells.nz + GROUP, cells.rows), like(2 * GROUP, cells.rows)],
        in_specs=[vmem()] * 3,
        out_specs=[vmem()] * 2,
        scratch_shapes=[pltpu.VMEM((2, cells.rows, LANES), f32)],
        compiler_params=params(),
        name="add_faces_y",
    )(totals, below, above)
    sides = neighbours(faces, "gz")
    below, above = sides[0], sides[-1]

    table, speed, moved, pay = pl.pallas_call(
        functools.partial(finish_cells, cells),
        out_shape=[
            like(7 * cells.height, cells.inner, dtype=bf16),
            bead_shape,
            bead_shape,
            bead_shape,
        ],
        in_specs=[smem()] + [vmem()] * 8,
        out_specs=[vmem()] * 4,
        scratch_shapes=[
            pltpu.VMEM((4 * cells.height, cells.inner), f32),
            pltpu.VMEM((4 * cells.height, LANES), f32),
        ],
        compiler_params=params(),
        name="finish_cells",
    )(meta, dirs, totals, below, above, bead_rows_pos, bead_rows_vel, start, push)

    solvent_shape = like(3, rows_all, LANES)
    windows = [("gz", "gx", "gy")] + [("gx", "gy") if home == 2 else ("gz", "gx", "gy")] * 2
    cuts = sum(len(axes) for axes in windows) - 3
    span = rows_here // cuts

    held_span = 2 * face_rows
    written, pending, packed_results, tokens = [], [], [], []

    def collide_piece(piece):
        token = like(GROUP, LANES)
        whole = [solvent_shape] * 2
        write_sems = [pltpu.SemaphoreType.DMA((2,))]
        if piece < cuts:
            before = ((piece - 1) * span, span) if piece else None
            extra = pending + written
            at = 5 + len(pending)
            *outs, order = pl.pallas_call(
                functools.partial(collide_residents, cells, piece * span, span, before),
                out_shape=whole + [like(3, span, LANES)] * 2 + [token],
                in_specs=[smem()] + [vmem()] * (4 + len(pending)) + [any_spec] * len(written),
                out_specs=[any_spec] * 2 + [vmem()] * 3,
                scratch_shapes=write_sems,
                input_output_aliases={at: 0, at + 1: 1} if written else {},
                compiler_params=params(),
                name=f"collide_{piece}",
            )(meta, dirs, table, position, velocity, *extra)
            written[:], pending[:] = outs[:2], outs[2:]
            tokens.append(order)
            return order
        before = ((cuts - 1) * span, span) if piece == cuts else None
        extra = pending + written if before else [tokens[-1]]
        outs = pl.pallas_call(
            functools.partial(
                collide_held, cells, (piece - cuts) * held_span, held_span, 6, before
            ),
            out_shape=(whole if before else []) + [like(6, held_span, LANES), token],
            in_specs=[smem()]
            + [vmem()] * 3
            + [smem()]
            + ([vmem()] * 2 + [any_spec] * 2 if before else [any_spec]),
            out_specs=([any_spec] * 2 if before else []) + [vmem()] * 2,
            scratch_shapes=write_sems if before else [],
            input_output_aliases={7: 0, 8: 1} if before else {},
            compiler_params=params(),
            name=f"collide_{piece}",
        )(meta, dirs, table, held, counted, *extra)
        if before:
            written[:] = outs[:2]
        packed_results.append(outs[-2])
        tokens.append(outs[-1])
        if piece < cuts + 2:
            return outs[-1]
        *pending[:], order = pl.pallas_call(
            functools.partial(place_arrivals, face_rows, sequence),
            out_shape=[like(3, 6 * face_rows, LANES)] * 2 + [token],
            in_specs=[smem()] + [vmem()] * 3,
            out_specs=[vmem()] * 3,
            scratch_shapes=[pltpu.VMEM((6, 7 * face_rows, LANES), f32)],
            compiler_params=params(),
            name="place_arrivals",
        )(counted, *packed_results)
        return order

    piece = 0
    for step, axes in enumerate(windows):
        last = step == 2
        thunks = [functools.partial(collide_piece, piece + k) for k in range(len(axes))]
        piece += len(axes)
        ghosts, order = halo(pay, axes, home, thunks)
        final = like(3, 1, 1, 1, bead_slots)
        state = like(home * GROUP, bead_slots)
        tail = pending + written if last else [order]
        at = 6 + len(ghosts) + 2
        outcome = pl.pallas_call(
            functools.partial(
                substep,
                sizes,
                lengths,
                len(ghosts),
                home,
                step,
                (rows_here, 6 * face_rows) if last else None,
            ),
            out_shape=[final] * 2 + [solvent_shape] * 2 if last else [state] * 3,
            in_specs=[smem(), vmem(), vmem(), smem()]
            + [vmem()] * (2 + len(ghosts))
            + ([vmem()] * 2 + [any_spec] * 2 if last else [any_spec]),
            out_specs=[vmem()] * 2 + [any_spec] * 2 if last else [vmem()] * 3,
            scratch_shapes=([pltpu.SemaphoreType.DMA((2,))] if last else [])
            + force_scratch(bead_slots, many, home, 1 if last else home),
            input_output_aliases={at: 2, at + 1: 3} if last else {},
            compiler_params=params(),
            name=f"substep_{step}",
        )(meta, starts, joins, counts, speed, moved, *ghosts, *tail)
        if last:
            written[:] = outcome[2:]
        speed, moved = outcome[:2]
        pay = outcome[-1]

    count_solvent = rows_all * LANES
    return (
        written[0].reshape(3, 1, 1, 1, count_solvent),
        written[1].reshape(3, 1, 1, 1, count_solvent),
        moved,
        speed,
    )


def solution(mesh):
    return jax.shard_map(
        shards,
        mesh=mesh,
        in_specs=(
            P(None, "gx", "gy", "gz", None),
            P(None, "gx", "gy", "gz", None),
            P("gx", "gy", "gz"),
            P(None, "gx", "gy", "gz", None, None),
            P(None, "gx", "gy", "gz", None, None),
            P("gx", "gy", "gz", None),
            P(None, "gx", "gy", "gz", None),
            P(None, "gx", "gy", "gz", None),
            P("gx", "gy", "gz"),
            P(None, "gx", "gy", "gz", None),
            P("gx", "gy", "gz"),
            P(),
        ),
        out_specs=(
            P(None, "gx", "gy", "gz", None),
            P(None, "gx", "gy", "gz", None),
            P(None, "gx", "gy", "gz", None),
            P(None, "gx", "gy", "gz", None),
        ),
        check_vma=False,
    )
```

```python
import functools
import math

import jax
import jax.numpy as jnp
from jax import lax
from jax.experimental import pallas as pl
from jax.experimental.pallas import tpu as pltpu
from jax.sharding import PartitionSpec as P

UNITS = 16
NAXES = 32
CHAIN = 8
LANES = 128
GROUP = 8
TWIN = 4
EIGHT = 8
SENT = 4
PAIR = 2
TRIO = 3

bead_mass = 5.0
step_size = 0.02
spring = 30.0
reach_square = 2.25
cut_square = 2.0 ** (1.0 / 3.0)
turn_cosine = math.cos(130.0 * math.pi / 180.0)
turn_sine = math.sin(130.0 * math.pi / 180.0)
golden = math.pi * (3.0 - math.sqrt(5.0))
half_kick = 0.5 * step_size / bead_mass
far_own = 3000.0
far_ghost = 9000.0
vmem_limit = 48 * 1024 * 1024
vmem_most = 48 * 1024 * 1024
NT = (((1,), (1,)), ((), ()))
NN = (((1,), (0,)), ((), ()))
exact = lax.Precision.HIGHEST
f32 = jnp.float32
bf16 = jnp.bfloat16


def params(limit=vmem_limit):
    return pltpu.CompilerParams(vmem_limit_bytes=limit)


def vmem():
    return pl.BlockSpec(memory_space=pltpu.VMEM)


def smem():
    return pl.BlockSpec(memory_space=pltpu.SMEM)


def moved_along(value, axis, by):
    peers = lax.axis_size(axis)
    return lax.ppermute(value, axis, [(i, (i + by) % peers) for i in range(peers)])


class Cells:
    def __init__(self, size_x, size_y, size_z):
        self.sx, self.sy, self.nz = size_x, size_y, size_z
        self.inner = size_x * size_y
        self.edges = size_x + size_y + 1
        self.rows = -(-(self.inner + self.edges) // 16) * 16
        self.middle = self.rows // 2
        self.per = self.inner // self.edges
        self.depths = size_z + 1
        self.extra = -(-self.depths // self.per)
        self.height = -(-(self.depths + self.extra) // GROUP) * GROUP


def levels_of(position, meta):
    return [
        jnp.floor(jnp.floor(position[d] * UNITS + meta[d].astype(f32)) * (1.0 / UNITS))
        - meta[3 + d].astype(f32)
        for d in range(3)
    ]


def edge_of(levels, cells):
    outer = (levels[0] == cells.sx) | (levels[1] == cells.sy)
    return outer, jnp.where(levels[0] == cells.sx, levels[1], cells.sy + 1 + levels[0])


def plane_of(levels, cells):
    outer, edge = edge_of(levels, cells)
    return jnp.where(outer, cells.inner + edge, levels[0] * cells.sy + levels[1])


def place_of(levels, cells):
    outer, edge = edge_of(levels, cells)
    fold = jnp.floor((levels[2] + 0.5) * (1.0 / cells.per))
    row = jnp.where(outer, cells.depths + fold, levels[2])
    column = jnp.where(
        outer,
        (levels[2] - fold * cells.per) * cells.edges + edge,
        levels[0] * cells.sy + levels[1],
    )
    return row, column


def wide(row):
    return jnp.broadcast_to(row, (16, LANES)).astype(bf16)


def one_hot_rows(rows, height):
    middle = height // 2
    ids = lax.broadcasted_iota(jnp.int32, (height, LANES), 0) - middle
    ids = ids.astype(f32).astype(bf16).reshape(height // 16, 16, LANES)
    one, zero = jnp.ones((), bf16), jnp.zeros((), bf16)
    pieces = [
        jnp.where(ids == wide(row - middle)[None], one, zero).reshape(height, LANES)
        for row in rows
    ]
    return jnp.concatenate(pieces, axis=1)


def one_hot(column, height):
    return one_hot_rows([column[r : r + 1] for r in range(column.shape[0])], height)


def split(value):
    high = value.astype(bf16).astype(f32)
    return high, value - high


def spread_moments(depth, weight, velocity, cells):
    nz = cells.nz
    ids = lax.broadcasted_iota(jnp.int32, (nz, LANES), 0).astype(f32).astype(bf16)
    ids = ids.reshape(nz // 16, 16, LANES)
    row_ids = lax.broadcasted_iota(jnp.int32, (16, LANES), 0).astype(f32).astype(bf16)
    zero = jnp.zeros((), bf16)
    parts = [split(weight * velocity[d]) for d in range(3)]
    channels = [weight] + [p[0] for p in parts] + [p[1] for p in parts]
    pieces = []
    for r in range(depth.shape[0]):
        at = wide(depth[r : r + 1])
        here = ids == at[None]
        values = [wide(c[r : r + 1]) for c in channels]
        tiles = [jnp.where(here, v[None], zero).reshape(nz, LANES) for v in values]
        top = jnp.zeros((16, LANES), bf16)
        for c, v in enumerate(values):
            top = jnp.where(row_ids == c, v, top)
        top = jnp.where(at == nz, top, zero)
        pieces.append(
            jnp.concatenate(
                tiles[:4] + [top, jnp.zeros((nz - 16, LANES), bf16)] + tiles[4:], axis=0
            )
        )
    return jnp.concatenate(pieces, axis=1)


def bin_group(total_ref, position, velocity, weight, meta, cells):
    levels = levels_of(position, meta)
    hot = one_hot(plane_of(levels, cells), cells.rows)
    spread = spread_moments(levels[2], weight, velocity, cells)
    total_ref[...] += lax.dot_general(hot, spread, NT, preferred_element_type=f32)


def row_iota():
    return lax.broadcasted_iota(jnp.int32, (GROUP, LANES), 0)


def bin_residents(cells, first, count, meta_ref, pos_ref, vel_ref, *refs):
    total_ref = refs[-1]
    meta = [meta_ref[k] for k in range(8)]
    if first == 0:
        total_ref[...] = jnp.zeros_like(total_ref)
    else:
        total_ref[...] = refs[0][...]
    live_rows = meta[6] - first
    stride = GROUP * EIGHT

    @pl.loop(0, jnp.clip((live_rows + stride - 1) // stride, 0, count // stride))
    def _(step):
        for part in range(EIGHT):
            offset = pl.multiple_of(step * stride + part * GROUP, GROUP)
            rows = pl.ds(first + offset, GROUP)
            position = [pos_ref[d, rows, :] for d in range(3)]
            velocity = [vel_ref[d, rows, :] for d in range(3)]
            weight = jnp.where(row_iota() + offset < live_rows, 1.0, 0.0)
            bin_group(total_ref, position, velocity, weight, meta, cells)


def face_count(ref, first, face_rows):
    return jnp.max(ref[pl.ds(first + 6 * face_rows, GROUP), :]).astype(jnp.int32)


def take_faces(faces, face_rows, held, counts_ref, index, offset):
    for k, (ref, first) in enumerate(faces):
        count = face_count(ref, first, face_rows)
        counts_ref[index + k] = count
        for c in range(6):
            begin = first + c * face_rows
            held[c, pl.ds(offset, face_rows), :] = ref[begin : begin + face_rows, :]
        offset = offset + count
    return offset


def bin_held(held, begin, end, sums, meta, cells):
    stride = GROUP * PAIR

    @pl.loop(0, (end - begin + stride - 1) // stride)
    def _(step):
        for part in range(PAIR):
            offset = begin + step * stride + part * GROUP
            rows = pl.ds(offset, GROUP)
            comps = [held[c, rows, :] for c in range(6)]
            weight = jnp.where(row_iota() + offset < end, 1.0, 0.0)
            bin_group(sums, comps[:3], comps[3:], weight, meta, cells)


def bead_mask(chains):
    slot = row_iota() * LANES + lax.broadcasted_iota(jnp.int32, (GROUP, LANES), 1)
    return slot < CHAIN * chains


def bin_first_arrivals(cells, face_rows, places, meta_ref, *refs):
    count = len(refs) - 7
    sources = refs[:count]
    bead_pos_ref, bead_vel_ref, start_ref, order_ref, total_ref, held, counts_ref = refs[count:]
    meta = [meta_ref[k] for k in range(8)]
    total_ref[...] = start_ref[...]
    held[...] = jnp.zeros_like(held)
    faces = [(sources[which], first) for which, first in places]
    end = take_faces(faces, face_rows, held, counts_ref, 0, 0)
    weight = jnp.where(bead_mask(meta[7]), bead_mass, 0.0)
    bin_group(
        total_ref,
        [bead_pos_ref[d] for d in range(3)],
        [bead_vel_ref[d] for d in range(3)],
        weight,
        meta,
        cells,
    )
    bin_held(held, 0, end, total_ref, meta, cells)


def bin_arrivals(cells, face_rows, places, known, meta_ref, *refs):
    count = len(refs) - 10
    sources = refs[:count]
    (
        axis_ref,
        held_ref,
        known_ref,
        start_ref,
        total_ref,
        low_ref,
        high_ref,
        held,
        counts_ref,
        sums,
    ) = refs[count:]
    meta = [meta_ref[k] for k in range(8)]
    sums[...] = start_ref[...]
    held[...] = held_ref[...]
    begin = 0
    for k in range(known):
        counts_ref[k] = known_ref[k]
        begin = begin + known_ref[k]
    faces = [(sources[which], first) for which, first in places]
    end = take_faces(faces, face_rows, held, counts_ref, known, begin)
    bin_held(held, begin, end, sums, meta, cells)
    nz, inner = cells.nz, cells.inner
    lane = lax.broadcasted_iota(jnp.int32, (cells.rows, LANES), 1)
    main, rest = sums[:, :LANES], sums[:, LANES:]
    main = main + jnp.where(lane < nz, 0.0, rest)
    top = jnp.where(lane == 0, rest, rest + pltpu.roll(rest, LANES - 3, axis=1))
    total_ref[0] = main
    total_ref[1] = jnp.where(lane < 4, top, 0.0)
    axis = axis_ref[...].astype(f32)
    total_ref[1, :inner, nz : 2 * nz] = axis
    sx, sy = cells.sx, cells.sy
    low_ref[...] = jnp.zeros_like(low_ref)
    high_ref[...] = jnp.zeros_like(high_ref)
    for half in range(2):
        corner = inner + sy + 1
        low_ref[half, :sy, :] = total_ref[half, :sy, :]
        low_ref[half, sy : sy + 1, :] = total_ref[half, corner : corner + 1, :]
        high_ref[half, : sy + 1, :] = total_ref[half, inner : inner + sy + 1, :]


def add_faces_x(cells, total_ref, below_ref, above_ref, order_ref, out_ref, low_ref, high_ref):
    sx, sy, inner = cells.sx, cells.sy, cells.inner
    corner = inner + sy + 1
    out_ref[...] = total_ref[...]
    low_ref[...] = jnp.zeros_like(low_ref)
    high_ref[...] = jnp.zeros_like(high_ref)
    for half in range(2):
        out_ref[half, :sy, :] += below_ref[half, :sy, :]
        out_ref[half, corner : corner + 1, :] += below_ref[half, sy : sy + 1, :]
        out_ref[half, inner : inner + sy + 1, :] += above_ref[half, : sy + 1, :]
        low_ref[half, :sx, :] = out_ref[half, pl.ds(0, sx, stride=sy), :]
        low_ref[half, sx : sx + 1, :] = out_ref[half, inner : inner + 1, :]
        high_ref[half, :sx, :] = out_ref[half, corner : corner + sx, :]
        high_ref[half, sx : sx + 1, :] = out_ref[half, inner + sy : inner + sy + 1, :]


def add_faces_y(cells, total_ref, below_ref, above_ref, out_ref, face_ref, sums):
    sx, sy, nz, inner = cells.sx, cells.sy, cells.nz, cells.inner
    corner = inner + sy + 1
    sums[...] = total_ref[...]
    for half in range(2):
        sums[half, pl.ds(0, sx, stride=sy), :] += below_ref[half, :sx, :]
        sums[half, inner : inner + 1, :] += below_ref[half, sx : sx + 1, :]
        sums[half, corner : corner + sx, :] += above_ref[half, :sx, :]
        sums[half, inner + sy : inner + sy + 1, :] += above_ref[half, sx : sx + 1, :]
    main = sums[0].T
    rest = sums[1].T
    out_ref[:LANES, :] = main
    out_ref[LANES : LANES + nz, :] = rest[nz : 2 * nz]
    out_ref[LANES + nz :, :] = jnp.zeros((GROUP, cells.rows), f32)
    out_ref[LANES + nz : LANES + nz + 4, :] = rest[:4]
    face_ref[...] = jnp.zeros_like(face_ref)
    for c in range(5):
        face_ref[c : c + 1, :] = out_ref[c * nz : c * nz + 1, :]
        face_ref[GROUP + c : GROUP + c + 1, :] = out_ref[5 * nz + c : 5 * nz + c + 1, :]


def cell_table(cells, total_ref, below_ref, above_ref, table_ref, sheet, edge):
    nz, inner, height = cells.nz, cells.inner, cells.height
    row_ids = lax.broadcasted_iota(jnp.int32, (nz, cells.rows), 0)
    parts = []
    tops = []
    for c in range(5):
        face = jnp.where(row_ids == 0, below_ref[GROUP + c : GROUP + c + 1, :], 0.0)
        parts.append(total_ref[c * nz : (c + 1) * nz, :] + face)
        tops.append(
            total_ref[5 * nz + c : 5 * nz + c + 1, :] + above_ref[c : c + 1, :]
        )
    mass = jnp.maximum(parts[0], 1.0)
    top_mass = jnp.maximum(tops[0], 1.0)
    values = [parts[4]] + [p / mass for p in parts[1:4]]
    top_values = [tops[4]] + [t / top_mass for t in tops[1:4]]
    sheet[...] = jnp.zeros_like(sheet)
    edge[...] = jnp.zeros_like(edge)
    lane = lax.broadcasted_iota(jnp.int32, (cells.extra, LANES), 1)
    spare = LANES - (cells.rows - inner)
    for c in range(4):
        base = c * height
        sheet[base : base + nz, :] = values[c][:, :inner]
        sheet[base + nz : base + nz + 1, :] = top_values[c][:, :inner]
        edge[base : base + nz, :] = jnp.concatenate(
            [values[c][:, inner:], jnp.zeros((nz, spare), f32)], axis=1
        )
        edge[base + nz : base + nz + 1, :] = jnp.concatenate(
            [top_values[c][:, inner:], jnp.zeros((1, spare), f32)], axis=1
        )
        folded = [jnp.zeros((cells.extra, LANES), f32) for _ in range(inner // LANES)]
        for m in range(cells.per):
            begin = m * cells.edges
            piece = edge[pl.ds(base + m, cells.extra, stride=cells.per), :]
            piece = pltpu.roll(piece, begin % LANES, axis=1) if begin % LANES else piece
            for t in range(inner // LANES):
                low, high = begin - t * LANES, begin + cells.edges - t * LANES
                if high > 0 and low < LANES:
                    folded[t] = jnp.where((lane >= low) & (lane < high), piece, folded[t])
        sheet[base + nz + 1 : base + nz + 1 + cells.extra, :] = jnp.concatenate(folded, axis=1)
    whole = sheet[...]
    high = whole.astype(bf16).astype(f32)
    low = (whole - high)[height:]
    table_ref[...] = jnp.concatenate([high, low], axis=0).astype(bf16)


def direction_table():
    counter = jnp.arange(LANES).astype(f32)
    height = 1.0 - (2.0 * counter + 1.0) / NAXES
    radius = jnp.sqrt(jnp.maximum(1.0 - height * height, 0.0))
    rows = jnp.stack([radius * jnp.cos(golden * counter), radius * jnp.sin(golden * counter)])
    return jnp.broadcast_to(rows[:, None], (2, GROUP, LANES))


def fold_rows(values):
    sub = lax.broadcasted_iota(jnp.int32, (GROUP, LANES), 0)
    step = GROUP // 2
    while step:
        upper = (sub & step) == 0
        half = len(values) // 2
        joined = []
        for a, b in zip(values[:half], values[half:]):
            a = a + pltpu.roll(a, GROUP - step, axis=0)
            b = b + pltpu.roll(b, step, axis=0)
            joined.append(jnp.where(upper, a, b))
        values = joined
        step //= 2
    return values[0]


def collide(position, velocity, meta, table, dirs_ref, cells):
    height = cells.height
    row, column = place_of(levels_of(position, meta), cells)
    found = lax.dot_general(
        table, one_hot(column, cells.inner), NN, preferred_element_type=f32
    )
    ids = lax.broadcasted_iota(jnp.int32, (height, LANES), 0).astype(f32)
    picked = [[] for _ in range(4)]
    for r in range(GROUP):
        block = found[:, r * LANES : (r + 1) * LANES]
        here = ids == row[r : r + 1]
        for c in range(4):
            value = block[c * height : (c + 1) * height]
            if c > 0:
                value = value + block[(3 + c) * height : (4 + c) * height]
            value = jnp.where(here, value, 0.0)
            picked[c].append(
                jnp.sum(value.reshape(height // GROUP, GROUP, LANES), axis=0)
            )
    picked = [fold_rows(p) for p in picked]
    axis, flow = picked[0].astype(jnp.int32), picked[1:]
    normal = [
        jnp.take_along_axis(dirs_ref[0], axis, axis=1, mode="promise_in_bounds"),
        jnp.take_along_axis(dirs_ref[1], axis, axis=1, mode="promise_in_bounds"),
        1.0 - (2.0 * picked[0] + 1.0) * (1.0 / NAXES),
    ]
    rel = [velocity[d] - flow[d] for d in range(3)]
    along = (1.0 - turn_cosine) * (
        normal[0] * rel[0] + normal[1] * rel[1] + normal[2] * rel[2]
    )
    result = []
    for d in range(3):
        e, f = (d + 1) % 3, (d + 2) % 3
        crossed = normal[e] * rel[f] - normal[f] * rel[e]
        result.append(
            flow[d] + (turn_cosine * rel[d] + turn_sine * crossed + along * normal[d])
        )
    return result


def passed(position, speed):
    return position - jnp.floor(position) - 0.5 + 3.0 * step_size * speed


def writing(spans, refs, sems):
    copies = []
    for k, ((first, count), (value, out)) in enumerate(zip(spans, refs)):
        copies.append(
            pltpu.make_async_copy(value, out.at[:, pl.ds(first, count), :], sems.at[k])
        )
    for copy in copies:
        copy.start()

    def finish():
        for copy in copies:
            copy.wait()

    return finish


def collide_residents(
    cells, first, count, before, meta_ref, dirs_ref, table_ref, pos_ref, vel_ref, *refs
):
    out_pos, out_vel, new_pos, new_vel, token, sems = refs[-6:]
    finish = writing([before] * 2, [(refs[0], out_pos), (refs[1], out_vel)], sems) if before else None
    token[...] = jnp.zeros_like(token)
    meta = [meta_ref[k] for k in range(8)]
    table = table_ref[...]
    live_rows = meta[6] - first
    new_pos[...] = jnp.zeros_like(new_pos)
    new_vel[...] = jnp.zeros_like(new_vel)
    stride = GROUP * TWIN

    @pl.loop(0, jnp.clip((live_rows + stride - 1) // stride, 0, count // stride))
    def _(step):
        for part in range(TWIN):
            offset = pl.multiple_of(step * stride + part * GROUP, GROUP)
            rows = pl.ds(first + offset, GROUP)
            position = [pos_ref[d, rows, :] for d in range(3)]
            velocity = [vel_ref[d, rows, :] for d in range(3)]
            live = row_iota() + offset < live_rows
            speed = collide(position, velocity, meta, table, dirs_ref, cells)
            rows = pl.ds(offset, GROUP)
            for d in range(3):
                new_vel[d, rows, :] = jnp.where(live, speed[d], 0.0)
                new_pos[d, rows, :] = jnp.where(live, passed(position[d], speed[d]), 0.0)

    if finish:
        finish()


def collide_held(
    cells, first, count, many, before, meta_ref, dirs_ref, table_ref, held, counts_ref, *refs
):
    if before:
        out_pos, out_vel, out_ref, token, sems = refs[-5:]
        finish = writing([before] * 2, [(refs[0], out_pos), (refs[1], out_vel)], sems)
    else:
        out_ref, token = refs[-2:]
        finish = None
    token[...] = jnp.zeros_like(token)
    meta = [meta_ref[k] for k in range(8)]
    table = table_ref[...]
    out_ref[...] = jnp.zeros_like(out_ref)
    end = sum([counts_ref[k] for k in range(many)], jnp.int32(0)) - first
    stride = GROUP * TRIO

    @pl.loop(0, jnp.clip((end + stride - 1) // stride, 0, count // stride))
    def _(step):
        for part in range(TRIO):
            offset = pl.multiple_of(step * stride + part * GROUP, GROUP)
            comps = [held[c, pl.ds(first + offset, GROUP), :] for c in range(6)]
            speed = collide(comps[:3], comps[3:], meta, table, dirs_ref, cells)
            for d in range(3):
                out_ref[d, pl.ds(offset, GROUP), :] = speed[d]
                out_ref[3 + d, pl.ds(offset, GROUP), :] = passed(comps[d], speed[d])

    if finish:
        finish()


def place_arrivals(face_rows, sequence, counts_ref, *refs):
    pieces = refs[:-4]
    new_pos, new_vel, token, packed = refs[-4:]
    token[...] = jnp.zeros_like(token)
    packed[...] = jnp.zeros_like(packed)
    at = 0
    for piece in pieces:
        packed[:, at : at + piece.shape[1], :] = piece[...]
        at += piece.shape[1]
    rows = lax.broadcasted_iota(jnp.int32, (face_rows, LANES), 0)
    offset = 0
    for k, face in enumerate(sequence):
        count = counts_ref[k]
        place = slice(face * face_rows, (face + 1) * face_rows)
        for d in range(3):
            speed = packed[d, pl.ds(offset, face_rows), :]
            moved = packed[3 + d, pl.ds(offset, face_rows), :]
            new_vel[d, place, :] = jnp.where(rows < count, speed, 0.0)
            new_pos[d, place, :] = jnp.where(rows < count, moved, 0.0)
        offset = offset + count


def pack_inputs(
    meta_ref,
    pos_ref,
    vel_ref,
    bead_pos_ref,
    bead_vel_ref,
    bond_ref,
    order_ref,
    start_ref,
    block_ref,
    rows_pos_ref,
    rows_vel_ref,
    *refs,
):
    out_refs, (held_pos, held_vel, sems) = refs[:6], refs[6:]
    copies = [(bead_pos_ref, held_pos), (bead_vel_ref, held_vel)]
    for face, out_ref in enumerate(out_refs):
        copies.append((pos_ref.at[:, face], out_ref.at[0:3]))
        copies.append((vel_ref.at[:, face], out_ref.at[3:6]))
    copies = [pltpu.make_async_copy(a, b, sems.at[k]) for k, (a, b) in enumerate(copies)]
    for copy in copies:
        copy.start()
    for face, out_ref in enumerate(out_refs):
        out_ref[6] = jnp.full(out_ref.shape[1:], meta_ref[8 + face], jnp.int32).astype(f32)
    slots = start_ref.shape[1]
    start_ref[...] = jnp.zeros_like(start_ref)
    rows_pos_ref[...] = jnp.zeros_like(rows_pos_ref)
    rows_vel_ref[...] = jnp.zeros_like(rows_vel_ref)
    for copy in copies:
        copy.wait()
    for d in range(3):
        for k in range(slots // LANES):
            lanes = slice(k * LANES, (k + 1) * LANES)
            start_ref[d : d + 1, lanes] = held_pos[d, k : k + 1, :]
            rows_pos_ref[d, k : k + 1, :] = held_pos[d, k : k + 1, :]
            rows_vel_ref[d, k : k + 1, :] = held_vel[d, k : k + 1, :]
    bond_slots = bond_ref.shape[-1]
    ends = jnp.concatenate(
        [bond_ref[k, 0, 0, :, :].astype(f32) for k in range(2)]
        + [jnp.zeros((GROUP - 2, bond_slots), f32)],
        axis=0,
    )
    if bond_slots < slots:
        ends = jnp.concatenate([ends, jnp.zeros((GROUP, slots - bond_slots), f32)], axis=1)
    start = start_ref[...]
    whole = payload(start, slot_live(slots, meta_ref[7], GROUP), ends)
    for k in range(slots // LANES):
        block_ref[k * GROUP : (k + 1) * GROUP, :] = whole[:, k * LANES : (k + 1) * LANES]


def stack_rows(parts, *refs):
    out_ref = refs[-1]
    at = 0
    for which, begin, count in parts:
        out_ref[at : at + count, :] = refs[which][begin : begin + count, :]
        at += count


def slot_live(slots, chains, rows):
    return lax.broadcasted_iota(jnp.int32, (rows, slots), 1) < CHAIN * chains


def payload(position, live, more):
    row_ids = lax.broadcasted_iota(jnp.int32, position.shape, 0)
    flag = jnp.where(live, 1.0, 0.0)
    rest = pltpu.roll(more, 4, axis=0)
    return jnp.where(row_ids == 3, flag, jnp.where(row_ids < 3, position, rest))


def thirds_of(value):
    high = value.astype(bf16).astype(f32)
    middle = (value - high).astype(bf16).astype(f32)
    low = value - high - middle
    return jnp.concatenate([high, middle, low, jnp.zeros_like(value)], axis=0).astype(bf16)


def summed_thirds(value):
    rows = value.shape[0] // 4
    return value[:rows] + (value[rows : 2 * rows] + value[2 * rows : 3 * rows])


def joins_of(block, chains, bond_slots):
    ends = block.T
    slots = block.shape[1]
    slot_ids = lax.broadcasted_iota(jnp.int32, (slots, slots), 1).astype(f32)
    bond_ids = lax.broadcasted_iota(jnp.int32, (slots, slots), 0)
    joins = jnp.where(slot_ids == ends[:, 4:5], 1.0, 0.0)
    joins = joins - jnp.where(slot_ids == ends[:, 5:6], 1.0, 0.0)
    live = jnp.minimum((CHAIN - 1) * chains, bond_slots)
    return jnp.where(bond_ids < live, joins, 0.0).astype(bf16)


def bond_forces(local, joins, chains):
    stretch = summed_thirds(
        lax.dot_general(thirds_of(local), joins, NT, preferred_element_type=f32)
    )
    square = (
        stretch[0:1] * stretch[0:1] + stretch[1:2] * stretch[1:2] + stretch[2:3] * stretch[2:3]
    )
    live = lax.broadcasted_iota(jnp.int32, (1, joins.shape[0]), 1) < (CHAIN - 1) * chains
    pull = jnp.where(live, -spring / (1.0 - square / reach_square), 0.0) * stretch
    return summed_thirds(lax.dot_general(thirds_of(pull), joins, NN, preferred_element_type=f32))


def forces(blocks, counts, joins, mains, home, centre, lengths, mine_ref, packed, push, near_mask):
    slots = blocks[0].shape[1]
    tiles = slots // LANES
    row_ids = lax.broadcasted_iota(jnp.int32, (GROUP, slots), 0)
    lane_ids = lax.broadcasted_iota(jnp.int32, (GROUP, slots), 1)
    mid = jnp.zeros((GROUP, slots), f32)
    length = jnp.full((GROUP, slots), 1e9, f32)
    for d in range(3):
        mid = jnp.where(row_ids == d, centre[d], mid)
        if d < 2:
            length = jnp.where(row_ids == d, lengths[d], length)
    inverse_length = 1.0 / length
    near = [block - mid for block in blocks[:home]]
    for block in blocks[home:]:
        rows = block.shape[0]
        value = block - mid[:rows]
        near.append(value - length[:rows] * jnp.floor(value * inverse_length[:rows] + 0.5))

    low = jnp.full((GROUP, slots), far_ghost, f32)
    high = jnp.full((GROUP, slots), -far_ghost, f32)
    bonds = []
    for b in range(mains):
        live = lane_ids < counts[b]
        columns = jnp.where(live, near[b], far_own).T
        for d in range(3):
            mine_ref[d, b * slots : (b + 1) * slots, :] = jnp.broadcast_to(
                columns[:, d : d + 1], (slots, LANES)
            )
        low = jnp.minimum(low, jnp.where(live, near[b], far_ghost))
        high = jnp.maximum(high, jnp.where(live, near[b], -far_ghost))
        local = jnp.where(live & (row_ids < 3), near[b], 0.0)
        bonds.append(bond_forces(local, joins[b], counts[b] // CHAIN))

    packed[...] = jnp.full(packed.shape, far_ghost, f32)
    lane = lax.broadcasted_iota(jnp.int32, (GROUP, LANES), 1)
    offset = jnp.int32(0)
    for value, count in zip(near[:home], counts[:home]):
        tile, turn = offset // LANES, offset % LANES
        turned = [
            pltpu.roll(value[:, k * LANES : (k + 1) * LANES], turn, axis=1)
            for k in range(tiles)
        ]
        for k in range(tiles + 1):
            if k == 0:
                piece = turned[0]
            elif k == tiles:
                piece = turned[-1]
            else:
                piece = jnp.where(lane < turn, turned[k - 1], turned[k])
            place = (tile + k) * LANES + lane
            taken = (place >= offset) & (place < offset + count)
            packed[tile + k] = jnp.where(taken, piece, packed[tile + k])
        offset = offset + count
    first_tile = (offset + LANES - 1) // LANES

    reach = 1.001 * math.sqrt(cut_square)
    low = jnp.min(low, axis=1, keepdims=True) - reach
    high = jnp.max(high, axis=1, keepdims=True) + reach
    others = near[home:]
    near_mask[...] = jnp.zeros_like(near_mask)
    for k, value in enumerate(others):
        inside = jnp.where((value >= low[:SENT]) & (value <= high[:SENT]), 1.0, 0.0)
        inside = inside[0:1] * inside[1:2]
        live = lane_ids[0:1] < counts[home + k]
        near_mask[k : k + 1, :] = jnp.where(live, inside, 0.0)
    mask = near_mask[...]
    height = mask.shape[0]
    mask_bf16 = mask.astype(bf16)
    upto = jnp.where(
        lax.broadcasted_iota(jnp.int32, (slots, slots), 0)
        <= lax.broadcasted_iota(jnp.int32, (slots, slots), 1),
        1.0,
        0.0,
    ).astype(bf16)
    above = jnp.where(
        lax.broadcasted_iota(jnp.int32, (height, height), 1)
        < lax.broadcasted_iota(jnp.int32, (height, height), 0),
        1.0,
        0.0,
    ).astype(bf16)
    within = lax.dot_general(mask_bf16, upto, NN, preferred_element_type=f32)
    before = lax.dot_general(above, mask_bf16, NN, preferred_element_type=f32)
    before = jnp.sum(before, axis=1, keepdims=True)
    place = jnp.where(mask > 0.5, within + before - 1.0, -1.0)
    found = jnp.sum(mask).astype(jnp.int32)
    parts = jnp.concatenate([thirds_of(value) for value in others], axis=1)
    found_tiles = (found + LANES - 1) // LANES

    @pl.loop(0, found_tiles)
    def _(tile):
        goal = place - (tile * LANES).astype(f32)
        rows = [
            goal[k : k + 1, t * LANES : (t + 1) * LANES]
            for k in range(len(others))
            for t in range(tiles)
        ]
        chosen = one_hot_rows(rows, LANES)
        value = summed_thirds(
            lax.dot_general(parts, chosen, NT, preferred_element_type=f32)
        )
        there = tile * LANES + lane[:SENT] < found
        packed[first_tile + tile, :SENT, :] = jnp.where(there, value, far_ghost)

    push[...] = jnp.zeros_like(push)
    chunk = 64
    steps = (first_tile + found_tiles + 1) // 2
    period = lengths[2]

    for b in range(mains):

        @pl.loop(0, (counts[b] + chunk - 1) // chunk)
        def _(part):
            rows = pl.ds(pl.multiple_of(b * slots + part * chunk, chunk), chunk)
            mine = [mine_ref[d, rows, :] for d in range(3)]

            def add_tiles(step, total):
                for k in range(2):
                    other = packed[2 * step + k]
                    differ = [mine[d] - other[d : d + 1] for d in range(3)]
                    differ[2] = differ[2] - period * jnp.floor(
                        differ[2] * (1.0 / period) + 0.5
                    )
                    square = (
                        differ[0] * differ[0] + differ[1] * differ[1] + differ[2] * differ[2]
                    )
                    inside = (square < cut_square) & (square > 0.25)
                    inverse = 1.0 / jnp.where(inside, square, 1e30)
                    sixth = inverse * inverse * inverse
                    weight = (sixth * inverse) * (48.0 * sixth - 24.0)
                    total = tuple(total[d] + weight * differ[d] for d in range(3))
                return total

            total = lax.fori_loop(
                0, steps, add_tiles, tuple(jnp.zeros((chunk, LANES), f32) for _ in range(3))
            )
            for d in range(3):
                push[d, rows, :] = total[d]

    result = []
    for b in range(mains):
        pair = jnp.zeros((GROUP, slots), f32)
        for d in range(3):
            line = jnp.sum(push[d, b * slots : (b + 1) * slots, :].T, axis=0, keepdims=True)
            pair = jnp.where(row_ids == d, line, pair)
        result.append(pair + bonds[b])
    return result


def force_scratch(slots, blocks, home, mains):
    tiles = home * slots // LANES + 2 + (blocks - home) * slots // LANES
    return [
        pltpu.VMEM((3, mains * slots, LANES), f32),
        pltpu.VMEM((-(-tiles // 2) * 2, GROUP, LANES), f32),
        pltpu.VMEM((3, mains * slots, LANES), f32),
        pltpu.VMEM((-(-(blocks - home) // 16) * 16, slots), f32),
    ]


def blocks_of(home, home_ref, refs):
    others = [
        ref[b * SENT : (b + 1) * SENT, :]
        for ref in refs
        for b in range(ref.shape[0] // SENT)
    ]
    return [home_ref[b * GROUP : (b + 1) * GROUP, :] for b in range(home)] + others[home:]


def centre_of(meta, sizes):
    return [meta[3 + d].astype(f32) + 0.5 * sizes[d] for d in range(3)]


def joined_blocks(ref, rows, tiles):
    return [
        jnp.concatenate(
            [ref[(b * tiles + k) * rows : (b * tiles + k + 1) * rows, :] for k in range(tiles)],
            axis=1,
        )
        for b in range(ref.shape[0] // (rows * tiles))
    ]


def first_forces(sizes, lengths, sources, home, bond_slots, meta_ref, home_ref, *refs):
    sources_refs, (push_ref, counts_ref, joins_ref, starts_ref), scratch = (
        refs[:sources],
        refs[sources : sources + 4],
        refs[sources + 4 :],
    )
    meta = [meta_ref[k] for k in range(8)]
    tiles = push_ref.shape[1] // LANES
    blocks = [block for ref in sources_refs for block in joined_blocks(ref, SENT, tiles)]
    blocks = joined_blocks(home_ref, GROUP, tiles) + blocks[home:]
    counts = [jnp.sum(block[3:4]).astype(jnp.int32) for block in blocks]
    for k, count in enumerate(counts):
        counts_ref[k] = count
    joins = []
    for b in range(home):
        starts_ref[b * GROUP : (b + 1) * GROUP, :] = blocks[b]
        joins.append(joins_of(blocks[b], counts[b] // CHAIN, bond_slots))
        joins_ref[b] = joins[b]
    push_ref[...] = forces(
        blocks, counts, joins, 1, home, centre_of(meta, sizes), lengths, *scratch
    )[0]


def finish_cells(
    cells,
    meta_ref,
    dirs_ref,
    total_ref,
    below_ref,
    above_ref,
    bead_pos_ref,
    bead_vel_ref,
    start_ref,
    push_ref,
    table_ref,
    speed_ref,
    moved_ref,
    pay_ref,
    sheet,
    edge,
):
    meta = [meta_ref[k] for k in range(8)]
    cell_table(cells, total_ref, below_ref, above_ref, table_ref, sheet, edge)
    fresh = collide(
        [bead_pos_ref[d] for d in range(3)],
        [bead_vel_ref[d] for d in range(3)],
        meta,
        table_ref[...],
        dirs_ref,
        cells,
    )
    start = start_ref[...]
    slots = start.shape[1]
    row_ids = lax.broadcasted_iota(jnp.int32, (GROUP, slots), 0)
    speed = jnp.zeros((GROUP, slots), f32)
    for d in range(3):
        line = jnp.concatenate([fresh[d][k : k + 1] for k in range(slots // LANES)], axis=1)
        speed = jnp.where(row_ids == d, line, speed)
    speed = speed + half_kick * push_ref[...]
    moved = step_size * speed
    live = slot_live(slots, meta[7], GROUP)
    speed_ref[...] = speed
    moved_ref[...] = moved
    pay_ref[...] = payload(start + moved, live, speed)


def substep(
    sizes, lengths, sources, home, step, last, meta_ref, start_ref, joins_ref, counts_ref, speed_ref, moved_ref, *refs
):
    came, rest = refs[:sources], refs[sources:]
    if last:
        new_pos, new_vel, _, _, *outs, sems, a, b, c, e = rest
        finish = writing([last] * 2, [(new_pos, outs[2]), (new_vel, outs[3])], sems)
    else:
        _, *outs, a, b, c, e = rest
    meta = [meta_ref[k] for k in range(8)]
    blocks = blocks_of(home, came[0], came[1:])
    counts = [counts_ref[k] for k in range(len(blocks))]
    mains = 1 if last else home
    joins = [joins_ref[b] for b in range(mains)]
    pushes = forces(
        blocks, counts, joins, mains, home, centre_of(meta, sizes), lengths, a, b, c, e
    )
    slots = start_ref.shape[1]
    row_ids = lax.broadcasted_iota(jnp.int32, (GROUP, slots), 0)
    for b in range(mains):
        rows = slice(b * GROUP, (b + 1) * GROUP)
        live = lax.broadcasted_iota(jnp.int32, (GROUP, slots), 1) < counts[b]
        start = start_ref[rows, :]
        if step == 0 and b > 0:
            speed = jnp.where(row_ids < 3, pltpu.roll(blocks[b], 4, axis=0), 0.0)
            moved = step_size * speed
        else:
            speed, moved = speed_ref[rows, :], moved_ref[rows, :]
        speed = speed + half_kick * pushes[b]
        if last:
            for d in range(3):
                outs[0][d, 0, 0, :, :] = jnp.where(live, speed, 0.0)[d : d + 1]
                outs[1][d, 0, 0, :, :] = jnp.where(live, moved, 0.0)[d : d + 1]
            finish()
            return
        speed = speed + half_kick * pushes[b]
        moved = moved + step_size * speed
        outs[0][rows, :] = speed
        outs[1][rows, :] = moved
        outs[2][rows, :] = payload(start + moved, live, speed)


def neighbours(value, axis):
    peers = lax.axis_size(axis)
    if peers == 2:
        return [moved_along(value, axis, 1)]
    return [moved_along(value, axis, 1), moved_along(value, axis, -1)]


def stacked(parts, operands, order=()):
    rows = sum(count for _, _, count in parts)
    width = operands[0].shape[1]
    return pl.pallas_call(
        functools.partial(stack_rows, tuple(parts)),
        out_shape=like(rows, width),
        in_specs=[vmem()] * len(operands) + [pl.BlockSpec(memory_space=pl.ANY)] * len(order),
        out_specs=vmem(),
        compiler_params=params(),
        name="stack_rows",
    )(*operands, *order)


def whole_rows(operands):
    return [(k, 0, value.shape[0]) for k, value in enumerate(operands)]


def halo(pay, axes, home, pieces):
    rows = pay
    axes, pieces = list(axes), list(pieces)
    if axes[0] == "gz":
        parts = [pay] + neighbours(pay, "gz")
        rows = stacked(whole_rows(parts), parts, [pieces.pop(0)()])
        axes.pop(0)
    count = rows.shape[0] // GROUP
    sent = stacked([(0, b * GROUP, SENT) for b in range(count)], [rows])
    for axis, piece in zip(axes[:-1], pieces):
        parts = [sent] + neighbours(sent, axis)
        sent = stacked(whole_rows(parts), parts, [piece()])
    sides = neighbours(sent, axes[-1])
    own = rows if count == home else pay
    return [own, sent] + sides, pieces[-1]()


def like(*shape, dtype=f32):
    return jax.ShapeDtypeStruct(shape, dtype)


def shards(
    sol_pos,
    sol_vel,
    sol_rows,
    mig_pos,
    mig_vel,
    mig_rows,
    bead_pos,
    bead_vel,
    bead_chains,
    bond_list,
    cell_axis,
    shift,
):
    sizes = cell_axis.shape
    cells = Cells(*sizes)
    names = ("gx", "gy", "gz")
    lengths = tuple(float(sizes[d] * lax.axis_size(names[d])) for d in range(3))
    slots_here = sol_pos.shape[-1]
    buffer_slots = mig_pos.shape[-1]
    bead_slots = bead_pos.shape[-1]
    bond_slots = bond_list.shape[-1]
    rows_here = slots_here // LANES
    face_rows = buffer_slots // LANES
    rows_all = rows_here + 6 * face_rows
    anchor = jnp.stack([lax.axis_index(names[d]) * sizes[d] for d in range(3)])
    meta = jnp.concatenate(
        [
            shift,
            anchor.astype(jnp.int32),
            sol_rows.reshape(1),
            bead_chains.reshape(1),
            mig_rows.reshape(6),
        ]
    )
    dirs = direction_table()
    position = sol_pos.reshape(3, rows_here, LANES)
    velocity = sol_vel.reshape(3, rows_here, LANES)

    any_spec = pl.BlockSpec(memory_space=pl.ANY)
    thirds = 3
    count = rows_here // thirds
    axis_rows = cell_axis.reshape(cells.inner, sizes[2])

    def bin_piece(piece, earlier, order):
        sources = [position, velocity] if piece else [position[:, :count], velocity[:, :count]]
        return pl.pallas_call(
            functools.partial(bin_residents, cells, piece * count, count),
            out_shape=like(cells.rows, 2 * LANES),
            in_specs=[smem()]
            + [vmem()] * (2 + len(earlier))
            + [any_spec] * len(order),
            out_specs=vmem(),
            compiler_params=params(),
            name=f"bin_residents_{piece}",
        )(meta, *sources, *earlier, *order)

    totals = bin_piece(0, [], [])
    face_height = 7 * face_rows
    bead_shape = like(GROUP, bead_slots)
    tiles = bead_slots // LANES
    rows_shape = like(3, GROUP, LANES)
    start, block, bead_rows_pos, bead_rows_vel, *packed = pl.pallas_call(
        pack_inputs,
        out_shape=[
            bead_shape,
            like(tiles * GROUP, LANES),
            rows_shape,
            rows_shape,
        ]
        + [like(7, face_rows, LANES)] * 6,
        in_specs=[smem()]
        + [pl.BlockSpec(memory_space=pltpu.HBM)] * 4
        + [vmem(), any_spec],
        out_specs=[vmem()] * 10,
        scratch_shapes=[pltpu.VMEM((3, tiles, LANES), f32)] * 2
        + [pltpu.SemaphoreType.DMA((14,))],
        compiler_params=params(vmem_most),
        name="pack_inputs",
    )(
        meta,
        mig_pos.reshape(3, 6, face_rows, LANES),
        mig_vel.reshape(3, 6, face_rows, LANES),
        bead_pos.reshape(3, tiles, LANES),
        bead_vel.reshape(3, tiles, LANES),
        bond_list,
        totals,
    )
    packed = [value.reshape(face_height, LANES) for value in packed]

    def swap(axis, low, high, body):
        if lax.axis_size(axis) == 2:
            both = [packed[low], packed[high], body]
            came = moved_along(stacked(whole_rows(both), both), axis, 1)
            return [came], [(0, face_height), (0, 0)], [(0, 2 * face_height)]
        up = stacked(whole_rows([packed[high], body]), [packed[high], body])
        down = stacked(whole_rows([packed[low], body]), [packed[low], body])
        came = [moved_along(up, axis, 1), moved_along(down, axis, -1)]
        return came, [(0, 0), (1, 0)], [(0, face_height), (1, face_height)]

    def short(operand, first):
        return [(operand, first + k * GROUP, SENT) for k in range(tiles)]

    home = 2 if lax.axis_size("gz") == 2 else 1
    arriving, spots, blocks = [], [None] * 6, block
    for piece, (axis, low) in enumerate((("gz", 4), ("gx", 0), ("gy", 2))):
        came, places, bodies = swap(axis, low, low + 1, blocks)
        for k, (which, at) in enumerate(places):
            spots[low + k] = (len(arriving) + which, at)
        arriving += came
        height = blocks.shape[0]
        if axis == "gy":
            around = [blocks] + [stacked([(0, at, height)], [came[w]]) for w, at in bodies]
            break
        totals = bin_piece(piece + 1, [totals], [blocks])
        if axis == "gz":
            own = [(0, 0, height)] + [(1 + w, at, height) for w, at in bodies][: home - 1]
            starts = stacked(own, [blocks] + came)
            parts = short(0, 0) + [p for w, at in bodies for p in short(1 + w, at)]
        else:
            parts = [(0, 0, height)] + [(1 + w, at, height) for w, at in bodies]
        blocks = stacked(parts, [blocks] + came, [totals])

    sequence = (4, 5, 0, 1, 2, 3)
    early, late = sequence[:4], sequence[4:]
    sooner = max(spots[face][0] for face in early) + 1
    held_rows = -(-6 * face_rows // 32) * 32
    held_shape = like(6, held_rows, LANES)
    totals, held, counted = pl.pallas_call(
        functools.partial(
            bin_first_arrivals, cells, face_rows, [spots[face] for face in early]
        ),
        out_shape=[like(cells.rows, 2 * LANES), held_shape, like(4, dtype=jnp.int32)],
        in_specs=[smem()] + [vmem()] * (sooner + 3) + [any_spec],
        out_specs=[vmem(), vmem(), smem()],
        compiler_params=params(),
        name="bin_first_arrivals",
    )(meta, *arriving[:sooner], bead_rows_pos, bead_rows_vel, totals, blocks)

    face_x = like(2, -(-(sizes[1] + 1) // GROUP) * GROUP, LANES)
    face_y = like(2, -(-(sizes[0] + 1) // GROUP) * GROUP, LANES)
    later = arriving[sooner:]
    totals, low, high, held, counted = pl.pallas_call(
        functools.partial(
            bin_arrivals,
            cells,
            face_rows,
            [(spots[face][0] - sooner, spots[face][1]) for face in late],
            len(early),
        ),
        out_shape=[
            like(2, cells.rows, LANES),
            face_x,
            face_x,
            held_shape,
            like(6, dtype=jnp.int32),
        ],
        in_specs=[smem()] + [vmem()] * (len(later) + 2) + [smem(), vmem()],
        out_specs=[vmem()] * 4 + [smem()],
        scratch_shapes=[pltpu.VMEM((cells.rows, 2 * LANES), f32)],
        compiler_params=params(),
        name="bin_arrivals",
    )(meta, *later, axis_rows, held, counted, totals)

    many = sum(value.shape[0] // (SENT * tiles) for value in around)
    push, counts, joins, starts = pl.pallas_call(
        functools.partial(first_forces, sizes, lengths, len(around), home, bond_slots),
        out_shape=[
            bead_shape,
            like(many, dtype=jnp.int32),
            like(home, bead_slots, bead_slots, dtype=bf16),
            like(home * GROUP, bead_slots),
        ],
        in_specs=[smem()] + [vmem()] * (1 + len(around)),
        out_specs=[vmem(), smem(), vmem(), vmem()],
        scratch_shapes=force_scratch(bead_slots, many, home, 1),
        compiler_params=params(),
        name="first_forces",
    )(meta, starts, *around)

    below, above = moved_along(high, "gx", 1), moved_along(low, "gx", -1)
    totals, low, high = pl.pallas_call(
        functools.partial(add_faces_x, cells),
        out_shape=[like(2, cells.rows, LANES), face_y, face_y],
        in_specs=[vmem()] * 3 + [any_spec],
        out_specs=[vmem()] * 3,
        compiler_params=params(),
        name="add_faces_x",
    )(totals, below, above, push)
    below, above = moved_along(high, "gy", 1), moved_along(low, "gy", -1)
    totals, faces = pl.pallas_call(
        functools.partial(add_faces_y, cells),
        out_shape=[like(LANES + cells.nz + GROUP, cells.rows), like(2 * GROUP, cells.rows)],
        in_specs=[vmem()] * 3,
        out_specs=[vmem()] * 2,
        scratch_shapes=[pltpu.VMEM((2, cells.rows, LANES), f32)],
        compiler_params=params(),
        name="add_faces_y",
    )(totals, below, above)
    sides = neighbours(faces, "gz")
    below, above = sides[0], sides[-1]

    table, speed, moved, pay = pl.pallas_call(
        functools.partial(finish_cells, cells),
        out_shape=[
            like(7 * cells.height, cells.inner, dtype=bf16),
            bead_shape,
            bead_shape,
            bead_shape,
        ],
        in_specs=[smem()] + [vmem()] * 8,
        out_specs=[vmem()] * 4,
        scratch_shapes=[
            pltpu.VMEM((4 * cells.height, cells.inner), f32),
            pltpu.VMEM((4 * cells.height, LANES), f32),
        ],
        compiler_params=params(),
        name="finish_cells",
    )(meta, dirs, totals, below, above, bead_rows_pos, bead_rows_vel, start, push)

    solvent_shape = like(3, rows_all, LANES)
    windows = [("gz", "gx", "gy")] + [("gx", "gy") if home == 2 else ("gz", "gx", "gy")] * 2
    cuts = sum(len(axes) for axes in windows) - 2
    step_rows = GROUP * TWIN
    steps = rows_here // step_rows
    spans = [steps // cuts + (k >= cuts - steps % cuts) for k in range(cuts)]
    spans = [(sum(spans[:k]) * step_rows, spans[k] * step_rows) for k in range(cuts)]

    held_span = 3 * face_rows
    written, pending, packed_results, tokens = [], [], [], []

    def collide_piece(piece):
        token = like(GROUP, LANES)
        whole = [solvent_shape] * 2
        write_sems = [pltpu.SemaphoreType.DMA((2,))]
        if piece < cuts:
            first, span = spans[piece]
            before = spans[piece - 1] if piece else None
            extra = pending + written
            at = 5 + len(pending)
            *outs, order = pl.pallas_call(
                functools.partial(collide_residents, cells, first, span, before),
                out_shape=whole + [like(3, span, LANES)] * 2 + [token],
                in_specs=[smem()] + [vmem()] * (4 + len(pending)) + [any_spec] * len(written),
                out_specs=[any_spec] * 2 + [vmem()] * 3,
                scratch_shapes=write_sems,
                input_output_aliases={at: 0, at + 1: 1} if written else {},
                compiler_params=params(),
                name=f"collide_{piece}",
            )(meta, dirs, table, position, velocity, *extra)
            written[:], pending[:] = outs[:2], outs[2:]
            tokens.append(order)
            return order
        before = spans[-1] if piece == cuts else None
        extra = pending + written if before else [tokens[-1]]
        outs = pl.pallas_call(
            functools.partial(
                collide_held, cells, (piece - cuts) * held_span, held_span, 6, before
            ),
            out_shape=(whole if before else []) + [like(6, held_span, LANES), token],
            in_specs=[smem()]
            + [vmem()] * 3
            + [smem()]
            + ([vmem()] * 2 + [any_spec] * 2 if before else [any_spec]),
            out_specs=([any_spec] * 2 if before else []) + [vmem()] * 2,
            scratch_shapes=write_sems if before else [],
            input_output_aliases={7: 0, 8: 1} if before else {},
            compiler_params=params(),
            name=f"collide_{piece}",
        )(meta, dirs, table, held, counted, *extra)
        if before:
            written[:] = outs[:2]
        packed_results.append(outs[-2])
        tokens.append(outs[-1])
        if piece < cuts + 1:
            return outs[-1]
        *pending[:], order = pl.pallas_call(
            functools.partial(place_arrivals, face_rows, sequence),
            out_shape=[like(3, 6 * face_rows, LANES)] * 2 + [token],
            in_specs=[smem()] + [vmem()] * 2,
            out_specs=[vmem()] * 3,
            scratch_shapes=[pltpu.VMEM((6, 7 * face_rows, LANES), f32)],
            compiler_params=params(),
            name="place_arrivals",
        )(counted, *packed_results)
        return order

    piece = 0
    for step, axes in enumerate(windows):
        last = step == 2
        thunks = [functools.partial(collide_piece, piece + k) for k in range(len(axes))]
        piece += len(axes)
        ghosts, order = halo(pay, axes, home, thunks)
        final = like(3, 1, 1, 1, bead_slots)
        state = like(home * GROUP, bead_slots)
        tail = pending + written if last else [order]
        at = 6 + len(ghosts) + 2
        outcome = pl.pallas_call(
            functools.partial(
                substep,
                sizes,
                lengths,
                len(ghosts),
                home,
                step,
                (rows_here, 6 * face_rows) if last else None,
            ),
            out_shape=[final] * 2 + [solvent_shape] * 2 if last else [state] * 3,
            in_specs=[smem(), vmem(), vmem(), smem()]
            + [vmem()] * (2 + len(ghosts))
            + ([vmem()] * 2 + [any_spec] * 2 if last else [any_spec]),
            out_specs=[vmem()] * 2 + [any_spec] * 2 if last else [vmem()] * 3,
            scratch_shapes=([pltpu.SemaphoreType.DMA((2,))] if last else [])
            + force_scratch(bead_slots, many, home, 1 if last else home),
            input_output_aliases={at: 2, at + 1: 3} if last else {},
            compiler_params=params(),
            name=f"substep_{step}",
        )(meta, starts, joins, counts, speed, moved, *ghosts, *tail)
        if last:
            written[:] = outcome[2:]
        speed, moved = outcome[:2]
        pay = outcome[-1]

    count_solvent = rows_all * LANES
    return (
        written[0].reshape(3, 1, 1, 1, count_solvent),
        written[1].reshape(3, 1, 1, 1, count_solvent),
        moved,
        speed,
    )


def solution(mesh):
    return jax.shard_map(
        shards,
        mesh=mesh,
        in_specs=(
            P(None, "gx", "gy", "gz", None),
            P(None, "gx", "gy", "gz", None),
            P("gx", "gy", "gz"),
            P(None, "gx", "gy", "gz", None, None),
            P(None, "gx", "gy", "gz", None, None),
            P("gx", "gy", "gz", None),
            P(None, "gx", "gy", "gz", None),
            P(None, "gx", "gy", "gz", None),
            P("gx", "gy", "gz"),
            P(None, "gx", "gy", "gz", None),
            P("gx", "gy", "gz"),
            P(),
        ),
        out_specs=(
            P(None, "gx", "gy", "gz", None),
            P(None, "gx", "gy", "gz", None),
            P(None, "gx", "gy", "gz", None),
            P(None, "gx", "gy", "gz", None),
        ),
        check_vma=False,
    )
```

```python
import functools
import math

import jax
import jax.numpy as jnp
from jax import lax
from jax.experimental import pallas as pl
from jax.experimental.pallas import tpu as pltpu
from jax.sharding import PartitionSpec as P

UNITS = 16
NAXES = 32
CHAIN = 8
LANES = 128
GROUP = 8
TWIN = 4
EIGHT = 8
SENT = 4
PAIR = 2
TRIO = 3

bead_mass = 5.0
step_size = 0.02
spring = 30.0
reach_square = 2.25
cut_square = 2.0 ** (1.0 / 3.0)
turn_cosine = math.cos(130.0 * math.pi / 180.0)
turn_sine = math.sin(130.0 * math.pi / 180.0)
golden = math.pi * (3.0 - math.sqrt(5.0))
half_kick = 0.5 * step_size / bead_mass
far_own = 3000.0
far_ghost = 9000.0
vmem_limit = 48 * 1024 * 1024
vmem_most = 48 * 1024 * 1024
NT = (((1,), (1,)), ((), ()))
NN = (((1,), (0,)), ((), ()))
exact = lax.Precision.HIGHEST
f32 = jnp.float32
bf16 = jnp.bfloat16


def params(limit=vmem_limit):
    return pltpu.CompilerParams(vmem_limit_bytes=limit)


def vmem():
    return pl.BlockSpec(memory_space=pltpu.VMEM)


def smem():
    return pl.BlockSpec(memory_space=pltpu.SMEM)


def moved_along(value, axis, by):
    peers = lax.axis_size(axis)
    return lax.ppermute(value, axis, [(i, (i + by) % peers) for i in range(peers)])


class Cells:
    def __init__(self, size_x, size_y, size_z):
        self.sx, self.sy, self.nz = size_x, size_y, size_z
        self.inner = size_x * size_y
        self.edges = size_x + size_y + 1
        self.rows = -(-(self.inner + self.edges) // 16) * 16
        self.middle = self.rows // 2
        self.per = self.inner // self.edges
        self.depths = size_z + 1
        self.extra = -(-self.depths // self.per)
        self.height = -(-(self.depths + self.extra) // GROUP) * GROUP


def levels_of(position, meta):
    return [
        jnp.floor(jnp.floor(position[d] * UNITS + meta[d].astype(f32)) * (1.0 / UNITS))
        - meta[3 + d].astype(f32)
        for d in range(3)
    ]


def edge_of(levels, cells):
    outer = (levels[0] == cells.sx) | (levels[1] == cells.sy)
    return outer, jnp.where(levels[0] == cells.sx, levels[1], cells.sy + 1 + levels[0])


def plane_of(levels, cells):
    outer, edge = edge_of(levels, cells)
    return jnp.where(outer, cells.inner + edge, levels[0] * cells.sy + levels[1])


def place_of(levels, cells):
    outer, edge = edge_of(levels, cells)
    fold = jnp.floor((levels[2] + 0.5) * (1.0 / cells.per))
    row = jnp.where(outer, cells.depths + fold, levels[2])
    column = jnp.where(
        outer,
        (levels[2] - fold * cells.per) * cells.edges + edge,
        levels[0] * cells.sy + levels[1],
    )
    return row, column


def wide(row):
    return jnp.broadcast_to(row, (16, LANES)).astype(bf16)


def one_hot_rows(rows, height):
    middle = height // 2
    ids = lax.broadcasted_iota(jnp.int32, (height, LANES), 0) - middle
    ids = ids.astype(f32).astype(bf16).reshape(height // 16, 16, LANES)
    one, zero = jnp.ones((), bf16), jnp.zeros((), bf16)
    pieces = [
        jnp.where(ids == wide(row - middle)[None], one, zero).reshape(height, LANES)
        for row in rows
    ]
    return jnp.concatenate(pieces, axis=1)


def one_hot(column, height):
    return one_hot_rows([column[r : r + 1] for r in range(column.shape[0])], height)


def split(value):
    high = value.astype(bf16).astype(f32)
    return high, value - high


def spread_moments(depth, weight, velocity, cells):
    nz = cells.nz
    ids = lax.broadcasted_iota(jnp.int32, (nz, LANES), 0).astype(f32).astype(bf16)
    ids = ids.reshape(nz // 16, 16, LANES)
    row_ids = lax.broadcasted_iota(jnp.int32, (16, LANES), 0).astype(f32).astype(bf16)
    zero = jnp.zeros((), bf16)
    parts = [split(weight * velocity[d]) for d in range(3)]
    channels = [weight] + [p[0] for p in parts] + [p[1] for p in parts]
    pieces = []
    for r in range(depth.shape[0]):
        at = wide(depth[r : r + 1])
        here = ids == at[None]
        values = [wide(c[r : r + 1]) for c in channels]
        tiles = [jnp.where(here, v[None], zero).reshape(nz, LANES) for v in values]
        top = jnp.zeros((16, LANES), bf16)
        for c, v in enumerate(values):
            top = jnp.where(row_ids == c, v, top)
        top = jnp.where(at == nz, top, zero)
        pieces.append(
            jnp.concatenate(
                tiles[:4] + [top, jnp.zeros((nz - 16, LANES), bf16)] + tiles[4:], axis=0
            )
        )
    return jnp.concatenate(pieces, axis=1)


def bin_group(total_ref, position, velocity, weight, meta, cells):
    levels = levels_of(position, meta)
    hot = one_hot(plane_of(levels, cells), cells.rows)
    spread = spread_moments(levels[2], weight, velocity, cells)
    total_ref[...] += lax.dot_general(hot, spread, NT, preferred_element_type=f32)


def row_iota():
    return lax.broadcasted_iota(jnp.int32, (GROUP, LANES), 0)


def bin_residents(cells, first, count, meta_ref, pos_ref, vel_ref, *refs):
    total_ref = refs[-1]
    meta = [meta_ref[k] for k in range(8)]
    if first == 0:
        total_ref[...] = jnp.zeros_like(total_ref)
    else:
        total_ref[...] = refs[0][...]
    live_rows = meta[6] - first
    stride = GROUP * EIGHT

    @pl.loop(0, jnp.clip((live_rows + stride - 1) // stride, 0, count // stride))
    def _(step):
        for part in range(EIGHT):
            offset = pl.multiple_of(step * stride + part * GROUP, GROUP)
            rows = pl.ds(first + offset, GROUP)
            position = [pos_ref[d, rows, :] for d in range(3)]
            velocity = [vel_ref[d, rows, :] for d in range(3)]
            weight = jnp.where(row_iota() + offset < live_rows, 1.0, 0.0)
            bin_group(total_ref, position, velocity, weight, meta, cells)


def face_count(ref, first, face_rows):
    return jnp.max(ref[pl.ds(first + 6 * face_rows, GROUP), :]).astype(jnp.int32)


def take_faces(faces, face_rows, held, counts_ref, index, offset):
    for k, (ref, first) in enumerate(faces):
        count = face_count(ref, first, face_rows)
        counts_ref[index + k] = count
        for c in range(6):
            begin = first + c * face_rows
            held[c, pl.ds(offset, face_rows), :] = ref[begin : begin + face_rows, :]
        offset = offset + count
    return offset


def bin_held(held, begin, end, sums, meta, cells):
    stride = GROUP * PAIR

    @pl.loop(0, (end - begin + stride - 1) // stride)
    def _(step):
        for part in range(PAIR):
            offset = begin + step * stride + part * GROUP
            rows = pl.ds(offset, GROUP)
            comps = [held[c, rows, :] for c in range(6)]
            weight = jnp.where(row_iota() + offset < end, 1.0, 0.0)
            bin_group(sums, comps[:3], comps[3:], weight, meta, cells)


def bead_mask(chains):
    slot = row_iota() * LANES + lax.broadcasted_iota(jnp.int32, (GROUP, LANES), 1)
    return slot < CHAIN * chains


def bin_first_arrivals(cells, face_rows, places, meta_ref, *refs):
    count = len(refs) - 7
    sources = refs[:count]
    bead_pos_ref, bead_vel_ref, start_ref, order_ref, total_ref, held, counts_ref = refs[count:]
    meta = [meta_ref[k] for k in range(8)]
    total_ref[...] = start_ref[...]
    held[...] = jnp.zeros_like(held)
    faces = [(sources[which], first) for which, first in places]
    end = take_faces(faces, face_rows, held, counts_ref, 0, 0)
    weight = jnp.where(bead_mask(meta[7]), bead_mass, 0.0)
    bin_group(
        total_ref,
        [bead_pos_ref[d] for d in range(3)],
        [bead_vel_ref[d] for d in range(3)],
        weight,
        meta,
        cells,
    )
    bin_held(held, 0, end, total_ref, meta, cells)


def bin_arrivals(cells, face_rows, places, known, meta_ref, *refs):
    count = len(refs) - 10
    sources = refs[:count]
    (
        axis_ref,
        held_ref,
        known_ref,
        start_ref,
        total_ref,
        low_ref,
        high_ref,
        held,
        counts_ref,
        sums,
    ) = refs[count:]
    meta = [meta_ref[k] for k in range(8)]
    sums[...] = start_ref[...]
    held[...] = held_ref[...]
    begin = 0
    for k in range(known):
        counts_ref[k] = known_ref[k]
        begin = begin + known_ref[k]
    faces = [(sources[which], first) for which, first in places]
    end = take_faces(faces, face_rows, held, counts_ref, known, begin)
    bin_held(held, begin, end, sums, meta, cells)
    nz, inner = cells.nz, cells.inner
    lane = lax.broadcasted_iota(jnp.int32, (cells.rows, LANES), 1)
    main, rest = sums[:, :LANES], sums[:, LANES:]
    main = main + jnp.where(lane < nz, 0.0, rest)
    top = jnp.where(lane == 0, rest, rest + pltpu.roll(rest, LANES - 3, axis=1))
    total_ref[0] = main
    total_ref[1] = jnp.where(lane < 4, top, 0.0)
    axis = axis_ref[...].astype(f32)
    total_ref[1, :inner, nz : 2 * nz] = axis
    sx, sy = cells.sx, cells.sy
    low_ref[...] = jnp.zeros_like(low_ref)
    high_ref[...] = jnp.zeros_like(high_ref)
    for half in range(2):
        corner = inner + sy + 1
        low_ref[half, :sy, :] = total_ref[half, :sy, :]
        low_ref[half, sy : sy + 1, :] = total_ref[half, corner : corner + 1, :]
        high_ref[half, : sy + 1, :] = total_ref[half, inner : inner + sy + 1, :]


def add_faces_x(cells, total_ref, below_ref, above_ref, order_ref, out_ref, low_ref, high_ref):
    sx, sy, inner = cells.sx, cells.sy, cells.inner
    corner = inner + sy + 1
    out_ref[...] = total_ref[...]
    low_ref[...] = jnp.zeros_like(low_ref)
    high_ref[...] = jnp.zeros_like(high_ref)
    for half in range(2):
        out_ref[half, :sy, :] += below_ref[half, :sy, :]
        out_ref[half, corner : corner + 1, :] += below_ref[half, sy : sy + 1, :]
        out_ref[half, inner : inner + sy + 1, :] += above_ref[half, : sy + 1, :]
        low_ref[half, :sx, :] = out_ref[half, pl.ds(0, sx, stride=sy), :]
        low_ref[half, sx : sx + 1, :] = out_ref[half, inner : inner + 1, :]
        high_ref[half, :sx, :] = out_ref[half, corner : corner + sx, :]
        high_ref[half, sx : sx + 1, :] = out_ref[half, inner + sy : inner + sy + 1, :]


def add_faces_y(cells, total_ref, below_ref, above_ref, out_ref, face_ref, sums):
    sx, sy, nz, inner = cells.sx, cells.sy, cells.nz, cells.inner
    corner = inner + sy + 1
    sums[...] = total_ref[...]
    for half in range(2):
        sums[half, pl.ds(0, sx, stride=sy), :] += below_ref[half, :sx, :]
        sums[half, inner : inner + 1, :] += below_ref[half, sx : sx + 1, :]
        sums[half, corner : corner + sx, :] += above_ref[half, :sx, :]
        sums[half, inner + sy : inner + sy + 1, :] += above_ref[half, sx : sx + 1, :]
    main = sums[0].T
    rest = sums[1].T
    out_ref[:LANES, :] = main
    out_ref[LANES : LANES + nz, :] = rest[nz : 2 * nz]
    out_ref[LANES + nz :, :] = jnp.zeros((GROUP, cells.rows), f32)
    out_ref[LANES + nz : LANES + nz + 4, :] = rest[:4]
    face_ref[...] = jnp.zeros_like(face_ref)
    for c in range(5):
        face_ref[c : c + 1, :] = out_ref[c * nz : c * nz + 1, :]
        face_ref[GROUP + c : GROUP + c + 1, :] = out_ref[5 * nz + c : 5 * nz + c + 1, :]


def cell_table(cells, total_ref, below_ref, above_ref, table_ref, sheet, edge):
    nz, inner, height = cells.nz, cells.inner, cells.height
    row_ids = lax.broadcasted_iota(jnp.int32, (nz, cells.rows), 0)
    parts = []
    tops = []
    for c in range(5):
        face = jnp.where(row_ids == 0, below_ref[GROUP + c : GROUP + c + 1, :], 0.0)
        parts.append(total_ref[c * nz : (c + 1) * nz, :] + face)
        tops.append(
            total_ref[5 * nz + c : 5 * nz + c + 1, :] + above_ref[c : c + 1, :]
        )
    mass = jnp.maximum(parts[0], 1.0)
    top_mass = jnp.maximum(tops[0], 1.0)
    values = [parts[4]] + [p / mass for p in parts[1:4]]
    top_values = [tops[4]] + [t / top_mass for t in tops[1:4]]
    sheet[...] = jnp.zeros_like(sheet)
    edge[...] = jnp.zeros_like(edge)
    lane = lax.broadcasted_iota(jnp.int32, (cells.extra, LANES), 1)
    spare = LANES - (cells.rows - inner)
    for c in range(4):
        base = c * height
        sheet[base : base + nz, :] = values[c][:, :inner]
        sheet[base + nz : base + nz + 1, :] = top_values[c][:, :inner]
        edge[base : base + nz, :] = jnp.concatenate(
            [values[c][:, inner:], jnp.zeros((nz, spare), f32)], axis=1
        )
        edge[base + nz : base + nz + 1, :] = jnp.concatenate(
            [top_values[c][:, inner:], jnp.zeros((1, spare), f32)], axis=1
        )
        folded = [jnp.zeros((cells.extra, LANES), f32) for _ in range(inner // LANES)]
        for m in range(cells.per):
            begin = m * cells.edges
            piece = edge[pl.ds(base + m, cells.extra, stride=cells.per), :]
            piece = pltpu.roll(piece, begin % LANES, axis=1) if begin % LANES else piece
            for t in range(inner // LANES):
                low, high = begin - t * LANES, begin + cells.edges - t * LANES
                if high > 0 and low < LANES:
                    folded[t] = jnp.where((lane >= low) & (lane < high), piece, folded[t])
        sheet[base + nz + 1 : base + nz + 1 + cells.extra, :] = jnp.concatenate(folded, axis=1)
    whole = sheet[...]
    high = whole.astype(bf16).astype(f32)
    low = (whole - high)[height:]
    table_ref[...] = jnp.concatenate([high, low], axis=0).astype(bf16)


def direction_table():
    counter = jnp.arange(LANES).astype(f32)
    height = 1.0 - (2.0 * counter + 1.0) / NAXES
    radius = jnp.sqrt(jnp.maximum(1.0 - height * height, 0.0))
    rows = jnp.stack([radius * jnp.cos(golden * counter), radius * jnp.sin(golden * counter)])
    return jnp.broadcast_to(rows[:, None], (2, GROUP, LANES))


def fold_rows(values):
    sub = lax.broadcasted_iota(jnp.int32, (GROUP, LANES), 0)
    step = GROUP // 2
    while step:
        upper = (sub & step) == 0
        half = len(values) // 2
        joined = []
        for a, b in zip(values[:half], values[half:]):
            a = a + pltpu.roll(a, GROUP - step, axis=0)
            b = b + pltpu.roll(b, step, axis=0)
            joined.append(jnp.where(upper, a, b))
        values = joined
        step //= 2
    return values[0]


def collide(position, velocity, meta, table, dirs_ref, cells):
    height = cells.height
    row, column = place_of(levels_of(position, meta), cells)
    found = lax.dot_general(
        table, one_hot(column, cells.inner), NN, preferred_element_type=f32
    )
    ids = lax.broadcasted_iota(jnp.int32, (height, LANES), 0).astype(f32)
    picked = [[] for _ in range(4)]
    for r in range(GROUP):
        block = found[:, r * LANES : (r + 1) * LANES]
        here = ids == row[r : r + 1]
        for c in range(4):
            value = block[c * height : (c + 1) * height]
            if c > 0:
                value = value + block[(3 + c) * height : (4 + c) * height]
            value = jnp.where(here, value, 0.0)
            picked[c].append(
                jnp.sum(value.reshape(height // GROUP, GROUP, LANES), axis=0)
            )
    picked = [fold_rows(p) for p in picked]
    axis, flow = picked[0].astype(jnp.int32), picked[1:]
    normal = [
        jnp.take_along_axis(dirs_ref[0], axis, axis=1, mode="promise_in_bounds"),
        jnp.take_along_axis(dirs_ref[1], axis, axis=1, mode="promise_in_bounds"),
        1.0 - (2.0 * picked[0] + 1.0) * (1.0 / NAXES),
    ]
    rel = [velocity[d] - flow[d] for d in range(3)]
    along = (1.0 - turn_cosine) * (
        normal[0] * rel[0] + normal[1] * rel[1] + normal[2] * rel[2]
    )
    result = []
    for d in range(3):
        e, f = (d + 1) % 3, (d + 2) % 3
        crossed = normal[e] * rel[f] - normal[f] * rel[e]
        result.append(
            flow[d] + (turn_cosine * rel[d] + turn_sine * crossed + along * normal[d])
        )
    return result


def passed(position, speed):
    return position - jnp.floor(position) - 0.5 + 3.0 * step_size * speed


def writing(spans, refs, sems):
    copies = []
    for k, ((first, count), (value, out)) in enumerate(zip(spans, refs)):
        copies.append(
            pltpu.make_async_copy(value, out.at[:, pl.ds(first, count), :], sems.at[k])
        )
    for copy in copies:
        copy.start()

    def finish():
        for copy in copies:
            copy.wait()

    return finish


def collide_residents(
    cells, first, count, before, meta_ref, dirs_ref, table_ref, pos_ref, vel_ref, *refs
):
    out_pos, out_vel, new_pos, new_vel, token, sems = refs[-6:]
    finish = writing([before] * 2, [(refs[0], out_pos), (refs[1], out_vel)], sems) if before else None
    token[...] = jnp.zeros_like(token)
    meta = [meta_ref[k] for k in range(8)]
    table = table_ref[...]
    live_rows = meta[6] - first
    new_pos[...] = jnp.zeros_like(new_pos)
    new_vel[...] = jnp.zeros_like(new_vel)
    stride = GROUP * TWIN

    @pl.loop(0, jnp.clip((live_rows + stride - 1) // stride, 0, count // stride))
    def _(step):
        for part in range(TWIN):
            offset = pl.multiple_of(step * stride + part * GROUP, GROUP)
            rows = pl.ds(first + offset, GROUP)
            position = [pos_ref[d, rows, :] for d in range(3)]
            velocity = [vel_ref[d, rows, :] for d in range(3)]
            live = row_iota() + offset < live_rows
            speed = collide(position, velocity, meta, table, dirs_ref, cells)
            rows = pl.ds(offset, GROUP)
            for d in range(3):
                new_vel[d, rows, :] = jnp.where(live, speed[d], 0.0)
                new_pos[d, rows, :] = jnp.where(live, passed(position[d], speed[d]), 0.0)

    if finish:
        finish()


def collide_held(
    cells, first, count, many, before, meta_ref, dirs_ref, table_ref, held, counts_ref, *refs
):
    if before:
        out_pos, out_vel, out_ref, token, sems = refs[-5:]
        finish = writing([before] * 2, [(refs[0], out_pos), (refs[1], out_vel)], sems)
        token[...] = jnp.zeros_like(token)
    else:
        out_ref = refs[-1]
        finish = None
    meta = [meta_ref[k] for k in range(8)]
    table = table_ref[...]
    out_ref[...] = jnp.zeros_like(out_ref)
    end = sum([counts_ref[k] for k in range(many)], jnp.int32(0)) - first
    stride = GROUP * TRIO

    @pl.loop(0, jnp.clip((end + stride - 1) // stride, 0, count // stride))
    def _(step):
        for part in range(TRIO):
            offset = pl.multiple_of(step * stride + part * GROUP, GROUP)
            comps = [held[c, pl.ds(first + offset, GROUP), :] for c in range(6)]
            speed = collide(comps[:3], comps[3:], meta, table, dirs_ref, cells)
            for d in range(3):
                out_ref[d, pl.ds(offset, GROUP), :] = speed[d]
                out_ref[3 + d, pl.ds(offset, GROUP), :] = passed(comps[d], speed[d])

    if finish:
        finish()


def place_arrivals(face_rows, sequence, counts_ref, *refs):
    pieces = refs[:-3]
    new_pos, new_vel, packed = refs[-3:]
    packed[...] = jnp.zeros_like(packed)
    at = 0
    for piece in pieces:
        packed[:, at : at + piece.shape[1], :] = piece[...]
        at += piece.shape[1]
    rows = lax.broadcasted_iota(jnp.int32, (face_rows, LANES), 0)
    offset = 0
    for k, face in enumerate(sequence):
        count = counts_ref[k]
        place = slice(face * face_rows, (face + 1) * face_rows)
        for d in range(3):
            speed = packed[d, pl.ds(offset, face_rows), :]
            moved = packed[3 + d, pl.ds(offset, face_rows), :]
            new_vel[d, place, :] = jnp.where(rows < count, speed, 0.0)
            new_pos[d, place, :] = jnp.where(rows < count, moved, 0.0)
        offset = offset + count


def pack_inputs(
    meta_ref,
    pos_ref,
    vel_ref,
    bead_pos_ref,
    bead_vel_ref,
    bond_ref,
    order_ref,
    start_ref,
    block_ref,
    rows_pos_ref,
    rows_vel_ref,
    *refs,
):
    out_refs, (held_pos, held_vel, sems) = refs[:6], refs[6:]
    copies = [(bead_pos_ref, held_pos), (bead_vel_ref, held_vel)]
    for face, out_ref in enumerate(out_refs):
        copies.append((pos_ref.at[:, face], out_ref.at[0:3]))
        copies.append((vel_ref.at[:, face], out_ref.at[3:6]))
    copies = [pltpu.make_async_copy(a, b, sems.at[k]) for k, (a, b) in enumerate(copies)]
    for copy in copies:
        copy.start()
    for face, out_ref in enumerate(out_refs):
        out_ref[6] = jnp.full(out_ref.shape[1:], meta_ref[8 + face], jnp.int32).astype(f32)
    slots = start_ref.shape[1]
    start_ref[...] = jnp.zeros_like(start_ref)
    rows_pos_ref[...] = jnp.zeros_like(rows_pos_ref)
    rows_vel_ref[...] = jnp.zeros_like(rows_vel_ref)
    for copy in copies:
        copy.wait()
    for d in range(3):
        for k in range(slots // LANES):
            lanes = slice(k * LANES, (k + 1) * LANES)
            start_ref[d : d + 1, lanes] = held_pos[d, k : k + 1, :]
            rows_pos_ref[d, k : k + 1, :] = held_pos[d, k : k + 1, :]
            rows_vel_ref[d, k : k + 1, :] = held_vel[d, k : k + 1, :]
    bond_slots = bond_ref.shape[-1]
    ends = jnp.concatenate(
        [bond_ref[k, 0, 0, :, :].astype(f32) for k in range(2)]
        + [jnp.zeros((GROUP - 2, bond_slots), f32)],
        axis=0,
    )
    if bond_slots < slots:
        ends = jnp.concatenate([ends, jnp.zeros((GROUP, slots - bond_slots), f32)], axis=1)
    start = start_ref[...]
    whole = payload(start, slot_live(slots, meta_ref[7], GROUP), ends)
    for k in range(slots // LANES):
        block_ref[k * GROUP : (k + 1) * GROUP, :] = whole[:, k * LANES : (k + 1) * LANES]


def stack_rows(parts, *refs):
    out_ref = refs[-1]
    at = 0
    for which, begin, count in parts:
        out_ref[at : at + count, :] = refs[which][begin : begin + count, :]
        at += count


def slot_live(slots, chains, rows):
    return lax.broadcasted_iota(jnp.int32, (rows, slots), 1) < CHAIN * chains


def payload(position, live, more):
    row_ids = lax.broadcasted_iota(jnp.int32, position.shape, 0)
    flag = jnp.where(live, 1.0, 0.0)
    rest = pltpu.roll(more, 4, axis=0)
    return jnp.where(row_ids == 3, flag, jnp.where(row_ids < 3, position, rest))


def thirds_of(value):
    high = value.astype(bf16).astype(f32)
    middle = (value - high).astype(bf16).astype(f32)
    low = value - high - middle
    return jnp.concatenate([high, middle, low, jnp.zeros_like(value)], axis=0).astype(bf16)


def summed_thirds(value):
    rows = value.shape[0] // 4
    return value[:rows] + (value[rows : 2 * rows] + value[2 * rows : 3 * rows])


def joins_of(block, chains, bond_slots):
    ends = block.T
    slots = block.shape[1]
    slot_ids = lax.broadcasted_iota(jnp.int32, (slots, slots), 1).astype(f32)
    bond_ids = lax.broadcasted_iota(jnp.int32, (slots, slots), 0)
    joins = jnp.where(slot_ids == ends[:, 4:5], 1.0, 0.0)
    joins = joins - jnp.where(slot_ids == ends[:, 5:6], 1.0, 0.0)
    live = jnp.minimum((CHAIN - 1) * chains, bond_slots)
    return jnp.where(bond_ids < live, joins, 0.0).astype(bf16)


def bond_forces(local, joins, chains):
    stretch = summed_thirds(
        lax.dot_general(thirds_of(local), joins, NT, preferred_element_type=f32)
    )
    square = (
        stretch[0:1] * stretch[0:1] + stretch[1:2] * stretch[1:2] + stretch[2:3] * stretch[2:3]
    )
    live = lax.broadcasted_iota(jnp.int32, (1, joins.shape[0]), 1) < (CHAIN - 1) * chains
    pull = jnp.where(live, -spring / (1.0 - square / reach_square), 0.0) * stretch
    return summed_thirds(lax.dot_general(thirds_of(pull), joins, NN, preferred_element_type=f32))


def forces(blocks, counts, joins, mains, home, centre, lengths, mine_ref, packed, push, near_mask):
    slots = blocks[0].shape[1]
    tiles = slots // LANES
    row_ids = lax.broadcasted_iota(jnp.int32, (GROUP, slots), 0)
    lane_ids = lax.broadcasted_iota(jnp.int32, (GROUP, slots), 1)
    mid = jnp.zeros((GROUP, slots), f32)
    length = jnp.full((GROUP, slots), 1e9, f32)
    for d in range(3):
        mid = jnp.where(row_ids == d, centre[d], mid)
        if d < 2:
            length = jnp.where(row_ids == d, lengths[d], length)
    inverse_length = 1.0 / length
    near = [block - mid for block in blocks[:home]]
    for block in blocks[home:]:
        rows = block.shape[0]
        value = block - mid[:rows]
        near.append(value - length[:rows] * jnp.floor(value * inverse_length[:rows] + 0.5))

    low = jnp.full((GROUP, slots), far_ghost, f32)
    high = jnp.full((GROUP, slots), -far_ghost, f32)
    bonds = []
    for b in range(mains):
        live = lane_ids < counts[b]
        columns = jnp.where(live, near[b], far_own).T
        for d in range(3):
            mine_ref[d, b * slots : (b + 1) * slots, :] = jnp.broadcast_to(
                columns[:, d : d + 1], (slots, LANES)
            )
        low = jnp.minimum(low, jnp.where(live, near[b], far_ghost))
        high = jnp.maximum(high, jnp.where(live, near[b], -far_ghost))
        local = jnp.where(live & (row_ids < 3), near[b], 0.0)
        bonds.append(bond_forces(local, joins[b], counts[b] // CHAIN))

    packed[...] = jnp.full(packed.shape, far_ghost, f32)
    lane = lax.broadcasted_iota(jnp.int32, (GROUP, LANES), 1)
    offset = jnp.int32(0)
    for value, count in zip(near[:home], counts[:home]):
        tile, turn = offset // LANES, offset % LANES
        turned = [
            pltpu.roll(value[:, k * LANES : (k + 1) * LANES], turn, axis=1)
            for k in range(tiles)
        ]
        for k in range(tiles + 1):
            if k == 0:
                piece = turned[0]
            elif k == tiles:
                piece = turned[-1]
            else:
                piece = jnp.where(lane < turn, turned[k - 1], turned[k])
            place = (tile + k) * LANES + lane
            taken = (place >= offset) & (place < offset + count)
            packed[tile + k] = jnp.where(taken, piece, packed[tile + k])
        offset = offset + count
    first_tile = (offset + LANES - 1) // LANES

    reach = 1.001 * math.sqrt(cut_square)
    low = jnp.min(low, axis=1, keepdims=True) - reach
    high = jnp.max(high, axis=1, keepdims=True) + reach
    others = near[home:]
    near_mask[...] = jnp.zeros_like(near_mask)
    for k, value in enumerate(others):
        inside = jnp.where((value >= low[:SENT]) & (value <= high[:SENT]), 1.0, 0.0)
        inside = inside[0:1] * inside[1:2]
        live = lane_ids[0:1] < counts[home + k]
        near_mask[k : k + 1, :] = jnp.where(live, inside, 0.0)
    mask = near_mask[...]
    height = mask.shape[0]
    mask_bf16 = mask.astype(bf16)
    upto = jnp.where(
        lax.broadcasted_iota(jnp.int32, (slots, slots), 0)
        <= lax.broadcasted_iota(jnp.int32, (slots, slots), 1),
        1.0,
        0.0,
    ).astype(bf16)
    above = jnp.where(
        lax.broadcasted_iota(jnp.int32, (height, height), 1)
        < lax.broadcasted_iota(jnp.int32, (height, height), 0),
        1.0,
        0.0,
    ).astype(bf16)
    within = lax.dot_general(mask_bf16, upto, NN, preferred_element_type=f32)
    before = lax.dot_general(above, mask_bf16, NN, preferred_element_type=f32)
    before = jnp.sum(before, axis=1, keepdims=True)
    place = jnp.where(mask > 0.5, within + before - 1.0, -1.0)
    found = jnp.sum(mask).astype(jnp.int32)
    parts = jnp.concatenate([thirds_of(value) for value in others], axis=1)
    found_tiles = (found + LANES - 1) // LANES

    @pl.loop(0, found_tiles)
    def _(tile):
        goal = place - (tile * LANES).astype(f32)
        rows = [
            goal[k : k + 1, t * LANES : (t + 1) * LANES]
            for k in range(len(others))
            for t in range(tiles)
        ]
        chosen = one_hot_rows(rows, LANES)
        value = summed_thirds(
            lax.dot_general(parts, chosen, NT, preferred_element_type=f32)
        )
        there = tile * LANES + lane[:SENT] < found
        packed[first_tile + tile, :SENT, :] = jnp.where(there, value, far_ghost)

    push[...] = jnp.zeros_like(push)
    chunk = 64
    steps = (first_tile + found_tiles + 1) // 2
    period = lengths[2]

    for b in range(mains):

        @pl.loop(0, (counts[b] + chunk - 1) // chunk)
        def _(part):
            rows = pl.ds(pl.multiple_of(b * slots + part * chunk, chunk), chunk)
            mine = [mine_ref[d, rows, :] for d in range(3)]

            def add_tiles(step, total):
                for k in range(2):
                    other = packed[2 * step + k]
                    differ = [mine[d] - other[d : d + 1] for d in range(3)]
                    differ[2] = differ[2] - period * jnp.floor(
                        differ[2] * (1.0 / period) + 0.5
                    )
                    square = (
                        differ[0] * differ[0] + differ[1] * differ[1] + differ[2] * differ[2]
                    )
                    inside = (square < cut_square) & (square > 0.25)
                    inverse = 1.0 / jnp.where(inside, square, 1e30)
                    sixth = inverse * inverse * inverse
                    weight = (sixth * inverse) * (48.0 * sixth - 24.0)
                    total = tuple(total[d] + weight * differ[d] for d in range(3))
                return total

            total = lax.fori_loop(
                0, steps, add_tiles, tuple(jnp.zeros((chunk, LANES), f32) for _ in range(3))
            )
            for d in range(3):
                push[d, rows, :] = total[d]

    result = []
    for b in range(mains):
        pair = jnp.zeros((GROUP, slots), f32)
        for d in range(3):
            line = jnp.sum(push[d, b * slots : (b + 1) * slots, :].T, axis=0, keepdims=True)
            pair = jnp.where(row_ids == d, line, pair)
        result.append(pair + bonds[b])
    return result


def force_scratch(slots, blocks, home, mains):
    tiles = home * slots // LANES + 2 + (blocks - home) * slots // LANES
    return [
        pltpu.VMEM((3, mains * slots, LANES), f32),
        pltpu.VMEM((-(-tiles // 2) * 2, GROUP, LANES), f32),
        pltpu.VMEM((3, mains * slots, LANES), f32),
        pltpu.VMEM((-(-(blocks - home) // 16) * 16, slots), f32),
    ]


def blocks_of(home, home_ref, refs):
    others = [
        ref[b * SENT : (b + 1) * SENT, :]
        for ref in refs
        for b in range(ref.shape[0] // SENT)
    ]
    return [home_ref[b * GROUP : (b + 1) * GROUP, :] for b in range(home)] + others[home:]


def centre_of(meta, sizes):
    return [meta[3 + d].astype(f32) + 0.5 * sizes[d] for d in range(3)]


def joined_blocks(ref, rows, tiles):
    return [
        jnp.concatenate(
            [ref[(b * tiles + k) * rows : (b * tiles + k + 1) * rows, :] for k in range(tiles)],
            axis=1,
        )
        for b in range(ref.shape[0] // (rows * tiles))
    ]


def first_forces(sizes, lengths, sources, home, bond_slots, meta_ref, home_ref, *refs):
    sources_refs, (push_ref, counts_ref, joins_ref, starts_ref), scratch = (
        refs[:sources],
        refs[sources : sources + 4],
        refs[sources + 4 :],
    )
    meta = [meta_ref[k] for k in range(8)]
    tiles = push_ref.shape[1] // LANES
    blocks = [block for ref in sources_refs for block in joined_blocks(ref, SENT, tiles)]
    blocks = joined_blocks(home_ref, GROUP, tiles) + blocks[home:]
    counts = [jnp.sum(block[3:4]).astype(jnp.int32) for block in blocks]
    for k, count in enumerate(counts):
        counts_ref[k] = count
    joins = []
    for b in range(home):
        starts_ref[b * GROUP : (b + 1) * GROUP, :] = blocks[b]
        joins.append(joins_of(blocks[b], counts[b] // CHAIN, bond_slots))
        joins_ref[b] = joins[b]
    push_ref[...] = forces(
        blocks, counts, joins, 1, home, centre_of(meta, sizes), lengths, *scratch
    )[0]


def finish_cells(
    cells,
    meta_ref,
    dirs_ref,
    total_ref,
    below_ref,
    above_ref,
    bead_pos_ref,
    bead_vel_ref,
    start_ref,
    push_ref,
    table_ref,
    speed_ref,
    moved_ref,
    pay_ref,
    sheet,
    edge,
):
    meta = [meta_ref[k] for k in range(8)]
    cell_table(cells, total_ref, below_ref, above_ref, table_ref, sheet, edge)
    fresh = collide(
        [bead_pos_ref[d] for d in range(3)],
        [bead_vel_ref[d] for d in range(3)],
        meta,
        table_ref[...],
        dirs_ref,
        cells,
    )
    start = start_ref[...]
    slots = start.shape[1]
    row_ids = lax.broadcasted_iota(jnp.int32, (GROUP, slots), 0)
    speed = jnp.zeros((GROUP, slots), f32)
    for d in range(3):
        line = jnp.concatenate([fresh[d][k : k + 1] for k in range(slots // LANES)], axis=1)
        speed = jnp.where(row_ids == d, line, speed)
    speed = speed + half_kick * push_ref[...]
    moved = step_size * speed
    live = slot_live(slots, meta[7], GROUP)
    speed_ref[...] = speed
    moved_ref[...] = moved
    pay_ref[...] = payload(start + moved, live, speed)


def substep(
    sizes, lengths, sources, home, step, last, meta_ref, start_ref, joins_ref, counts_ref, speed_ref, moved_ref, *refs
):
    came, rest = refs[:sources], refs[sources:]
    if last:
        new_pos, new_vel, _, _, *outs, sems, a, b, c, e = rest
        finish = writing([last] * 2, [(new_pos, outs[2]), (new_vel, outs[3])], sems)
    else:
        _, *outs, a, b, c, e = rest
    meta = [meta_ref[k] for k in range(8)]
    blocks = blocks_of(home, came[0], came[1:])
    counts = [counts_ref[k] for k in range(len(blocks))]
    mains = 1 if last else home
    joins = [joins_ref[b] for b in range(mains)]
    pushes = forces(
        blocks, counts, joins, mains, home, centre_of(meta, sizes), lengths, a, b, c, e
    )
    slots = start_ref.shape[1]
    row_ids = lax.broadcasted_iota(jnp.int32, (GROUP, slots), 0)
    for b in range(mains):
        rows = slice(b * GROUP, (b + 1) * GROUP)
        live = lax.broadcasted_iota(jnp.int32, (GROUP, slots), 1) < counts[b]
        start = start_ref[rows, :]
        if step == 0 and b > 0:
            speed = jnp.where(row_ids < 3, pltpu.roll(blocks[b], 4, axis=0), 0.0)
            moved = step_size * speed
        else:
            speed, moved = speed_ref[rows, :], moved_ref[rows, :]
        speed = speed + half_kick * pushes[b]
        if last:
            for d in range(3):
                outs[0][d, 0, 0, :, :] = jnp.where(live, speed, 0.0)[d : d + 1]
                outs[1][d, 0, 0, :, :] = jnp.where(live, moved, 0.0)[d : d + 1]
            finish()
            return
        speed = speed + half_kick * pushes[b]
        moved = moved + step_size * speed
        outs[0][rows, :] = speed
        outs[1][rows, :] = moved
        outs[2][rows, :] = payload(start + moved, live, speed)


def neighbours(value, axis):
    peers = lax.axis_size(axis)
    if peers == 2:
        return [moved_along(value, axis, 1)]
    return [moved_along(value, axis, 1), moved_along(value, axis, -1)]


def stacked(parts, operands, order=()):
    rows = sum(count for _, _, count in parts)
    width = operands[0].shape[1]
    return pl.pallas_call(
        functools.partial(stack_rows, tuple(parts)),
        out_shape=like(rows, width),
        in_specs=[vmem()] * len(operands) + [pl.BlockSpec(memory_space=pl.ANY)] * len(order),
        out_specs=vmem(),
        compiler_params=params(),
        name="stack_rows",
    )(*operands, *order)


def whole_rows(operands):
    return [(k, 0, value.shape[0]) for k, value in enumerate(operands)]


def halo(pay, axes, home, pieces):
    rows = pay
    axes, pieces = list(axes), list(pieces)
    if axes[0] == "gz":
        parts = [pay] + neighbours(pay, "gz")
        rows = stacked(whole_rows(parts), parts, [pieces.pop(0)()])
        axes.pop(0)
    count = rows.shape[0] // GROUP
    sent = stacked([(0, b * GROUP, SENT) for b in range(count)], [rows])
    for axis, piece in zip(axes[:-1], pieces):
        parts = [sent] + neighbours(sent, axis)
        sent = stacked(whole_rows(parts), parts, [piece()])
    sides = neighbours(sent, axes[-1])
    own = rows if count == home else pay
    return [own, sent] + sides, pieces[-1]()


def like(*shape, dtype=f32):
    return jax.ShapeDtypeStruct(shape, dtype)


def shards(
    sol_pos,
    sol_vel,
    sol_rows,
    mig_pos,
    mig_vel,
    mig_rows,
    bead_pos,
    bead_vel,
    bead_chains,
    bond_list,
    cell_axis,
    shift,
):
    sizes = cell_axis.shape
    cells = Cells(*sizes)
    names = ("gx", "gy", "gz")
    lengths = tuple(float(sizes[d] * lax.axis_size(names[d])) for d in range(3))
    slots_here = sol_pos.shape[-1]
    buffer_slots = mig_pos.shape[-1]
    bead_slots = bead_pos.shape[-1]
    bond_slots = bond_list.shape[-1]
    rows_here = slots_here // LANES
    face_rows = buffer_slots // LANES
    rows_all = rows_here + 6 * face_rows
    anchor = jnp.stack([lax.axis_index(names[d]) * sizes[d] for d in range(3)])
    meta = jnp.concatenate(
        [
            shift,
            anchor.astype(jnp.int32),
            sol_rows.reshape(1),
            bead_chains.reshape(1),
            mig_rows.reshape(6),
        ]
    )
    dirs = direction_table()
    position = sol_pos.reshape(3, rows_here, LANES)
    velocity = sol_vel.reshape(3, rows_here, LANES)

    any_spec = pl.BlockSpec(memory_space=pl.ANY)
    thirds = 3
    count = rows_here // thirds
    axis_rows = cell_axis.reshape(cells.inner, sizes[2])

    def bin_piece(piece, earlier, order):
        sources = [position, velocity] if piece else [position[:, :count], velocity[:, :count]]
        return pl.pallas_call(
            functools.partial(bin_residents, cells, piece * count, count),
            out_shape=like(cells.rows, 2 * LANES),
            in_specs=[smem()]
            + [vmem()] * (2 + len(earlier))
            + [any_spec] * len(order),
            out_specs=vmem(),
            compiler_params=params(),
            name=f"bin_residents_{piece}",
        )(meta, *sources, *earlier, *order)

    totals = bin_piece(0, [], [])
    face_height = 7 * face_rows
    bead_shape = like(GROUP, bead_slots)
    tiles = bead_slots // LANES
    rows_shape = like(3, GROUP, LANES)
    start, block, bead_rows_pos, bead_rows_vel, *packed = pl.pallas_call(
        pack_inputs,
        out_shape=[
            bead_shape,
            like(tiles * GROUP, LANES),
            rows_shape,
            rows_shape,
        ]
        + [like(7, face_rows, LANES)] * 6,
        in_specs=[smem()]
        + [pl.BlockSpec(memory_space=pltpu.HBM)] * 4
        + [vmem(), any_spec],
        out_specs=[vmem()] * 10,
        scratch_shapes=[pltpu.VMEM((3, tiles, LANES), f32)] * 2
        + [pltpu.SemaphoreType.DMA((14,))],
        compiler_params=params(vmem_most),
        name="pack_inputs",
    )(
        meta,
        mig_pos.reshape(3, 6, face_rows, LANES),
        mig_vel.reshape(3, 6, face_rows, LANES),
        bead_pos.reshape(3, tiles, LANES),
        bead_vel.reshape(3, tiles, LANES),
        bond_list,
        totals,
    )
    packed = [value.reshape(face_height, LANES) for value in packed]

    def swap(axis, low, high, body):
        if lax.axis_size(axis) == 2:
            both = [packed[low], packed[high], body]
            came = moved_along(stacked(whole_rows(both), both), axis, 1)
            return [came], [(0, face_height), (0, 0)], [(0, 2 * face_height)]
        up = stacked(whole_rows([packed[high], body]), [packed[high], body])
        down = stacked(whole_rows([packed[low], body]), [packed[low], body])
        came = [moved_along(up, axis, 1), moved_along(down, axis, -1)]
        return came, [(0, 0), (1, 0)], [(0, face_height), (1, face_height)]

    def short(operand, first):
        return [(operand, first + k * GROUP, SENT) for k in range(tiles)]

    home = 2 if lax.axis_size("gz") == 2 else 1
    arriving, spots, blocks = [], [None] * 6, block
    for piece, (axis, low) in enumerate((("gz", 4), ("gx", 0), ("gy", 2))):
        came, places, bodies = swap(axis, low, low + 1, blocks)
        for k, (which, at) in enumerate(places):
            spots[low + k] = (len(arriving) + which, at)
        arriving += came
        height = blocks.shape[0]
        if axis == "gy":
            around = [blocks] + [stacked([(0, at, height)], [came[w]]) for w, at in bodies]
            break
        totals = bin_piece(piece + 1, [totals], [blocks])
        if axis == "gz":
            own = [(0, 0, height)] + [(1 + w, at, height) for w, at in bodies][: home - 1]
            starts = stacked(own, [blocks] + came)
            parts = short(0, 0) + [p for w, at in bodies for p in short(1 + w, at)]
        else:
            parts = [(0, 0, height)] + [(1 + w, at, height) for w, at in bodies]
        blocks = stacked(parts, [blocks] + came, [totals])

    sequence = (4, 5, 0, 1, 2, 3)
    early, late = sequence[:4], sequence[4:]
    sooner = max(spots[face][0] for face in early) + 1
    held_rows = -(-6 * face_rows // 32) * 32
    held_shape = like(6, held_rows, LANES)
    totals, held, counted = pl.pallas_call(
        functools.partial(
            bin_first_arrivals, cells, face_rows, [spots[face] for face in early]
        ),
        out_shape=[like(cells.rows, 2 * LANES), held_shape, like(4, dtype=jnp.int32)],
        in_specs=[smem()] + [vmem()] * (sooner + 3) + [any_spec],
        out_specs=[vmem(), vmem(), smem()],
        compiler_params=params(),
        name="bin_first_arrivals",
    )(meta, *arriving[:sooner], bead_rows_pos, bead_rows_vel, totals, blocks)

    face_x = like(2, -(-(sizes[1] + 1) // GROUP) * GROUP, LANES)
    face_y = like(2, -(-(sizes[0] + 1) // GROUP) * GROUP, LANES)
    later = arriving[sooner:]
    totals, low, high, held, counted = pl.pallas_call(
        functools.partial(
            bin_arrivals,
            cells,
            face_rows,
            [(spots[face][0] - sooner, spots[face][1]) for face in late],
            len(early),
        ),
        out_shape=[
            like(2, cells.rows, LANES),
            face_x,
            face_x,
            held_shape,
            like(6, dtype=jnp.int32),
        ],
        in_specs=[smem()] + [vmem()] * (len(later) + 2) + [smem(), vmem()],
        out_specs=[vmem()] * 4 + [smem()],
        scratch_shapes=[pltpu.VMEM((cells.rows, 2 * LANES), f32)],
        compiler_params=params(),
        name="bin_arrivals",
    )(meta, *later, axis_rows, held, counted, totals)

    many = sum(value.shape[0] // (SENT * tiles) for value in around)
    push, counts, joins, starts = pl.pallas_call(
        functools.partial(first_forces, sizes, lengths, len(around), home, bond_slots),
        out_shape=[
            bead_shape,
            like(many, dtype=jnp.int32),
            like(home, bead_slots, bead_slots, dtype=bf16),
            like(home * GROUP, bead_slots),
        ],
        in_specs=[smem()] + [vmem()] * (1 + len(around)),
        out_specs=[vmem(), smem(), vmem(), vmem()],
        scratch_shapes=force_scratch(bead_slots, many, home, 1),
        compiler_params=params(),
        name="first_forces",
    )(meta, starts, *around)

    below, above = moved_along(high, "gx", 1), moved_along(low, "gx", -1)
    totals, low, high = pl.pallas_call(
        functools.partial(add_faces_x, cells),
        out_shape=[like(2, cells.rows, LANES), face_y, face_y],
        in_specs=[vmem()] * 3 + [any_spec],
        out_specs=[vmem()] * 3,
        compiler_params=params(),
        name="add_faces_x",
    )(totals, below, above, push)
    below, above = moved_along(high, "gy", 1), moved_along(low, "gy", -1)
    totals, faces = pl.pallas_call(
        functools.partial(add_faces_y, cells),
        out_shape=[like(LANES + cells.nz + GROUP, cells.rows), like(2 * GROUP, cells.rows)],
        in_specs=[vmem()] * 3,
        out_specs=[vmem()] * 2,
        scratch_shapes=[pltpu.VMEM((2, cells.rows, LANES), f32)],
        compiler_params=params(),
        name="add_faces_y",
    )(totals, below, above)
    sides = neighbours(faces, "gz")
    below, above = sides[0], sides[-1]

    table, speed, moved, pay = pl.pallas_call(
        functools.partial(finish_cells, cells),
        out_shape=[
            like(7 * cells.height, cells.inner, dtype=bf16),
            bead_shape,
            bead_shape,
            bead_shape,
        ],
        in_specs=[smem()] + [vmem()] * 8,
        out_specs=[vmem()] * 4,
        scratch_shapes=[
            pltpu.VMEM((4 * cells.height, cells.inner), f32),
            pltpu.VMEM((4 * cells.height, LANES), f32),
        ],
        compiler_params=params(),
        name="finish_cells",
    )(meta, dirs, totals, below, above, bead_rows_pos, bead_rows_vel, start, push)

    solvent_shape = like(3, rows_all, LANES)
    windows = [("gz", "gx", "gy")] + [("gx", "gy") if home == 2 else ("gz", "gx", "gy")] * 2
    cuts = sum(len(axes) for axes in windows) - 2
    step_rows = GROUP * TWIN
    steps = rows_here // step_rows
    spans = [steps // cuts + (k >= cuts - steps % cuts) for k in range(cuts)]
    spans = [(sum(spans[:k]) * step_rows, spans[k] * step_rows) for k in range(cuts)]

    held_span = 3 * face_rows
    written, pending, packed_results, tokens = [], [], [], []

    def collide_piece(piece):
        token = like(GROUP, LANES)
        whole = [solvent_shape] * 2
        write_sems = [pltpu.SemaphoreType.DMA((2,))]
        if piece < cuts:
            first, span = spans[piece]
            before = spans[piece - 1] if piece else None
            extra = pending + written
            at = 5 + len(pending)
            *outs, order = pl.pallas_call(
                functools.partial(collide_residents, cells, first, span, before),
                out_shape=whole + [like(3, span, LANES)] * 2 + [token],
                in_specs=[smem()] + [vmem()] * (4 + len(pending)) + [any_spec] * len(written),
                out_specs=[any_spec] * 2 + [vmem()] * 3,
                scratch_shapes=write_sems,
                input_output_aliases={at: 0, at + 1: 1} if written else {},
                compiler_params=params(),
                name=f"collide_{piece}",
            )(meta, dirs, table, position, velocity, *extra)
            written[:], pending[:] = outs[:2], outs[2:]
            tokens.append(order)
            return order
        before = spans[-1] if piece == cuts else None
        extra = pending + written if before else [tokens[-1]]
        outs = pl.pallas_call(
            functools.partial(
                collide_held, cells, (piece - cuts) * held_span, held_span, 6, before
            ),
            out_shape=(whole if before else [])
            + [like(6, held_span, LANES)]
            + ([token] if before else []),
            in_specs=[smem()]
            + [vmem()] * 3
            + [smem()]
            + ([vmem()] * 2 + [any_spec] * 2 if before else [any_spec]),
            out_specs=([any_spec] * 2 if before else []) + [vmem()] * (2 if before else 1),
            scratch_shapes=write_sems if before else [],
            input_output_aliases={7: 0, 8: 1} if before else {},
            compiler_params=params(),
            name=f"collide_{piece}",
        )(meta, dirs, table, held, counted, *extra)
        if before:
            written[:] = outs[:2]
            packed_results.append(outs[2])
            tokens.append(outs[3])
            return outs[3]
        packed_results.append(outs[0])
        pending[:] = pl.pallas_call(
            functools.partial(place_arrivals, face_rows, sequence),
            out_shape=[like(3, 6 * face_rows, LANES)] * 2,
            in_specs=[smem()] + [vmem()] * 2,
            out_specs=[vmem()] * 2,
            scratch_shapes=[pltpu.VMEM((6, 7 * face_rows, LANES), f32)],
            compiler_params=params(),
            name="place_arrivals",
        )(counted, *packed_results)
        return None

    piece = 0
    for step, axes in enumerate(windows):
        last = step == 2
        thunks = [functools.partial(collide_piece, piece + k) for k in range(len(axes))]
        piece += len(axes)
        ghosts, order = halo(pay, axes, home, thunks)
        final = like(3, 1, 1, 1, bead_slots)
        state = like(home * GROUP, bead_slots)
        tail = pending + written if last else [order]
        at = 6 + len(ghosts) + 2
        outcome = pl.pallas_call(
            functools.partial(
                substep,
                sizes,
                lengths,
                len(ghosts),
                home,
                step,
                (rows_here, 6 * face_rows) if last else None,
            ),
            out_shape=[final] * 2 + [solvent_shape] * 2 if last else [state] * 3,
            in_specs=[smem(), vmem(), vmem(), smem()]
            + [vmem()] * (2 + len(ghosts))
            + ([vmem()] * 2 + [any_spec] * 2 if last else [any_spec]),
            out_specs=[vmem()] * 2 + [any_spec] * 2 if last else [vmem()] * 3,
            scratch_shapes=([pltpu.SemaphoreType.DMA((2,))] if last else [])
            + force_scratch(bead_slots, many, home, 1 if last else home),
            input_output_aliases={at: 2, at + 1: 3} if last else {},
            compiler_params=params(),
            name=f"substep_{step}",
        )(meta, starts, joins, counts, speed, moved, *ghosts, *tail)
        if last:
            written[:] = outcome[2:]
        speed, moved = outcome[:2]
        pay = outcome[-1]

    count_solvent = rows_all * LANES
    return (
        written[0].reshape(3, 1, 1, 1, count_solvent),
        written[1].reshape(3, 1, 1, 1, count_solvent),
        moved,
        speed,
    )


def solution(mesh):
    return jax.shard_map(
        shards,
        mesh=mesh,
        in_specs=(
            P(None, "gx", "gy", "gz", None),
            P(None, "gx", "gy", "gz", None),
            P("gx", "gy", "gz"),
            P(None, "gx", "gy", "gz", None, None),
            P(None, "gx", "gy", "gz", None, None),
            P("gx", "gy", "gz", None),
            P(None, "gx", "gy", "gz", None),
            P(None, "gx", "gy", "gz", None),
            P("gx", "gy", "gz"),
            P(None, "gx", "gy", "gz", None),
            P("gx", "gy", "gz"),
            P(),
        ),
        out_specs=(
            P(None, "gx", "gy", "gz", None),
            P(None, "gx", "gy", "gz", None),
            P(None, "gx", "gy", "gz", None),
            P(None, "gx", "gy", "gz", None),
        ),
        check_vma=False,
    )
```

```python
import functools
import math

import jax
import jax.numpy as jnp
from jax import lax
from jax.experimental import pallas as pl
from jax.experimental.pallas import tpu as pltpu
from jax.sharding import PartitionSpec as P

UNITS = 16
NAXES = 32
CHAIN = 8
LANES = 128
GROUP = 8
TWIN = 4
EIGHT = 8
SENT = 4
PAIR = 2
TRIO = 3

bead_mass = 5.0
step_size = 0.02
spring = 30.0
reach_square = 2.25
cut_square = 2.0 ** (1.0 / 3.0)
turn_cosine = math.cos(130.0 * math.pi / 180.0)
turn_sine = math.sin(130.0 * math.pi / 180.0)
golden = math.pi * (3.0 - math.sqrt(5.0))
half_kick = 0.5 * step_size / bead_mass
far_own = 3000.0
far_ghost = 9000.0
vmem_limit = 48 * 1024 * 1024
vmem_most = 48 * 1024 * 1024
NT = (((1,), (1,)), ((), ()))
NN = (((1,), (0,)), ((), ()))
exact = lax.Precision.HIGHEST
f32 = jnp.float32
bf16 = jnp.bfloat16


def params(limit=vmem_limit):
    return pltpu.CompilerParams(vmem_limit_bytes=limit)


def vmem():
    return pl.BlockSpec(memory_space=pltpu.VMEM)


def smem():
    return pl.BlockSpec(memory_space=pltpu.SMEM)


def moved_along(value, axis, by):
    peers = lax.axis_size(axis)
    return lax.ppermute(value, axis, [(i, (i + by) % peers) for i in range(peers)])


class Cells:
    def __init__(self, size_x, size_y, size_z):
        self.sx, self.sy, self.nz = size_x, size_y, size_z
        self.inner = size_x * size_y
        self.edges = size_x + size_y + 1
        self.rows = -(-(self.inner + self.edges) // 16) * 16
        self.middle = self.rows // 2
        self.per = self.inner // self.edges
        self.depths = size_z + 1
        self.extra = -(-self.depths // self.per)
        self.height = -(-(self.depths + self.extra) // GROUP) * GROUP


def levels_of(position, meta):
    return [
        jnp.floor(jnp.floor(position[d] * UNITS + meta[d].astype(f32)) * (1.0 / UNITS))
        - meta[3 + d].astype(f32)
        for d in range(3)
    ]


def edge_of(levels, cells):
    outer = (levels[0] == cells.sx) | (levels[1] == cells.sy)
    return outer, jnp.where(levels[0] == cells.sx, levels[1], cells.sy + 1 + levels[0])


def plane_of(levels, cells):
    outer, edge = edge_of(levels, cells)
    return jnp.where(outer, cells.inner + edge, levels[0] * cells.sy + levels[1])


def place_of(levels, cells):
    outer, edge = edge_of(levels, cells)
    fold = jnp.floor((levels[2] + 0.5) * (1.0 / cells.per))
    row = jnp.where(outer, cells.depths + fold, levels[2])
    column = jnp.where(
        outer,
        (levels[2] - fold * cells.per) * cells.edges + edge,
        levels[0] * cells.sy + levels[1],
    )
    return row, column


def wide(row):
    return jnp.broadcast_to(row, (16, LANES)).astype(bf16)


def one_hot_rows(rows, height):
    middle = height // 2
    ids = lax.broadcasted_iota(jnp.int32, (height, LANES), 0) - middle
    ids = ids.astype(f32).astype(bf16).reshape(height // 16, 16, LANES)
    one, zero = jnp.ones((), bf16), jnp.zeros((), bf16)
    pieces = [
        jnp.where(ids == wide(row - middle)[None], one, zero).reshape(height, LANES)
        for row in rows
    ]
    return jnp.concatenate(pieces, axis=1)


def one_hot(column, height):
    return one_hot_rows([column[r : r + 1] for r in range(column.shape[0])], height)


def split(value):
    high = value.astype(bf16).astype(f32)
    return high, value - high


def spread_moments(depth, weight, velocity, cells):
    nz = cells.nz
    ids = lax.broadcasted_iota(jnp.int32, (nz, LANES), 0).astype(f32).astype(bf16)
    ids = ids.reshape(nz // 16, 16, LANES)
    row_ids = lax.broadcasted_iota(jnp.int32, (16, LANES), 0).astype(f32).astype(bf16)
    zero = jnp.zeros((), bf16)
    parts = [split(weight * velocity[d]) for d in range(3)]
    channels = [weight] + [p[0] for p in parts] + [p[1] for p in parts]
    pieces = []
    for r in range(depth.shape[0]):
        at = wide(depth[r : r + 1])
        here = ids == at[None]
        values = [wide(c[r : r + 1]) for c in channels]
        tiles = [jnp.where(here, v[None], zero).reshape(nz, LANES) for v in values]
        top = jnp.zeros((16, LANES), bf16)
        for c, v in enumerate(values):
            top = jnp.where(row_ids == c, v, top)
        top = jnp.where(at == nz, top, zero)
        pieces.append(
            jnp.concatenate(
                tiles[:4] + [top, jnp.zeros((nz - 16, LANES), bf16)] + tiles[4:], axis=0
            )
        )
    return jnp.concatenate(pieces, axis=1)


def bin_group(total_ref, position, velocity, weight, meta, cells):
    levels = levels_of(position, meta)
    hot = one_hot(plane_of(levels, cells), cells.rows)
    spread = spread_moments(levels[2], weight, velocity, cells)
    total_ref[...] += lax.dot_general(hot, spread, NT, preferred_element_type=f32)


def row_iota():
    return lax.broadcasted_iota(jnp.int32, (GROUP, LANES), 0)


def bin_residents(cells, first, count, meta_ref, pos_ref, vel_ref, *refs):
    total_ref = refs[-1]
    meta = [meta_ref[k] for k in range(8)]
    if first == 0:
        total_ref[...] = jnp.zeros_like(total_ref)
    else:
        total_ref[...] = refs[0][...]
    live_rows = meta[6] - first
    stride = GROUP * EIGHT

    @pl.loop(0, jnp.clip((live_rows + stride - 1) // stride, 0, count // stride))
    def _(step):
        for part in range(EIGHT):
            offset = pl.multiple_of(step * stride + part * GROUP, GROUP)
            rows = pl.ds(first + offset, GROUP)
            position = [pos_ref[d, rows, :] for d in range(3)]
            velocity = [vel_ref[d, rows, :] for d in range(3)]
            weight = jnp.where(row_iota() + offset < live_rows, 1.0, 0.0)
            bin_group(total_ref, position, velocity, weight, meta, cells)


def face_count(ref, first, face_rows):
    return jnp.max(ref[pl.ds(first + 6 * face_rows, GROUP), :]).astype(jnp.int32)


def take_faces(faces, face_rows, held, counts_ref, index, offset):
    for k, (ref, first) in enumerate(faces):
        count = face_count(ref, first, face_rows)
        counts_ref[index + k] = count
        for c in range(6):
            begin = first + c * face_rows
            held[c, pl.ds(offset, face_rows), :] = ref[begin : begin + face_rows, :]
        offset = offset + count
    return offset


def bin_held(held, begin, end, sums, meta, cells):
    stride = GROUP * PAIR

    @pl.loop(0, (end - begin + stride - 1) // stride)
    def _(step):
        for part in range(PAIR):
            offset = begin + step * stride + part * GROUP
            rows = pl.ds(offset, GROUP)
            comps = [held[c, rows, :] for c in range(6)]
            weight = jnp.where(row_iota() + offset < end, 1.0, 0.0)
            bin_group(sums, comps[:3], comps[3:], weight, meta, cells)


def bead_mask(chains):
    slot = row_iota() * LANES + lax.broadcasted_iota(jnp.int32, (GROUP, LANES), 1)
    return slot < CHAIN * chains


def bin_first_arrivals(cells, face_rows, places, meta_ref, *refs):
    count = len(refs) - 7
    sources = refs[:count]
    bead_pos_ref, bead_vel_ref, start_ref, order_ref, total_ref, held, counts_ref = refs[count:]
    meta = [meta_ref[k] for k in range(8)]
    total_ref[...] = start_ref[...]
    held[...] = jnp.zeros_like(held)
    faces = [(sources[which], first) for which, first in places]
    end = take_faces(faces, face_rows, held, counts_ref, 0, 0)
    weight = jnp.where(bead_mask(meta[7]), bead_mass, 0.0)
    bin_group(
        total_ref,
        [bead_pos_ref[d] for d in range(3)],
        [bead_vel_ref[d] for d in range(3)],
        weight,
        meta,
        cells,
    )
    bin_held(held, 0, end, total_ref, meta, cells)


def bin_arrivals(cells, face_rows, places, known, meta_ref, *refs):
    count = len(refs) - 10
    sources = refs[:count]
    (
        axis_ref,
        held_ref,
        known_ref,
        start_ref,
        total_ref,
        low_ref,
        high_ref,
        held,
        counts_ref,
        sums,
    ) = refs[count:]
    meta = [meta_ref[k] for k in range(8)]
    sums[...] = start_ref[...]
    held[...] = held_ref[...]
    begin = 0
    for k in range(known):
        counts_ref[k] = known_ref[k]
        begin = begin + known_ref[k]
    faces = [(sources[which], first) for which, first in places]
    end = take_faces(faces, face_rows, held, counts_ref, known, begin)
    bin_held(held, begin, end, sums, meta, cells)
    nz, inner = cells.nz, cells.inner
    lane = lax.broadcasted_iota(jnp.int32, (cells.rows, LANES), 1)
    main, rest = sums[:, :LANES], sums[:, LANES:]
    main = main + jnp.where(lane < nz, 0.0, rest)
    top = jnp.where(lane == 0, rest, rest + pltpu.roll(rest, LANES - 3, axis=1))
    total_ref[0] = main
    total_ref[1] = jnp.where(lane < 4, top, 0.0)
    axis = axis_ref[...].astype(f32)
    total_ref[1, :inner, nz : 2 * nz] = axis
    sx, sy = cells.sx, cells.sy
    low_ref[...] = jnp.zeros_like(low_ref)
    high_ref[...] = jnp.zeros_like(high_ref)
    for half in range(2):
        corner = inner + sy + 1
        low_ref[half, :sy, :] = total_ref[half, :sy, :]
        low_ref[half, sy : sy + 1, :] = total_ref[half, corner : corner + 1, :]
        high_ref[half, : sy + 1, :] = total_ref[half, inner : inner + sy + 1, :]


def add_faces_x(cells, total_ref, below_ref, above_ref, order_ref, out_ref, low_ref, high_ref):
    sx, sy, inner = cells.sx, cells.sy, cells.inner
    corner = inner + sy + 1
    out_ref[...] = total_ref[...]
    low_ref[...] = jnp.zeros_like(low_ref)
    high_ref[...] = jnp.zeros_like(high_ref)
    for half in range(2):
        out_ref[half, :sy, :] += below_ref[half, :sy, :]
        out_ref[half, corner : corner + 1, :] += below_ref[half, sy : sy + 1, :]
        out_ref[half, inner : inner + sy + 1, :] += above_ref[half, : sy + 1, :]
        low_ref[half, :sx, :] = out_ref[half, pl.ds(0, sx, stride=sy), :]
        low_ref[half, sx : sx + 1, :] = out_ref[half, inner : inner + 1, :]
        high_ref[half, :sx, :] = out_ref[half, corner : corner + sx, :]
        high_ref[half, sx : sx + 1, :] = out_ref[half, inner + sy : inner + sy + 1, :]


def add_faces_y(cells, total_ref, below_ref, above_ref, out_ref, face_ref, sums):
    sx, sy, nz, inner = cells.sx, cells.sy, cells.nz, cells.inner
    corner = inner + sy + 1
    sums[...] = total_ref[...]
    for half in range(2):
        sums[half, pl.ds(0, sx, stride=sy), :] += below_ref[half, :sx, :]
        sums[half, inner : inner + 1, :] += below_ref[half, sx : sx + 1, :]
        sums[half, corner : corner + sx, :] += above_ref[half, :sx, :]
        sums[half, inner + sy : inner + sy + 1, :] += above_ref[half, sx : sx + 1, :]
    main = sums[0].T
    rest = sums[1].T
    out_ref[:LANES, :] = main
    out_ref[LANES : LANES + nz, :] = rest[nz : 2 * nz]
    out_ref[LANES + nz :, :] = jnp.zeros((GROUP, cells.rows), f32)
    out_ref[LANES + nz : LANES + nz + 4, :] = rest[:4]
    face_ref[...] = jnp.zeros_like(face_ref)
    for c in range(5):
        face_ref[c : c + 1, :] = out_ref[c * nz : c * nz + 1, :]
        face_ref[GROUP + c : GROUP + c + 1, :] = out_ref[5 * nz + c : 5 * nz + c + 1, :]


def cell_table(cells, total_ref, below_ref, above_ref, table_ref, sheet, edge):
    nz, inner, height = cells.nz, cells.inner, cells.height
    row_ids = lax.broadcasted_iota(jnp.int32, (nz, cells.rows), 0)
    parts = []
    tops = []
    for c in range(5):
        face = jnp.where(row_ids == 0, below_ref[GROUP + c : GROUP + c + 1, :], 0.0)
        parts.append(total_ref[c * nz : (c + 1) * nz, :] + face)
        tops.append(
            total_ref[5 * nz + c : 5 * nz + c + 1, :] + above_ref[c : c + 1, :]
        )
    mass = jnp.maximum(parts[0], 1.0)
    top_mass = jnp.maximum(tops[0], 1.0)
    values = [parts[4]] + [p / mass for p in parts[1:4]]
    top_values = [tops[4]] + [t / top_mass for t in tops[1:4]]
    sheet[...] = jnp.zeros_like(sheet)
    edge[...] = jnp.zeros_like(edge)
    lane = lax.broadcasted_iota(jnp.int32, (cells.extra, LANES), 1)
    spare = LANES - (cells.rows - inner)
    for c in range(4):
        base = c * height
        sheet[base : base + nz, :] = values[c][:, :inner]
        sheet[base + nz : base + nz + 1, :] = top_values[c][:, :inner]
        edge[base : base + nz, :] = jnp.concatenate(
            [values[c][:, inner:], jnp.zeros((nz, spare), f32)], axis=1
        )
        edge[base + nz : base + nz + 1, :] = jnp.concatenate(
            [top_values[c][:, inner:], jnp.zeros((1, spare), f32)], axis=1
        )
        folded = [jnp.zeros((cells.extra, LANES), f32) for _ in range(inner // LANES)]
        for m in range(cells.per):
            begin = m * cells.edges
            piece = edge[pl.ds(base + m, cells.extra, stride=cells.per), :]
            piece = pltpu.roll(piece, begin % LANES, axis=1) if begin % LANES else piece
            for t in range(inner // LANES):
                low, high = begin - t * LANES, begin + cells.edges - t * LANES
                if high > 0 and low < LANES:
                    folded[t] = jnp.where((lane >= low) & (lane < high), piece, folded[t])
        sheet[base + nz + 1 : base + nz + 1 + cells.extra, :] = jnp.concatenate(folded, axis=1)
    whole = sheet[...]
    high = whole.astype(bf16).astype(f32)
    low = (whole - high)[height:]
    table_ref[...] = jnp.concatenate([high, low], axis=0).astype(bf16)


def direction_table():
    counter = jnp.arange(LANES).astype(f32)
    height = 1.0 - (2.0 * counter + 1.0) / NAXES
    radius = jnp.sqrt(jnp.maximum(1.0 - height * height, 0.0))
    rows = jnp.stack([radius * jnp.cos(golden * counter), radius * jnp.sin(golden * counter)])
    return jnp.broadcast_to(rows[:, None], (2, GROUP, LANES))


def fold_rows(values):
    sub = lax.broadcasted_iota(jnp.int32, (GROUP, LANES), 0)
    step = GROUP // 2
    while step:
        upper = (sub & step) == 0
        half = len(values) // 2
        joined = []
        for a, b in zip(values[:half], values[half:]):
            a = a + pltpu.roll(a, GROUP - step, axis=0)
            b = b + pltpu.roll(b, step, axis=0)
            joined.append(jnp.where(upper, a, b))
        values = joined
        step //= 2
    return values[0]


def collide(position, velocity, meta, table, dirs_ref, cells):
    height = cells.height
    row, column = place_of(levels_of(position, meta), cells)
    found = lax.dot_general(
        table, one_hot(column, cells.inner), NN, preferred_element_type=f32
    )
    ids = lax.broadcasted_iota(jnp.int32, (height, LANES), 0).astype(f32)
    picked = [[] for _ in range(4)]
    for r in range(GROUP):
        block = found[:, r * LANES : (r + 1) * LANES]
        here = ids == row[r : r + 1]
        for c in range(4):
            value = block[c * height : (c + 1) * height]
            if c > 0:
                value = value + block[(3 + c) * height : (4 + c) * height]
            value = jnp.where(here, value, 0.0)
            picked[c].append(
                jnp.sum(value.reshape(height // GROUP, GROUP, LANES), axis=0)
            )
    picked = [fold_rows(p) for p in picked]
    axis, flow = picked[0].astype(jnp.int32), picked[1:]
    normal = [
        jnp.take_along_axis(dirs_ref[0], axis, axis=1, mode="promise_in_bounds"),
        jnp.take_along_axis(dirs_ref[1], axis, axis=1, mode="promise_in_bounds"),
        1.0 - (2.0 * picked[0] + 1.0) * (1.0 / NAXES),
    ]
    rel = [velocity[d] - flow[d] for d in range(3)]
    along = (1.0 - turn_cosine) * (
        normal[0] * rel[0] + normal[1] * rel[1] + normal[2] * rel[2]
    )
    result = []
    for d in range(3):
        e, f = (d + 1) % 3, (d + 2) % 3
        crossed = normal[e] * rel[f] - normal[f] * rel[e]
        result.append(
            flow[d] + (turn_cosine * rel[d] + turn_sine * crossed + along * normal[d])
        )
    return result


def passed(position, speed):
    return position - jnp.floor(position) - 0.5 + 3.0 * step_size * speed


def writing(spans, refs, sems):
    copies = []
    for k, ((first, count), (value, out)) in enumerate(zip(spans, refs)):
        copies.append(
            pltpu.make_async_copy(value, out.at[:, pl.ds(first, count), :], sems.at[k])
        )
    for copy in copies:
        copy.start()

    def finish():
        for copy in copies:
            copy.wait()

    return finish


def collide_residents(
    cells, first, count, before, meta_ref, dirs_ref, table_ref, pos_ref, vel_ref, *refs
):
    out_pos, out_vel, new_pos, new_vel, token, sems = refs[-6:]
    finish = writing([before] * 2, [(refs[0], out_pos), (refs[1], out_vel)], sems) if before else None
    token[...] = jnp.zeros_like(token)
    meta = [meta_ref[k] for k in range(8)]
    table = table_ref[...]
    live_rows = meta[6] - first
    new_pos[...] = jnp.zeros_like(new_pos)
    new_vel[...] = jnp.zeros_like(new_vel)
    stride = GROUP * TWIN

    @pl.loop(0, jnp.clip((live_rows + stride - 1) // stride, 0, count // stride))
    def _(step):
        for part in range(TWIN):
            offset = pl.multiple_of(step * stride + part * GROUP, GROUP)
            rows = pl.ds(first + offset, GROUP)
            position = [pos_ref[d, rows, :] for d in range(3)]
            velocity = [vel_ref[d, rows, :] for d in range(3)]
            live = row_iota() + offset < live_rows
            speed = collide(position, velocity, meta, table, dirs_ref, cells)
            rows = pl.ds(offset, GROUP)
            for d in range(3):
                new_vel[d, rows, :] = jnp.where(live, speed[d], 0.0)
                new_pos[d, rows, :] = jnp.where(live, passed(position[d], speed[d]), 0.0)

    if finish:
        finish()


def collide_held(
    cells, first, count, many, before, meta_ref, dirs_ref, table_ref, held, counts_ref, *refs
):
    if before:
        out_pos, out_vel, out_ref, token, sems = refs[-5:]
        finish = writing([before] * 2, [(refs[0], out_pos), (refs[1], out_vel)], sems)
        token[...] = jnp.zeros_like(token)
    else:
        out_ref = refs[-1]
        finish = None
    meta = [meta_ref[k] for k in range(8)]
    table = table_ref[...]
    out_ref[...] = jnp.zeros_like(out_ref)
    end = sum([counts_ref[k] for k in range(many)], jnp.int32(0)) - first
    stride = GROUP * TRIO

    @pl.loop(0, jnp.clip((end + stride - 1) // stride, 0, count // stride))
    def _(step):
        for part in range(TRIO):
            offset = pl.multiple_of(step * stride + part * GROUP, GROUP)
            comps = [held[c, pl.ds(first + offset, GROUP), :] for c in range(6)]
            speed = collide(comps[:3], comps[3:], meta, table, dirs_ref, cells)
            for d in range(3):
                out_ref[d, pl.ds(offset, GROUP), :] = speed[d]
                out_ref[3 + d, pl.ds(offset, GROUP), :] = passed(comps[d], speed[d])

    if finish:
        finish()


def place_arrivals(face_rows, sequence, counts_ref, *refs):
    pieces = refs[:-3]
    new_pos, new_vel, packed = refs[-3:]
    packed[...] = jnp.zeros_like(packed)
    at = 0
    for piece in pieces:
        packed[:, at : at + piece.shape[1], :] = piece[...]
        at += piece.shape[1]
    rows = lax.broadcasted_iota(jnp.int32, (face_rows, LANES), 0)
    offset = 0
    for k, face in enumerate(sequence):
        count = counts_ref[k]
        place = slice(face * face_rows, (face + 1) * face_rows)
        for d in range(3):
            speed = packed[d, pl.ds(offset, face_rows), :]
            moved = packed[3 + d, pl.ds(offset, face_rows), :]
            new_vel[d, place, :] = jnp.where(rows < count, speed, 0.0)
            new_pos[d, place, :] = jnp.where(rows < count, moved, 0.0)
        offset = offset + count


def pack_inputs(
    meta_ref,
    pos_ref,
    vel_ref,
    bead_pos_ref,
    bead_vel_ref,
    bond_ref,
    order_ref,
    start_ref,
    block_ref,
    rows_pos_ref,
    rows_vel_ref,
    *refs,
):
    out_refs, (held_pos, held_vel, sems) = refs[:6], refs[6:]
    copies = [(bead_pos_ref, held_pos), (bead_vel_ref, held_vel)]
    for face, out_ref in enumerate(out_refs):
        copies.append((pos_ref.at[:, face], out_ref.at[0:3]))
        copies.append((vel_ref.at[:, face], out_ref.at[3:6]))
    copies = [pltpu.make_async_copy(a, b, sems.at[k]) for k, (a, b) in enumerate(copies)]
    for copy in copies:
        copy.start()
    for face, out_ref in enumerate(out_refs):
        out_ref[6] = jnp.full(out_ref.shape[1:], meta_ref[8 + face], jnp.int32).astype(f32)
    slots = start_ref.shape[1]
    start_ref[...] = jnp.zeros_like(start_ref)
    rows_pos_ref[...] = jnp.zeros_like(rows_pos_ref)
    rows_vel_ref[...] = jnp.zeros_like(rows_vel_ref)
    for copy in copies:
        copy.wait()
    for d in range(3):
        for k in range(slots // LANES):
            lanes = slice(k * LANES, (k + 1) * LANES)
            start_ref[d : d + 1, lanes] = held_pos[d, k : k + 1, :]
            rows_pos_ref[d, k : k + 1, :] = held_pos[d, k : k + 1, :]
            rows_vel_ref[d, k : k + 1, :] = held_vel[d, k : k + 1, :]
    bond_slots = bond_ref.shape[-1]
    ends = jnp.concatenate(
        [bond_ref[k, 0, 0, :, :].astype(f32) for k in range(2)]
        + [jnp.zeros((GROUP - 2, bond_slots), f32)],
        axis=0,
    )
    if bond_slots < slots:
        ends = jnp.concatenate([ends, jnp.zeros((GROUP, slots - bond_slots), f32)], axis=1)
    start = start_ref[...]
    whole = payload(start, slot_live(slots, meta_ref[7], GROUP), ends)
    for k in range(slots // LANES):
        block_ref[k * GROUP : (k + 1) * GROUP, :] = whole[:, k * LANES : (k + 1) * LANES]


def stack_rows(parts, *refs):
    out_ref = refs[-1]
    at = 0
    for which, begin, count in parts:
        out_ref[at : at + count, :] = refs[which][begin : begin + count, :]
        at += count


def slot_live(slots, chains, rows):
    return lax.broadcasted_iota(jnp.int32, (rows, slots), 1) < CHAIN * chains


def payload(position, live, more):
    row_ids = lax.broadcasted_iota(jnp.int32, position.shape, 0)
    flag = jnp.where(live, 1.0, 0.0)
    rest = pltpu.roll(more, 4, axis=0)
    return jnp.where(row_ids == 3, flag, jnp.where(row_ids < 3, position, rest))


def thirds_of(value):
    high = value.astype(bf16).astype(f32)
    middle = (value - high).astype(bf16).astype(f32)
    low = value - high - middle
    return jnp.concatenate([high, middle, low, jnp.zeros_like(value)], axis=0).astype(bf16)


def summed_thirds(value):
    rows = value.shape[0] // 4
    return value[:rows] + (value[rows : 2 * rows] + value[2 * rows : 3 * rows])


def joins_of(block, chains, bond_slots):
    ends = block.T
    slots = block.shape[1]
    slot_ids = lax.broadcasted_iota(jnp.int32, (slots, slots), 1).astype(f32)
    bond_ids = lax.broadcasted_iota(jnp.int32, (slots, slots), 0)
    joins = jnp.where(slot_ids == ends[:, 4:5], 1.0, 0.0)
    joins = joins - jnp.where(slot_ids == ends[:, 5:6], 1.0, 0.0)
    live = jnp.minimum((CHAIN - 1) * chains, bond_slots)
    return jnp.where(bond_ids < live, joins, 0.0).astype(bf16)


def bond_forces(local, joins, chains):
    stretch = summed_thirds(
        lax.dot_general(thirds_of(local), joins, NT, preferred_element_type=f32)
    )
    square = (
        stretch[0:1] * stretch[0:1] + stretch[1:2] * stretch[1:2] + stretch[2:3] * stretch[2:3]
    )
    live = lax.broadcasted_iota(jnp.int32, (1, joins.shape[0]), 1) < (CHAIN - 1) * chains
    pull = jnp.where(live, -spring / (1.0 - square / reach_square), 0.0) * stretch
    return summed_thirds(lax.dot_general(thirds_of(pull), joins, NN, preferred_element_type=f32))


def forces(blocks, counts, joins, mains, home, centre, lengths, mine_ref, packed, push, near_mask):
    slots = blocks[0].shape[1]
    tiles = slots // LANES
    row_ids = lax.broadcasted_iota(jnp.int32, (GROUP, slots), 0)
    lane_ids = lax.broadcasted_iota(jnp.int32, (GROUP, slots), 1)
    mid = jnp.zeros((GROUP, slots), f32)
    length = jnp.full((GROUP, slots), 1e9, f32)
    for d in range(3):
        mid = jnp.where(row_ids == d, centre[d], mid)
        if d < 2:
            length = jnp.where(row_ids == d, lengths[d], length)
    inverse_length = 1.0 / length
    near = [block - mid for block in blocks[:home]]
    for block in blocks[home:]:
        rows = block.shape[0]
        value = block - mid[:rows]
        near.append(value - length[:rows] * jnp.floor(value * inverse_length[:rows] + 0.5))

    low = jnp.full((GROUP, slots), far_ghost, f32)
    high = jnp.full((GROUP, slots), -far_ghost, f32)
    bonds = []
    for b in range(mains):
        live = lane_ids < counts[b]
        columns = jnp.where(live, near[b], far_own).T
        for d in range(3):
            mine_ref[d, b * slots : (b + 1) * slots, :] = jnp.broadcast_to(
                columns[:, d : d + 1], (slots, LANES)
            )
        low = jnp.minimum(low, jnp.where(live, near[b], far_ghost))
        high = jnp.maximum(high, jnp.where(live, near[b], -far_ghost))
        local = jnp.where(live & (row_ids < 3), near[b], 0.0)
        bonds.append(bond_forces(local, joins[b], counts[b] // CHAIN))

    packed[...] = jnp.full(packed.shape, far_ghost, f32)
    lane = lax.broadcasted_iota(jnp.int32, (GROUP, LANES), 1)
    offset = jnp.int32(0)
    for value, count in zip(near[:home], counts[:home]):
        tile, turn = offset // LANES, offset % LANES
        turned = [
            pltpu.roll(value[:, k * LANES : (k + 1) * LANES], turn, axis=1)
            for k in range(tiles)
        ]
        for k in range(tiles + 1):
            if k == 0:
                piece = turned[0]
            elif k == tiles:
                piece = turned[-1]
            else:
                piece = jnp.where(lane < turn, turned[k - 1], turned[k])
            place = (tile + k) * LANES + lane
            taken = (place >= offset) & (place < offset + count)
            packed[tile + k] = jnp.where(taken, piece, packed[tile + k])
        offset = offset + count
    first_tile = (offset + LANES - 1) // LANES

    reach = 1.001 * math.sqrt(cut_square)
    low = jnp.min(low, axis=1, keepdims=True) - reach
    high = jnp.max(high, axis=1, keepdims=True) + reach
    others = near[home:]
    near_mask[...] = jnp.zeros_like(near_mask)
    for k, value in enumerate(others):
        inside = jnp.where((value >= low[:SENT]) & (value <= high[:SENT]), 1.0, 0.0)
        inside = inside[0:1] * inside[1:2]
        live = lane_ids[0:1] < counts[home + k]
        near_mask[k : k + 1, :] = jnp.where(live, inside, 0.0)
    mask = near_mask[...]
    height = mask.shape[0]
    mask_bf16 = mask.astype(bf16)
    upto = jnp.where(
        lax.broadcasted_iota(jnp.int32, (slots, slots), 0)
        <= lax.broadcasted_iota(jnp.int32, (slots, slots), 1),
        1.0,
        0.0,
    ).astype(bf16)
    above = jnp.where(
        lax.broadcasted_iota(jnp.int32, (height, height), 1)
        < lax.broadcasted_iota(jnp.int32, (height, height), 0),
        1.0,
        0.0,
    ).astype(bf16)
    within = lax.dot_general(mask_bf16, upto, NN, preferred_element_type=f32)
    before = lax.dot_general(above, mask_bf16, NN, preferred_element_type=f32)
    before = jnp.sum(before, axis=1, keepdims=True)
    place = jnp.where(mask > 0.5, within + before - 1.0, -1.0)
    found = jnp.sum(mask).astype(jnp.int32)
    parts = jnp.concatenate([thirds_of(value) for value in others], axis=1)
    found_tiles = (found + LANES - 1) // LANES

    @pl.loop(0, found_tiles)
    def _(tile):
        goal = place - (tile * LANES).astype(f32)
        rows = [
            goal[k : k + 1, t * LANES : (t + 1) * LANES]
            for k in range(len(others))
            for t in range(tiles)
        ]
        chosen = one_hot_rows(rows, LANES)
        value = summed_thirds(
            lax.dot_general(parts, chosen, NT, preferred_element_type=f32)
        )
        there = tile * LANES + lane[:SENT] < found
        packed[first_tile + tile, :SENT, :] = jnp.where(there, value, far_ghost)

    push[...] = jnp.zeros_like(push)
    chunk = 64
    steps = (first_tile + found_tiles + 1) // 2
    period = lengths[2]

    for b in range(mains):

        @pl.loop(0, (counts[b] + chunk - 1) // chunk)
        def _(part):
            rows = pl.ds(pl.multiple_of(b * slots + part * chunk, chunk), chunk)
            mine = [mine_ref[d, rows, :] for d in range(3)]

            def add_tiles(step, total):
                for k in range(2):
                    other = packed[2 * step + k]
                    differ = [mine[d] - other[d : d + 1] for d in range(3)]
                    differ[2] = differ[2] - period * jnp.floor(
                        differ[2] * (1.0 / period) + 0.5
                    )
                    square = (
                        differ[0] * differ[0] + differ[1] * differ[1] + differ[2] * differ[2]
                    )
                    inside = (square < cut_square) & (square > 0.25)
                    inverse = 1.0 / jnp.where(inside, square, 1e30)
                    sixth = inverse * inverse * inverse
                    weight = (sixth * inverse) * (48.0 * sixth - 24.0)
                    total = tuple(total[d] + weight * differ[d] for d in range(3))
                return total

            total = lax.fori_loop(
                0, steps, add_tiles, tuple(jnp.zeros((chunk, LANES), f32) for _ in range(3))
            )
            for d in range(3):
                push[d, rows, :] = total[d]

    result = []
    for b in range(mains):
        pair = jnp.zeros((GROUP, slots), f32)
        for d in range(3):
            line = jnp.sum(push[d, b * slots : (b + 1) * slots, :].T, axis=0, keepdims=True)
            pair = jnp.where(row_ids == d, line, pair)
        result.append(pair + bonds[b])
    return result


def force_scratch(slots, blocks, home, mains):
    tiles = home * slots // LANES + 2 + (blocks - home) * slots // LANES
    return [
        pltpu.VMEM((3, mains * slots, LANES), f32),
        pltpu.VMEM((-(-tiles // 2) * 2, GROUP, LANES), f32),
        pltpu.VMEM((3, mains * slots, LANES), f32),
        pltpu.VMEM((-(-(blocks - home) // 16) * 16, slots), f32),
    ]


def blocks_of(home, home_ref, refs):
    others = [
        ref[b * SENT : (b + 1) * SENT, :]
        for ref in refs
        for b in range(ref.shape[0] // SENT)
    ]
    return [home_ref[b * GROUP : (b + 1) * GROUP, :] for b in range(home)] + others[home:]


def centre_of(meta, sizes):
    return [meta[3 + d].astype(f32) + 0.5 * sizes[d] for d in range(3)]


def joined_blocks(ref, rows, tiles):
    return [
        jnp.concatenate(
            [ref[(b * tiles + k) * rows : (b * tiles + k + 1) * rows, :] for k in range(tiles)],
            axis=1,
        )
        for b in range(ref.shape[0] // (rows * tiles))
    ]


def first_forces(sizes, lengths, sources, home, bond_slots, meta_ref, home_ref, *refs):
    sources_refs, (push_ref, counts_ref, joins_ref, starts_ref), scratch = (
        refs[:sources],
        refs[sources : sources + 4],
        refs[sources + 4 :],
    )
    meta = [meta_ref[k] for k in range(8)]
    tiles = push_ref.shape[1] // LANES
    blocks = [block for ref in sources_refs for block in joined_blocks(ref, SENT, tiles)]
    blocks = joined_blocks(home_ref, GROUP, tiles) + blocks[home:]
    counts = [jnp.sum(block[3:4]).astype(jnp.int32) for block in blocks]
    for k, count in enumerate(counts):
        counts_ref[k] = count
    joins = []
    for b in range(home):
        starts_ref[b * GROUP : (b + 1) * GROUP, :] = blocks[b]
        joins.append(joins_of(blocks[b], counts[b] // CHAIN, bond_slots))
        joins_ref[b] = joins[b]
    push_ref[...] = forces(
        blocks, counts, joins, 1, home, centre_of(meta, sizes), lengths, *scratch
    )[0]


def finish_cells(
    cells,
    meta_ref,
    dirs_ref,
    total_ref,
    below_ref,
    above_ref,
    bead_pos_ref,
    bead_vel_ref,
    start_ref,
    push_ref,
    table_ref,
    speed_ref,
    moved_ref,
    pay_ref,
    sheet,
    edge,
):
    meta = [meta_ref[k] for k in range(8)]
    cell_table(cells, total_ref, below_ref, above_ref, table_ref, sheet, edge)
    fresh = collide(
        [bead_pos_ref[d] for d in range(3)],
        [bead_vel_ref[d] for d in range(3)],
        meta,
        table_ref[...],
        dirs_ref,
        cells,
    )
    start = start_ref[...]
    slots = start.shape[1]
    row_ids = lax.broadcasted_iota(jnp.int32, (GROUP, slots), 0)
    speed = jnp.zeros((GROUP, slots), f32)
    for d in range(3):
        line = jnp.concatenate([fresh[d][k : k + 1] for k in range(slots // LANES)], axis=1)
        speed = jnp.where(row_ids == d, line, speed)
    speed = speed + half_kick * push_ref[...]
    moved = step_size * speed
    live = slot_live(slots, meta[7], GROUP)
    speed_ref[...] = speed
    moved_ref[...] = moved
    pay_ref[...] = payload(start + moved, live, speed)


def substep(
    sizes, lengths, sources, home, step, last, meta_ref, start_ref, joins_ref, counts_ref, speed_ref, moved_ref, *refs
):
    came, rest = refs[:sources], refs[sources:]
    if last:
        new_pos, new_vel, _, _, *outs, sems, a, b, c, e = rest
        finish = writing([last] * 2, [(new_pos, outs[2]), (new_vel, outs[3])], sems)
    else:
        _, *outs, a, b, c, e = rest
    meta = [meta_ref[k] for k in range(8)]
    blocks = blocks_of(home, came[0], came[1:])
    counts = [counts_ref[k] for k in range(len(blocks))]
    mains = 1 if last else home
    joins = [joins_ref[b] for b in range(mains)]
    pushes = forces(
        blocks, counts, joins, mains, home, centre_of(meta, sizes), lengths, a, b, c, e
    )
    slots = start_ref.shape[1]
    row_ids = lax.broadcasted_iota(jnp.int32, (GROUP, slots), 0)
    for b in range(mains):
        rows = slice(b * GROUP, (b + 1) * GROUP)
        live = lax.broadcasted_iota(jnp.int32, (GROUP, slots), 1) < counts[b]
        start = start_ref[rows, :]
        if step == 0 and b > 0:
            speed = jnp.where(row_ids < 3, pltpu.roll(blocks[b], 4, axis=0), 0.0)
            moved = step_size * speed
        else:
            speed, moved = speed_ref[rows, :], moved_ref[rows, :]
        speed = speed + half_kick * pushes[b]
        if last:
            for d in range(3):
                outs[0][d, 0, 0, :, :] = jnp.where(live, speed, 0.0)[d : d + 1]
                outs[1][d, 0, 0, :, :] = jnp.where(live, moved, 0.0)[d : d + 1]
            finish()
            return
        speed = speed + half_kick * pushes[b]
        moved = moved + step_size * speed
        outs[0][rows, :] = speed
        outs[1][rows, :] = moved
        outs[2][rows, :] = payload(start + moved, live, speed)


def neighbours(value, axis):
    peers = lax.axis_size(axis)
    if peers == 2:
        return [moved_along(value, axis, 1)]
    return [moved_along(value, axis, 1), moved_along(value, axis, -1)]


def stacked(parts, operands, order=()):
    rows = sum(count for _, _, count in parts)
    width = operands[0].shape[1]
    return pl.pallas_call(
        functools.partial(stack_rows, tuple(parts)),
        out_shape=like(rows, width),
        in_specs=[vmem()] * len(operands) + [pl.BlockSpec(memory_space=pl.ANY)] * len(order),
        out_specs=vmem(),
        compiler_params=params(),
        name="stack_rows",
    )(*operands, *order)


def whole_rows(operands):
    return [(k, 0, value.shape[0]) for k, value in enumerate(operands)]


def halo(pay, axes, home, pieces):
    rows = pay
    axes, pieces = list(axes), list(pieces)
    if axes[0] == "gz":
        parts = [pay] + neighbours(pay, "gz")
        rows = stacked(whole_rows(parts), parts, [pieces.pop(0)()])
        axes.pop(0)
    count = rows.shape[0] // GROUP
    sent = stacked([(0, b * GROUP, SENT) for b in range(count)], [rows])
    for axis, piece in zip(axes[:-1], pieces):
        parts = [sent] + neighbours(sent, axis)
        sent = stacked(whole_rows(parts), parts, [piece()])
    sides = neighbours(sent, axes[-1])
    own = rows if count == home else pay
    return [own, sent] + sides, pieces[-1]()


def like(*shape, dtype=f32):
    return jax.ShapeDtypeStruct(shape, dtype)


def shards(
    sol_pos,
    sol_vel,
    sol_rows,
    mig_pos,
    mig_vel,
    mig_rows,
    bead_pos,
    bead_vel,
    bead_chains,
    bond_list,
    cell_axis,
    shift,
):
    sizes = cell_axis.shape
    cells = Cells(*sizes)
    names = ("gx", "gy", "gz")
    lengths = tuple(float(sizes[d] * lax.axis_size(names[d])) for d in range(3))
    slots_here = sol_pos.shape[-1]
    buffer_slots = mig_pos.shape[-1]
    bead_slots = bead_pos.shape[-1]
    bond_slots = bond_list.shape[-1]
    rows_here = slots_here // LANES
    face_rows = buffer_slots // LANES
    rows_all = rows_here + 6 * face_rows
    anchor = jnp.stack([lax.axis_index(names[d]) * sizes[d] for d in range(3)])
    meta = jnp.concatenate(
        [
            shift,
            anchor.astype(jnp.int32),
            sol_rows.reshape(1),
            bead_chains.reshape(1),
            mig_rows.reshape(6),
        ]
    )
    dirs = direction_table()
    position = sol_pos.reshape(3, rows_here, LANES)
    velocity = sol_vel.reshape(3, rows_here, LANES)

    any_spec = pl.BlockSpec(memory_space=pl.ANY)
    unit = GROUP * EIGHT
    units = rows_here // unit
    heights = [units // 6 * unit, units // 6 * 2 * unit]
    heights.append(rows_here - sum(heights))
    axis_rows = cell_axis.reshape(cells.inner, sizes[2])

    def bin_piece(piece, earlier, order):
        count = heights[piece]
        sources = [position, velocity] if piece else [position[:, :count], velocity[:, :count]]
        return pl.pallas_call(
            functools.partial(bin_residents, cells, sum(heights[:piece]), count),
            out_shape=like(cells.rows, 2 * LANES),
            in_specs=[smem()]
            + [vmem()] * (2 + len(earlier))
            + [any_spec] * len(order),
            out_specs=vmem(),
            compiler_params=params(),
            name=f"bin_residents_{piece}",
        )(meta, *sources, *earlier, *order)

    totals = bin_piece(0, [], [])
    face_height = 7 * face_rows
    bead_shape = like(GROUP, bead_slots)
    tiles = bead_slots // LANES
    rows_shape = like(3, GROUP, LANES)
    start, block, bead_rows_pos, bead_rows_vel, *packed = pl.pallas_call(
        pack_inputs,
        out_shape=[
            bead_shape,
            like(tiles * GROUP, LANES),
            rows_shape,
            rows_shape,
        ]
        + [like(7, face_rows, LANES)] * 6,
        in_specs=[smem()]
        + [pl.BlockSpec(memory_space=pltpu.HBM)] * 4
        + [vmem(), any_spec],
        out_specs=[vmem()] * 10,
        scratch_shapes=[pltpu.VMEM((3, tiles, LANES), f32)] * 2
        + [pltpu.SemaphoreType.DMA((14,))],
        compiler_params=params(vmem_most),
        name="pack_inputs",
    )(
        meta,
        mig_pos.reshape(3, 6, face_rows, LANES),
        mig_vel.reshape(3, 6, face_rows, LANES),
        bead_pos.reshape(3, tiles, LANES),
        bead_vel.reshape(3, tiles, LANES),
        bond_list,
        totals,
    )
    packed = [value.reshape(face_height, LANES) for value in packed]

    def swap(axis, low, high, body):
        if lax.axis_size(axis) == 2:
            both = [packed[low], packed[high], body]
            came = moved_along(stacked(whole_rows(both), both), axis, 1)
            return [came], [(0, face_height), (0, 0)], [(0, 2 * face_height)]
        up = stacked(whole_rows([packed[high], body]), [packed[high], body])
        down = stacked(whole_rows([packed[low], body]), [packed[low], body])
        came = [moved_along(up, axis, 1), moved_along(down, axis, -1)]
        return came, [(0, 0), (1, 0)], [(0, face_height), (1, face_height)]

    def short(operand, first):
        return [(operand, first + k * GROUP, SENT) for k in range(tiles)]

    home = 2 if lax.axis_size("gz") == 2 else 1
    arriving, spots, blocks = [], [None] * 6, block
    for piece, (axis, low) in enumerate((("gz", 4), ("gx", 0), ("gy", 2))):
        came, places, bodies = swap(axis, low, low + 1, blocks)
        for k, (which, at) in enumerate(places):
            spots[low + k] = (len(arriving) + which, at)
        arriving += came
        height = blocks.shape[0]
        if axis == "gy":
            around = [blocks] + [stacked([(0, at, height)], [came[w]]) for w, at in bodies]
            break
        totals = bin_piece(piece + 1, [totals], [blocks])
        if axis == "gz":
            own = [(0, 0, height)] + [(1 + w, at, height) for w, at in bodies][: home - 1]
            starts = stacked(own, [blocks] + came)
            parts = short(0, 0) + [p for w, at in bodies for p in short(1 + w, at)]
        else:
            parts = [(0, 0, height)] + [(1 + w, at, height) for w, at in bodies]
        blocks = stacked(parts, [blocks] + came, [totals])

    sequence = (4, 5, 0, 1, 2, 3)
    early, late = sequence[:4], sequence[4:]
    sooner = max(spots[face][0] for face in early) + 1
    held_rows = -(-6 * face_rows // 32) * 32
    held_shape = like(6, held_rows, LANES)
    totals, held, counted = pl.pallas_call(
        functools.partial(
            bin_first_arrivals, cells, face_rows, [spots[face] for face in early]
        ),
        out_shape=[like(cells.rows, 2 * LANES), held_shape, like(4, dtype=jnp.int32)],
        in_specs=[smem()] + [vmem()] * (sooner + 3) + [any_spec],
        out_specs=[vmem(), vmem(), smem()],
        compiler_params=params(),
        name="bin_first_arrivals",
    )(meta, *arriving[:sooner], bead_rows_pos, bead_rows_vel, totals, blocks)

    face_x = like(2, -(-(sizes[1] + 1) // GROUP) * GROUP, LANES)
    face_y = like(2, -(-(sizes[0] + 1) // GROUP) * GROUP, LANES)
    later = arriving[sooner:]
    totals, low, high, held, counted = pl.pallas_call(
        functools.partial(
            bin_arrivals,
            cells,
            face_rows,
            [(spots[face][0] - sooner, spots[face][1]) for face in late],
            len(early),
        ),
        out_shape=[
            like(2, cells.rows, LANES),
            face_x,
            face_x,
            held_shape,
            like(6, dtype=jnp.int32),
        ],
        in_specs=[smem()] + [vmem()] * (len(later) + 2) + [smem(), vmem()],
        out_specs=[vmem()] * 4 + [smem()],
        scratch_shapes=[pltpu.VMEM((cells.rows, 2 * LANES), f32)],
        compiler_params=params(),
        name="bin_arrivals",
    )(meta, *later, axis_rows, held, counted, totals)

    many = sum(value.shape[0] // (SENT * tiles) for value in around)
    push, counts, joins, starts = pl.pallas_call(
        functools.partial(first_forces, sizes, lengths, len(around), home, bond_slots),
        out_shape=[
            bead_shape,
            like(many, dtype=jnp.int32),
            like(home, bead_slots, bead_slots, dtype=bf16),
            like(home * GROUP, bead_slots),
        ],
        in_specs=[smem()] + [vmem()] * (1 + len(around)),
        out_specs=[vmem(), smem(), vmem(), vmem()],
        scratch_shapes=force_scratch(bead_slots, many, home, 1),
        compiler_params=params(),
        name="first_forces",
    )(meta, starts, *around)

    below, above = moved_along(high, "gx", 1), moved_along(low, "gx", -1)
    totals, low, high = pl.pallas_call(
        functools.partial(add_faces_x, cells),
        out_shape=[like(2, cells.rows, LANES), face_y, face_y],
        in_specs=[vmem()] * 3 + [any_spec],
        out_specs=[vmem()] * 3,
        compiler_params=params(),
        name="add_faces_x",
    )(totals, below, above, push)
    below, above = moved_along(high, "gy", 1), moved_along(low, "gy", -1)
    totals, faces = pl.pallas_call(
        functools.partial(add_faces_y, cells),
        out_shape=[like(LANES + cells.nz + GROUP, cells.rows), like(2 * GROUP, cells.rows)],
        in_specs=[vmem()] * 3,
        out_specs=[vmem()] * 2,
        scratch_shapes=[pltpu.VMEM((2, cells.rows, LANES), f32)],
        compiler_params=params(),
        name="add_faces_y",
    )(totals, below, above)
    sides = neighbours(faces, "gz")
    below, above = sides[0], sides[-1]

    table, speed, moved, pay = pl.pallas_call(
        functools.partial(finish_cells, cells),
        out_shape=[
            like(7 * cells.height, cells.inner, dtype=bf16),
            bead_shape,
            bead_shape,
            bead_shape,
        ],
        in_specs=[smem()] + [vmem()] * 8,
        out_specs=[vmem()] * 4,
        scratch_shapes=[
            pltpu.VMEM((4 * cells.height, cells.inner), f32),
            pltpu.VMEM((4 * cells.height, LANES), f32),
        ],
        compiler_params=params(),
        name="finish_cells",
    )(meta, dirs, totals, below, above, bead_rows_pos, bead_rows_vel, start, push)

    solvent_shape = like(3, rows_all, LANES)
    windows = [("gz", "gx", "gy")] + [("gx", "gy") if home == 2 else ("gz", "gx", "gy")] * 2
    cuts = sum(len(axes) for axes in windows) - 2
    step_rows = GROUP * TWIN
    steps = rows_here // step_rows
    spans = [steps // cuts + (k >= cuts - steps % cuts) for k in range(cuts)]
    spans = [(sum(spans[:k]) * step_rows, spans[k] * step_rows) for k in range(cuts)]

    held_span = 3 * face_rows
    written, pending, packed_results, tokens = [], [], [], []

    def collide_piece(piece):
        token = like(GROUP, LANES)
        whole = [solvent_shape] * 2
        write_sems = [pltpu.SemaphoreType.DMA((2,))]
        if piece < cuts:
            first, span = spans[piece]
            before = spans[piece - 1] if piece else None
            extra = pending + written
            at = 5 + len(pending)
            *outs, order = pl.pallas_call(
                functools.partial(collide_residents, cells, first, span, before),
                out_shape=whole + [like(3, span, LANES)] * 2 + [token],
                in_specs=[smem()] + [vmem()] * (4 + len(pending)) + [any_spec] * len(written),
                out_specs=[any_spec] * 2 + [vmem()] * 3,
                scratch_shapes=write_sems,
                input_output_aliases={at: 0, at + 1: 1} if written else {},
                compiler_params=params(),
                name=f"collide_{piece}",
            )(meta, dirs, table, position, velocity, *extra)
            written[:], pending[:] = outs[:2], outs[2:]
            tokens.append(order)
            return order
        before = spans[-1] if piece == cuts else None
        extra = pending + written if before else [tokens[-1]]
        outs = pl.pallas_call(
            functools.partial(
                collide_held, cells, (piece - cuts) * held_span, held_span, 6, before
            ),
            out_shape=(whole if before else [])
            + [like(6, held_span, LANES)]
            + ([token] if before else []),
            in_specs=[smem()]
            + [vmem()] * 3
            + [smem()]
            + ([vmem()] * 2 + [any_spec] * 2 if before else [any_spec]),
            out_specs=([any_spec] * 2 if before else []) + [vmem()] * (2 if before else 1),
            scratch_shapes=write_sems if before else [],
            input_output_aliases={7: 0, 8: 1} if before else {},
            compiler_params=params(),
            name=f"collide_{piece}",
        )(meta, dirs, table, held, counted, *extra)
        if before:
            written[:] = outs[:2]
            packed_results.append(outs[2])
            tokens.append(outs[3])
            return outs[3]
        packed_results.append(outs[0])
        pending[:] = pl.pallas_call(
            functools.partial(place_arrivals, face_rows, sequence),
            out_shape=[like(3, 6 * face_rows, LANES)] * 2,
            in_specs=[smem()] + [vmem()] * 2,
            out_specs=[vmem()] * 2,
            scratch_shapes=[pltpu.VMEM((6, 7 * face_rows, LANES), f32)],
            compiler_params=params(),
            name="place_arrivals",
        )(counted, *packed_results)
        return None

    piece = 0
    for step, axes in enumerate(windows):
        last = step == 2
        thunks = [functools.partial(collide_piece, piece + k) for k in range(len(axes))]
        piece += len(axes)
        ghosts, order = halo(pay, axes, home, thunks)
        final = like(3, 1, 1, 1, bead_slots)
        state = like(home * GROUP, bead_slots)
        tail = pending + written if last else [order]
        at = 6 + len(ghosts) + 2
        outcome = pl.pallas_call(
            functools.partial(
                substep,
                sizes,
                lengths,
                len(ghosts),
                home,
                step,
                (rows_here, 6 * face_rows) if last else None,
            ),
            out_shape=[final] * 2 + [solvent_shape] * 2 if last else [state] * 3,
            in_specs=[smem(), vmem(), vmem(), smem()]
            + [vmem()] * (2 + len(ghosts))
            + ([vmem()] * 2 + [any_spec] * 2 if last else [any_spec]),
            out_specs=[vmem()] * 2 + [any_spec] * 2 if last else [vmem()] * 3,
            scratch_shapes=([pltpu.SemaphoreType.DMA((2,))] if last else [])
            + force_scratch(bead_slots, many, home, 1 if last else home),
            input_output_aliases={at: 2, at + 1: 3} if last else {},
            compiler_params=params(),
            name=f"substep_{step}",
        )(meta, starts, joins, counts, speed, moved, *ghosts, *tail)
        if last:
            written[:] = outcome[2:]
        speed, moved = outcome[:2]
        pay = outcome[-1]

    count_solvent = rows_all * LANES
    return (
        written[0].reshape(3, 1, 1, 1, count_solvent),
        written[1].reshape(3, 1, 1, 1, count_solvent),
        moved,
        speed,
    )


def solution(mesh):
    return jax.shard_map(
        shards,
        mesh=mesh,
        in_specs=(
            P(None, "gx", "gy", "gz", None),
            P(None, "gx", "gy", "gz", None),
            P("gx", "gy", "gz"),
            P(None, "gx", "gy", "gz", None, None),
            P(None, "gx", "gy", "gz", None, None),
            P("gx", "gy", "gz", None),
            P(None, "gx", "gy", "gz", None),
            P(None, "gx", "gy", "gz", None),
            P("gx", "gy", "gz"),
            P(None, "gx", "gy", "gz", None),
            P("gx", "gy", "gz"),
            P(),
        ),
        out_specs=(
            P(None, "gx", "gy", "gz", None),
            P(None, "gx", "gy", "gz", None),
            P(None, "gx", "gy", "gz", None),
            P(None, "gx", "gy", "gz", None),
        ),
        check_vma=False,
    )
```
